32 devices in a mesh: ctx: 8 (over y, x, core), wt: 4 (over z).
Axes of the slice: x: 2, y: 2, z: 4, core: 2. Of those that a mesh axis runs over, the one named last changes fastest.
Arguments:
- layer_input: bfloat16 [4, 6144, 1024], P('wt', 'ctx'), may hold values from -6 to 6
- attention_gain: bfloat16 [1024], P(('ctx', 'wt')), may hold values from 0.5 to 1.5
- query_weight: bfloat16 [1024, 1024], P(('ctx', 'wt')), may hold values from -0.75 to 0.75
- key_matrix: bfloat16 [1024, 512], P(('ctx', 'wt')), may hold values from -0.75 to 0.75
- value_matrix: bfloat16 [1024, 512], P(('ctx', 'wt')), may hold values from -0.5 to 0.5
- output_weight: bfloat16 [1024, 1024], P(None, ('ctx', 'wt')), may hold values from -1.75 to 1.75
- mixture_gain: bfloat16 [1024], P(('ctx', 'wt')), may hold values from 0.5 to 1.5
- router_weight: bfloat16 [1024, 32], P(('ctx', 'wt')), may hold values from -0.09375 to 0.09375
- gate_weight: bfloat16 [32, 1024, 512], P('wt', 'ctx'), may hold values from -0.375 to 0.375
- up_weight: bfloat16 [32, 1024, 512], P('wt', 'ctx'), may hold values from -0.375 to 0.375
- down_weight: bfloat16 [32, 512, 1024], P('wt', None, 'ctx'), may hold values from -1.5 to 1.5
- expert_routes: int32 [4, 6144, 8], P('wt', 'ctx'), may hold values from 0 to 31, all different within a row; in each aligned block of 768 rows (0 to 767, 768 to 1535, ..., all dimensions but the last counted through in order) at most 336 rows name the same one
- prompt_deal: int32 [4, 16], P('wt'), may hold values from 0 to 15, as said below
- output_grad: bfloat16 [4, 6144, 1024], P('wt', 'ctx'), may hold values from -6 to 6
Outputs:
- layer_output: bfloat16 [4, 6144, 1024], P('wt', 'ctx')
- input_grad: bfloat16 [4, 6144, 1024], P('wt', 'ctx')
- attention_gain_grad: float32 [1024], P(('ctx', 'wt'))
- query_grad: float32 [1024, 1024], P(('ctx', 'wt'))
- key_grad: float32 [1024, 512], P(('ctx', 'wt'))
- value_grad: float32 [1024, 512], P(('ctx', 'wt'))
- output_proj_grad: float32 [1024, 1024], P(None, ('ctx', 'wt'))
- mixture_gain_grad: float32 [1024], P(('ctx', 'wt'))
- router_grad: float32 [1024, 32], P(('ctx', 'wt'))
- gate_grad: float32 [32, 1024, 512], P('wt', 'ctx')
- up_grad: float32 [32, 1024, 512], P('wt', 'ctx')
- down_grad: float32 [32, 512, 1024], P('wt', None, 'ctx')
The draws below stay inside these ranges and needn't reach their ends.
Inputs may be any that keep to these rules, and one draw needn't show every extreme that they name: `expert_routes`: each token names 8 different experts. In the 768 rows of one device (aligned blocks of the first two dimensions taken together), no expert is named by more than 336 tokens, and in some block one expert is named by exactly 336. `prompt_deal`: each row is a permutation of the prompt's 16 blocks of 128 tokens; entries 2c and 2c + 1 add up to 15.
All inputs are finite; a program needn't handle non-finite values.
Results may differ from the reference program's by a relative error of at most 0.02.
Values may be sent and summed in bfloat16 or wider, within the bound.
A program may use at most 384 MiB of HBM per device.

```python
import math
import jax
import jax.numpy as jnp
import numpy as np
from jax import lax

MODEL_WIDTH = 1024
HQ = 16
KEY_VALUE_HEADS = 8
HEAD_SIZE = 64
FF = 512
EXPERTS = 32
TOP = 8
PROMPT = 2048
CLEN = 256
CONT_DEV = 2
QUERIES_PER_KEY = 2
PBLOCKS = 16
PBLK = 128
PDEV = 256
TOK_DEV = 768
TOK_CTX = 6144
GROUPS = 4
CONTS = 16
CAP = 336
N_CTX = 8


def draw_prompt_deal(key, part):
    order_key = jax.random.fold_in(key, 17)
    flip_key = jax.random.fold_in(key, 29)
    pair_count = PBLOCKS // 2
    base = jnp.broadcast_to(jnp.arange(pair_count, dtype=jnp.int32)[None, :], (GROUPS, pair_count))
    shuffled = jax.random.permutation(order_key, base, axis=1, independent=True)
    flips = jax.random.randint(flip_key, (GROUPS, pair_count), 0, 2, dtype=jnp.int32)
    first = jnp.where(flips == 1, PBLOCKS - 1 - shuffled, shuffled)
    second = PBLOCKS - 1 - first
    return jnp.stack([first, second], 2).reshape(GROUPS, PBLOCKS).astype(jnp.int32)


def level_of(stream_key, extent, shards, smallest, high):
    loudness, own = 1.0, jax.random.fold_in(stream_key, 6)
    for axis_at, parts in shards:
        heights = jnp.exp(jax.random.uniform(jax.random.fold_in(own, axis_at), (parts,), jnp.float32, smallest / len(shards), high / len(shards)))
        loudness = loudness * jnp.repeat(heights, extent[axis_at] // parts).reshape([-1 if axis == axis_at else 1 for axis in range(len(extent))])
    return loudness


def deal_out(stream_key, own, number, rows, amount, top, bound, slope):
    order = jax.random.permutation(stream_key, amount)
    heavy_load, common = shares(amount, rows * top, bound, slope, True), shares(amount, rows * top, bound, slope, False)
    places = jnp.arange(amount)

    def named(tallies, turn):
        used = int((tallies > 0).sum())
        fixed = max(1, used // 4)
        moved = fixed + (places - fixed + turn * (used - fixed)) % max(1, amount - fixed)
        return jnp.zeros((amount,), jnp.int32).at[order[jnp.where(places < fixed, places, moved)]].set(jnp.asarray(tallies, jnp.int32))

    tallies = jnp.where(number % 4 == 0, named(heavy_load, number // 4), named(common, number - number // 4 - 1))
    mixed = jax.random.permutation(jax.random.fold_in(own, 3), amount)
    source_of, sink = mixed[0:amount // 2 * 2:2], mixed[1:amount // 2 * 2:2]
    room = jnp.minimum(tallies[source_of] - 1, bound - tallies[sink]) // 2
    room = jnp.where((source_of == order[0]) | (sink == order[0]) | (tallies[sink] == 0), 0, jnp.maximum(room, 0))
    moved = jax.random.randint(jax.random.fold_in(own, 4), (amount // 2,), 0, 1 << 20) % (room + 1)
    tallies = tallies.at[source_of].add(-moved).at[sink].add(moved)
    labels = jnp.searchsorted(jnp.cumsum(tallies), jnp.arange(rows * top), side="right").astype(jnp.int32)
    listing = labels.reshape(top, rows).T
    listing = listing[jax.random.permutation(jax.random.fold_in(own, 1), rows)]
    turn = jax.random.randint(jax.random.fold_in(own, 2), (rows, 1), 0, top)
    return jnp.take_along_axis(listing, (jnp.arange(top)[None, :] + turn) % top, axis=1)


def shares(amount, total, most, slope, full):
    weights = [(1 << 20) // math.isqrt(rank ** slope) + 1 for rank in range(1, amount + 1)]
    largest = most if full else min(most, max(-(-total // amount), total * weights[0] // sum(weights)))
    least = 1 if total - largest >= amount - 1 else 0
    holding, rest = [largest] + [least] * (amount - 1), total - largest - least * (amount - 1)
    while rest > 0:
        candidates = [i for i in range(1, amount) if holding[i] < largest] or [i for i in range(1, amount) if holding[i] < most]
        mass, budget = sum([weights[i] for i in candidates]), rest
        for i in candidates:
            more = min(most - holding[i], max(1, budget * weights[i] // mass), rest)
            holding[i] = holding[i] + more
            rest = rest - more
    return np.array(holding)


def centred(key, extent, width, reach, split=(), held_as=jnp.bfloat16):
    level = level_of(key, extent, split, -0.22, 0.18) if split else 1.0
    drawn = jax.random.normal(key, extent, jnp.float32) * width * level
    return jnp.minimum(jnp.maximum(drawn, -reach), reach).astype(held_as)


def setup_inputs(seed: int = 0) -> dict:
    key_list = jax.random.split(jax.random.key(seed), 15)
    layer_input = centred(key_list[0], (GROUPS, TOK_CTX, MODEL_WIDTH), 1.0, 6.0, ((0, 4), (1, 8)))
    attention_gain = jnp.clip(1.0 + 0.1 * jax.random.normal(key_list[1], (MODEL_WIDTH,), jnp.float32), 0.5, 1.5).astype(jnp.bfloat16)
    query_weight = centred(key_list[2], (MODEL_WIDTH, HQ * HEAD_SIZE), (4.0 / MODEL_WIDTH ** 0.5), 0.75, ((0, 32),))
    key_matrix = centred(key_list[3], (MODEL_WIDTH, KEY_VALUE_HEADS * HEAD_SIZE), (4.0 / MODEL_WIDTH ** 0.5), 0.75, ((0, 32),))
    value_matrix = centred(key_list[4], (MODEL_WIDTH, KEY_VALUE_HEADS * HEAD_SIZE), (3.0 / MODEL_WIDTH ** 0.5), 0.5, ((0, 32),))
    output_weight = centred(key_list[5], (HQ * HEAD_SIZE, MODEL_WIDTH), (9.6 / (HQ * HEAD_SIZE) ** 0.5), 1.75, ((1, 32),))
    mixture_gain = jnp.clip(1.0 + 0.1 * jax.random.normal(key_list[6], (MODEL_WIDTH,), jnp.float32), 0.5, 1.5).astype(jnp.bfloat16)
    router_weight = centred(key_list[7], (MODEL_WIDTH, EXPERTS), (0.5 / MODEL_WIDTH ** 0.5), 0.09375, ((0, 32),))
    gate_weight = centred(key_list[8], (EXPERTS, MODEL_WIDTH, FF), (2.0 / MODEL_WIDTH ** 0.5), 0.375, ((0, 4), (1, 8)))
    up_weight = centred(key_list[9], (EXPERTS, MODEL_WIDTH, FF), (2.0 / MODEL_WIDTH ** 0.5), 0.375, ((0, 4), (1, 8)))
    down_weight = centred(key_list[10], (EXPERTS, FF, MODEL_WIDTH), (5.6 / FF ** 0.5), 1.5, ((0, 4), (2, 8)))
    expert_routes_keys = jax.random.split(jax.random.fold_in(key_list[11], 1), GROUPS * TOK_CTX // TOK_DEV)
    expert_routes_turns = jax.random.permutation(jax.random.fold_in(key_list[11], 3), GROUPS * TOK_CTX // TOK_DEV)
    expert_routes = jax.vmap(lambda own, number: deal_out(jax.random.fold_in(key_list[11], 2), own, number, TOK_DEV, EXPERTS, TOP, CAP, 1))(expert_routes_keys, expert_routes_turns).reshape((GROUPS, TOK_CTX, TOP))
    prompt_deal = draw_prompt_deal(jax.random.fold_in(key_list[14], 71), 0)
    output_grad = centred(key_list[13], (GROUPS, TOK_CTX, MODEL_WIDTH), 1.0, 6.0, ((0, 4), (1, 8)))
    return {"layer_input": layer_input, "attention_gain": attention_gain, "query_weight": query_weight, "key_matrix": key_matrix, "value_matrix": value_matrix, "output_weight": output_weight, "mixture_gain": mixture_gain, "router_weight": router_weight, "gate_weight": gate_weight, "up_weight": up_weight, "down_weight": down_weight, "expert_routes": expert_routes, "prompt_deal": prompt_deal, "output_grad": output_grad}


att_scale = 0.015625
resid_scale = 0.22
norm_eps = 1e-06
rope_base = 10000.0
masked_score = -1e+30
highest = lax.Precision.HIGHEST

@jax.custom_vjp
def narrow_precise(v):
    return lax.optimization_barrier(v.astype(jnp.bfloat16)).astype(jnp.float32)

@jax.custom_vjp
def low_back(v):
    return v

def low_keep(v):
    return (narrow_precise(v), None)

def low_pass(kept, grad):
    return (grad,)

def back_keep(v):
    return (v, None)

def back_low(kept, grad):
    return (narrow_precise(grad),)
narrow_precise.defvjp(low_keep, low_pass)
low_back.defvjp(back_keep, back_low)

def matmul(left, right):
    return jnp.dot(left, right, precision=highest, preferred_element_type=jnp.float32)

def rms_scale(values, gain):
    return values * lax.rsqrt(lax.optimization_barrier(jnp.mean(values * values, -1, keepdims=True)) + norm_eps) * gain

def rope_tables(positions):
    middle = HEAD_SIZE // 2
    frequency = jnp.power(jnp.float32(rope_base), -2.0 * jnp.arange(middle, dtype=jnp.float32) / HEAD_SIZE)
    angles = positions.astype(jnp.float32)[:, None] * frequency[None, :]
    cosine_table = jnp.cos(angles)
    sinusoid_table = jnp.sin(angles)
    return (jnp.concatenate([cosine_table, cosine_table], 1), jnp.concatenate([sinusoid_table, sinusoid_table], 1))

def apply_turning(values, cosine_table, sinusoid_table, heads, direction):
    shaped = values.reshape(values.shape[0], heads, HEAD_SIZE)
    middle = HEAD_SIZE // 2
    turned = jnp.concatenate([-shaped[..., middle:], shaped[..., :middle]], -1)
    rotated = shaped * cosine_table[:, None, :] + direction * turned * sinusoid_table[:, None, :]
    return rotated.reshape(values.shape)

def token_positions(deal_row):
    local_rows = jnp.arange(TOK_DEV, dtype=jnp.int32)[None, :]
    device_rows = jnp.arange(N_CTX, dtype=jnp.int32)[:, None]
    slot_index = jnp.minimum(2 * device_rows + local_rows // PBLK, PBLOCKS - 1)
    prompt_place = deal_row[slot_index] * PBLK + local_rows % PBLK
    later_place = PROMPT + (local_rows - PDEV) % CLEN
    return jnp.where(local_rows < PDEV, prompt_place, later_place).reshape(TOK_CTX)

def attend(query_row_matrix, key_row_matrix, value_row_matrix, allowed):
    count_of_rows = query_row_matrix.shape[0]
    reshaped_query = query_row_matrix.reshape(count_of_rows, KEY_VALUE_HEADS, QUERIES_PER_KEY, HEAD_SIZE)
    reshaped_key = key_row_matrix.reshape(key_row_matrix.shape[0], KEY_VALUE_HEADS, HEAD_SIZE)
    reshaped_value = value_row_matrix.reshape(value_row_matrix.shape[0], KEY_VALUE_HEADS, HEAD_SIZE)
    scores = att_scale * jnp.einsum('tgrd,kgd->grtk', reshaped_query, reshaped_key, precision=highest)
    scores = jnp.where(allowed[None, None], low_back(scores), masked_score)
    row_max = lax.optimization_barrier(jnp.max(scores, -1, keepdims=True))
    exponent = jnp.exp(scores - row_max)
    probability = exponent / lax.optimization_barrier(jnp.sum(exponent, -1, keepdims=True))
    attended = jnp.einsum('grtk,kgd->tgrd', narrow_precise(probability), reshaped_value, precision=highest)
    return attended.reshape(count_of_rows, HQ * HEAD_SIZE)

def group_attention(turned_query, spun_key, values, deal_row):
    block_slot = jnp.zeros((PBLOCKS,), jnp.int32).at[deal_row].set(jnp.arange(PBLOCKS, dtype=jnp.int32))
    prompt_place = jnp.arange(PROMPT, dtype=jnp.int32)
    slot_index = block_slot[prompt_place // PBLK]
    prompt_rows = slot_index // 2 * TOK_DEV + slot_index % 2 * PBLK + prompt_place % PBLK
    later_index = jnp.arange(CONTS, dtype=jnp.int32)
    later_start = later_index // CONT_DEV * TOK_DEV + PDEV + later_index % CONT_DEV * CLEN
    later_rows = later_start[:, None] + jnp.arange(CLEN, dtype=jnp.int32)[None, :]
    prompt_query = turned_query[prompt_rows]
    prompt_key = spun_key[prompt_rows]
    prompt_value = values[prompt_rows]
    block_rows = min(512, PROMPT)

    def prompt_block(number):
        offset = number * block_rows
        block_query = lax.dynamic_slice_in_dim(prompt_query, offset, block_rows, 0)
        query_place = offset + jnp.arange(block_rows, dtype=jnp.int32)
        allowed = prompt_place[None, :] <= query_place[:, None]
        return attend(block_query, prompt_key, prompt_value, allowed)
    prompt_out = lax.map(jax.checkpoint(prompt_block), jnp.arange(PROMPT // block_rows, dtype=jnp.int32))
    triangle = jnp.arange(CLEN, dtype=jnp.int32)[None, :] <= jnp.arange(CLEN, dtype=jnp.int32)[:, None]
    later_allowed = jnp.concatenate([jnp.ones((CLEN, PROMPT), jnp.bool_), triangle], 1)

    def later_block(row_index):
        key_row_matrix = jnp.concatenate([prompt_key, spun_key[row_index]], 0)
        value_row_matrix = jnp.concatenate([prompt_value, values[row_index]], 0)
        return attend(turned_query[row_index], key_row_matrix, value_row_matrix, later_allowed)
    later_out = lax.map(jax.checkpoint(later_block), later_rows)
    merged = jnp.zeros((TOK_CTX, HQ * HEAD_SIZE), jnp.float32)
    merged = merged.at[prompt_rows].set(prompt_out.reshape(PROMPT, HQ * HEAD_SIZE))
    return merged.at[later_rows.reshape(-1)].set(later_out.reshape(CONTS * CLEN, HQ * HEAD_SIZE))

def expert_tables(group_routes):
    pairs = group_routes.reshape(N_CTX, TOK_DEV * TOP)
    selection = (pairs[:, :, None] == jnp.arange(EXPERTS, dtype=jnp.int32)[None, None, :]).astype(jnp.int32)
    slot_numbers = lax.optimization_barrier(jnp.sum((jnp.cumsum(selection, 1) - selection) * selection, 2))
    block_index = jnp.broadcast_to(jnp.arange(N_CTX, dtype=jnp.int32)[:, None], pairs.shape)
    pair_index = block_index * (TOK_DEV * TOP) + jnp.arange(TOK_DEV * TOP, dtype=jnp.int32)[None, :]
    slot_table = jnp.full((EXPERTS, N_CTX, CAP), -1, jnp.int32).at[pairs, block_index, slot_numbers].set(pair_index)
    position = (pairs * N_CTX + block_index) * CAP + slot_numbers
    return (slot_table.reshape(EXPERTS, N_CTX * CAP), position.reshape(TOK_CTX, TOP))

def group_layer(params, group_input, group_routes, deal_row):
    first_gain, query_float, key_float, value_float, output_float, second_gain, router_float, gate_float, up_float, down_float = params
    normed_one = narrow_precise(rms_scale(group_input, first_gain))
    raw_queries = low_back(matmul(normed_one, query_float))
    unrotated_keys = low_back(matmul(normed_one, key_float))
    values = narrow_precise(low_back(matmul(normed_one, value_float)))
    cosine_table, sinusoid_table = rope_tables(token_positions(deal_row))
    turned_query = narrow_precise(apply_turning(raw_queries, cosine_table, sinusoid_table, HQ, 1.0))
    spun_key = narrow_precise(apply_turning(unrotated_keys, cosine_table, sinusoid_table, KEY_VALUE_HEADS, 1.0))
    attended = low_back(narrow_precise(group_attention(turned_query, spun_key, values, deal_row)))
    branch = low_back(matmul(attended, output_float))
    middle = group_input + resid_scale * branch
    normed_two = narrow_precise(rms_scale(middle, second_gain))
    logits = low_back(matmul(normed_two, router_float))
    gates = jax.nn.softmax(jnp.take_along_axis(logits, group_routes, 1), -1)
    slot_table, position = expert_tables(group_routes)

    def expert_apply(packed):
        table_row, gate_one, up_one, down_one = packed
        live_rows = (table_row >= 0).astype(jnp.float32)
        pair_index = jnp.maximum(table_row, 0)
        routed_rows = low_back(normed_two[pair_index // TOP]) * live_rows[:, None]
        gate_part = low_back(matmul(routed_rows, gate_one))
        up_part = low_back(matmul(routed_rows, up_one))
        activated = narrow_precise(jax.nn.silu(gate_part) * up_part)
        return narrow_precise(low_back(matmul(activated, down_one)))
    outputs = lax.map(jax.checkpoint(expert_apply), (slot_table, gate_float, up_float, down_float))
    picked = outputs.reshape(-1, MODEL_WIDTH)[position]
    mixture = jnp.einsum('tk,tkd->td', gates, picked, precision=highest)
    return middle + resid_scale * mixture

def reference(layer_input, attention_gain, query_weight, key_matrix, value_matrix, output_weight, mixture_gain, router_weight, gate_weight, up_weight, down_weight, expert_routes, prompt_deal, output_grad):

    def whole(inputs, first_gain, query_float, key_float, value_float, output_float, second_gain, router_float, gate_float, up_float, down_float):
        params = (first_gain, query_float, key_float, value_float, output_float, second_gain, router_float, gate_float, up_float, down_float)

        def one_group(packed):
            group_input, group_routes, deal_row = packed
            return group_layer(params, group_input, group_routes, deal_row)
        return lax.map(jax.checkpoint(one_group), (inputs, expert_routes, prompt_deal))
    result, pullback = jax.vjp(whole, layer_input.astype(jnp.float32), attention_gain.astype(jnp.float32), query_weight.astype(jnp.float32), key_matrix.astype(jnp.float32), value_matrix.astype(jnp.float32), output_weight.astype(jnp.float32), mixture_gain.astype(jnp.float32), router_weight.astype(jnp.float32), gate_weight.astype(jnp.float32), up_weight.astype(jnp.float32), down_weight.astype(jnp.float32))
    grads = pullback(output_grad.astype(jnp.float32))
    return (result.astype(jnp.bfloat16), grads[0].astype(jnp.bfloat16), grads[1], grads[2], grads[3], grads[4], grads[5], grads[6], grads[7], grads[8], grads[9], grads[10])
```

```python
import functools

import jax
import jax.numpy as jnp
from jax import lax
from jax.experimental import pallas as pl
from jax.experimental.pallas import tpu as pltpu
from jax.sharding import PartitionSpec as P

MODEL_WIDTH = 1024
HQ = 16
KEY_VALUE_HEADS = 8
HEAD_SIZE = 64
EXPERTS = 32
TOP = 8
PROMPT = 2048
CLEN = 256
CONT_DEV = 2
FF = 512
QTILE = 128
KV_WIDTH = KEY_VALUE_HEADS * HEAD_SIZE
ALL = ("ctx", "wt")

att_scale = 0.015625
resid_scale = 0.22
norm_eps = 1e-06
rope_base = 10000.0
masked_score = -1e30

bf16 = jnp.bfloat16
f32 = jnp.float32
VMEM_LIMIT = 60 * 1024 * 1024

NT = (((1,), (1,)), ((), ()))
TN = (((0,), (0,)), ((), ()))


def dot(a, b):
    return jnp.dot(a, b, preferred_element_type=f32)


def dot_nt(a, b):
    return lax.dot_general(a, b, NT, preferred_element_type=f32)


def dot_tn(a, b):
    return lax.dot_general(a, b, TN, preferred_element_type=f32)


def turn_tile(values, cosine, sine, direction):
    middle = HEAD_SIZE // 2
    first = lax.broadcasted_iota(jnp.int32, values.shape, 1) % HEAD_SIZE < middle
    turned = jnp.where(first, -pltpu.roll(values, 128 - middle, 1), pltpu.roll(values, middle, 1))
    return values * cosine + direction * turned * sine


def project_kernel(places, x_ref, cos_ref, sin_ref, *refs, counts):
    pieces = refs[: len(counts)]
    normed_ref, q_ref, kv_ref, qkv_ref, out_ref, rest_ref, gains_ref = refs[len(counts) :]
    rows = MODEL_WIDTH // sum(counts)
    at = 0
    for piece, count in zip(pieces, counts):
        for i in range(count):
            source = slice(i * rows, (i + 1) * rows)
            target = pl.ds(pl.multiple_of(places[at] * rows, rows), rows)
            qkv_ref[target, :] = piece[source, :2048]
            out_ref[target, :] = piece[source, 2048:3072]
            rest_ref[target, :] = piece[source, 3072:]
            at += 1
    gains = rest_ref[...].astype(f32).T[EXPERTS : EXPERTS + 8]
    gains_ref[...] = gains
    x = x_ref[...].astype(f32)
    inverse = lax.rsqrt(jnp.mean(x * x, -1, keepdims=True) + norm_eps)
    normed_ref[...] = (x * inverse * gains[:1]).astype(bf16)
    for c in range(8):
        raw = dot(normed_ref[...], qkv_ref[:, 256 * c : 256 * (c + 1)])
        for h in range(2):
            part = raw[:, 128 * h : 128 * (h + 1)]
            if c < 6:
                part = turn_tile(part, cos_ref[...], sin_ref[...], 1.0)
            column = 256 * c + 128 * h
            if column < 1024:
                q_ref[:, column : column + 128] = part.astype(bf16)
            else:
                kv_ref[:, column - 1024 : column - 896] = part.astype(bf16)


def project(x, cosine, sine, pieces, counts, places):
    tok = x.shape[0]
    shape = jax.ShapeDtypeStruct
    whole = pl.BlockSpec(memory_space=pltpu.VMEM)
    return pl.pallas_call(
        functools.partial(project_kernel, counts=counts),
        in_specs=[pl.BlockSpec(memory_space=pltpu.SMEM)] + [whole] * (3 + len(pieces)),
        out_specs=[whole] * 7,
        out_shape=[
            shape((tok, MODEL_WIDTH), bf16),
            shape((tok, HQ * HEAD_SIZE), bf16),
            shape((tok, 2 * KV_WIDTH), bf16),
            shape((MODEL_WIDTH, 2048), bf16),
            shape((MODEL_WIDTH, 1024), bf16),
            shape((MODEL_WIDTH, 128), bf16),
            shape((8, MODEL_WIDTH), f32),
        ],
        compiler_params=pltpu.CompilerParams(vmem_limit_bytes=VMEM_LIMIT),
        cost_estimate=pl.CostEstimate(
            flops=3_300_000_000, bytes_accessed=22_000_000, transcendentals=0
        ),
        name="project",
    )(places, x, cosine, sine, *pieces)


def outer_kernel(mine, a_ref, b_ref, out_ref):
    out_ref[...] = dot_tn(a_ref[...], b_ref[...]).astype(bf16)


def outer(a, b):
    tok, columns = b.shape
    mine = lax.axis_index("ctx").astype(jnp.int32).reshape(1)
    return pl.pallas_call(
        outer_kernel,
        grid_spec=pltpu.PrefetchScalarGridSpec(
            num_scalar_prefetch=1,
            grid=(8,),
            in_specs=[
                pl.BlockSpec((tok, 128), lambda m, mine: (0, m ^ mine[0])),
                pl.BlockSpec((tok, columns), lambda m, mine: (0, 0)),
            ],
            out_specs=pl.BlockSpec((128, columns), lambda m, mine: (m, 0)),
        ),
        out_shape=jax.ShapeDtypeStruct((MODEL_WIDTH, columns), bf16),
        compiler_params=pltpu.CompilerParams(vmem_limit_bytes=VMEM_LIMIT),
        cost_estimate=pl.CostEstimate(
            flops=2 * tok * MODEL_WIDTH * columns, bytes_accessed=8_000_000, transcendentals=0
        ),
        name="outer",
    )(mine, a, b)


def gather_keys(k_ref, scratch, slots, block_rows):
    for b in range(PROMPT // block_rows):
        start = pl.multiple_of(slots[b] * block_rows, block_rows)
        scratch[b * block_rows : (b + 1) * block_rows, :] = k_ref[pl.ds(start, block_rows), :]


def pair_rows(ref, start, rows, j):
    both = ref[pl.ds(start, rows), 2 * HEAD_SIZE * j : 2 * HEAD_SIZE * (j + 1)]
    return jnp.concatenate([both[:, :HEAD_SIZE], both[:, HEAD_SIZE:]], 0)


def attention_forward_kernel(
    slots, starts, q_ref, k_ref, v_ref, kc_ref, vc_ref, o_ref, lse_ref, k_scr, v_scr, *, block_rows
):
    tok = q_ref.shape[0]
    prompt_local = 2 * block_rows
    gather_keys(k_ref, k_scr, slots, block_rows)
    gather_keys(v_ref, v_scr, slots, block_rows)

    def store(start, rows, j, out, m, total, at):
        out = (out / total).astype(bf16)
        lse = m + jnp.log(total)
        o_ref[pl.ds(start, rows), 2 * HEAD_SIZE * j : 2 * HEAD_SIZE * (j + 1)] = jnp.concatenate(
            [out[:rows], out[rows:]], 1
        )
        row = jnp.broadcast_to(lse, (2 * rows, 128)).T[:1]
        lse_ref[0, 2 * j : 2 * j + 2, pl.ds(at, rows)] = jnp.concatenate(
            [row[:, :rows], row[:, rows:]], 0
        )

    for j in range(2):
        lanes = slice(HEAD_SIZE * j, HEAD_SIZE * (j + 1))

        def tile(i, _):
            start = pl.multiple_of(prompt_local + i * QTILE, 64)
            per = CLEN // QTILE
            seg = pl.multiple_of((i // per) * CLEN, CLEN)
            q = pair_rows(q_ref, start, QTILE, j) * bf16(att_scale)
            s1 = dot_nt(q, k_scr[:, lanes])
            s2 = dot_nt(q, kc_ref[pl.ds(seg, CLEN), lanes])
            place = lax.broadcasted_iota(jnp.int32, s2.shape, 0) % QTILE + (i % per) * QTILE
            s2 = jnp.where(lax.broadcasted_iota(jnp.int32, s2.shape, 1) <= place, s2, masked_score)
            m = jnp.maximum(jnp.max(s1, 1, keepdims=True), jnp.max(s2, 1, keepdims=True))
            e1 = jnp.exp(s1 - m)
            e2 = jnp.exp(s2 - m)
            total = jnp.sum(e1, 1, keepdims=True) + jnp.sum(e2, 1, keepdims=True)
            out = dot(e1.astype(bf16), v_scr[:, lanes])
            out = out + dot(e2.astype(bf16), vc_ref[pl.ds(seg, CLEN), lanes])
            store(start, QTILE, j, out, m, total, pl.multiple_of(i * QTILE, QTILE))
            return 0

        lax.fori_loop(0, CONT_DEV * CLEN // QTILE, tile, 0)

        for half, keys in enumerate((PROMPT // 2, PROMPT)):
            start = pl.multiple_of(starts[half], block_rows)
            q = pair_rows(q_ref, start, block_rows, j) * bf16(att_scale)
            s = dot_nt(q, k_scr[:keys, lanes])
            place = lax.broadcasted_iota(jnp.int32, s.shape, 0) % block_rows + starts[2 + half]
            s = jnp.where(lax.broadcasted_iota(jnp.int32, s.shape, 1) <= place, s, masked_score)
            m = jnp.max(s, 1, keepdims=True)
            e = jnp.exp(s - m)
            total = jnp.sum(e, 1, keepdims=True)
            out = dot(e.astype(bf16), v_scr[:keys, lanes])
            store(
                start, block_rows, j, out, m, total, CONT_DEV * CLEN + half * block_rows
            )


def attention_forward(q, kv, kv_own, slots, starts, block_rows):
    tok = q.shape[0]
    own = kv_own.shape[0]
    pairs = KEY_VALUE_HEADS // 2
    spec = pl.BlockSpec
    return pl.pallas_call(
        functools.partial(attention_forward_kernel, block_rows=block_rows),
        grid_spec=pltpu.PrefetchScalarGridSpec(
            num_scalar_prefetch=2,
            grid=(pairs,),
            in_specs=[
                spec((tok, 4 * HEAD_SIZE), lambda g, *_: (0, g)),
                spec((PROMPT, 2 * HEAD_SIZE), lambda g, *_: (0, g)),
                spec((PROMPT, 2 * HEAD_SIZE), lambda g, *_: (0, pairs + g)),
                spec((own, 2 * HEAD_SIZE), lambda g, *_: (0, g)),
                spec((own, 2 * HEAD_SIZE), lambda g, *_: (0, pairs + g)),
            ],
            out_specs=[
                spec((tok, 4 * HEAD_SIZE), lambda g, *_: (0, g)),
                spec((1, 4, tok), lambda g, *_: (g, 0, 0)),
            ],
            scratch_shapes=[
                pltpu.VMEM((PROMPT, 2 * HEAD_SIZE), bf16),
                pltpu.VMEM((PROMPT, 2 * HEAD_SIZE), bf16),
            ],
        ),
        out_shape=[
            jax.ShapeDtypeStruct((tok, HQ * HEAD_SIZE), bf16),
            jax.ShapeDtypeStruct((pairs, 4, tok), f32),
        ],
        compiler_params=pltpu.CompilerParams(vmem_limit_bytes=VMEM_LIMIT),
        cost_estimate=pl.CostEstimate(
            flops=60_000_000_000, bytes_accessed=12_000_000, transcendentals=25_000_000
        ),
        name="attention_forward",
    )(slots, starts, q, kv, kv, kv_own, kv_own)


def attention_backward_kernel(
    slots,
    starts,
    q_ref,
    do_ref,
    k_ref,
    v_ref,
    kc_ref,
    vc_ref,
    lse_ref,
    o_ref,
    cos_ref,
    sin_ref,
    dq_ref,
    dk_ref,
    dv_ref,
    dkc_ref,
    dvc_ref,
    k_scr,
    v_scr,
    dk_acc,
    dv_acc,
    dq_acc,
    *,
    block_rows,
):
    prompt_local = 2 * block_rows
    gather_keys(k_ref, k_scr, slots, block_rows)
    gather_keys(v_ref, v_scr, slots, block_rows)
    dk_acc[...] = jnp.zeros_like(dk_acc)
    dv_acc[...] = jnp.zeros_like(dv_acc)
    dkc_ref[...] = jnp.zeros_like(dkc_ref)
    dvc_ref[...] = jnp.zeros_like(dvc_ref)

    def row_pair(ref, start, rows, j):
        both = ref[0, 2 * j : 2 * j + 2, pl.ds(start, rows)]
        return jnp.concatenate([both[:1], both[1:]], 1)

    def centre(start, rows, j, d_out):
        product = d_out.astype(f32) * pair_rows(o_ref, start, rows, j).astype(f32)
        ones = jnp.ones((8, HEAD_SIZE), f32)
        return lax.dot_general(
            ones, product, NT, precision=lax.Precision.HIGHEST, preferred_element_type=f32
        )[:1]

    def part(k, v, q, d_out, lse, delta, allowed):
        s = dot_nt(k, q)
        if allowed is not None:
            s = jnp.where(allowed(s.shape), s, masked_score)
        p = jnp.exp(s - lse)
        d_p = dot_nt(v, d_out)
        d_s = (p * (d_p - delta)).astype(bf16)
        return dot_tn(d_s, k), dot(d_s, q), dot(p.astype(bf16), d_out)

    def store(start, rows, j, d_q):
        d_q = d_q * att_scale
        dq_acc[pl.ds(start, rows), 2 * HEAD_SIZE * j : 2 * HEAD_SIZE * (j + 1)] = jnp.concatenate(
            [d_q[:rows], d_q[rows:]], 1
        )

    for j in range(2):
        lanes = slice(HEAD_SIZE * j, HEAD_SIZE * (j + 1))

        def tile(i, _):
            start = pl.multiple_of(prompt_local + i * QTILE, 64)
            per = CLEN // QTILE
            seg = pl.multiple_of((i // per) * CLEN, CLEN)
            own = pl.ds(seg, CLEN)
            q = pair_rows(q_ref, start, QTILE, j) * bf16(att_scale)
            d_out = pair_rows(do_ref, start, QTILE, j)
            lane_start = pl.multiple_of(i * QTILE, QTILE)
            lse = row_pair(lse_ref, lane_start, QTILE, j)
            delta = centre(start, QTILE, j, d_out)

            def allowed(shape):
                place = lax.broadcasted_iota(jnp.int32, shape, 1) % QTILE + (i % per) * QTILE
                return lax.broadcasted_iota(jnp.int32, shape, 0) <= place

            a, b, c = part(k_scr[:, lanes], v_scr[:, lanes], q, d_out, lse, delta, None)
            dk_acc[:, lanes] += b
            dv_acc[:, lanes] += c
            d_q = a
            a, b, c = part(
                kc_ref[own, lanes], vc_ref[own, lanes], q, d_out, lse, delta, allowed
            )
            dkc_ref[own, lanes] += b
            dvc_ref[own, lanes] += c
            store(start, QTILE, j, d_q + a)
            return 0

        lax.fori_loop(0, CONT_DEV * CLEN // QTILE, tile, 0)

        for half, keys in enumerate((PROMPT // 2, PROMPT)):
            start = pl.multiple_of(starts[half], block_rows)
            q = pair_rows(q_ref, start, block_rows, j) * bf16(att_scale)
            d_out = pair_rows(do_ref, start, block_rows, j)
            at = CONT_DEV * CLEN + half * block_rows
            lse = row_pair(lse_ref, at, block_rows, j)
            delta = centre(start, block_rows, j, d_out)

            def allowed(shape):
                place = lax.broadcasted_iota(jnp.int32, shape, 1) % block_rows + starts[2 + half]
                return lax.broadcasted_iota(jnp.int32, shape, 0) <= place

            a, b, c = part(
                k_scr[:keys, lanes], v_scr[:keys, lanes], q, d_out, lse, delta, allowed
            )
            dk_acc[:keys, lanes] += b
            dv_acc[:keys, lanes] += c
            store(start, block_rows, j, a)

    for b in range(PROMPT // block_rows):
        start = pl.multiple_of(slots[b] * block_rows, block_rows)
        rows = slice(b * block_rows, (b + 1) * block_rows)
        dk_ref[pl.ds(start, block_rows), :] = dk_acc[rows, :].astype(bf16)
        dv_ref[pl.ds(start, block_rows), :] = dv_acc[rows, :].astype(bf16)
    for c in range(2):
        lanes = slice(128 * c, 128 * (c + 1))
        dq_ref[:, lanes] = turn_tile(dq_acc[:, lanes], cos_ref[...], sin_ref[...], -1.0).astype(
            bf16
        )


def attention_backward(
    q, d_out, kv, kv_own, lse, attended, cosine, sine, slots, starts, block_rows
):
    tok = q.shape[0]
    own = kv_own.shape[0]
    pairs = KEY_VALUE_HEADS // 2
    spec = pl.BlockSpec
    wide = spec((tok, 4 * HEAD_SIZE), lambda g, *_: (0, g))
    first = spec((PROMPT, 2 * HEAD_SIZE), lambda g, *_: (0, g))
    first_own = spec((own, 2 * HEAD_SIZE), lambda g, *_: (0, g))
    row = spec((1, 4, tok), lambda g, *_: (g, 0, 0))
    table = spec((tok, 128), lambda g, *_: (0, 0))
    return pl.pallas_call(
        functools.partial(attention_backward_kernel, block_rows=block_rows),
        grid_spec=pltpu.PrefetchScalarGridSpec(
            num_scalar_prefetch=2,
            grid=(pairs,),
            in_specs=[
                wide,
                wide,
                first,
                spec((PROMPT, 2 * HEAD_SIZE), lambda g, *_: (0, pairs + g)),
                first_own,
                spec((own, 2 * HEAD_SIZE), lambda g, *_: (0, pairs + g)),
                row,
                wide,
                table,
                table,
            ],
            out_specs=[wide, first, first, first_own, first_own],
            scratch_shapes=[
                pltpu.VMEM((PROMPT, 2 * HEAD_SIZE), bf16),
                pltpu.VMEM((PROMPT, 2 * HEAD_SIZE), bf16),
                pltpu.VMEM((PROMPT, 2 * HEAD_SIZE), f32),
                pltpu.VMEM((PROMPT, 2 * HEAD_SIZE), f32),
                pltpu.VMEM((tok, 4 * HEAD_SIZE), f32),
            ],
        ),
        out_shape=[
            jax.ShapeDtypeStruct((tok, HQ * HEAD_SIZE), bf16),
            jax.ShapeDtypeStruct((PROMPT, KV_WIDTH), bf16),
            jax.ShapeDtypeStruct((PROMPT, KV_WIDTH), bf16),
            jax.ShapeDtypeStruct((own, KV_WIDTH), f32),
            jax.ShapeDtypeStruct((own, KV_WIDTH), f32),
        ],
        compiler_params=pltpu.CompilerParams(vmem_limit_bytes=VMEM_LIMIT),
        cost_estimate=pl.CostEstimate(
            flops=120_000_000_000, bytes_accessed=24_000_000, transcendentals=25_000_000
        ),
        name="attention_backward",
    )(slots, starts, q, d_out, kv, kv, kv_own, kv_own, lse, attended, cosine, sine)


def expert_kernel(
    a2_ref,
    df_ref,
    rank_ref,
    gate_ref,
    wg_ref,
    wu_ref,
    wd_ref,
    mix_ref,
    da_ref,
    dg_ref,
    x_ref,
    dy_ref,
    z_ref,
    dgate_ref,
    dup_ref,
    mix_acc,
    da_acc,
    *,
    capacity,
):
    e = pl.program_id(0)

    @pl.when(e == 0)
    def _():
        mix_acc[...] = jnp.zeros_like(mix_acc)
        da_acc[...] = jnp.zeros_like(da_acc)

    rank = rank_ref[0]
    gates = gate_ref[0]
    tok = rank.shape[1]
    slot = lax.broadcasted_iota(jnp.int32, (capacity, tok), 0).astype(f32)
    hit = slot == rank
    chosen = hit.astype(f32).astype(bf16)
    gate = jnp.sum(jnp.where(hit, gates, 0.0), 1, keepdims=True)
    x = dot(chosen, a2_ref[...]).astype(bf16)
    d_mix = resid_scale * dot(chosen, df_ref[...])
    wg = wg_ref[:, 0].reshape(MODEL_WIDTH, FF)
    wu = wu_ref[:, 0].reshape(MODEL_WIDTH, FF)
    wd = jnp.concatenate([wd_ref[c, 0] for c in range(wd_ref.shape[0])], 1)
    g = dot(x, wg)
    u = dot(x, wu)
    sig = jax.nn.sigmoid(g)
    z = (g * sig * u).astype(bf16)
    y = dot(z, wd).astype(bf16).astype(f32)
    d_gate_value = jnp.sum(d_mix * y, 1, keepdims=True)
    dg_ref[0] = jnp.sum(jnp.where(hit, d_gate_value, 0.0), 0, keepdims=True)
    mix_acc[...] += dot_tn(chosen, (gate * y).astype(bf16))
    d_y = (gate * d_mix).astype(bf16)
    d_z = dot_nt(d_y, wd)
    d_g = (d_z * u * sig * (1.0 + g * (1.0 - sig))).astype(bf16)
    d_u = (d_z * g * sig).astype(bf16)
    d_r = (dot_nt(d_g, wg) + dot_nt(d_u, wu)).astype(bf16)
    da_acc[...] += dot_tn(chosen, d_r)
    x_ref[0] = x
    dy_ref[0] = d_y
    z_ref[0] = z
    dgate_ref[0] = d_g
    dup_ref[0] = d_u

    @pl.when(e == pl.num_programs(0) - 1)
    def _():
        mix_ref[...] = mix_acc[...].astype(bf16)
        da_ref[...] = da_acc[...].astype(bf16)


def expert_pass(a2, df, rank, gates, wg, wu, wd, capacity):
    tok = a2.shape[0]
    parts, experts = wg.shape[0], wg.shape[1]
    spec = pl.BlockSpec
    whole = spec((tok, MODEL_WIDTH), lambda e: (0, 0))
    row = spec((1, 1, tok), lambda e: (e, 0, 0))
    up = spec((parts, 1, MODEL_WIDTH // parts, FF), lambda e: (0, e, 0, 0))
    rows_wide = spec((1, capacity, MODEL_WIDTH), lambda e: (e, 0, 0))
    rows_thin = spec((1, capacity, FF), lambda e: (e, 0, 0))
    shape = jax.ShapeDtypeStruct
    return pl.pallas_call(
        functools.partial(expert_kernel, capacity=capacity),
        grid=(experts,),
        in_specs=[
            whole,
            whole,
            row,
            row,
            up,
            up,
            spec((parts, 1, FF, MODEL_WIDTH // parts), lambda e: (0, e, 0, 0)),
        ],
        out_specs=[whole, whole, row, rows_wide, rows_wide, rows_thin, rows_thin, rows_thin],
        out_shape=[
            shape((tok, MODEL_WIDTH), bf16),
            shape((tok, MODEL_WIDTH), bf16),
            shape((experts, 1, tok), f32),
            shape((experts, capacity, MODEL_WIDTH), bf16),
            shape((experts, capacity, MODEL_WIDTH), bf16),
            shape((experts, capacity, FF), bf16),
            shape((experts, capacity, FF), bf16),
            shape((experts, capacity, FF), bf16),
        ],
        scratch_shapes=[
            pltpu.VMEM((tok, MODEL_WIDTH), f32),
            pltpu.VMEM((tok, MODEL_WIDTH), f32),
        ],
        compiler_params=pltpu.CompilerParams(vmem_limit_bytes=VMEM_LIMIT),
        cost_estimate=pl.CostEstimate(
            flops=35_000_000_000, bytes_accessed=50_000_000, transcendentals=1_500_000
        ),
        name="expert_pass",
    )(a2, df, rank.reshape(experts, 1, tok), gates.reshape(experts, 1, tok), wg, wu, wd)


def weight_grad_kernel(*refs, sources, parts):
    rows = refs[: 5 * sources]
    gate_ref, up_ref, down_ref = refs[5 * sources :]
    width = MODEL_WIDTH // parts

    def add(which, other):
        total = None
        for s in range(sources):
            term = dot_tn(rows[5 * s + which][0], rows[5 * s + other][0])
            total = term if total is None else total + term
        return total

    gate_ref[...] = add(0, 3).astype(bf16).reshape(gate_ref.shape)
    up_ref[...] = add(0, 4).astype(bf16).reshape(up_ref.shape)
    down = add(2, 1).astype(bf16)
    for c in range(parts):
        down_ref[c, 0] = down[:, c * width : (c + 1) * width]


def weight_grads(rows, parts):
    sources = len(rows)
    experts, capacity = rows[0][0].shape[:2]
    spec = pl.BlockSpec
    wide = spec((1, capacity, MODEL_WIDTH), lambda e: (e, 0, 0))
    thin = spec((1, capacity, FF), lambda e: (e, 0, 0))
    up = (parts, experts, MODEL_WIDTH // parts, FF)
    down = (parts, experts, FF, MODEL_WIDTH // parts)
    up_spec = spec((parts, 1) + up[2:], lambda e: (0, e, 0, 0))
    return pl.pallas_call(
        functools.partial(weight_grad_kernel, sources=sources, parts=parts),
        grid=(experts,),
        in_specs=[wide, wide, thin, thin, thin] * sources,
        out_specs=[up_spec, up_spec, spec((parts, 1) + down[2:], lambda e: (0, e, 0, 0))],
        out_shape=[
            jax.ShapeDtypeStruct(up, bf16),
            jax.ShapeDtypeStruct(up, bf16),
            jax.ShapeDtypeStruct(down, bf16),
        ],
        compiler_params=pltpu.CompilerParams(vmem_limit_bytes=VMEM_LIMIT),
        cost_estimate=pl.CostEstimate(
            flops=34_000_000_000, bytes_accessed=100_000_000, transcendentals=0
        ),
        name="weight_grads",
    )(*[a for source in rows for a in source])


def swap(x, mask):
    return lax.ppermute(x, "ctx", [(i, i ^ mask) for i in range(lax.axis_size("ctx"))])


def blocks_ctx(x):
    half = x.shape[0] // 2
    near, far = swap(x, 2), swap(x, 4)
    diagonal = jnp.concatenate([swap(near[:half], 4), swap(far[half:], 2)], 0)
    even = [x, near, far, diagonal]
    odd = [swap(block, 1) for block in even]
    return [b for pair in zip(even, odd) for b in pair]


def gather_ctx(x):
    if lax.axis_size("ctx") != 8:
        return lax.all_gather(x, "ctx", axis=0, tiled=True)
    return jnp.concatenate(blocks_ctx(x), 0)


def scatter_ctx(x):
    if lax.axis_size("ctx") != 8:
        return lax.psum_scatter(x, "ctx", scatter_dimension=0, tiled=True).astype(f32)
    rows = x.shape[0] // 8
    half = rows // 2
    block = [x[m * rows : (m + 1) * rows] for m in range(8)]
    diagonal, near, far, own = (
        block[m].astype(f32) + swap(block[m + 1], 1).astype(f32) for m in (6, 2, 4, 0)
    )
    diagonal = diagonal.astype(bf16)
    near_top = near[:half] + swap(diagonal[:half], 4).astype(f32)
    far_end = far[half:] + swap(diagonal[half:], 2).astype(f32)
    near = jnp.concatenate([near_top.astype(bf16), near[half:].astype(bf16)], 0)
    far = jnp.concatenate([far[:half].astype(bf16), far_end.astype(bf16)], 0)
    return own + swap(near, 2).astype(f32) + swap(far, 4).astype(f32)


def shift(x, distance):
    n = lax.axis_size("wt")
    return lax.ppermute(x, "wt", [(i, (i + distance) % n) for i in range(n)])


def gather_all(x):
    ctx, wt = lax.axis_size("ctx"), lax.axis_size("wt")
    if ctx != 8 or wt != 4:
        return [lax.all_gather(x, ALL, axis=0, tiled=True)], [1], jnp.zeros((1,), jnp.int32)
    ctx_index, wt_index = lax.axis_index("ctx"), lax.axis_index("wt")
    others = jnp.concatenate([shift(x, d) for d in (1, 2, 3)], 0)
    pieces = blocks_ctx(x) + blocks_ctx(others)
    m = jnp.arange(8, dtype=jnp.int32)
    own = (ctx_index ^ m) * wt + wt_index
    d = jnp.arange(1, 4, dtype=jnp.int32)
    rest = ((ctx_index ^ m) * wt)[:, None] + ((wt_index - d) % wt)[None, :]
    places = jnp.concatenate([own, rest.reshape(-1)]).astype(jnp.int32)
    return pieces, [1] * 8 + [3] * 8, places


def outer_sum(a, b):
    ctx, wt = lax.axis_size("ctx"), lax.axis_size("wt")
    if ctx != 8 or wt != 4:
        return lax.psum_scatter(
            dot_tn(a, b).astype(bf16), ALL, scatter_dimension=0, tiled=True
        ).astype(f32)
    part = scatter_ctx(outer(a, b))
    rows = part.shape[0] // wt
    low = part.astype(bf16)
    at = lambda d: ((lax.axis_index("wt") + d) % wt) * rows
    total = lax.dynamic_slice_in_dim(part, at(0), rows, 0)
    for d in range(1, wt):
        total = total + shift(lax.dynamic_slice_in_dim(low, at(d), rows, 0), d).astype(f32)
    return total


def spread_sum(x):
    return jnp.sum(lax.all_to_all(x, ALL, 0, 0, tiled=True), 0)


def after(x, *others):
    return lax.optimization_barrier((x,) + others)[0]


def rope_tables(positions, width):
    middle = HEAD_SIZE // 2
    frequency = jnp.power(
        jnp.float32(rope_base), -2.0 * jnp.arange(middle, dtype=f32) / HEAD_SIZE
    )
    angles = positions.astype(f32)[:, None] * frequency[None, :]
    times = width // middle
    return jnp.tile(jnp.cos(angles), (1, times)), jnp.tile(jnp.sin(angles), (1, times))


def turn(values, cosine, sine, direction):
    middle = HEAD_SIZE // 2
    first = lax.broadcasted_iota(jnp.int32, values.shape, 1) % HEAD_SIZE < middle
    turned = jnp.where(first, -jnp.roll(values, -middle, 1), jnp.roll(values, middle, 1))
    width = values.shape[1]
    return values * cosine[:, :width] + direction * turned * sine[:, :width]


def norm_forward(values, gain):
    inverse = lax.rsqrt(jnp.mean(values * values, -1, keepdims=True) + norm_eps)
    return (values * inverse * gain, inverse)


def norm_backward(values, inverse, gain, grad_out):
    scaled = gain * grad_out
    gain_grad = jnp.sum(grad_out * values * inverse, 0)
    projection = jnp.mean(scaled * values, -1, keepdims=True)
    return (inverse * scaled - values * inverse * inverse * inverse * projection, gain_grad)


def per_device(
    layer_input,
    attention_gain,
    query_weight,
    key_matrix,
    value_matrix,
    output_weight,
    mixture_gain,
    router_weight,
    gate_weight,
    up_weight,
    down_weight,
    expert_routes,
    prompt_deal,
    output_grad,
):
    tok = layer_input.shape[1]
    prompt_local = tok - CONT_DEV * CLEN
    block_rows = prompt_local // 2
    context_size = lax.axis_size("ctx")
    shard_count = lax.axis_size("wt")
    expert_count = gate_weight.shape[0]
    capacity = 8 * ((tok * TOP * 7 // (4 * EXPERTS) + 7) // 8)
    ctx_index = lax.axis_index("ctx")
    wt_index = lax.axis_index("wt")
    inputs = layer_input[0].astype(f32)
    routes = expert_routes[0]
    deal_row = prompt_deal[0]
    out_low = output_grad[0]
    out_grad = out_low.astype(f32)

    own_rows = query_weight.shape[0]
    packed = jnp.concatenate(
        [
            query_weight,
            key_matrix,
            value_matrix,
            output_weight.T,
            router_weight,
            attention_gain[:, None],
            mixture_gain[:, None],
            jnp.zeros((own_rows, 94), bf16),
        ],
        1,
    )
    pieces, counts, block_places = gather_all(packed)

    gate_full = lax.all_gather(gate_weight, "ctx", axis=0, tiled=False)
    up_full = lax.all_gather(up_weight, "ctx", axis=0, tiled=False)
    down_full = lax.all_gather(down_weight, "ctx", axis=0, tiled=False)

    mask = jnp.any(
        routes[:, :, None] == jnp.arange(EXPERTS, dtype=jnp.int32)[None, None, :], 1
    )
    order = jnp.arange(tok, dtype=jnp.int32)
    before = (order[None, :] < order[:, None]).astype(bf16)
    rank = jnp.where(mask, dot(before, mask.astype(bf16)), -1.0)
    ranks = lax.all_to_all(
        rank.T.reshape(shard_count, expert_count, tok), "wt", 0, 0, tiled=True
    )
    grads_in = [out_low] + [shift(out_low, d) for d in range(1, shard_count)]

    local_rows = jnp.arange(tok, dtype=jnp.int32)
    mine = lax.dynamic_slice_in_dim(deal_row, 2 * ctx_index, 2, 0)
    prompt_place = (
        jnp.where(local_rows < block_rows, mine[0], mine[1]) * block_rows
        + local_rows % block_rows
    )
    positions = jnp.where(
        local_rows < prompt_local, prompt_place, PROMPT + (local_rows - prompt_local) % CLEN
    )
    cosine, sine = rope_tables(positions, 128)
    normed_one, turned_query, kv_low, qkv_full, output_t, rest, gain_rows = project(
        layer_input[0], cosine, sine, pieces, counts, block_places
    )
    router_full = rest[:, :EXPERTS]
    first_gain, second_gain = gain_rows[0], gain_rows[1]
    inverse_one = lax.rsqrt(jnp.mean(inputs * inputs, -1, keepdims=True) + norm_eps)
    kv_own = kv_low[prompt_local:]
    kv_all = gather_ctx(kv_low[:prompt_local])

    order = jnp.arange(2 * context_size, dtype=jnp.int32)
    place_of = jnp.sum(jnp.where(deal_row[None, :] == order[:, None], order[None, :], 0), 1)
    if context_size == 8:
        place_of = ((place_of // 2) ^ ctx_index) * 2 + place_of % 2
    low = (mine[0] > mine[1]).astype(jnp.int32)
    starts = jnp.stack(
        [
            low * block_rows,
            (1 - low) * block_rows,
            jnp.min(mine) * block_rows,
            jnp.max(mine) * block_rows,
        ]
    ).astype(jnp.int32)
    attended, lse = attention_forward(turned_query, kv_all, kv_own, place_of, starts, block_rows)

    branch = dot_nt(attended, output_t)
    middle = inputs + resid_scale * branch
    normed_mid, inverse_two = norm_forward(middle, second_gain)
    normed_two = normed_mid.astype(bf16)
    logits = dot(normed_two, router_full)
    top = jnp.max(jnp.where(mask, logits, masked_score), -1, keepdims=True)
    raised = jnp.where(mask, jnp.exp(jnp.where(mask, logits - top, 0.0)), 0.0)
    gates = raised / jnp.sum(raised, -1, keepdims=True)

    gates_out = gates.T.reshape(shard_count, expert_count, tok)
    arrived, gates_in = [normed_two], []
    for d in range(shard_count):
        piece = lax.dynamic_index_in_dim(gates_out, (wt_index + d) % shard_count, 0, False)
        gates_in.append(shift(piece, d) if d else piece)
    sequence = [0, 1, shard_count - 1] + list(range(2, shard_count - 1))
    got = {0: normed_two}
    for d in sequence[1:3]:
        got[d] = shift(normed_two, d)
    mixed, returned, gate_grads, rows = {}, {}, {}, []
    for d in sequence:
        source = (wt_index - d) % shard_count
        rank_in = lax.dynamic_index_in_dim(ranks, source, 0, False)
        mix, d_a, d_gate, *kept = expert_pass(
            got[d], grads_in[d], rank_in, gates_in[d], gate_full, up_full, down_full, capacity
        )
        rows.append(kept)
        d_gate = d_gate.reshape(expert_count, tok)
        back = shard_count - d
        mixed[d] = mix
        if d == 0:
            for other in sequence[3:]:
                got[other] = shift(after(normed_two, mix), other)
        returned[d] = shift(d_a, back) if d else d_a
        gate_grads[d] = shift(d_gate, back) if d else d_gate
    gate_grad, up_grad, down_grad = weight_grads(rows, context_size)
    returned[0] = after(returned[0], gate_grad)
    gate_share = lax.psum_scatter(gate_grad, "ctx", scatter_dimension=0, tiled=False).astype(f32)
    up_share = lax.psum_scatter(up_grad, "ctx", scatter_dimension=0, tiled=False).astype(f32)
    down_share = lax.psum_scatter(down_grad, "ctx", scatter_dimension=0, tiled=False).astype(f32)

    stacked = jnp.stack([gate_grads[d] for d in range(shard_count)], 0)
    stacked = jnp.roll(stacked, wt_index, 0).reshape(EXPERTS, tok).T
    grad_logits = (gates * (stacked - jnp.sum(gates * stacked, -1, keepdims=True))).astype(bf16)
    grad_normed_two = sum(returned[d].astype(f32) for d in range(shard_count))
    grad_normed_two = grad_normed_two + dot_nt(grad_logits, router_full)
    grad_mid_norm, second_gain_grad = norm_backward(
        middle, inverse_two, second_gain, grad_normed_two
    )
    grad_middle = out_grad + grad_mid_norm
    grad_branch = (resid_scale * grad_middle).astype(bf16)
    grad_attended = dot(grad_branch, output_t).astype(bf16)
    output_share = outer_sum(grad_branch, attended)
    devices = context_size * shard_count
    small = jnp.concatenate(
        [
            dot_tn(normed_two, grad_logits).reshape(devices, own_rows * EXPERTS),
            second_gain_grad.reshape(devices, own_rows),
        ],
        1,
    )
    small = spread_sum(small)

    mixture = mixed[0].astype(f32)
    for d in sequence[1:]:
        mixture = mixture + shift(after(mixed[d], returned[d]), shard_count - d).astype(f32)
    layer_output = (middle + resid_scale * mixture).astype(bf16)

    grad_query_low, d_key, d_value, d_key_own, d_value_own = attention_backward(
        turned_query,
        grad_attended,
        kv_all,
        kv_own,
        lse,
        attended,
        cosine,
        sine,
        place_of,
        starts,
        block_rows,
    )
    owned = scatter_ctx(jnp.concatenate([d_key, d_value], 1))
    d_key_all = jnp.concatenate([owned[:, :KV_WIDTH], d_key_own], 0)
    d_value_all = jnp.concatenate([owned[:, KV_WIDTH:], d_value_own], 0)
    grad_key_low = turn(
        d_key_all, jnp.tile(cosine, (1, 4)), jnp.tile(sine, (1, 4)), -1.0
    ).astype(bf16)
    grad_qkv = jnp.concatenate([grad_query_low, grad_key_low, d_value_all.astype(bf16)], 1)
    qkv_share = outer_sum(normed_one, grad_qkv)
    grad_normed_one = dot_nt(grad_qkv, qkv_full)
    grad_input_norm, first_gain_grad = norm_backward(
        inputs, inverse_one, first_gain, grad_normed_one
    )
    input_grad = (grad_middle + grad_input_norm).astype(bf16)

    first_gain_share = spread_sum(first_gain_grad.reshape(devices, own_rows))
    return (
        layer_output[None],
        input_grad[None],
        first_gain_share,
        qkv_share[:, :1024],
        qkv_share[:, 1024:1536],
        qkv_share[:, 1536:],
        output_share.T,
        small[own_rows * EXPERTS :],
        small[: own_rows * EXPERTS].reshape(own_rows, EXPERTS),
        gate_share,
        up_share,
        down_share,
    )


def solution(mesh):
    return jax.shard_map(
        per_device,
        mesh=mesh,
        in_specs=(
            P("wt", "ctx", None),
            P(("ctx", "wt")),
            P(("ctx", "wt"), None),
            P(("ctx", "wt"), None),
            P(("ctx", "wt"), None),
            P(None, ("ctx", "wt")),
            P(("ctx", "wt")),
            P(("ctx", "wt"), None),
            P("wt", "ctx", None),
            P("wt", "ctx", None),
            P("wt", None, "ctx"),
            P("wt", "ctx", None),
            P("wt", None),
            P("wt", "ctx", None),
        ),
        out_specs=(
            P("wt", "ctx", None),
            P("wt", "ctx", None),
            P(("ctx", "wt")),
            P(("ctx", "wt"), None),
            P(("ctx", "wt"), None),
            P(("ctx", "wt"), None),
            P(None, ("ctx", "wt")),
            P(("ctx", "wt")),
            P(("ctx", "wt"), None),
            P("wt", "ctx", None),
            P("wt", "ctx", None),
            P("wt", None, "ctx"),
        ),
        check_vma=False,
    )
```

```python
import functools

import jax
import jax.numpy as jnp
from jax import lax
from jax.experimental import pallas as pl
from jax.experimental.pallas import tpu as pltpu
from jax.sharding import PartitionSpec as P

MODEL_WIDTH = 1024
HQ = 16
KEY_VALUE_HEADS = 8
HEAD_SIZE = 64
EXPERTS = 32
TOP = 8
PROMPT = 2048
CLEN = 256
CONT_DEV = 2
FF = 512
QTILE = 128
KV_WIDTH = KEY_VALUE_HEADS * HEAD_SIZE
ALL = ("ctx", "wt")

att_scale = 0.015625
resid_scale = 0.22
norm_eps = 1e-06
rope_base = 10000.0
masked_score = -1e30

bf16 = jnp.bfloat16
f32 = jnp.float32
VMEM_LIMIT = 60 * 1024 * 1024
SMALL = pl.CostEstimate(flops=1_000_000_000, bytes_accessed=1_000_000, transcendentals=0)

NT = (((1,), (1,)), ((), ()))
TN = (((0,), (0,)), ((), ()))


def dot(a, b):
    return jnp.dot(a, b, preferred_element_type=f32)


def dot_nt(a, b):
    return lax.dot_general(a, b, NT, preferred_element_type=f32)


def dot_tn(a, b):
    return lax.dot_general(a, b, TN, preferred_element_type=f32)


def turn_tile(values, cosine, sine, direction):
    middle = HEAD_SIZE // 2
    first = lax.broadcasted_iota(jnp.int32, values.shape, 1) % HEAD_SIZE < middle
    turned = jnp.where(first, -pltpu.roll(values, 128 - middle, 1), pltpu.roll(values, middle, 1))
    return values * cosine + direction * turned * sine


def project_kernel(places, x_ref, cos_ref, sin_ref, *refs, counts):
    pieces = refs[: len(counts)]
    normed_ref, q_ref, *kv_refs, qkv_ref, out_ref, rest_ref, gains_ref = refs[len(counts) :]
    rows = MODEL_WIDTH // sum(counts)
    at = 0
    for piece, count in zip(pieces, counts):
        for i in range(count):
            source = slice(i * rows, (i + 1) * rows)
            target = pl.ds(pl.multiple_of(places[at] * rows, rows), rows)
            qkv_ref[target, :] = piece[source, :2048]
            out_ref[target, :] = piece[source, 2048:3072]
            rest_ref[target, :] = piece[source, 3072:]
            at += 1
    gains = rest_ref[...].astype(f32).T[EXPERTS : EXPERTS + 8]
    gains_ref[...] = gains
    x = x_ref[...].astype(f32)
    inverse = lax.rsqrt(jnp.mean(x * x, -1, keepdims=True) + norm_eps)
    normed_ref[...] = (x * inverse * gains[:1]).astype(bf16)
    for c in range(8):
        raw = dot(normed_ref[...], qkv_ref[:, 256 * c : 256 * (c + 1)])
        for h in range(2):
            part = raw[:, 128 * h : 128 * (h + 1)]
            if c < 6:
                part = turn_tile(part, cos_ref[...], sin_ref[...], 1.0)
            column = 256 * c + 128 * h
            if column < 1024:
                q_ref[:, column : column + 128] = part.astype(bf16)
            else:
                column -= 1024
                at = column // KV_WIDTH * 256 + column % 256
                kv_refs[column % KV_WIDTH // 256][:, at : at + 128] = part.astype(bf16)


def project(x, cosine, sine, pieces, counts, places):
    tok = x.shape[0]
    shape = jax.ShapeDtypeStruct
    whole = pl.BlockSpec(memory_space=pltpu.VMEM)
    return pl.pallas_call(
        functools.partial(project_kernel, counts=counts),
        in_specs=[pl.BlockSpec(memory_space=pltpu.SMEM)] + [whole] * (3 + len(pieces)),
        out_specs=[whole] * 8,
        out_shape=[
            shape((tok, MODEL_WIDTH), bf16),
            shape((tok, HQ * HEAD_SIZE), bf16),
            shape((tok, KV_WIDTH), bf16),
            shape((tok, KV_WIDTH), bf16),
            shape((MODEL_WIDTH, 2048), bf16),
            shape((MODEL_WIDTH, 1024), bf16),
            shape((MODEL_WIDTH, 128), bf16),
            shape((8, MODEL_WIDTH), f32),
        ],
        compiler_params=pltpu.CompilerParams(vmem_limit_bytes=VMEM_LIMIT),
        cost_estimate=SMALL,
        name="project",
    )(places, x, cosine, sine, *pieces)


def outer_kernel(mine, a_ref, b_ref, out_ref):
    out_ref[...] = dot_tn(a_ref[...], b_ref[...]).astype(bf16)


def outer(a, b):
    tok, columns = b.shape
    mine = lax.axis_index("ctx").astype(jnp.int32).reshape(1)
    return pl.pallas_call(
        outer_kernel,
        grid_spec=pltpu.PrefetchScalarGridSpec(
            num_scalar_prefetch=1,
            grid=(8,),
            in_specs=[
                pl.BlockSpec((tok, 128), lambda m, mine: (0, m ^ mine[0])),
                pl.BlockSpec((tok, columns), lambda m, mine: (0, 0)),
            ],
            out_specs=pl.BlockSpec((128, columns), lambda m, mine: (m, 0)),
        ),
        out_shape=jax.ShapeDtypeStruct((MODEL_WIDTH, columns), bf16),
        compiler_params=pltpu.CompilerParams(vmem_limit_bytes=VMEM_LIMIT),
        cost_estimate=SMALL,
        name="outer",
    )(mine, a, b)


def gather_keys(pieces, scratch, places, block_rows):
    at = 0
    for piece in pieces:
        for b in range(piece.shape[0] // block_rows):
            start = pl.multiple_of(places[at] * block_rows, block_rows)
            scratch[pl.ds(start, block_rows), :] = piece[b * block_rows : (b + 1) * block_rows, :]
            at += 1


def pair_rows(ref, start, rows, j):
    both = ref[pl.ds(start, rows), 2 * HEAD_SIZE * j : 2 * HEAD_SIZE * (j + 1)]
    return jnp.concatenate([both[:, :HEAD_SIZE], both[:, HEAD_SIZE:]], 0)


def attention_forward_kernel(places, starts, q_ref, *refs, block_rows, pieces):
    k_refs, v_refs = refs[:pieces], refs[pieces : 2 * pieces]
    kc_ref, vc_ref, o_ref, lse_ref, k_scr, v_scr = refs[2 * pieces :]
    prompt_local = 2 * block_rows
    gather_keys(k_refs, k_scr, places, block_rows)
    gather_keys(v_refs, v_scr, places, block_rows)

    def store(start, rows, j, out, m, total, at):
        out = (out / total).astype(bf16)
        lse = m + jnp.log(total)
        o_ref[pl.ds(start, rows), 2 * HEAD_SIZE * j : 2 * HEAD_SIZE * (j + 1)] = jnp.concatenate(
            [out[:rows], out[rows:]], 1
        )
        row = jnp.broadcast_to(lse, (2 * rows, 128)).T[:1]
        lse_ref[0, 2 * j : 2 * j + 2, pl.ds(at, rows)] = jnp.concatenate(
            [row[:, :rows], row[:, rows:]], 0
        )

    def tile(i, _):
        start = pl.multiple_of(prompt_local + i * QTILE, 64)
        per = CLEN // QTILE
        seg = pl.multiple_of((i // per) * CLEN, CLEN)
        for j in range(2):
            lanes = slice(HEAD_SIZE * j, HEAD_SIZE * (j + 1))
            q = pair_rows(q_ref, start, QTILE, j) * bf16(att_scale)
            s1 = dot_nt(q, k_scr[:, lanes])
            s2 = dot_nt(q, kc_ref[pl.ds(seg, CLEN), lanes])
            place = lax.broadcasted_iota(jnp.int32, s2.shape, 0) % QTILE + (i % per) * QTILE
            s2 = jnp.where(lax.broadcasted_iota(jnp.int32, s2.shape, 1) <= place, s2, masked_score)
            m = jnp.maximum(jnp.max(s1, 1, keepdims=True), jnp.max(s2, 1, keepdims=True))
            e1 = jnp.exp(s1 - m)
            e2 = jnp.exp(s2 - m)
            total = jnp.sum(e1, 1, keepdims=True) + jnp.sum(e2, 1, keepdims=True)
            out = dot(e1.astype(bf16), v_scr[:, lanes])
            out = out + dot(e2.astype(bf16), vc_ref[pl.ds(seg, CLEN), lanes])
            store(start, QTILE, j, out, m, total, pl.multiple_of(i * QTILE, QTILE))
        return 0

    lax.fori_loop(0, CONT_DEV * CLEN // QTILE, tile, 0)

    for half, keys in enumerate((PROMPT // 2, PROMPT)):
        start = pl.multiple_of(starts[half], block_rows)
        for j in range(2):
            lanes = slice(HEAD_SIZE * j, HEAD_SIZE * (j + 1))
            q = pair_rows(q_ref, start, block_rows, j) * bf16(att_scale)
            s = dot_nt(q, k_scr[:keys, lanes])
            place = lax.broadcasted_iota(jnp.int32, s.shape, 0) % block_rows + starts[2 + half]
            s = jnp.where(lax.broadcasted_iota(jnp.int32, s.shape, 1) <= place, s, masked_score)
            m = jnp.max(s, 1, keepdims=True)
            e = jnp.exp(s - m)
            total = jnp.sum(e, 1, keepdims=True)
            out = dot(e.astype(bf16), v_scr[:keys, lanes])
            store(start, block_rows, j, out, m, total, CONT_DEV * CLEN + half * block_rows)


def key_specs(pieces, own):
    spec = pl.BlockSpec
    keys = [spec((p.shape[0], 128), lambda g, *_: (0, g)) for p in pieces]
    values = [spec((p.shape[0], 128), lambda g, *_: (0, 2 + g)) for p in pieces]
    ours = [spec((own, 128), lambda g, *_: (0, g)), spec((own, 128), lambda g, *_: (0, 2 + g))]
    return keys + values + ours


def attention_forward(q, pieces, kv_own, places, starts, block_rows, half):
    tok = q.shape[0]
    spec = pl.BlockSpec
    return pl.pallas_call(
        functools.partial(
            attention_forward_kernel, block_rows=block_rows, pieces=len(pieces)
        ),
        grid_spec=pltpu.PrefetchScalarGridSpec(
            num_scalar_prefetch=2,
            grid=(2,),
            in_specs=[spec((tok, 256), lambda g, *_: (0, 2 * half + g))]
            + key_specs(pieces, kv_own.shape[0]),
            out_specs=[
                spec((tok, 256), lambda g, *_: (0, g)),
                spec((1, 4, tok), lambda g, *_: (g, 0, 0)),
            ],
            scratch_shapes=[
                pltpu.VMEM((PROMPT, 2 * HEAD_SIZE), bf16),
                pltpu.VMEM((PROMPT, 2 * HEAD_SIZE), bf16),
            ],
        ),
        out_shape=[
            jax.ShapeDtypeStruct((tok, HQ * HEAD_SIZE // 2), bf16),
            jax.ShapeDtypeStruct((2, 4, tok), f32),
        ],
        compiler_params=pltpu.CompilerParams(vmem_limit_bytes=VMEM_LIMIT),
        cost_estimate=SMALL,
        name="attention_forward",
    )(places, starts, q, *pieces, *pieces, kv_own, kv_own)


def attention_backward_kernel(
    places, starts, q_ref, do_ref, lse_ref, o_ref, cos_ref, sin_ref, *refs, block_rows, pieces
):
    k_refs, v_refs = refs[:pieces], refs[pieces : 2 * pieces]
    kc_ref, vc_ref, dq_ref, dkv_ref, dkc_ref, dvc_ref = refs[2 * pieces : 2 * pieces + 6]
    k_scr, v_scr, dk_acc, dv_acc, dq_acc = refs[2 * pieces + 6 :]
    prompt_local = 2 * block_rows
    gather_keys(k_refs, k_scr, places, block_rows)
    gather_keys(v_refs, v_scr, places, block_rows)
    dk_acc[...] = jnp.zeros_like(dk_acc)
    dv_acc[...] = jnp.zeros_like(dv_acc)
    dkc_ref[...] = jnp.zeros_like(dkc_ref)
    dvc_ref[...] = jnp.zeros_like(dvc_ref)

    def row_pair(ref, start, rows, j):
        both = ref[0, 2 * j : 2 * j + 2, pl.ds(start, rows)]
        return jnp.concatenate([both[:1], both[1:]], 1)

    def centre(start, rows, j, d_out):
        product = d_out.astype(f32) * pair_rows(o_ref, start, rows, j).astype(f32)
        ones = jnp.ones((8, HEAD_SIZE), f32)
        return lax.dot_general(
            ones, product, NT, precision=lax.Precision.HIGHEST, preferred_element_type=f32
        )[:1]

    def part(k, v, q, d_out, lse, delta, allowed):
        s = dot_nt(k, q)
        if allowed is not None:
            s = jnp.where(allowed(s.shape), s, masked_score)
        p = jnp.exp(s - lse)
        d_p = dot_nt(v, d_out)
        d_s = (p * (d_p - delta)).astype(bf16)
        return dot_tn(d_s, k), dot(d_s, q), dot(p.astype(bf16), d_out)

    def store(start, rows, j, d_q):
        d_q = d_q * att_scale
        dq_acc[pl.ds(start, rows), 2 * HEAD_SIZE * j : 2 * HEAD_SIZE * (j + 1)] = jnp.concatenate(
            [d_q[:rows], d_q[rows:]], 1
        )

    def tile(i, _):
        start = pl.multiple_of(prompt_local + i * QTILE, 64)
        per = CLEN // QTILE
        seg = pl.multiple_of((i // per) * CLEN, CLEN)
        own = pl.ds(seg, CLEN)
        lane_start = pl.multiple_of(i * QTILE, QTILE)

        def allowed(shape):
            place = lax.broadcasted_iota(jnp.int32, shape, 1) % QTILE + (i % per) * QTILE
            return lax.broadcasted_iota(jnp.int32, shape, 0) <= place

        for j in range(2):
            lanes = slice(HEAD_SIZE * j, HEAD_SIZE * (j + 1))
            q = pair_rows(q_ref, start, QTILE, j) * bf16(att_scale)
            d_out = pair_rows(do_ref, start, QTILE, j)
            lse = row_pair(lse_ref, lane_start, QTILE, j)
            delta = centre(start, QTILE, j, d_out)
            a, b, c = part(k_scr[:, lanes], v_scr[:, lanes], q, d_out, lse, delta, None)
            dk_acc[:, lanes] += b
            dv_acc[:, lanes] += c
            d_q = a
            a, b, c = part(
                kc_ref[own, lanes], vc_ref[own, lanes], q, d_out, lse, delta, allowed
            )
            dkc_ref[own, lanes] += b
            dvc_ref[own, lanes] += c
            store(start, QTILE, j, d_q + a)
        return 0

    lax.fori_loop(0, CONT_DEV * CLEN // QTILE, tile, 0)

    for half, keys in enumerate((PROMPT // 2, PROMPT)):
        start = pl.multiple_of(starts[half], block_rows)
        at = CONT_DEV * CLEN + half * block_rows

        def allowed(shape):
            place = lax.broadcasted_iota(jnp.int32, shape, 1) % block_rows + starts[2 + half]
            return lax.broadcasted_iota(jnp.int32, shape, 0) <= place

        for j in range(2):
            lanes = slice(HEAD_SIZE * j, HEAD_SIZE * (j + 1))
            q = pair_rows(q_ref, start, block_rows, j) * bf16(att_scale)
            d_out = pair_rows(do_ref, start, block_rows, j)
            lse = row_pair(lse_ref, at, block_rows, j)
            delta = centre(start, block_rows, j, d_out)
            a, b, c = part(
                k_scr[:keys, lanes], v_scr[:keys, lanes], q, d_out, lse, delta, allowed
            )
            dk_acc[:keys, lanes] += b
            dv_acc[:keys, lanes] += c
            store(start, block_rows, j, a)

    g = pl.program_id(0)
    key_lanes = pl.ds(pl.multiple_of(g * 128, 128), 128)
    value_lanes = pl.ds(pl.multiple_of(256 + g * 128, 128), 128)
    for b in range(PROMPT // block_rows):
        source = pl.ds(pl.multiple_of(places[b] * block_rows, block_rows), block_rows)
        rows = slice(b * block_rows, (b + 1) * block_rows)
        dkv_ref[rows, key_lanes] = dk_acc[source, :].astype(bf16)
        dkv_ref[rows, value_lanes] = dv_acc[source, :].astype(bf16)
    for c in range(2):
        lanes = slice(128 * c, 128 * (c + 1))
        dq_ref[:, lanes] = turn_tile(dq_acc[:, lanes], cos_ref[...], sin_ref[...], -1.0).astype(
            bf16
        )


def attention_backward(
    q, d_out, lse, attended, cosine, sine, pieces, kv_own, places, starts, block_rows, half
):
    tok = q.shape[0]
    own = kv_own.shape[0]
    spec = pl.BlockSpec
    wide = spec((tok, 256), lambda g, *_: (0, 2 * half + g))
    ours = spec((own, 128), lambda g, *_: (0, g))
    table = spec((tok, 128), lambda g, *_: (0, 0))
    return pl.pallas_call(
        functools.partial(
            attention_backward_kernel, block_rows=block_rows, pieces=len(pieces)
        ),
        grid_spec=pltpu.PrefetchScalarGridSpec(
            num_scalar_prefetch=2,
            grid=(2,),
            in_specs=[wide, wide, spec((1, 4, tok), lambda g, *_: (g, 0, 0)), wide, table, table]
            + key_specs(pieces, own),
            out_specs=[
                spec((tok, 256), lambda g, *_: (0, g)),
                spec((PROMPT, KV_WIDTH), lambda g, *_: (0, 0)),
                ours,
                ours,
            ],
            scratch_shapes=[
                pltpu.VMEM((PROMPT, 2 * HEAD_SIZE), bf16),
                pltpu.VMEM((PROMPT, 2 * HEAD_SIZE), bf16),
                pltpu.VMEM((PROMPT, 2 * HEAD_SIZE), f32),
                pltpu.VMEM((PROMPT, 2 * HEAD_SIZE), f32),
                pltpu.VMEM((tok, 4 * HEAD_SIZE), f32),
            ],
        ),
        out_shape=[
            jax.ShapeDtypeStruct((tok, HQ * HEAD_SIZE // 2), bf16),
            jax.ShapeDtypeStruct((PROMPT, KV_WIDTH), bf16),
            jax.ShapeDtypeStruct((own, KV_WIDTH // 2), f32),
            jax.ShapeDtypeStruct((own, KV_WIDTH // 2), f32),
        ],
        compiler_params=pltpu.CompilerParams(vmem_limit_bytes=VMEM_LIMIT),
        cost_estimate=SMALL,
        name="attention_backward",
    )(places, starts, q, d_out, lse, attended, cosine, sine, *pieces, *pieces, kv_own, kv_own)


def expert_kernel(
    counts,
    a2_ref,
    df_ref,
    rank_ref,
    gate_ref,
    wg_ref,
    wu_ref,
    wd_ref,
    mix_ref,
    da_ref,
    dg_ref,
    x_ref,
    dy_ref,
    z_ref,
    dgate_ref,
    dup_ref,
    mix_acc,
    da_acc,
    *,
    sizes,
):
    e = pl.program_id(0)

    @pl.when(e == 0)
    def _():
        mix_acc[...] = jnp.zeros_like(mix_acc)
        da_acc[...] = jnp.zeros_like(da_acc)

    def body(size):
        rank = rank_ref[0]
        gates = gate_ref[0]
        tok = rank.shape[1]
        slot = lax.broadcasted_iota(jnp.int32, (size, tok), 0).astype(f32)
        hit = slot == rank
        chosen = hit.astype(f32).astype(bf16)
        gate = jnp.sum(jnp.where(hit, gates, 0.0), 1, keepdims=True)
        x = dot(chosen, a2_ref[...]).astype(bf16)
        d_mix = resid_scale * dot(chosen, df_ref[...])
        wg = wg_ref[:, 0].reshape(MODEL_WIDTH, FF)
        wu = wu_ref[:, 0].reshape(MODEL_WIDTH, FF)
        wd = jnp.concatenate([wd_ref[c, 0] for c in range(wd_ref.shape[0])], 1)
        g = dot(x, wg)
        u = dot(x, wu)
        sig = jax.nn.sigmoid(g)
        z = (g * sig * u).astype(bf16)
        y = dot(z, wd).astype(bf16).astype(f32)
        d_gate_value = jnp.sum(d_mix * y, 1, keepdims=True)
        dg_ref[0] = jnp.sum(jnp.where(hit, d_gate_value, 0.0), 0, keepdims=True)
        mix_acc[...] += dot_tn(chosen, (gate * y).astype(bf16))
        d_y = (gate * d_mix).astype(bf16)
        d_z = dot_nt(d_y, wd)
        d_g = (d_z * u * sig * (1.0 + g * (1.0 - sig))).astype(bf16)
        d_u = (d_z * g * sig).astype(bf16)
        d_r = (dot_nt(d_g, wg) + dot_nt(d_u, wu)).astype(bf16)
        da_acc[...] += dot_tn(chosen, d_r)
        for ref, value in (
            (x_ref, x),
            (dy_ref, d_y),
            (z_ref, z),
            (dgate_ref, d_g),
            (dup_ref, d_u),
        ):
            ref[0, :size] = value
            if size < ref.shape[1]:
                ref[0, size:] = jnp.zeros((ref.shape[1] - size, ref.shape[2]), bf16)

    least = -1
    for size in sizes:
        pl.when((counts[e] > least) & (counts[e] <= size))(functools.partial(body, size))
        least = size

    @pl.when(e == pl.num_programs(0) - 1)
    def _():
        mix_ref[...] = mix_acc[...].astype(bf16)
        da_ref[...] = da_acc[...].astype(bf16)


def expert_pass(a2, df, rank, gates, wg, wu, wd, capacity):
    tok = a2.shape[0]
    parts, experts = wg.shape[0], wg.shape[1]
    sizes = sorted({min(size, capacity) for size in (128, 192, 256, capacity)})
    counts = (jnp.max(rank, 1) + 1.0).astype(jnp.int32)
    spec = pl.BlockSpec
    whole = spec((tok, MODEL_WIDTH), lambda e, *_: (0, 0))
    row = spec((1, 1, tok), lambda e, *_: (e, 0, 0))
    up = spec((parts, 1, MODEL_WIDTH // parts, FF), lambda e, *_: (0, e, 0, 0))
    down = spec((parts, 1, FF, MODEL_WIDTH // parts), lambda e, *_: (0, e, 0, 0))
    rows_wide = spec((1, capacity, MODEL_WIDTH), lambda e, *_: (e, 0, 0))
    rows_thin = spec((1, capacity, FF), lambda e, *_: (e, 0, 0))
    shape = jax.ShapeDtypeStruct
    return pl.pallas_call(
        functools.partial(expert_kernel, sizes=sizes),
        grid_spec=pltpu.PrefetchScalarGridSpec(
            num_scalar_prefetch=1,
            grid=(experts,),
            in_specs=[whole, whole, row, row, up, up, down],
            out_specs=[whole, whole, row, rows_wide, rows_wide, rows_thin, rows_thin, rows_thin],
            scratch_shapes=[
                pltpu.VMEM((tok, MODEL_WIDTH), f32),
                pltpu.VMEM((tok, MODEL_WIDTH), f32),
            ],
        ),
        out_shape=[
            shape((tok, MODEL_WIDTH), bf16),
            shape((tok, MODEL_WIDTH), bf16),
            shape((experts, 1, tok), f32),
            shape((experts, capacity, MODEL_WIDTH), bf16),
            shape((experts, capacity, MODEL_WIDTH), bf16),
            shape((experts, capacity, FF), bf16),
            shape((experts, capacity, FF), bf16),
            shape((experts, capacity, FF), bf16),
        ],
        compiler_params=pltpu.CompilerParams(vmem_limit_bytes=VMEM_LIMIT),
        cost_estimate=SMALL,
        name="expert_pass",
    )(counts, a2, df, rank.reshape(experts, 1, tok), gates.reshape(experts, 1, tok), wg, wu, wd)


def up_grad_kernel(*refs, sources):
    rows = refs[: 3 * sources]
    gate_ref, up_ref = refs[3 * sources :]
    for n, out_ref in ((1, gate_ref), (2, up_ref)):
        total = None
        for s in range(sources):
            term = dot_tn(rows[3 * s][0], rows[3 * s + n][0])
            total = term if total is None else total + term
        out_ref[...] = total.astype(bf16).reshape(out_ref.shape)


def down_grad_kernel(*refs, sources, parts):
    rows, down_ref = refs[: 2 * sources], refs[-1]
    width = MODEL_WIDTH // parts
    total = None
    for s in range(sources):
        term = dot_tn(rows[2 * s][0], rows[2 * s + 1][0])
        total = term if total is None else total + term
    total = total.astype(bf16)
    for c in range(parts):
        down_ref[c, 0] = total[:, c * width : (c + 1) * width]


def row_specs(rows):
    return [pl.BlockSpec((1,) + a.shape[1:], lambda e: (e, 0, 0)) for r in rows for a in r]


def up_weight_grads(rows, parts):
    experts = rows[0][0].shape[0]
    shape = (parts, experts, MODEL_WIDTH // parts, FF)
    out = pl.BlockSpec((parts, 1) + shape[2:], lambda e: (0, e, 0, 0))
    return pl.pallas_call(
        functools.partial(up_grad_kernel, sources=len(rows)),
        grid=(experts,),
        in_specs=row_specs(rows),
        out_specs=[out, out],
        out_shape=[jax.ShapeDtypeStruct(shape, bf16)] * 2,
        compiler_params=pltpu.CompilerParams(vmem_limit_bytes=VMEM_LIMIT),
        cost_estimate=SMALL,
        name="up_weight_grads",
    )(*[a for r in rows for a in r])


def down_weight_grads(rows, parts):
    experts = rows[0][0].shape[0]
    shape = (parts, experts, FF, MODEL_WIDTH // parts)
    return pl.pallas_call(
        functools.partial(down_grad_kernel, sources=len(rows), parts=parts),
        grid=(experts,),
        in_specs=row_specs(rows),
        out_specs=pl.BlockSpec((parts, 1) + shape[2:], lambda e: (0, e, 0, 0)),
        out_shape=jax.ShapeDtypeStruct(shape, bf16),
        compiler_params=pltpu.CompilerParams(vmem_limit_bytes=VMEM_LIMIT),
        cost_estimate=SMALL,
        name="down_weight_grads",
    )(*[a for r in rows for a in r])


def swap(x, mask):
    return lax.ppermute(x, "ctx", [(i, i ^ mask) for i in range(lax.axis_size("ctx"))])


def blocks_ctx(x):
    half = x.shape[0] // 2
    near, far = swap(x, 2), swap(x, 4)
    diagonal = jnp.concatenate([swap(near[:half], 4), swap(far[half:], 2)], 0)
    even = [x, near, far, diagonal]
    odd = [swap(block, 1) for block in even]
    return [b for pair in zip(even, odd) for b in pair]


def gather_ctx(x):
    if lax.axis_size("ctx") != 8:
        return [lax.all_gather(x, "ctx", axis=0, tiled=True)]
    return blocks_ctx(x)


def scatter_ctx(x):
    if lax.axis_size("ctx") != 8:
        return lax.psum_scatter(x, "ctx", scatter_dimension=0, tiled=True).astype(f32)
    rows = x.shape[0] // 8
    half = rows // 2
    block = [x[m * rows : (m + 1) * rows] for m in range(8)]
    diagonal, near, far, own = (
        block[m].astype(f32) + swap(block[m + 1], 1).astype(f32) for m in (6, 2, 4, 0)
    )
    diagonal = diagonal.astype(bf16)
    near_top = near[:half] + swap(diagonal[:half], 4).astype(f32)
    far_end = far[half:] + swap(diagonal[half:], 2).astype(f32)
    near = jnp.concatenate([near_top.astype(bf16), near[half:].astype(bf16)], 0)
    far = jnp.concatenate([far[:half].astype(bf16), far_end.astype(bf16)], 0)
    return own + swap(near, 2).astype(f32) + swap(far, 4).astype(f32)


def shift(x, distance):
    n = lax.axis_size("wt")
    return lax.ppermute(x, "wt", [(i, (i + distance) % n) for i in range(n)])


def beside(results, *arrivals):
    out = lax.optimization_barrier((results, arrivals))
    return (out[0],) + tuple(out[1])


def gather_all(x):
    ctx, wt = lax.axis_size("ctx"), lax.axis_size("wt")
    if ctx != 8 or wt != 4:
        return [lax.all_gather(x, ALL, axis=0, tiled=True)], [1], jnp.zeros((1,), jnp.int32), x
    ctx_index, wt_index = lax.axis_index("ctx"), lax.axis_index("wt")
    others = jnp.concatenate([shift(x, d) for d in (1, 2, 3)], 0)
    pieces = blocks_ctx(x) + blocks_ctx(others)
    m = jnp.arange(8, dtype=jnp.int32)
    own = (ctx_index ^ m) * wt + wt_index
    d = jnp.arange(1, 4, dtype=jnp.int32)
    rest = ((ctx_index ^ m) * wt)[:, None] + ((wt_index - d) % wt)[None, :]
    places = jnp.concatenate([own, rest.reshape(-1)]).astype(jnp.int32)
    return pieces, [1] * 8 + [3] * 8, places, others


def outer_sum(a, b):
    ctx, wt = lax.axis_size("ctx"), lax.axis_size("wt")
    if ctx != 8 or wt != 4:
        return lax.psum_scatter(
            dot_tn(a, b).astype(bf16), ALL, scatter_dimension=0, tiled=True
        ).astype(f32)
    part = scatter_ctx(outer(a, b))
    rows = part.shape[0] // wt
    low = part.astype(bf16)
    at = lambda d: ((lax.axis_index("wt") + d) % wt) * rows
    total = lax.dynamic_slice_in_dim(part, at(0), rows, 0)
    for d in range(1, wt):
        total = total + shift(lax.dynamic_slice_in_dim(low, at(d), rows, 0), d).astype(f32)
    return total


def spread_sum(x):
    return jnp.sum(lax.all_to_all(x, ALL, 0, 0, tiled=True), 0)


def after(x, *others):
    return lax.optimization_barrier((x,) + others)[0]


def rope_tables(positions, width):
    middle = HEAD_SIZE // 2
    frequency = jnp.power(
        jnp.float32(rope_base), -2.0 * jnp.arange(middle, dtype=f32) / HEAD_SIZE
    )
    angles = positions.astype(f32)[:, None] * frequency[None, :]
    times = width // middle
    return jnp.tile(jnp.cos(angles), (1, times)), jnp.tile(jnp.sin(angles), (1, times))


def turn(values, cosine, sine, direction):
    middle = HEAD_SIZE // 2
    first = lax.broadcasted_iota(jnp.int32, values.shape, 1) % HEAD_SIZE < middle
    turned = jnp.where(first, -jnp.roll(values, -middle, 1), jnp.roll(values, middle, 1))
    width = values.shape[1]
    return values * cosine[:, :width] + direction * turned * sine[:, :width]


def norm_forward(values, gain):
    inverse = lax.rsqrt(jnp.mean(values * values, -1, keepdims=True) + norm_eps)
    return (values * inverse * gain, inverse)


def norm_backward(values, inverse, gain, grad_out):
    scaled = gain * grad_out
    gain_grad = jnp.sum(grad_out * values * inverse, 0)
    projection = jnp.mean(scaled * values, -1, keepdims=True)
    return (inverse * scaled - values * inverse * inverse * inverse * projection, gain_grad)


def per_device(
    layer_input,
    attention_gain,
    query_weight,
    key_matrix,
    value_matrix,
    output_weight,
    mixture_gain,
    router_weight,
    gate_weight,
    up_weight,
    down_weight,
    expert_routes,
    prompt_deal,
    output_grad,
):
    tok = layer_input.shape[1]
    prompt_local = tok - CONT_DEV * CLEN
    block_rows = prompt_local // 2
    context_size = lax.axis_size("ctx")
    shard_count = lax.axis_size("wt")
    expert_count = gate_weight.shape[0]
    capacity = 8 * ((tok * TOP * 7 // (4 * EXPERTS) + 7) // 8)
    ctx_index = lax.axis_index("ctx")
    wt_index = lax.axis_index("wt")
    inputs = layer_input[0].astype(f32)
    routes = expert_routes[0]
    deal_row = prompt_deal[0]
    out_low = output_grad[0]
    out_grad = out_low.astype(f32)

    own_rows = query_weight.shape[0]
    packed = jnp.concatenate(
        [
            query_weight,
            key_matrix,
            value_matrix,
            output_weight.T,
            router_weight,
            attention_gain[:, None],
            mixture_gain[:, None],
            jnp.zeros((own_rows, 94), bf16),
        ],
        1,
    )
    pieces, counts, block_places, first_part = gather_all(packed)

    gate_full = lax.all_gather(gate_weight, "ctx", axis=0, tiled=False)
    up_full = lax.all_gather(up_weight, "ctx", axis=0, tiled=False)
    down_full = lax.all_gather(down_weight, "ctx", axis=0, tiled=False)

    mask = jnp.any(
        routes[:, :, None] == jnp.arange(EXPERTS, dtype=jnp.int32)[None, None, :], 1
    )
    order = jnp.arange(tok, dtype=jnp.int32)
    before = (order[None, :] < order[:, None]).astype(bf16)
    rank = jnp.where(mask, dot(before, mask.astype(bf16)), -1.0)
    ranks = lax.all_to_all(
        rank.T.reshape(shard_count, expert_count, tok), "wt", 0, 0, tiled=True
    )
    last = shard_count - 1
    grads_in = {0: out_low, last: shift(after(out_low, first_part), -1)}

    pieces, grads_in[last] = beside(pieces, grads_in[last])
    local_rows = jnp.arange(tok, dtype=jnp.int32)
    mine = lax.dynamic_slice_in_dim(deal_row, 2 * ctx_index, 2, 0)
    prompt_place = (
        jnp.where(local_rows < block_rows, mine[0], mine[1]) * block_rows
        + local_rows % block_rows
    )
    positions = jnp.where(
        local_rows < prompt_local, prompt_place, PROMPT + (local_rows - prompt_local) % CLEN
    )
    cosine, sine = rope_tables(positions, 128)
    normed_one, turned_query, *kv_low, qkv_full, output_t, rest, gain_rows = project(
        layer_input[0], cosine, sine, pieces, counts, block_places
    )
    router_full = rest[:, :EXPERTS]
    first_gain, second_gain = gain_rows[0], gain_rows[1]
    inverse_one = lax.rsqrt(jnp.mean(inputs * inputs, -1, keepdims=True) + norm_eps)
    kv_own = [low[prompt_local:] for low in kv_low]
    kv_pieces = [gather_ctx(low[:prompt_local]) for low in kv_low]

    places = deal_row
    if context_size == 8:
        pairs = deal_row.reshape(2, 2, 2, 2)
        for axis, bit in ((0, 4), (1, 2), (2, 1)):
            pairs = jnp.where(ctx_index & bit > 0, jnp.flip(pairs, axis), pairs)
        places = pairs.reshape(-1)
    low = (mine[0] > mine[1]).astype(jnp.int32)
    starts = jnp.stack(
        [
            low * block_rows,
            (1 - low) * block_rows,
            jnp.min(mine) * block_rows,
            jnp.max(mine) * block_rows,
        ]
    ).astype(jnp.int32)
    heads = []
    for half in range(2):
        result = attention_forward(
            turned_query, kv_pieces[half], kv_own[half], places, starts, block_rows, half
        )
        d = last - 1 - half
        grads_in[d] = shift(grads_in[d + 1], -1)
        result, grads_in[d] = beside(result, grads_in[d])
        if half == 0:
            turned_query = after(turned_query, result[0])
        heads.append(result)
    for d in range(last - 3, 0, -1):
        grads_in[d] = shift(grads_in[d + 1], -1)
    attended = jnp.concatenate([out for out, _ in heads], 1)
    lse = [row for _, row in heads]

    branch = dot_nt(attended, output_t)
    middle = inputs + resid_scale * branch
    normed_mid, inverse_two = norm_forward(middle, second_gain)
    normed_two = normed_mid.astype(bf16)
    logits = dot(normed_two, router_full)
    top = jnp.max(jnp.where(mask, logits, masked_score), -1, keepdims=True)
    raised = jnp.where(mask, jnp.exp(jnp.where(mask, logits - top, 0.0)), 0.0)
    gates = raised / jnp.sum(raised, -1, keepdims=True)

    gates_out = gates.T.reshape(shard_count, expert_count, tok)
    gates_in = []
    for d in range(shard_count):
        piece = lax.dynamic_index_in_dim(gates_out, (wt_index + d) % shard_count, 0, False)
        gates_in.append(shift(piece, d) if d else piece)
    got = {0: normed_two}
    partial, mixed, gate_grads, rows = {}, {}, {}, []
    carried = None

    def add(a, b):
        return b if a is None else (a.astype(f32) + b.astype(f32)).astype(bf16)

    for d in [0] + list(range(last, 0, -1)):
        source = (wt_index - d) % shard_count
        rank_in = lax.dynamic_index_in_dim(ranks, source, 0, False)
        result = expert_pass(
            got[d], grads_in[d], rank_in, gates_in[d], gate_full, up_full, down_full, capacity
        )
        coming = d - 1 if d else last
        if coming:
            result, got[coming] = beside(result, shift(got[(coming + 1) % shard_count], -1))
        if 0 < d <= last - 2:
            carried = shift(after(add(carried, partial[d + 2]), got[d]), -1)
            result, carried = beside(result, carried)
        mixed[d], partial[d], d_gate, *kept = result
        rows.append(kept)
        d_gate = d_gate.reshape(expert_count, tok)
        gate_grads[d] = shift(d_gate, shard_count - d) if d else d_gate
        if coming:
            got[coming] = after(got[coming], partial[d])
    carried = shift(add(carried, partial[2]), -1)
    (gate_grad, up_grad), carried = beside(
        up_weight_grads([(after(r[0], partial[1]), r[3], r[4]) for r in rows], context_size),
        carried,
    )
    carried = shift(add(carried, partial[1]), -1)
    down_grad, carried = beside(
        down_weight_grads([(after(r[2], gate_grad), r[1]) for r in rows], context_size), carried
    )

    stacked = jnp.stack([gate_grads[d] for d in range(shard_count)], 0)
    stacked = jnp.roll(stacked, wt_index, 0).reshape(EXPERTS, tok).T
    grad_logits = (gates * (stacked - jnp.sum(gates * stacked, -1, keepdims=True))).astype(bf16)
    grad_normed_two = partial[0].astype(f32) + carried.astype(f32)
    grad_normed_two = grad_normed_two + dot_nt(grad_logits, router_full)
    grad_mid_norm, second_gain_grad = norm_backward(
        middle, inverse_two, second_gain, grad_normed_two
    )
    grad_middle = out_grad + grad_mid_norm
    grad_branch = (resid_scale * grad_middle).astype(bf16)
    grad_attended = dot(grad_branch, output_t).astype(bf16)
    gate_share, up_share, down_share = (
        lax.psum_scatter(grad, "ctx", scatter_dimension=0, tiled=False).astype(f32)
        for grad in (gate_grad, up_grad, down_grad)
    )
    output_share = outer_sum(grad_branch, attended)
    devices = context_size * shard_count
    small = jnp.concatenate(
        [
            dot_tn(normed_two, grad_logits).reshape(devices, own_rows * EXPERTS),
            second_gain_grad.reshape(devices, own_rows),
        ],
        1,
    )
    small = spread_sum(small)

    d_query, owned, ours = [], [], []
    carried = None
    query = after(turned_query, grad_attended)
    for half in range(2):
        result = attention_backward(
            query,
            grad_attended,
            lse[half],
            attended,
            cosine,
            sine,
            kv_pieces[half],
            kv_own[half],
            places,
            starts,
            block_rows,
            half,
        )
        d = last - half
        carried = shift(after(add(carried, mixed[d]), query), -1)
        result, carried = beside(result, carried)
        d_q, d_kv, d_key_own, d_value_own = result
        query = after(query, d_q)
        d_query.append(d_q)
        owned.append(scatter_ctx(d_kv))
        ours.append((d_key_own, d_value_own))
    for d in range(last - 2, 0, -1):
        carried = shift(add(carried, mixed[d]), -1)
    mixture = mixed[0].astype(f32) + carried.astype(f32)
    layer_output = (middle + resid_scale * mixture).astype(bf16)
    d_key, d_value = (
        jnp.concatenate(
            [
                jnp.concatenate([owned[half][:, 256 * n : 256 * n + 256], ours[half][n]], 0)
                for half in range(2)
            ],
            1,
        )
        for n in range(2)
    )
    grad_key_low = turn(d_key, jnp.tile(cosine, (1, 4)), jnp.tile(sine, (1, 4)), -1.0).astype(
        bf16
    )
    grad_qkv = jnp.concatenate(d_query + [grad_key_low, d_value.astype(bf16)], 1)
    grad_qkv, layer_output = beside(grad_qkv, layer_output)
    qkv_share = outer_sum(normed_one, grad_qkv)
    grad_normed_one = dot_nt(grad_qkv, qkv_full)
    grad_input_norm, first_gain_grad = norm_backward(
        inputs, inverse_one, first_gain, grad_normed_one
    )
    input_grad = (grad_middle + grad_input_norm).astype(bf16)

    first_gain_share = spread_sum(first_gain_grad.reshape(devices, own_rows))
    return (
        layer_output[None],
        input_grad[None],
        first_gain_share,
        qkv_share[:, :1024],
        qkv_share[:, 1024:1536],
        qkv_share[:, 1536:],
        output_share.T,
        small[own_rows * EXPERTS :],
        small[: own_rows * EXPERTS].reshape(own_rows, EXPERTS),
        gate_share,
        up_share,
        down_share,
    )


def solution(mesh):
    return jax.shard_map(
        per_device,
        mesh=mesh,
        in_specs=(
            P("wt", "ctx", None),
            P(("ctx", "wt")),
            P(("ctx", "wt"), None),
            P(("ctx", "wt"), None),
            P(("ctx", "wt"), None),
            P(None, ("ctx", "wt")),
            P(("ctx", "wt")),
            P(("ctx", "wt"), None),
            P("wt", "ctx", None),
            P("wt", "ctx", None),
            P("wt", None, "ctx"),
            P("wt", "ctx", None),
            P("wt", None),
            P("wt", "ctx", None),
        ),
        out_specs=(
            P("wt", "ctx", None),
            P("wt", "ctx", None),
            P(("ctx", "wt")),
            P(("ctx", "wt"), None),
            P(("ctx", "wt"), None),
            P(("ctx", "wt"), None),
            P(None, ("ctx", "wt")),
            P(("ctx", "wt")),
            P(("ctx", "wt"), None),
            P("wt", "ctx", None),
            P("wt", "ctx", None),
            P("wt", None, "ctx"),
        ),
        check_vma=False,
    )
```

```python
import functools

import jax
import jax.numpy as jnp
from jax import lax
from jax.experimental import pallas as pl
from jax.experimental.pallas import tpu as pltpu
from jax.sharding import PartitionSpec as P

MODEL_WIDTH = 1024
HQ = 16
KEY_VALUE_HEADS = 8
HEAD_SIZE = 64
EXPERTS = 32
TOP = 8
PROMPT = 2048
CLEN = 256
CONT_DEV = 2
FF = 512
QTILE = 128
KV_WIDTH = KEY_VALUE_HEADS * HEAD_SIZE
ALL = ("ctx", "wt")

att_scale = 0.015625
resid_scale = 0.22
norm_eps = 1e-06
rope_base = 10000.0
masked_score = -1e30

bf16 = jnp.bfloat16
f32 = jnp.float32
VMEM_LIMIT = 60 * 1024 * 1024
SMALL = pl.CostEstimate(flops=1_000_000_000, bytes_accessed=1_000_000, transcendentals=0)

NT = (((1,), (1,)), ((), ()))
TN = (((0,), (0,)), ((), ()))


def dot(a, b):
    return jnp.dot(a, b, preferred_element_type=f32)


def dot_nt(a, b):
    return lax.dot_general(a, b, NT, preferred_element_type=f32)


def dot_tn(a, b):
    return lax.dot_general(a, b, TN, preferred_element_type=f32)


def turn_tile(values, cosine, sine, direction):
    middle = HEAD_SIZE // 2
    first = lax.broadcasted_iota(jnp.int32, values.shape, 1) % HEAD_SIZE < middle
    turned = jnp.where(first, -pltpu.roll(values, 128 - middle, 1), pltpu.roll(values, middle, 1))
    return values * cosine + direction * turned * sine


def project_kernel(places, x_ref, cos_ref, sin_ref, *refs, counts):
    pieces = refs[: len(counts)]
    normed_ref, q_ref, *kv_refs, qkv_ref, out_ref, rest_ref, gains_ref = refs[len(counts) :]
    rows = MODEL_WIDTH // sum(counts)
    at = 0
    for piece, count in zip(pieces, counts):
        for i in range(count):
            source = slice(i * rows, (i + 1) * rows)
            target = pl.ds(pl.multiple_of(places[at] * rows, rows), rows)
            qkv_ref[target, :] = piece[source, :2048]
            out_ref[target, :] = piece[source, 2048:3072]
            rest_ref[target, :] = piece[source, 3072:]
            at += 1
    gains = rest_ref[...].astype(f32).T[EXPERTS : EXPERTS + 8]
    gains_ref[...] = gains
    x = x_ref[...].astype(f32)
    inverse = lax.rsqrt(jnp.mean(x * x, -1, keepdims=True) + norm_eps)
    normed_ref[...] = (x * inverse * gains[:1]).astype(bf16)
    for c in range(8):
        raw = dot(normed_ref[...], qkv_ref[:, 256 * c : 256 * (c + 1)])
        for h in range(2):
            part = raw[:, 128 * h : 128 * (h + 1)]
            if c < 6:
                part = turn_tile(part, cos_ref[...], sin_ref[...], 1.0)
            column = 256 * c + 128 * h
            if column < 1024:
                q_ref[:, column : column + 128] = part.astype(bf16)
            else:
                column -= 1024
                at = column // KV_WIDTH * 256 + column % 256
                kv_refs[column % KV_WIDTH // 256][:, at : at + 128] = part.astype(bf16)


def project(x, cosine, sine, pieces, counts, places):
    tok = x.shape[0]
    shape = jax.ShapeDtypeStruct
    whole = pl.BlockSpec(memory_space=pltpu.VMEM)
    return pl.pallas_call(
        functools.partial(project_kernel, counts=counts),
        in_specs=[pl.BlockSpec(memory_space=pltpu.SMEM)] + [whole] * (3 + len(pieces)),
        out_specs=[whole] * 8,
        out_shape=[
            shape((tok, MODEL_WIDTH), bf16),
            shape((tok, HQ * HEAD_SIZE), bf16),
            shape((tok, KV_WIDTH), bf16),
            shape((tok, KV_WIDTH), bf16),
            shape((MODEL_WIDTH, 2048), bf16),
            shape((MODEL_WIDTH, 1024), bf16),
            shape((MODEL_WIDTH, 128), bf16),
            shape((8, MODEL_WIDTH), f32),
        ],
        compiler_params=pltpu.CompilerParams(vmem_limit_bytes=VMEM_LIMIT),
        cost_estimate=SMALL,
        name="project",
    )(places, x, cosine, sine, *pieces)


def outer_kernel(mine, a_ref, b_ref, out_ref):
    out_ref[...] = dot_tn(a_ref[...], b_ref[...]).astype(bf16)


def outer(a, b):
    tok, columns = b.shape
    mine = lax.axis_index("ctx").astype(jnp.int32).reshape(1)
    return pl.pallas_call(
        outer_kernel,
        grid_spec=pltpu.PrefetchScalarGridSpec(
            num_scalar_prefetch=1,
            grid=(8,),
            in_specs=[
                pl.BlockSpec((tok, 128), lambda m, mine: (0, m ^ mine[0])),
                pl.BlockSpec((tok, columns), lambda m, mine: (0, 0)),
            ],
            out_specs=pl.BlockSpec((128, columns), lambda m, mine: (m, 0)),
        ),
        out_shape=jax.ShapeDtypeStruct((MODEL_WIDTH, columns), bf16),
        compiler_params=pltpu.CompilerParams(vmem_limit_bytes=VMEM_LIMIT),
        cost_estimate=SMALL,
        name="outer",
    )(mine, a, b)


def gather_keys(pieces, scratch, places, block_rows):
    at = 0
    for piece in pieces:
        for b in range(piece.shape[0] // block_rows):
            start = pl.multiple_of(places[at] * block_rows, block_rows)
            scratch[pl.ds(start, block_rows), :] = piece[b * block_rows : (b + 1) * block_rows, :]
            at += 1


def pair_rows(ref, start, rows, j):
    both = ref[pl.ds(start, rows), 2 * HEAD_SIZE * j : 2 * HEAD_SIZE * (j + 1)]
    return jnp.concatenate([both[:, :HEAD_SIZE], both[:, HEAD_SIZE:]], 0)


def attention_forward_kernel(places, starts, q_ref, *refs, block_rows, pieces):
    k_refs, v_refs = refs[:pieces], refs[pieces : 2 * pieces]
    kc_ref, vc_ref, o_ref, lse_ref, k_scr, v_scr = refs[2 * pieces :]
    prompt_local = 2 * block_rows
    gather_keys(k_refs, k_scr, places, block_rows)
    gather_keys(v_refs, v_scr, places, block_rows)

    def store(start, rows, j, out, m, total, at):
        out = (out / total).astype(bf16)
        lse = m + jnp.log(total)
        o_ref[pl.ds(start, rows), 2 * HEAD_SIZE * j : 2 * HEAD_SIZE * (j + 1)] = jnp.concatenate(
            [out[:rows], out[rows:]], 1
        )
        row = jnp.broadcast_to(lse, (2 * rows, 128)).T[:1]
        lse_ref[0, 2 * j : 2 * j + 2, pl.ds(at, rows)] = jnp.concatenate(
            [row[:, :rows], row[:, rows:]], 0
        )

    def tile(i, _):
        start = pl.multiple_of(prompt_local + i * QTILE, 64)
        per = CLEN // QTILE
        seg = pl.multiple_of((i // per) * CLEN, CLEN)
        for j in range(2):
            lanes = slice(HEAD_SIZE * j, HEAD_SIZE * (j + 1))
            q = pair_rows(q_ref, start, QTILE, j) * bf16(att_scale)
            s1 = dot_nt(q, k_scr[:, lanes])
            s2 = dot_nt(q, kc_ref[pl.ds(seg, CLEN), lanes])
            place = lax.broadcasted_iota(jnp.int32, s2.shape, 0) % QTILE + (i % per) * QTILE
            s2 = jnp.where(lax.broadcasted_iota(jnp.int32, s2.shape, 1) <= place, s2, masked_score)
            m = jnp.maximum(jnp.max(s1, 1, keepdims=True), jnp.max(s2, 1, keepdims=True))
            e1 = jnp.exp(s1 - m)
            e2 = jnp.exp(s2 - m)
            total = jnp.sum(e1, 1, keepdims=True) + jnp.sum(e2, 1, keepdims=True)
            out = dot(e1.astype(bf16), v_scr[:, lanes])
            out = out + dot(e2.astype(bf16), vc_ref[pl.ds(seg, CLEN), lanes])
            store(start, QTILE, j, out, m, total, pl.multiple_of(i * QTILE, QTILE))
        return 0

    lax.fori_loop(0, CONT_DEV * CLEN // QTILE, tile, 0)

    for half, keys in enumerate((PROMPT // 2, PROMPT)):
        start = pl.multiple_of(starts[half], block_rows)
        for j in range(2):
            lanes = slice(HEAD_SIZE * j, HEAD_SIZE * (j + 1))
            q = pair_rows(q_ref, start, block_rows, j) * bf16(att_scale)
            s = dot_nt(q, k_scr[:keys, lanes])
            place = lax.broadcasted_iota(jnp.int32, s.shape, 0) % block_rows + starts[2 + half]
            s = jnp.where(lax.broadcasted_iota(jnp.int32, s.shape, 1) <= place, s, masked_score)
            m = jnp.max(s, 1, keepdims=True)
            e = jnp.exp(s - m)
            total = jnp.sum(e, 1, keepdims=True)
            out = dot(e.astype(bf16), v_scr[:keys, lanes])
            store(start, block_rows, j, out, m, total, CONT_DEV * CLEN + half * block_rows)


def key_specs(pieces, own):
    spec = pl.BlockSpec
    keys = [spec((p.shape[0], 128), lambda g, *_: (0, g)) for p in pieces]
    values = [spec((p.shape[0], 128), lambda g, *_: (0, 2 + g)) for p in pieces]
    ours = [spec((own, 128), lambda g, *_: (0, g)), spec((own, 128), lambda g, *_: (0, 2 + g))]
    return keys + values + ours


def attention_forward(q, pieces, kv_own, places, starts, block_rows, half):
    tok = q.shape[0]
    spec = pl.BlockSpec
    return pl.pallas_call(
        functools.partial(
            attention_forward_kernel, block_rows=block_rows, pieces=len(pieces)
        ),
        grid_spec=pltpu.PrefetchScalarGridSpec(
            num_scalar_prefetch=2,
            grid=(2,),
            in_specs=[spec((tok, 256), lambda g, *_: (0, 2 * half + g))]
            + key_specs(pieces, kv_own.shape[0]),
            out_specs=[
                spec((tok, 256), lambda g, *_: (0, g)),
                spec((1, 4, tok), lambda g, *_: (g, 0, 0)),
            ],
            scratch_shapes=[
                pltpu.VMEM((PROMPT, 2 * HEAD_SIZE), bf16),
                pltpu.VMEM((PROMPT, 2 * HEAD_SIZE), bf16),
            ],
        ),
        out_shape=[
            jax.ShapeDtypeStruct((tok, HQ * HEAD_SIZE // 2), bf16),
            jax.ShapeDtypeStruct((2, 4, tok), f32),
        ],
        compiler_params=pltpu.CompilerParams(vmem_limit_bytes=VMEM_LIMIT),
        cost_estimate=SMALL,
        name="attention_forward",
    )(places, starts, q, *pieces, *pieces, kv_own, kv_own)


def attention_backward_kernel(
    places, starts, q_ref, do_ref, lse_ref, o_ref, cos_ref, sin_ref, *refs, block_rows, pieces
):
    k_refs, v_refs = refs[:pieces], refs[pieces : 2 * pieces]
    kc_ref, vc_ref, dq_ref, dkv_ref, dkc_ref, dvc_ref = refs[2 * pieces : 2 * pieces + 6]
    k_scr, v_scr, dk_acc, dv_acc, dq_acc = refs[2 * pieces + 6 :]
    prompt_local = 2 * block_rows
    gather_keys(k_refs, k_scr, places, block_rows)
    gather_keys(v_refs, v_scr, places, block_rows)
    dk_acc[...] = jnp.zeros_like(dk_acc)
    dv_acc[...] = jnp.zeros_like(dv_acc)
    dkc_ref[...] = jnp.zeros_like(dkc_ref)
    dvc_ref[...] = jnp.zeros_like(dvc_ref)

    def row_pair(ref, start, rows, j):
        both = ref[0, 2 * j : 2 * j + 2, pl.ds(start, rows)]
        return jnp.concatenate([both[:1], both[1:]], 1)

    def centre(start, rows, j, d_out):
        product = d_out.astype(f32) * pair_rows(o_ref, start, rows, j).astype(f32)
        ones = jnp.ones((8, HEAD_SIZE), f32)
        return lax.dot_general(
            ones, product, NT, precision=lax.Precision.HIGHEST, preferred_element_type=f32
        )[:1]

    def part(k, v, q, d_out, lse, delta, allowed):
        s = dot_nt(k, q)
        if allowed is not None:
            s = jnp.where(allowed(s.shape), s, masked_score)
        p = jnp.exp(s - lse)
        d_p = dot_nt(v, d_out)
        d_s = (p * (d_p - delta)).astype(bf16)
        return dot_tn(d_s, k), dot(d_s, q), dot(p.astype(bf16), d_out)

    def store(start, rows, j, d_q):
        d_q = d_q * att_scale
        dq_acc[pl.ds(start, rows), 2 * HEAD_SIZE * j : 2 * HEAD_SIZE * (j + 1)] = jnp.concatenate(
            [d_q[:rows], d_q[rows:]], 1
        )

    def tile(i, _):
        start = pl.multiple_of(prompt_local + i * QTILE, 64)
        per = CLEN // QTILE
        seg = pl.multiple_of((i // per) * CLEN, CLEN)
        own = pl.ds(seg, CLEN)
        lane_start = pl.multiple_of(i * QTILE, QTILE)

        def allowed(shape):
            place = lax.broadcasted_iota(jnp.int32, shape, 1) % QTILE + (i % per) * QTILE
            return lax.broadcasted_iota(jnp.int32, shape, 0) <= place

        for j in range(2):
            lanes = slice(HEAD_SIZE * j, HEAD_SIZE * (j + 1))
            q = pair_rows(q_ref, start, QTILE, j) * bf16(att_scale)
            d_out = pair_rows(do_ref, start, QTILE, j)
            lse = row_pair(lse_ref, lane_start, QTILE, j)
            delta = centre(start, QTILE, j, d_out)
            a, b, c = part(k_scr[:, lanes], v_scr[:, lanes], q, d_out, lse, delta, None)
            dk_acc[:, lanes] += b
            dv_acc[:, lanes] += c
            d_q = a
            a, b, c = part(
                kc_ref[own, lanes], vc_ref[own, lanes], q, d_out, lse, delta, allowed
            )
            dkc_ref[own, lanes] += b
            dvc_ref[own, lanes] += c
            store(start, QTILE, j, d_q + a)
        return 0

    lax.fori_loop(0, CONT_DEV * CLEN // QTILE, tile, 0)

    for half, keys in enumerate((PROMPT // 2, PROMPT)):
        start = pl.multiple_of(starts[half], block_rows)
        at = CONT_DEV * CLEN + half * block_rows

        def allowed(shape):
            place = lax.broadcasted_iota(jnp.int32, shape, 1) % block_rows + starts[2 + half]
            return lax.broadcasted_iota(jnp.int32, shape, 0) <= place

        for j in range(2):
            lanes = slice(HEAD_SIZE * j, HEAD_SIZE * (j + 1))
            q = pair_rows(q_ref, start, block_rows, j) * bf16(att_scale)
            d_out = pair_rows(do_ref, start, block_rows, j)
            lse = row_pair(lse_ref, at, block_rows, j)
            delta = centre(start, block_rows, j, d_out)
            a, b, c = part(
                k_scr[:keys, lanes], v_scr[:keys, lanes], q, d_out, lse, delta, allowed
            )
            dk_acc[:keys, lanes] += b
            dv_acc[:keys, lanes] += c
            store(start, block_rows, j, a)

    g = pl.program_id(0)
    key_lanes = pl.ds(pl.multiple_of(g * 128, 128), 128)
    value_lanes = pl.ds(pl.multiple_of(256 + g * 128, 128), 128)
    for b in range(PROMPT // block_rows):
        source = pl.ds(pl.multiple_of(places[b] * block_rows, block_rows), block_rows)
        rows = slice(b * block_rows, (b + 1) * block_rows)
        dkv_ref[rows, key_lanes] = dk_acc[source, :].astype(bf16)
        dkv_ref[rows, value_lanes] = dv_acc[source, :].astype(bf16)
    for c in range(2):
        lanes = slice(128 * c, 128 * (c + 1))
        dq_ref[:, lanes] = turn_tile(dq_acc[:, lanes], cos_ref[...], sin_ref[...], -1.0).astype(
            bf16
        )


def attention_backward(
    q, d_out, lse, attended, cosine, sine, pieces, kv_own, places, starts, block_rows, half
):
    tok = q.shape[0]
    own = kv_own.shape[0]
    spec = pl.BlockSpec
    wide = spec((tok, 256), lambda g, *_: (0, 2 * half + g))
    ours = spec((own, 128), lambda g, *_: (0, g))
    table = spec((tok, 128), lambda g, *_: (0, 0))
    return pl.pallas_call(
        functools.partial(
            attention_backward_kernel, block_rows=block_rows, pieces=len(pieces)
        ),
        grid_spec=pltpu.PrefetchScalarGridSpec(
            num_scalar_prefetch=2,
            grid=(2,),
            in_specs=[wide, wide, spec((1, 4, tok), lambda g, *_: (g, 0, 0)), wide, table, table]
            + key_specs(pieces, own),
            out_specs=[
                spec((tok, 256), lambda g, *_: (0, g)),
                spec((PROMPT, KV_WIDTH), lambda g, *_: (0, 0)),
                ours,
                ours,
            ],
            scratch_shapes=[
                pltpu.VMEM((PROMPT, 2 * HEAD_SIZE), bf16),
                pltpu.VMEM((PROMPT, 2 * HEAD_SIZE), bf16),
                pltpu.VMEM((PROMPT, 2 * HEAD_SIZE), f32),
                pltpu.VMEM((PROMPT, 2 * HEAD_SIZE), f32),
                pltpu.VMEM((tok, 4 * HEAD_SIZE), f32),
            ],
        ),
        out_shape=[
            jax.ShapeDtypeStruct((tok, HQ * HEAD_SIZE // 2), bf16),
            jax.ShapeDtypeStruct((PROMPT, KV_WIDTH), bf16),
            jax.ShapeDtypeStruct((own, KV_WIDTH // 2), f32),
            jax.ShapeDtypeStruct((own, KV_WIDTH // 2), f32),
        ],
        compiler_params=pltpu.CompilerParams(vmem_limit_bytes=VMEM_LIMIT),
        cost_estimate=SMALL,
        name="attention_backward",
    )(places, starts, q, d_out, lse, attended, cosine, sine, *pieces, *pieces, kv_own, kv_own)


def expert_kernel(
    counts,
    a2_ref,
    df_ref,
    rank_ref,
    gate_ref,
    wg_ref,
    wu_ref,
    wd_ref,
    mix_ref,
    da_ref,
    dg_ref,
    x_ref,
    dy_ref,
    z_ref,
    dgate_ref,
    dup_ref,
    mix_acc,
    da_acc,
    *,
    sizes,
):
    e = pl.program_id(0)

    @pl.when(e == 0)
    def _():
        mix_acc[...] = jnp.zeros_like(mix_acc)
        da_acc[...] = jnp.zeros_like(da_acc)

    def body(size):
        rank = rank_ref[0]
        gates = gate_ref[0]
        tok = rank.shape[1]
        slot = lax.broadcasted_iota(jnp.int32, (size, tok), 0).astype(f32)
        hit = slot == rank
        chosen = hit.astype(f32).astype(bf16)
        gate = jnp.sum(jnp.where(hit, gates, 0.0), 1, keepdims=True)
        x = dot(chosen, a2_ref[...]).astype(bf16)
        d_mix = resid_scale * dot(chosen, df_ref[...])
        wg = wg_ref[:, 0].reshape(MODEL_WIDTH, FF)
        wu = wu_ref[:, 0].reshape(MODEL_WIDTH, FF)
        wd = jnp.concatenate([wd_ref[c, 0] for c in range(wd_ref.shape[0])], 1)
        g = dot(x, wg)
        u = dot(x, wu)
        sig = jax.nn.sigmoid(g)
        z = (g * sig * u).astype(bf16)
        y = dot(z, wd).astype(bf16).astype(f32)
        d_gate_value = jnp.sum(d_mix * y, 1, keepdims=True)
        dg_ref[0] = jnp.sum(jnp.where(hit, d_gate_value, 0.0), 0, keepdims=True)
        mix_acc[...] += dot_tn(chosen, (gate * y).astype(bf16))
        d_y = (gate * d_mix).astype(bf16)
        d_z = dot_nt(d_y, wd)
        d_g = (d_z * u * sig * (1.0 + g * (1.0 - sig))).astype(bf16)
        d_u = (d_z * g * sig).astype(bf16)
        d_r = (dot_nt(d_g, wg) + dot_nt(d_u, wu)).astype(bf16)
        da_acc[...] += dot_tn(chosen, d_r)
        for ref, value in (
            (x_ref, x),
            (dy_ref, d_y),
            (z_ref, z),
            (dgate_ref, d_g),
            (dup_ref, d_u),
        ):
            ref[0, :size] = value
            if size < ref.shape[1]:
                ref[0, size:] = jnp.zeros((ref.shape[1] - size, ref.shape[2]), bf16)

    least = -1
    for size in sizes:
        pl.when((counts[e] > least) & (counts[e] <= size))(functools.partial(body, size))
        least = size

    @pl.when(e == pl.num_programs(0) - 1)
    def _():
        mix_ref[...] = mix_acc[...].astype(bf16)
        da_ref[...] = da_acc[...].astype(bf16)


def expert_pass(a2, df, rank, gates, wg, wu, wd, capacity):
    tok = a2.shape[0]
    parts, experts = wg.shape[0], wg.shape[1]
    sizes = sorted({min(size, capacity) for size in (128, 192, 256, capacity)})
    counts = (jnp.max(rank, 1) + 1.0).astype(jnp.int32)
    spec = pl.BlockSpec
    whole = spec((tok, MODEL_WIDTH), lambda e, *_: (0, 0))
    row = spec((1, 1, tok), lambda e, *_: (e, 0, 0))
    up = spec((parts, 1, MODEL_WIDTH // parts, FF), lambda e, *_: (0, e, 0, 0))
    down = spec((parts, 1, FF, MODEL_WIDTH // parts), lambda e, *_: (0, e, 0, 0))
    rows_wide = spec((1, capacity, MODEL_WIDTH), lambda e, *_: (e, 0, 0))
    rows_thin = spec((1, capacity, FF), lambda e, *_: (e, 0, 0))
    shape = jax.ShapeDtypeStruct
    return pl.pallas_call(
        functools.partial(expert_kernel, sizes=sizes),
        grid_spec=pltpu.PrefetchScalarGridSpec(
            num_scalar_prefetch=1,
            grid=(experts,),
            in_specs=[whole, whole, row, row, up, up, down],
            out_specs=[whole, whole, row, rows_wide, rows_wide, rows_thin, rows_thin, rows_thin],
            scratch_shapes=[
                pltpu.VMEM((tok, MODEL_WIDTH), f32),
                pltpu.VMEM((tok, MODEL_WIDTH), f32),
            ],
        ),
        out_shape=[
            shape((tok, MODEL_WIDTH), bf16),
            shape((tok, MODEL_WIDTH), bf16),
            shape((experts, 1, tok), f32),
            shape((experts, capacity, MODEL_WIDTH), bf16),
            shape((experts, capacity, MODEL_WIDTH), bf16),
            shape((experts, capacity, FF), bf16),
            shape((experts, capacity, FF), bf16),
            shape((experts, capacity, FF), bf16),
        ],
        compiler_params=pltpu.CompilerParams(vmem_limit_bytes=VMEM_LIMIT),
        cost_estimate=SMALL,
        name="expert_pass",
    )(counts, a2, df, rank.reshape(experts, 1, tok), gates.reshape(experts, 1, tok), wg, wu, wd)


def up_grad_kernel(*refs, sources):
    rows = refs[: 3 * sources]
    gate_ref, up_ref = refs[3 * sources :]
    for n, out_ref in ((1, gate_ref), (2, up_ref)):
        total = None
        for s in range(sources):
            term = dot_tn(rows[3 * s][0], rows[3 * s + n][0])
            total = term if total is None else total + term
        out_ref[...] = total.astype(bf16).reshape(out_ref.shape)


def down_grad_kernel(*refs, sources, parts):
    rows, down_ref = refs[: 2 * sources], refs[-1]
    width = MODEL_WIDTH // parts
    total = None
    for s in range(sources):
        term = dot_tn(rows[2 * s][0], rows[2 * s + 1][0])
        total = term if total is None else total + term
    total = total.astype(bf16)
    for c in range(parts):
        down_ref[c, 0] = total[:, c * width : (c + 1) * width]


def row_specs(rows):
    return [pl.BlockSpec((1,) + a.shape[1:], lambda e: (e, 0, 0)) for r in rows for a in r]


def up_weight_grads(rows, parts):
    experts = rows[0][0].shape[0]
    shape = (parts, experts, MODEL_WIDTH // parts, FF)
    out = pl.BlockSpec((parts, 1) + shape[2:], lambda e: (0, e, 0, 0))
    return pl.pallas_call(
        functools.partial(up_grad_kernel, sources=len(rows)),
        grid=(experts,),
        in_specs=row_specs(rows),
        out_specs=[out, out],
        out_shape=[jax.ShapeDtypeStruct(shape, bf16)] * 2,
        compiler_params=pltpu.CompilerParams(vmem_limit_bytes=VMEM_LIMIT),
        cost_estimate=SMALL,
        name="up_weight_grads",
    )(*[a for r in rows for a in r])


def down_weight_grads(rows, parts):
    experts = rows[0][0].shape[0]
    shape = (parts, experts, FF, MODEL_WIDTH // parts)
    return pl.pallas_call(
        functools.partial(down_grad_kernel, sources=len(rows), parts=parts),
        grid=(experts,),
        in_specs=row_specs(rows),
        out_specs=pl.BlockSpec((parts, 1) + shape[2:], lambda e: (0, e, 0, 0)),
        out_shape=jax.ShapeDtypeStruct(shape, bf16),
        compiler_params=pltpu.CompilerParams(vmem_limit_bytes=VMEM_LIMIT),
        cost_estimate=SMALL,
        name="down_weight_grads",
    )(*[a for r in rows for a in r])


def swap(x, mask):
    return lax.ppermute(x, "ctx", [(i, i ^ mask) for i in range(lax.axis_size("ctx"))])


def blocks_ctx(x):
    return both_cores(even_blocks(x))


def even_blocks(x):
    half = x.shape[0] // 2
    near, far = swap(x, 2), swap(x, 4)
    diagonal = jnp.concatenate([swap(near[:half], 4), swap(far[half:], 2)], 0)
    return [x, near, far, diagonal]


def both_cores(even):
    odd = [swap(block, 1) for block in even]
    return [b for pair in zip(even, odd) for b in pair]


def gather_ctx(x):
    if lax.axis_size("ctx") != 8:
        return [lax.all_gather(x, "ctx", axis=0, tiled=True)]
    return blocks_ctx(x)


def scatter_ctx(x):
    if lax.axis_size("ctx") != 8:
        return lax.psum_scatter(x, "ctx", scatter_dimension=0, tiled=True).astype(f32)
    rows = x.shape[0] // 8
    half = rows // 2
    block = [x[m * rows : (m + 1) * rows] for m in range(8)]
    diagonal, near, far, own = (
        block[m].astype(f32) + swap(block[m + 1], 1).astype(f32) for m in (6, 2, 4, 0)
    )
    diagonal = diagonal.astype(bf16)
    near_top = near[:half] + swap(diagonal[:half], 4).astype(f32)
    far_end = far[half:] + swap(diagonal[half:], 2).astype(f32)
    near = jnp.concatenate([near_top.astype(bf16), near[half:].astype(bf16)], 0)
    far = jnp.concatenate([far[:half].astype(bf16), far_end.astype(bf16)], 0)
    return own + swap(near, 2).astype(f32) + swap(far, 4).astype(f32)


def shift(x, distance):
    n = lax.axis_size("wt")
    return lax.ppermute(x, "wt", [(i, (i + distance) % n) for i in range(n)])


def beside(results, *arrivals):
    out = lax.optimization_barrier((results, arrivals))
    return (out[0],) + tuple(out[1])


def gather_all(x):
    ctx, wt = lax.axis_size("ctx"), lax.axis_size("wt")
    if ctx != 8 or wt != 4:
        return [lax.all_gather(x, ALL, axis=0, tiled=True)], [1], jnp.zeros((1,), jnp.int32), x
    ctx_index, wt_index = lax.axis_index("ctx"), lax.axis_index("wt")
    others = jnp.concatenate([shift(x, d) for d in (1, 2, 3)], 0)
    pieces = blocks_ctx(x) + blocks_ctx(others)
    m = jnp.arange(8, dtype=jnp.int32)
    own = (ctx_index ^ m) * wt + wt_index
    d = jnp.arange(1, 4, dtype=jnp.int32)
    rest = ((ctx_index ^ m) * wt)[:, None] + ((wt_index - d) % wt)[None, :]
    places = jnp.concatenate([own, rest.reshape(-1)]).astype(jnp.int32)
    return pieces, [1] * 8 + [3] * 8, places, others


def outer_part(a, b):
    if lax.axis_size("ctx") != 8 or lax.axis_size("wt") != 4:
        return dot_tn(a, b)
    return scatter_ctx(outer(a, b))


def row_sum(part):
    wt = lax.axis_size("wt")
    if lax.axis_size("ctx") != 8 or wt != 4:
        return lax.psum_scatter(
            part.astype(bf16), ALL, scatter_dimension=0, tiled=True
        ).astype(f32)
    rows = part.shape[0] // wt
    low = part.astype(bf16)
    at = lambda d: ((lax.axis_index("wt") + d) % wt) * rows
    total = lax.dynamic_slice_in_dim(part, at(0), rows, 0)
    for d in range(1, wt):
        total = total + shift(lax.dynamic_slice_in_dim(low, at(d), rows, 0), d).astype(f32)
    return total


def spread_sum(x):
    return jnp.sum(lax.all_to_all(x, ALL, 0, 0, tiled=True), 0)


def after(x, *others):
    return lax.optimization_barrier((x,) + others)[0]


def rope_tables(positions, width):
    middle = HEAD_SIZE // 2
    frequency = jnp.power(
        jnp.float32(rope_base), -2.0 * jnp.arange(middle, dtype=f32) / HEAD_SIZE
    )
    angles = positions.astype(f32)[:, None] * frequency[None, :]
    times = width // middle
    return jnp.tile(jnp.cos(angles), (1, times)), jnp.tile(jnp.sin(angles), (1, times))


def turn(values, cosine, sine, direction):
    middle = HEAD_SIZE // 2
    first = lax.broadcasted_iota(jnp.int32, values.shape, 1) % HEAD_SIZE < middle
    turned = jnp.where(first, -jnp.roll(values, -middle, 1), jnp.roll(values, middle, 1))
    width = values.shape[1]
    return values * cosine[:, :width] + direction * turned * sine[:, :width]


def norm_forward(values, gain):
    inverse = lax.rsqrt(jnp.mean(values * values, -1, keepdims=True) + norm_eps)
    return (values * inverse * gain, inverse)


def norm_backward(values, inverse, gain, grad_out):
    scaled = gain * grad_out
    gain_grad = jnp.sum(grad_out * values * inverse, 0)
    projection = jnp.mean(scaled * values, -1, keepdims=True)
    return (inverse * scaled - values * inverse * inverse * inverse * projection, gain_grad)


def per_device(
    layer_input,
    attention_gain,
    query_weight,
    key_matrix,
    value_matrix,
    output_weight,
    mixture_gain,
    router_weight,
    gate_weight,
    up_weight,
    down_weight,
    expert_routes,
    prompt_deal,
    output_grad,
):
    tok = layer_input.shape[1]
    prompt_local = tok - CONT_DEV * CLEN
    block_rows = prompt_local // 2
    context_size = lax.axis_size("ctx")
    shard_count = lax.axis_size("wt")
    expert_count = gate_weight.shape[0]
    capacity = 8 * ((tok * TOP * 7 // (4 * EXPERTS) + 7) // 8)
    ctx_index = lax.axis_index("ctx")
    wt_index = lax.axis_index("wt")
    inputs = layer_input[0].astype(f32)
    routes = expert_routes[0]
    deal_row = prompt_deal[0]
    out_low = output_grad[0]
    out_grad = out_low.astype(f32)

    own_rows = query_weight.shape[0]
    packed = jnp.concatenate(
        [
            query_weight,
            key_matrix,
            value_matrix,
            output_weight.T,
            router_weight,
            attention_gain[:, None],
            mixture_gain[:, None],
            jnp.zeros((own_rows, 94), bf16),
        ],
        1,
    )
    pieces, counts, block_places, first_part = gather_all(packed)

    gate_full = lax.all_gather(gate_weight, "ctx", axis=0, tiled=False)
    up_full = lax.all_gather(up_weight, "ctx", axis=0, tiled=False)
    down_full = lax.all_gather(down_weight, "ctx", axis=0, tiled=False)

    mask = jnp.any(
        routes[:, :, None] == jnp.arange(EXPERTS, dtype=jnp.int32)[None, None, :], 1
    )
    order = jnp.arange(tok, dtype=jnp.int32)
    before = (order[None, :] < order[:, None]).astype(bf16)
    rank = jnp.where(mask, dot(before, mask.astype(bf16)), -1.0)
    ranks = lax.all_to_all(
        rank.T.reshape(shard_count, expert_count, tok), "wt", 0, 0, tiled=True
    )
    last = shard_count - 1
    grads_in = {0: out_low, last: shift(after(out_low, first_part), -1)}

    pieces, grads_in[last], ranks = beside(pieces, grads_in[last], ranks)
    local_rows = jnp.arange(tok, dtype=jnp.int32)
    mine = lax.dynamic_slice_in_dim(deal_row, 2 * ctx_index, 2, 0)
    prompt_place = (
        jnp.where(local_rows < block_rows, mine[0], mine[1]) * block_rows
        + local_rows % block_rows
    )
    positions = jnp.where(
        local_rows < prompt_local, prompt_place, PROMPT + (local_rows - prompt_local) % CLEN
    )
    cosine, sine = rope_tables(positions, 128)
    normed_one, turned_query, *kv_low, qkv_full, output_t, rest, gain_rows = project(
        layer_input[0], cosine, sine, pieces, counts, block_places
    )
    router_full = rest[:, :EXPERTS]
    first_gain, second_gain = gain_rows[0], gain_rows[1]
    inverse_one = lax.rsqrt(jnp.mean(inputs * inputs, -1, keepdims=True) + norm_eps)
    kv_own = [low[prompt_local:] for low in kv_low]
    kv_prompt = [low[:prompt_local] for low in kv_low]
    if context_size == 8:
        kv_even = [even_blocks(low) for low in kv_prompt]
        kv_even[0], turned_query = beside(kv_even[0], after(turned_query, *kv_even[1]))
        kv_pieces = [both_cores(even) for even in kv_even]
    else:
        kv_pieces = [gather_ctx(low) for low in kv_prompt]

    places = deal_row
    if context_size == 8:
        pairs = deal_row.reshape(2, 2, 2, 2)
        for axis, bit in ((0, 4), (1, 2), (2, 1)):
            pairs = jnp.where(ctx_index & bit > 0, jnp.flip(pairs, axis), pairs)
        places = pairs.reshape(-1)
    low = (mine[0] > mine[1]).astype(jnp.int32)
    starts = jnp.stack(
        [
            low * block_rows,
            (1 - low) * block_rows,
            jnp.min(mine) * block_rows,
            jnp.max(mine) * block_rows,
        ]
    ).astype(jnp.int32)
    heads = []
    for half in range(2):
        result = attention_forward(
            turned_query, kv_pieces[half], kv_own[half], places, starts, block_rows, half
        )
        d = last - 1 - half
        grads_in[d] = shift(grads_in[d + 1], -1)
        result, grads_in[d] = beside(result, grads_in[d])
        if half == 0:
            turned_query = after(turned_query, result[0])
        heads.append(result)
    for d in range(last - 3, 0, -1):
        grads_in[d] = shift(grads_in[d + 1], -1)
    attended = jnp.concatenate([out for out, _ in heads], 1)
    lse = [row for _, row in heads]

    branch = dot_nt(attended, output_t)
    middle = inputs + resid_scale * branch
    normed_mid, inverse_two = norm_forward(middle, second_gain)
    normed_two = normed_mid.astype(bf16)
    logits = dot(normed_two, router_full)
    top = jnp.max(jnp.where(mask, logits, masked_score), -1, keepdims=True)
    raised = jnp.where(mask, jnp.exp(jnp.where(mask, logits - top, 0.0)), 0.0)
    gates = raised / jnp.sum(raised, -1, keepdims=True)

    gates_out = gates.T.reshape(shard_count, expert_count, tok)
    gates_in = []
    for d in range(shard_count):
        piece = lax.dynamic_index_in_dim(gates_out, (wt_index + d) % shard_count, 0, False)
        gates_in.append(shift(piece, d) if d else piece)
    got = {0: normed_two}
    partial, mixed, gate_grads, rows = {}, {}, {}, []
    carried = None

    def add(a, b):
        return b if a is None else (a.astype(f32) + b.astype(f32)).astype(bf16)

    for d in [0] + list(range(last, 0, -1)):
        source = (wt_index - d) % shard_count
        rank_in = lax.dynamic_index_in_dim(ranks, source, 0, False)
        result = expert_pass(
            got[d], grads_in[d], rank_in, gates_in[d], gate_full, up_full, down_full, capacity
        )
        coming = d - 1 if d else last
        if coming:
            result, got[coming] = beside(result, shift(got[(coming + 1) % shard_count], -1))
        if d == 0:
            result, gates_in = beside(result, gates_in)
        if 0 < d <= last - 2:
            carried = shift(after(add(carried, partial[d + 2]), got[d]), -1)
            result, carried = beside(result, carried)
        mixed[d], partial[d], d_gate, *kept = result
        rows.append(kept)
        d_gate = d_gate.reshape(expert_count, tok)
        gate_grads[d] = shift(d_gate, shard_count - d) if d else d_gate
        if coming:
            got[coming] = after(got[coming], partial[d])
    carried = shift(add(carried, partial[2]), -1)
    (gate_grad, up_grad), carried = beside(
        up_weight_grads([(after(r[0], partial[1]), r[3], r[4]) for r in rows], context_size),
        carried,
    )
    carried = shift(add(carried, partial[1]), -1)
    down_grad, home = beside(
        down_weight_grads([(after(r[2], gate_grad), r[1]) for r in rows], context_size), carried
    )

    stacked = jnp.stack([gate_grads[d] for d in range(shard_count)], 0)
    stacked = jnp.roll(stacked, wt_index, 0).reshape(EXPERTS, tok).T
    grad_logits = (gates * (stacked - jnp.sum(gates * stacked, -1, keepdims=True))).astype(bf16)
    grad_normed_two = partial[0].astype(f32) + home.astype(f32)
    grad_normed_two = grad_normed_two + dot_nt(grad_logits, router_full)
    grad_mid_norm, second_gain_grad = norm_backward(
        middle, inverse_two, second_gain, grad_normed_two
    )
    grad_middle = out_grad + grad_mid_norm
    grad_branch = (resid_scale * grad_middle).astype(bf16)
    grad_attended = dot(grad_branch, output_t).astype(bf16)
    gate_share, up_share, down_share = (
        lax.psum_scatter(grad, "ctx", scatter_dimension=0, tiled=False).astype(f32)
        for grad in (gate_grad, up_grad, down_grad)
    )
    output_share = row_sum(outer_part(grad_branch, attended))
    devices = context_size * shard_count
    small = jnp.concatenate(
        [
            dot_tn(normed_two, grad_logits).reshape(devices, own_rows * EXPERTS),
            second_gain_grad.reshape(devices, own_rows),
        ],
        1,
    )
    small = spread_sum(small)

    carried = shift(after(mixed[last], home), -1)
    query, carried = beside(after(turned_query, grad_attended), carried)
    d_query, owned, ours = [], [], []
    for half in range(2):
        result = attention_backward(
            query,
            grad_attended,
            lse[half],
            attended,
            cosine,
            sine,
            kv_pieces[half],
            kv_own[half],
            places,
            starts,
            block_rows,
            half,
        )
        carried = shift(add(carried, mixed[last - 1 - half]), -1)
        result, carried = beside(result, carried)
        d_q, d_kv, d_key_own, d_value_own = result
        query = after(query, d_q)
        d_query.append(d_q)
        owned.append(scatter_ctx(d_kv))
        ours.append((d_key_own, d_value_own))
    for d in range(last - 3, 0, -1):
        carried = shift(add(carried, mixed[d]), -1)
    mixture = mixed[0].astype(f32) + carried.astype(f32)
    layer_output = (middle + resid_scale * mixture).astype(bf16)
    d_query = jnp.concatenate(d_query, 1)
    query_part = outer_part(normed_one, d_query)
    d_key, d_value = (
        jnp.concatenate(
            [
                jnp.concatenate([owned[half][:, 256 * n : 256 * n + 256], ours[half][n]], 0)
                for half in range(2)
            ],
            1,
        )
        for n in range(2)
    )
    grad_key_low = turn(d_key, jnp.tile(cosine, (1, 4)), jnp.tile(sine, (1, 4)), -1.0).astype(
        bf16
    )
    grad_kv = jnp.concatenate([grad_key_low, d_value.astype(bf16)], 1)
    grad_kv, query_part = beside(grad_kv, query_part)
    kv_share = row_sum(outer_part(normed_one, grad_kv))
    query_share = row_sum(query_part)
    grad_normed_one = dot_nt(d_query, qkv_full[:, :1024]) + dot_nt(grad_kv, qkv_full[:, 1024:])
    grad_input_norm, first_gain_grad = norm_backward(
        inputs, inverse_one, first_gain, grad_normed_one
    )
    input_grad = (grad_middle + grad_input_norm).astype(bf16)

    first_gain_share = spread_sum(first_gain_grad.reshape(devices, own_rows))
    return (
        layer_output[None],
        input_grad[None],
        first_gain_share,
        query_share,
        kv_share[:, :KV_WIDTH],
        kv_share[:, KV_WIDTH:],
        output_share.T,
        small[own_rows * EXPERTS :],
        small[: own_rows * EXPERTS].reshape(own_rows, EXPERTS),
        gate_share,
        up_share,
        down_share,
    )


def solution(mesh):
    return jax.shard_map(
        per_device,
        mesh=mesh,
        in_specs=(
            P("wt", "ctx", None),
            P(("ctx", "wt")),
            P(("ctx", "wt"), None),
            P(("ctx", "wt"), None),
            P(("ctx", "wt"), None),
            P(None, ("ctx", "wt")),
            P(("ctx", "wt")),
            P(("ctx", "wt"), None),
            P("wt", "ctx", None),
            P("wt", "ctx", None),
            P("wt", None, "ctx"),
            P("wt", "ctx", None),
            P("wt", None),
            P("wt", "ctx", None),
        ),
        out_specs=(
            P("wt", "ctx", None),
            P("wt", "ctx", None),
            P(("ctx", "wt")),
            P(("ctx", "wt"), None),
            P(("ctx", "wt"), None),
            P(("ctx", "wt"), None),
            P(None, ("ctx", "wt")),
            P(("ctx", "wt")),
            P(("ctx", "wt"), None),
            P("wt", "ctx", None),
            P("wt", "ctx", None),
            P("wt", None, "ctx"),
        ),
        check_vma=False,
    )
```

```python
import functools

import jax
import jax.numpy as jnp
from jax import lax
from jax.experimental import pallas as pl
from jax.experimental.pallas import tpu as pltpu
from jax.sharding import PartitionSpec as P

MODEL_WIDTH = 1024
HQ = 16
KEY_VALUE_HEADS = 8
HEAD_SIZE = 64
EXPERTS = 32
TOP = 8
PROMPT = 2048
CLEN = 256
CONT_DEV = 2
FF = 512
QTILE = 128
KV_WIDTH = KEY_VALUE_HEADS * HEAD_SIZE
ALL = ("ctx", "wt")

att_scale = 0.015625
resid_scale = 0.22
norm_eps = 1e-06
rope_base = 10000.0
masked_score = -1e30

bf16 = jnp.bfloat16
f32 = jnp.float32
VMEM_LIMIT = 60 * 1024 * 1024
SMALL = pl.CostEstimate(flops=1_000_000_000, bytes_accessed=1_000_000, transcendentals=0)

NT = (((1,), (1,)), ((), ()))
TN = (((0,), (0,)), ((), ()))


def dot(a, b):
    return jnp.dot(a, b, preferred_element_type=f32)


def dot_nt(a, b):
    return lax.dot_general(a, b, NT, preferred_element_type=f32)


def dot_tn(a, b):
    return lax.dot_general(a, b, TN, preferred_element_type=f32)


def turn_tile(values, cosine, sine, direction):
    middle = HEAD_SIZE // 2
    first = lax.broadcasted_iota(jnp.int32, values.shape, 1) % HEAD_SIZE < middle
    turned = jnp.where(first, -pltpu.roll(values, 128 - middle, 1), pltpu.roll(values, middle, 1))
    return values * cosine + direction * turned * sine


def project_kernel(places, x_ref, cos_ref, sin_ref, *refs, counts):
    pieces = refs[: len(counts)]
    normed_ref, q_ref, *kv_refs, qkv_ref, out_ref, rest_ref, gains_ref = refs[len(counts) :]
    rows = MODEL_WIDTH // sum(counts)
    at = 0
    for piece, count in zip(pieces, counts):
        for i in range(count):
            source = slice(i * rows, (i + 1) * rows)
            target = pl.ds(pl.multiple_of(places[at] * rows, rows), rows)
            qkv_ref[target, :] = piece[source, :2048]
            out_ref[target, :] = piece[source, 2048:3072]
            rest_ref[target, :] = piece[source, 3072:]
            at += 1
    gains = rest_ref[...].astype(f32).T[EXPERTS : EXPERTS + 8]
    gains_ref[...] = gains
    x = x_ref[...].astype(f32)
    inverse = lax.rsqrt(jnp.mean(x * x, -1, keepdims=True) + norm_eps)
    normed_ref[...] = (x * inverse * gains[:1]).astype(bf16)
    for c in range(8):
        raw = dot(normed_ref[...], qkv_ref[:, 256 * c : 256 * (c + 1)])
        for h in range(2):
            part = raw[:, 128 * h : 128 * (h + 1)]
            if c < 6:
                part = turn_tile(part, cos_ref[...], sin_ref[...], 1.0)
            column = 256 * c + 128 * h
            if column < 1024:
                q_ref[:, column : column + 128] = part.astype(bf16)
            else:
                column -= 1024
                at = column // KV_WIDTH * 256 + column % 256
                kv_refs[column % KV_WIDTH // 256][:, at : at + 128] = part.astype(bf16)


def project(x, cosine, sine, pieces, counts, places):
    tok = x.shape[0]
    shape = jax.ShapeDtypeStruct
    whole = pl.BlockSpec(memory_space=pltpu.VMEM)
    return pl.pallas_call(
        functools.partial(project_kernel, counts=counts),
        in_specs=[pl.BlockSpec(memory_space=pltpu.SMEM)] + [whole] * (3 + len(pieces)),
        out_specs=[whole] * 8,
        out_shape=[
            shape((tok, MODEL_WIDTH), bf16),
            shape((tok, HQ * HEAD_SIZE), bf16),
            shape((tok, KV_WIDTH), bf16),
            shape((tok, KV_WIDTH), bf16),
            shape((MODEL_WIDTH, 2048), bf16),
            shape((MODEL_WIDTH, 1024), bf16),
            shape((MODEL_WIDTH, 128), bf16),
            shape((8, MODEL_WIDTH), f32),
        ],
        compiler_params=pltpu.CompilerParams(vmem_limit_bytes=VMEM_LIMIT),
        cost_estimate=SMALL,
        name="project",
    )(places, x, cosine, sine, *pieces)


def outer_kernel(mine, *refs):
    out_ref = refs[-1]
    at = 0
    for n in range(len(refs) // 2):
        columns = refs[2 * n + 1].shape[1]
        out_ref[:, at : at + columns] = dot_tn(refs[2 * n][...], refs[2 * n + 1][...]).astype(bf16)
        at += columns


def outer(*pairs):
    tok = pairs[0][0].shape[0]
    mine = lax.axis_index("ctx").astype(jnp.int32).reshape(1)
    specs = []
    for _, b in pairs:
        specs.append(pl.BlockSpec((tok, 128), lambda m, mine: (0, m ^ mine[0])))
        specs.append(pl.BlockSpec(b.shape, lambda m, mine: (0, 0)))
    columns = sum(b.shape[1] for _, b in pairs)
    return pl.pallas_call(
        outer_kernel,
        grid_spec=pltpu.PrefetchScalarGridSpec(
            num_scalar_prefetch=1,
            grid=(8,),
            in_specs=specs,
            out_specs=pl.BlockSpec((128, columns), lambda m, mine: (m, 0)),
        ),
        out_shape=jax.ShapeDtypeStruct((MODEL_WIDTH, columns), bf16),
        compiler_params=pltpu.CompilerParams(vmem_limit_bytes=VMEM_LIMIT),
        cost_estimate=SMALL,
        name="outer",
    )(mine, *[x for pair in pairs for x in pair])


def gather_keys(pieces, scratch, places, block_rows):
    at = 0
    for piece in pieces:
        for b in range(piece.shape[0] // block_rows):
            start = pl.multiple_of(places[at] * block_rows, block_rows)
            scratch[pl.ds(start, block_rows), :] = piece[b * block_rows : (b + 1) * block_rows, :]
            at += 1


def pair_rows(ref, start, rows, j):
    both = ref[pl.ds(start, rows), 2 * HEAD_SIZE * j : 2 * HEAD_SIZE * (j + 1)]
    return jnp.concatenate([both[:, :HEAD_SIZE], both[:, HEAD_SIZE:]], 0)


def attention_forward_kernel(places, starts, q_ref, *refs, block_rows, pieces):
    k_refs, v_refs = refs[:pieces], refs[pieces : 2 * pieces]
    kc_ref, vc_ref, o_ref, lse_ref, k_scr, v_scr = refs[2 * pieces :]
    prompt_local = 2 * block_rows
    gather_keys(k_refs, k_scr, places, block_rows)
    gather_keys(v_refs, v_scr, places, block_rows)

    def store(start, rows, j, out, m, total, at):
        out = (out / total).astype(bf16)
        lse = m + jnp.log(total)
        o_ref[pl.ds(start, rows), 2 * HEAD_SIZE * j : 2 * HEAD_SIZE * (j + 1)] = jnp.concatenate(
            [out[:rows], out[rows:]], 1
        )
        row = jnp.broadcast_to(lse, (2 * rows, 128)).T[:1]
        lse_ref[0, 2 * j : 2 * j + 2, pl.ds(at, rows)] = jnp.concatenate(
            [row[:, :rows], row[:, rows:]], 0
        )

    def tile(i, _):
        start = pl.multiple_of(prompt_local + i * QTILE, 64)
        per = CLEN // QTILE
        seg = pl.multiple_of((i // per) * CLEN, CLEN)
        for j in range(2):
            lanes = slice(HEAD_SIZE * j, HEAD_SIZE * (j + 1))
            q = pair_rows(q_ref, start, QTILE, j) * bf16(att_scale)
            s1 = dot_nt(q, k_scr[:, lanes])
            s2 = dot_nt(q, kc_ref[pl.ds(seg, CLEN), lanes])
            place = lax.broadcasted_iota(jnp.int32, s2.shape, 0) % QTILE + (i % per) * QTILE
            s2 = jnp.where(lax.broadcasted_iota(jnp.int32, s2.shape, 1) <= place, s2, masked_score)
            m = jnp.maximum(jnp.max(s1, 1, keepdims=True), jnp.max(s2, 1, keepdims=True))
            e1 = jnp.exp(s1 - m)
            e2 = jnp.exp(s2 - m)
            total = jnp.sum(e1, 1, keepdims=True) + jnp.sum(e2, 1, keepdims=True)
            out = dot(e1.astype(bf16), v_scr[:, lanes])
            out = out + dot(e2.astype(bf16), vc_ref[pl.ds(seg, CLEN), lanes])
            store(start, QTILE, j, out, m, total, pl.multiple_of(i * QTILE, QTILE))
        return 0

    lax.fori_loop(0, CONT_DEV * CLEN // QTILE, tile, 0)

    for half, keys in enumerate((PROMPT // 2, PROMPT)):
        start = pl.multiple_of(starts[half], block_rows)
        for j in range(2):
            lanes = slice(HEAD_SIZE * j, HEAD_SIZE * (j + 1))
            q = pair_rows(q_ref, start, block_rows, j) * bf16(att_scale)
            s = dot_nt(q, k_scr[:keys, lanes])
            place = lax.broadcasted_iota(jnp.int32, s.shape, 0) % block_rows + starts[2 + half]
            s = jnp.where(lax.broadcasted_iota(jnp.int32, s.shape, 1) <= place, s, masked_score)
            m = jnp.max(s, 1, keepdims=True)
            e = jnp.exp(s - m)
            total = jnp.sum(e, 1, keepdims=True)
            out = dot(e.astype(bf16), v_scr[:keys, lanes])
            store(start, block_rows, j, out, m, total, CONT_DEV * CLEN + half * block_rows)


def key_specs(pieces, own):
    spec = pl.BlockSpec
    keys = [spec((p.shape[0], 128), lambda g, *_: (0, g)) for p in pieces]
    values = [spec((p.shape[0], 128), lambda g, *_: (0, 2 + g)) for p in pieces]
    ours = [spec((own, 128), lambda g, *_: (0, g)), spec((own, 128), lambda g, *_: (0, 2 + g))]
    return keys + values + ours


def attention_forward(q, pieces, kv_own, places, starts, block_rows, half):
    tok = q.shape[0]
    spec = pl.BlockSpec
    return pl.pallas_call(
        functools.partial(
            attention_forward_kernel, block_rows=block_rows, pieces=len(pieces)
        ),
        grid_spec=pltpu.PrefetchScalarGridSpec(
            num_scalar_prefetch=2,
            grid=(2,),
            in_specs=[spec((tok, 256), lambda g, *_: (0, 2 * half + g))]
            + key_specs(pieces, kv_own.shape[0]),
            out_specs=[
                spec((tok, 256), lambda g, *_: (0, g)),
                spec((1, 4, tok), lambda g, *_: (g, 0, 0)),
            ],
            scratch_shapes=[
                pltpu.VMEM((PROMPT, 2 * HEAD_SIZE), bf16),
                pltpu.VMEM((PROMPT, 2 * HEAD_SIZE), bf16),
            ],
        ),
        out_shape=[
            jax.ShapeDtypeStruct((tok, HQ * HEAD_SIZE // 2), bf16),
            jax.ShapeDtypeStruct((2, 4, tok), f32),
        ],
        compiler_params=pltpu.CompilerParams(vmem_limit_bytes=VMEM_LIMIT),
        cost_estimate=SMALL,
        name="attention_forward",
    )(places, starts, q, *pieces, *pieces, kv_own, kv_own)


def attention_backward_kernel(
    places, starts, q_ref, do_ref, lse_ref, o_ref, cos_ref, sin_ref, *refs, block_rows, pieces
):
    k_refs, v_refs = refs[:pieces], refs[pieces : 2 * pieces]
    kc_ref, vc_ref, dq_ref, dkv_ref, dkc_ref, dvc_ref = refs[2 * pieces : 2 * pieces + 6]
    k_scr, v_scr, dk_acc, dv_acc, dq_acc = refs[2 * pieces + 6 :]
    prompt_local = 2 * block_rows
    gather_keys(k_refs, k_scr, places, block_rows)
    gather_keys(v_refs, v_scr, places, block_rows)
    dk_acc[...] = jnp.zeros_like(dk_acc)
    dv_acc[...] = jnp.zeros_like(dv_acc)
    dkc_ref[...] = jnp.zeros_like(dkc_ref)
    dvc_ref[...] = jnp.zeros_like(dvc_ref)

    def row_pair(ref, start, rows, j):
        both = ref[0, 2 * j : 2 * j + 2, pl.ds(start, rows)]
        return jnp.concatenate([both[:1], both[1:]], 1)

    def centre(start, rows, j, d_out):
        product = d_out.astype(f32) * pair_rows(o_ref, start, rows, j).astype(f32)
        ones = jnp.ones((8, HEAD_SIZE), f32)
        return lax.dot_general(
            ones, product, NT, precision=lax.Precision.HIGHEST, preferred_element_type=f32
        )[:1]

    def part(k, v, q, d_out, lse, delta, allowed):
        s = dot_nt(k, q)
        if allowed is not None:
            s = jnp.where(allowed(s.shape), s, masked_score)
        p = jnp.exp(s - lse)
        d_p = dot_nt(v, d_out)
        d_s = (p * (d_p - delta)).astype(bf16)
        return dot_tn(d_s, k), dot(d_s, q), dot(p.astype(bf16), d_out)

    def store(start, rows, j, d_q):
        d_q = d_q * att_scale
        dq_acc[pl.ds(start, rows), 2 * HEAD_SIZE * j : 2 * HEAD_SIZE * (j + 1)] = jnp.concatenate(
            [d_q[:rows], d_q[rows:]], 1
        )

    def tile(i, _):
        start = pl.multiple_of(prompt_local + i * QTILE, 64)
        per = CLEN // QTILE
        seg = pl.multiple_of((i // per) * CLEN, CLEN)
        own = pl.ds(seg, CLEN)
        lane_start = pl.multiple_of(i * QTILE, QTILE)

        def allowed(shape):
            place = lax.broadcasted_iota(jnp.int32, shape, 1) % QTILE + (i % per) * QTILE
            return lax.broadcasted_iota(jnp.int32, shape, 0) <= place

        for j in range(2):
            lanes = slice(HEAD_SIZE * j, HEAD_SIZE * (j + 1))
            q = pair_rows(q_ref, start, QTILE, j) * bf16(att_scale)
            d_out = pair_rows(do_ref, start, QTILE, j)
            lse = row_pair(lse_ref, lane_start, QTILE, j)
            delta = centre(start, QTILE, j, d_out)
            a, b, c = part(k_scr[:, lanes], v_scr[:, lanes], q, d_out, lse, delta, None)
            dk_acc[:, lanes] += b
            dv_acc[:, lanes] += c
            d_q = a
            a, b, c = part(
                kc_ref[own, lanes], vc_ref[own, lanes], q, d_out, lse, delta, allowed
            )
            dkc_ref[own, lanes] += b
            dvc_ref[own, lanes] += c
            store(start, QTILE, j, d_q + a)
        return 0

    lax.fori_loop(0, CONT_DEV * CLEN // QTILE, tile, 0)

    for half, keys in enumerate((PROMPT // 2, PROMPT)):
        start = pl.multiple_of(starts[half], block_rows)
        at = CONT_DEV * CLEN + half * block_rows

        def allowed(shape):
            place = lax.broadcasted_iota(jnp.int32, shape, 1) % block_rows + starts[2 + half]
            return lax.broadcasted_iota(jnp.int32, shape, 0) <= place

        for j in range(2):
            lanes = slice(HEAD_SIZE * j, HEAD_SIZE * (j + 1))
            q = pair_rows(q_ref, start, block_rows, j) * bf16(att_scale)
            d_out = pair_rows(do_ref, start, block_rows, j)
            lse = row_pair(lse_ref, at, block_rows, j)
            delta = centre(start, block_rows, j, d_out)
            a, b, c = part(
                k_scr[:keys, lanes], v_scr[:keys, lanes], q, d_out, lse, delta, allowed
            )
            dk_acc[:keys, lanes] += b
            dv_acc[:keys, lanes] += c
            store(start, block_rows, j, a)

    g = pl.program_id(0)
    key_lanes = pl.ds(pl.multiple_of(g * 128, 128), 128)
    value_lanes = pl.ds(pl.multiple_of(256 + g * 128, 128), 128)
    for b in range(PROMPT // block_rows):
        source = pl.ds(pl.multiple_of(places[b] * block_rows, block_rows), block_rows)
        rows = slice(b * block_rows, (b + 1) * block_rows)
        dkv_ref[rows, key_lanes] = dk_acc[source, :].astype(bf16)
        dkv_ref[rows, value_lanes] = dv_acc[source, :].astype(bf16)
    for c in range(2):
        lanes = slice(128 * c, 128 * (c + 1))
        dq_ref[:, lanes] = turn_tile(dq_acc[:, lanes], cos_ref[...], sin_ref[...], -1.0).astype(
            bf16
        )


def attention_backward(
    q, d_out, lse, attended, cosine, sine, pieces, kv_own, places, starts, block_rows, half
):
    tok = q.shape[0]
    own = kv_own.shape[0]
    spec = pl.BlockSpec
    wide = spec((tok, 256), lambda g, *_: (0, 2 * half + g))
    ours = spec((own, 128), lambda g, *_: (0, g))
    table = spec((tok, 128), lambda g, *_: (0, 0))
    return pl.pallas_call(
        functools.partial(
            attention_backward_kernel, block_rows=block_rows, pieces=len(pieces)
        ),
        grid_spec=pltpu.PrefetchScalarGridSpec(
            num_scalar_prefetch=2,
            grid=(2,),
            in_specs=[wide, wide, spec((1, 4, tok), lambda g, *_: (g, 0, 0)), wide, table, table]
            + key_specs(pieces, own),
            out_specs=[
                spec((tok, 256), lambda g, *_: (0, g)),
                spec((PROMPT, KV_WIDTH), lambda g, *_: (0, 0)),
                ours,
                ours,
            ],
            scratch_shapes=[
                pltpu.VMEM((PROMPT, 2 * HEAD_SIZE), bf16),
                pltpu.VMEM((PROMPT, 2 * HEAD_SIZE), bf16),
                pltpu.VMEM((PROMPT, 2 * HEAD_SIZE), f32),
                pltpu.VMEM((PROMPT, 2 * HEAD_SIZE), f32),
                pltpu.VMEM((tok, 4 * HEAD_SIZE), f32),
            ],
        ),
        out_shape=[
            jax.ShapeDtypeStruct((tok, HQ * HEAD_SIZE // 2), bf16),
            jax.ShapeDtypeStruct((PROMPT, KV_WIDTH), bf16),
            jax.ShapeDtypeStruct((own, KV_WIDTH // 2), f32),
            jax.ShapeDtypeStruct((own, KV_WIDTH // 2), f32),
        ],
        compiler_params=pltpu.CompilerParams(vmem_limit_bytes=VMEM_LIMIT),
        cost_estimate=SMALL,
        name="attention_backward",
    )(places, starts, q, d_out, lse, attended, cosine, sine, *pieces, *pieces, kv_own, kv_own)


def expert_kernel(
    counts,
    a2_ref,
    df_ref,
    rank_ref,
    gate_ref,
    wg_ref,
    wu_ref,
    wd_ref,
    mix_ref,
    da_ref,
    dg_ref,
    x_ref,
    dy_ref,
    z_ref,
    dgate_ref,
    dup_ref,
    mix_acc,
    da_acc,
    *,
    sizes,
):
    e = pl.program_id(0)

    @pl.when(e == 0)
    def _():
        mix_acc[...] = jnp.zeros_like(mix_acc)
        da_acc[...] = jnp.zeros_like(da_acc)

    def body(size):
        rank = rank_ref[0]
        gates = gate_ref[0]
        tok = rank.shape[1]
        slot = lax.broadcasted_iota(jnp.int32, (size, tok), 0).astype(f32)
        hit = slot == rank
        chosen = hit.astype(f32).astype(bf16)
        gate = jnp.sum(jnp.where(hit, gates, 0.0), 1, keepdims=True)
        x = dot(chosen, a2_ref[...]).astype(bf16)
        d_mix = resid_scale * dot(chosen, df_ref[...])
        wg = wg_ref[:, 0].reshape(MODEL_WIDTH, FF)
        wu = wu_ref[:, 0].reshape(MODEL_WIDTH, FF)
        wd = jnp.concatenate([wd_ref[c, 0] for c in range(wd_ref.shape[0])], 1)
        g = dot(x, wg)
        u = dot(x, wu)
        sig = jax.nn.sigmoid(g)
        z = (g * sig * u).astype(bf16)
        y = dot(z, wd).astype(bf16).astype(f32)
        d_gate_value = jnp.sum(d_mix * y, 1, keepdims=True)
        dg_ref[0] = jnp.sum(jnp.where(hit, d_gate_value, 0.0), 0, keepdims=True)
        mix_acc[...] += dot_tn(chosen, (gate * y).astype(bf16))
        d_y = (gate * d_mix).astype(bf16)
        d_z = dot_nt(d_y, wd)
        d_g = (d_z * u * sig * (1.0 + g * (1.0 - sig))).astype(bf16)
        d_u = (d_z * g * sig).astype(bf16)
        d_r = (dot_nt(d_g, wg) + dot_nt(d_u, wu)).astype(bf16)
        da_acc[...] += dot_tn(chosen, d_r)
        for ref, value in (
            (x_ref, x),
            (dy_ref, d_y),
            (z_ref, z),
            (dgate_ref, d_g),
            (dup_ref, d_u),
        ):
            ref[0, :size] = value
            if size < ref.shape[1]:
                ref[0, size:] = jnp.zeros((ref.shape[1] - size, ref.shape[2]), bf16)

    least = -1
    for size in sizes:
        pl.when((counts[e] > least) & (counts[e] <= size))(functools.partial(body, size))
        least = size

    @pl.when(e == pl.num_programs(0) - 1)
    def _():
        mix_ref[...] = mix_acc[...].astype(bf16)
        da_ref[...] = da_acc[...].astype(bf16)


def expert_pass(a2, df, rank, gates, wg, wu, wd, capacity):
    tok = a2.shape[0]
    parts, experts = wg.shape[0], wg.shape[1]
    sizes = sorted({min(size, capacity) for size in (128, 192, 256, capacity)})
    counts = (jnp.max(rank, 1) + 1.0).astype(jnp.int32)
    spec = pl.BlockSpec
    whole = spec((tok, MODEL_WIDTH), lambda e, *_: (0, 0))
    row = spec((1, 1, tok), lambda e, *_: (e, 0, 0))
    up = spec((parts, 1, MODEL_WIDTH // parts, FF), lambda e, *_: (0, e, 0, 0))
    down = spec((parts, 1, FF, MODEL_WIDTH // parts), lambda e, *_: (0, e, 0, 0))
    rows_wide = spec((1, capacity, MODEL_WIDTH), lambda e, *_: (e, 0, 0))
    rows_thin = spec((1, capacity, FF), lambda e, *_: (e, 0, 0))
    shape = jax.ShapeDtypeStruct
    return pl.pallas_call(
        functools.partial(expert_kernel, sizes=sizes),
        grid_spec=pltpu.PrefetchScalarGridSpec(
            num_scalar_prefetch=1,
            grid=(experts,),
            in_specs=[whole, whole, row, row, up, up, down],
            out_specs=[whole, whole, row, rows_wide, rows_wide, rows_thin, rows_thin, rows_thin],
            scratch_shapes=[
                pltpu.VMEM((tok, MODEL_WIDTH), f32),
                pltpu.VMEM((tok, MODEL_WIDTH), f32),
            ],
        ),
        out_shape=[
            shape((tok, MODEL_WIDTH), bf16),
            shape((tok, MODEL_WIDTH), bf16),
            shape((experts, 1, tok), f32),
            shape((experts, capacity, MODEL_WIDTH), bf16),
            shape((experts, capacity, MODEL_WIDTH), bf16),
            shape((experts, capacity, FF), bf16),
            shape((experts, capacity, FF), bf16),
            shape((experts, capacity, FF), bf16),
        ],
        compiler_params=pltpu.CompilerParams(vmem_limit_bytes=VMEM_LIMIT),
        cost_estimate=SMALL,
        name="expert_pass",
    )(counts, a2, df, rank.reshape(experts, 1, tok), gates.reshape(experts, 1, tok), wg, wu, wd)


def up_grad_kernel(*refs, sources):
    rows = refs[: 3 * sources]
    gate_ref, up_ref = refs[3 * sources :]
    for n, out_ref in ((1, gate_ref), (2, up_ref)):
        total = None
        for s in range(sources):
            term = dot_tn(rows[3 * s][0], rows[3 * s + n][0])
            total = term if total is None else total + term
        out_ref[...] = total.astype(bf16).reshape(out_ref.shape)


def down_grad_kernel(*refs, sources, parts):
    rows, down_ref = refs[: 2 * sources], refs[-1]
    width = MODEL_WIDTH // parts
    total = None
    for s in range(sources):
        term = dot_tn(rows[2 * s][0], rows[2 * s + 1][0])
        total = term if total is None else total + term
    total = total.astype(bf16)
    for c in range(parts):
        down_ref[c, 0] = total[:, c * width : (c + 1) * width]


def row_specs(rows):
    return [pl.BlockSpec((1,) + a.shape[1:], lambda e: (e, 0, 0)) for r in rows for a in r]


def up_weight_grads(rows, parts):
    experts = rows[0][0].shape[0]
    shape = (parts, experts, MODEL_WIDTH // parts, FF)
    out = pl.BlockSpec((parts, 1) + shape[2:], lambda e: (0, e, 0, 0))
    return pl.pallas_call(
        functools.partial(up_grad_kernel, sources=len(rows)),
        grid=(experts,),
        in_specs=row_specs(rows),
        out_specs=[out, out],
        out_shape=[jax.ShapeDtypeStruct(shape, bf16)] * 2,
        compiler_params=pltpu.CompilerParams(vmem_limit_bytes=VMEM_LIMIT),
        cost_estimate=SMALL,
        name="up_weight_grads",
    )(*[a for r in rows for a in r])


def down_weight_grads(rows, parts):
    experts = rows[0][0].shape[0]
    shape = (parts, experts, FF, MODEL_WIDTH // parts)
    return pl.pallas_call(
        functools.partial(down_grad_kernel, sources=len(rows), parts=parts),
        grid=(experts,),
        in_specs=row_specs(rows),
        out_specs=pl.BlockSpec((parts, 1) + shape[2:], lambda e: (0, e, 0, 0)),
        out_shape=jax.ShapeDtypeStruct(shape, bf16),
        compiler_params=pltpu.CompilerParams(vmem_limit_bytes=VMEM_LIMIT),
        cost_estimate=SMALL,
        name="down_weight_grads",
    )(*[a for r in rows for a in r])


def swap(x, mask):
    return lax.ppermute(x, "ctx", [(i, i ^ mask) for i in range(lax.axis_size("ctx"))])


def blocks_ctx(x):
    return both_cores(even_blocks(x))


def even_blocks(x):
    half = x.shape[0] // 2
    near, far = swap(x, 2), swap(x, 4)
    diagonal = jnp.concatenate([swap(near[:half], 4), swap(far[half:], 2)], 0)
    return [x, near, far, diagonal]


def both_cores(even):
    odd = [swap(block, 1) for block in even]
    return [b for pair in zip(even, odd) for b in pair]


def gather_ctx(x):
    if lax.axis_size("ctx") != 8:
        return [lax.all_gather(x, "ctx", axis=0, tiled=True)]
    return blocks_ctx(x)


def scatter_ctx(x):
    if lax.axis_size("ctx") != 8:
        return lax.psum_scatter(x, "ctx", scatter_dimension=0, tiled=True).astype(f32)
    rows = x.shape[0] // 8
    half = rows // 2
    block = [x[m * rows : (m + 1) * rows] for m in range(8)]
    diagonal, near, far, own = (
        block[m].astype(f32) + swap(block[m + 1], 1).astype(f32) for m in (6, 2, 4, 0)
    )
    diagonal = diagonal.astype(bf16)
    near_top = near[:half] + swap(diagonal[:half], 4).astype(f32)
    far_end = far[half:] + swap(diagonal[half:], 2).astype(f32)
    near = jnp.concatenate([near_top.astype(bf16), near[half:].astype(bf16)], 0)
    far = jnp.concatenate([far[:half].astype(bf16), far_end.astype(bf16)], 0)
    return own + swap(near, 2).astype(f32) + swap(far, 4).astype(f32)


def shift(x, distance):
    n = lax.axis_size("wt")
    return lax.ppermute(x, "wt", [(i, (i + distance) % n) for i in range(n)])


def beside(results, *arrivals):
    out = lax.optimization_barrier((results, arrivals))
    return (out[0],) + tuple(out[1])


def gather_all(x):
    ctx, wt = lax.axis_size("ctx"), lax.axis_size("wt")
    if ctx != 8 or wt != 4:
        return [lax.all_gather(x, ALL, axis=0, tiled=True)], [1], jnp.zeros((1,), jnp.int32), x
    ctx_index, wt_index = lax.axis_index("ctx"), lax.axis_index("wt")
    others = jnp.concatenate([shift(x, d) for d in (1, 2, 3)], 0)
    pieces = blocks_ctx(x) + blocks_ctx(others)
    m = jnp.arange(8, dtype=jnp.int32)
    own = (ctx_index ^ m) * wt + wt_index
    d = jnp.arange(1, 4, dtype=jnp.int32)
    rest = ((ctx_index ^ m) * wt)[:, None] + ((wt_index - d) % wt)[None, :]
    places = jnp.concatenate([own, rest.reshape(-1)]).astype(jnp.int32)
    return pieces, [1] * 8 + [3] * 8, places, others


def outer_part(*pairs):
    if lax.axis_size("ctx") != 8 or lax.axis_size("wt") != 4:
        return jnp.concatenate([dot_tn(a, b) for a, b in pairs], 1)
    return scatter_ctx(outer(*pairs))


def row_sum(part):
    wt = lax.axis_size("wt")
    if lax.axis_size("ctx") != 8 or wt != 4:
        return lax.psum_scatter(
            part.astype(bf16), ALL, scatter_dimension=0, tiled=True
        ).astype(f32)
    rows = part.shape[0] // wt
    low = part.astype(bf16)
    at = lambda d: ((lax.axis_index("wt") + d) % wt) * rows
    total = lax.dynamic_slice_in_dim(part, at(0), rows, 0)
    for d in range(1, wt):
        total = total + shift(lax.dynamic_slice_in_dim(low, at(d), rows, 0), d).astype(f32)
    return total


def spread_sum(x):
    return jnp.sum(lax.all_to_all(x, ALL, 0, 0, tiled=True), 0)


def after(x, *others):
    return lax.optimization_barrier((x,) + others)[0]


def rope_tables(positions, width):
    middle = HEAD_SIZE // 2
    frequency = jnp.power(
        jnp.float32(rope_base), -2.0 * jnp.arange(middle, dtype=f32) / HEAD_SIZE
    )
    angles = positions.astype(f32)[:, None] * frequency[None, :]
    times = width // middle
    return jnp.tile(jnp.cos(angles), (1, times)), jnp.tile(jnp.sin(angles), (1, times))


def turn(values, cosine, sine, direction):
    middle = HEAD_SIZE // 2
    first = lax.broadcasted_iota(jnp.int32, values.shape, 1) % HEAD_SIZE < middle
    turned = jnp.where(first, -jnp.roll(values, -middle, 1), jnp.roll(values, middle, 1))
    width = values.shape[1]
    return values * cosine[:, :width] + direction * turned * sine[:, :width]


def norm_forward(values, gain):
    inverse = lax.rsqrt(jnp.mean(values * values, -1, keepdims=True) + norm_eps)
    return (values * inverse * gain, inverse)


def norm_backward(values, inverse, gain, grad_out):
    scaled = gain * grad_out
    gain_grad = jnp.sum(grad_out * values * inverse, 0)
    projection = jnp.mean(scaled * values, -1, keepdims=True)
    return (inverse * scaled - values * inverse * inverse * inverse * projection, gain_grad)


def per_device(
    layer_input,
    attention_gain,
    query_weight,
    key_matrix,
    value_matrix,
    output_weight,
    mixture_gain,
    router_weight,
    gate_weight,
    up_weight,
    down_weight,
    expert_routes,
    prompt_deal,
    output_grad,
):
    tok = layer_input.shape[1]
    prompt_local = tok - CONT_DEV * CLEN
    block_rows = prompt_local // 2
    context_size = lax.axis_size("ctx")
    shard_count = lax.axis_size("wt")
    expert_count = gate_weight.shape[0]
    capacity = 8 * ((tok * TOP * 7 // (4 * EXPERTS) + 7) // 8)
    ctx_index = lax.axis_index("ctx")
    wt_index = lax.axis_index("wt")
    inputs = layer_input[0].astype(f32)
    routes = expert_routes[0]
    deal_row = prompt_deal[0]
    out_low = output_grad[0]
    out_grad = out_low.astype(f32)

    own_rows = query_weight.shape[0]
    packed = jnp.concatenate(
        [
            query_weight,
            key_matrix,
            value_matrix,
            output_weight.T,
            router_weight,
            attention_gain[:, None],
            mixture_gain[:, None],
            jnp.zeros((own_rows, 94), bf16),
        ],
        1,
    )
    pieces, counts, block_places, first_part = gather_all(packed)

    gate_full = lax.all_gather(gate_weight, "ctx", axis=0, tiled=False)
    up_full = lax.all_gather(up_weight, "ctx", axis=0, tiled=False)
    down_full = lax.all_gather(down_weight, "ctx", axis=0, tiled=False)

    mask = jnp.any(
        routes[:, :, None] == jnp.arange(EXPERTS, dtype=jnp.int32)[None, None, :], 1
    )
    order = jnp.arange(tok, dtype=jnp.int32)
    before = (order[None, :] < order[:, None]).astype(bf16)
    rank = jnp.where(mask, dot(before, mask.astype(bf16)), -1.0)
    ranks = lax.all_to_all(
        rank.T.reshape(shard_count, expert_count, tok), "wt", 0, 0, tiled=True
    )
    last = shard_count - 1
    grads_in = {0: out_low, last: shift(after(out_low, first_part), -1)}

    pieces, grads_in[last], ranks = beside(pieces, grads_in[last], ranks)
    local_rows = jnp.arange(tok, dtype=jnp.int32)
    mine = lax.dynamic_slice_in_dim(deal_row, 2 * ctx_index, 2, 0)
    prompt_place = (
        jnp.where(local_rows < block_rows, mine[0], mine[1]) * block_rows
        + local_rows % block_rows
    )
    positions = jnp.where(
        local_rows < prompt_local, prompt_place, PROMPT + (local_rows - prompt_local) % CLEN
    )
    cosine, sine = rope_tables(positions, 128)
    normed_one, turned_query, *kv_low, qkv_full, output_t, rest, gain_rows = project(
        layer_input[0], cosine, sine, pieces, counts, block_places
    )
    router_full = rest[:, :EXPERTS]
    first_gain, second_gain = gain_rows[0], gain_rows[1]
    inverse_one = lax.rsqrt(jnp.mean(inputs * inputs, -1, keepdims=True) + norm_eps)
    kv_own = [low[prompt_local:] for low in kv_low]
    kv_prompt = [low[:prompt_local] for low in kv_low]
    if context_size == 8:
        kv_even = [even_blocks(low) for low in kv_prompt]
        kv_even[0], turned_query = beside(kv_even[0], after(turned_query, *kv_even[1]))
        kv_pieces = [both_cores(even) for even in kv_even]
    else:
        kv_pieces = [gather_ctx(low) for low in kv_prompt]

    places = deal_row
    if context_size == 8:
        pairs = deal_row.reshape(2, 2, 2, 2)
        for axis, bit in ((0, 4), (1, 2), (2, 1)):
            pairs = jnp.where(ctx_index & bit > 0, jnp.flip(pairs, axis), pairs)
        places = pairs.reshape(-1)
    low = (mine[0] > mine[1]).astype(jnp.int32)
    starts = jnp.stack(
        [
            low * block_rows,
            (1 - low) * block_rows,
            jnp.min(mine) * block_rows,
            jnp.max(mine) * block_rows,
        ]
    ).astype(jnp.int32)
    heads = []
    for half in range(2):
        result = attention_forward(
            turned_query, kv_pieces[half], kv_own[half], places, starts, block_rows, half
        )
        d = last - 1 - half
        grads_in[d] = shift(grads_in[d + 1], -1)
        result, grads_in[d] = beside(result, grads_in[d])
        if half == 0:
            turned_query = after(turned_query, result[0])
        heads.append(result)
    for d in range(last - 3, 0, -1):
        grads_in[d] = shift(grads_in[d + 1], -1)
    attended = jnp.concatenate([out for out, _ in heads], 1)
    lse = [row for _, row in heads]

    branch = dot_nt(attended, output_t)
    middle = inputs + resid_scale * branch
    normed_mid, inverse_two = norm_forward(middle, second_gain)
    normed_two = normed_mid.astype(bf16)
    logits = dot(normed_two, router_full)
    top = jnp.max(jnp.where(mask, logits, masked_score), -1, keepdims=True)
    raised = jnp.where(mask, jnp.exp(jnp.where(mask, logits - top, 0.0)), 0.0)
    gates = raised / jnp.sum(raised, -1, keepdims=True)

    gates_out = gates.T.reshape(shard_count, expert_count, tok)
    gates_in = []
    for d in range(shard_count):
        piece = lax.dynamic_index_in_dim(gates_out, (wt_index + d) % shard_count, 0, False)
        gates_in.append(shift(piece, d) if d else piece)
    got = {0: normed_two}
    partial, mixed, gate_grads, rows = {}, {}, {}, []
    carried = None

    def add(a, b):
        return b if a is None else (a.astype(f32) + b.astype(f32)).astype(bf16)

    for d in [0] + list(range(last, 0, -1)):
        source = (wt_index - d) % shard_count
        rank_in = lax.dynamic_index_in_dim(ranks, source, 0, False)
        result = expert_pass(
            got[d], grads_in[d], rank_in, gates_in[d], gate_full, up_full, down_full, capacity
        )
        coming = d - 1 if d else last
        if coming:
            result, got[coming] = beside(result, shift(got[(coming + 1) % shard_count], -1))
        if d == 0:
            result, gates_in = beside(result, gates_in)
        if 0 < d <= last - 2:
            carried = shift(after(add(carried, partial[d + 2]), got[d]), -1)
            result, carried = beside(result, carried)
        mixed[d], partial[d], d_gate, *kept = result
        rows.append(kept)
        d_gate = d_gate.reshape(expert_count, tok)
        gate_grads[d] = shift(d_gate, shard_count - d) if d else d_gate
        if coming:
            got[coming] = after(got[coming], partial[d])
    carried = shift(add(carried, partial[2]), -1)
    (gate_grad, up_grad), carried = beside(
        up_weight_grads([(after(r[0], partial[1]), r[3], r[4]) for r in rows], context_size),
        carried,
    )
    carried = shift(add(carried, partial[1]), -1)
    down_grad, home = beside(
        down_weight_grads([(after(r[2], gate_grad), r[1]) for r in rows], context_size), carried
    )

    stacked = jnp.stack([gate_grads[d] for d in range(shard_count)], 0)
    stacked = jnp.roll(stacked, wt_index, 0).reshape(EXPERTS, tok).T
    grad_logits = (gates * (stacked - jnp.sum(gates * stacked, -1, keepdims=True))).astype(bf16)
    grad_normed_two = partial[0].astype(f32) + home.astype(f32)
    grad_normed_two = grad_normed_two + dot_nt(grad_logits, router_full)
    grad_mid_norm, second_gain_grad = norm_backward(
        middle, inverse_two, second_gain, grad_normed_two
    )
    grad_middle = out_grad + grad_mid_norm
    grad_branch = (resid_scale * grad_middle).astype(bf16)
    grad_attended = dot(grad_branch, output_t).astype(bf16)
    gate_share, up_share, down_share = (
        lax.psum_scatter(grad, "ctx", scatter_dimension=0, tiled=False).astype(f32)
        for grad in (gate_grad, up_grad, down_grad)
    )
    devices = context_size * shard_count
    small = jnp.concatenate(
        [
            dot_tn(normed_two, grad_logits).reshape(devices, own_rows * EXPERTS),
            second_gain_grad.reshape(devices, own_rows),
        ],
        1,
    )

    carried = shift(after(mixed[last], home), -1)
    query, carried = beside(after(turned_query, grad_attended), carried)
    d_query, owned, ours = [], [], []
    for half in range(2):
        result = attention_backward(
            query,
            grad_attended,
            lse[half],
            attended,
            cosine,
            sine,
            kv_pieces[half],
            kv_own[half],
            places,
            starts,
            block_rows,
            half,
        )
        carried = shift(add(carried, mixed[last - 1 - half]), -1)
        result, carried = beside(result, carried)
        d_q, d_kv, d_key_own, d_value_own = result
        query = after(query, d_q)
        if half == 0:
            small = spread_sum(after(small, d_q))
        d_query.append(d_q)
        owned.append(scatter_ctx(d_kv))
        ours.append((d_key_own, d_value_own))
    for d in range(last - 3, 0, -1):
        carried = shift(add(carried, mixed[d]), -1)
    mixture = mixed[0].astype(f32) + carried.astype(f32)
    layer_output = (middle + resid_scale * mixture).astype(bf16)
    d_query = jnp.concatenate(d_query, 1)
    query_part = outer_part((normed_one, d_query), (after(grad_branch, d_query), attended))
    d_key, d_value = (
        jnp.concatenate(
            [
                jnp.concatenate([owned[half][:, 256 * n : 256 * n + 256], ours[half][n]], 0)
                for half in range(2)
            ],
            1,
        )
        for n in range(2)
    )
    grad_key_low = turn(d_key, jnp.tile(cosine, (1, 4)), jnp.tile(sine, (1, 4)), -1.0).astype(
        bf16
    )
    grad_kv = jnp.concatenate([grad_key_low, d_value.astype(bf16)], 1)
    grad_kv, query_part = beside(grad_kv, query_part)
    kv_share = row_sum(outer_part((normed_one, grad_kv)))
    query_share, output_share = jnp.split(row_sum(query_part), 2, 1)
    grad_normed_one = dot_nt(d_query, qkv_full[:, :1024]) + dot_nt(grad_kv, qkv_full[:, 1024:])
    grad_input_norm, first_gain_grad = norm_backward(
        inputs, inverse_one, first_gain, grad_normed_one
    )
    input_grad = (grad_middle + grad_input_norm).astype(bf16)

    first_gain_share = spread_sum(first_gain_grad.reshape(devices, own_rows))
    return (
        layer_output[None],
        input_grad[None],
        first_gain_share,
        query_share,
        kv_share[:, :KV_WIDTH],
        kv_share[:, KV_WIDTH:],
        output_share.T,
        small[own_rows * EXPERTS :],
        small[: own_rows * EXPERTS].reshape(own_rows, EXPERTS),
        gate_share,
        up_share,
        down_share,
    )


def solution(mesh):
    return jax.shard_map(
        per_device,
        mesh=mesh,
        in_specs=(
            P("wt", "ctx", None),
            P(("ctx", "wt")),
            P(("ctx", "wt"), None),
            P(("ctx", "wt"), None),
            P(("ctx", "wt"), None),
            P(None, ("ctx", "wt")),
            P(("ctx", "wt")),
            P(("ctx", "wt"), None),
            P("wt", "ctx", None),
            P("wt", "ctx", None),
            P("wt", None, "ctx"),
            P("wt", "ctx", None),
            P("wt", None),
            P("wt", "ctx", None),
        ),
        out_specs=(
            P("wt", "ctx", None),
            P("wt", "ctx", None),
            P(("ctx", "wt")),
            P(("ctx", "wt"), None),
            P(("ctx", "wt"), None),
            P(("ctx", "wt"), None),
            P(None, ("ctx", "wt")),
            P(("ctx", "wt")),
            P(("ctx", "wt"), None),
            P("wt", "ctx", None),
            P("wt", "ctx", None),
            P("wt", None, "ctx"),
        ),
        check_vma=False,
    )
```

```python
import functools

import jax
import jax.numpy as jnp
from jax import lax
from jax.experimental import pallas as pl
from jax.experimental.pallas import tpu as pltpu
from jax.sharding import PartitionSpec as P

MODEL_WIDTH = 1024
HQ = 16
KEY_VALUE_HEADS = 8
HEAD_SIZE = 64
EXPERTS = 32
TOP = 8
PROMPT = 2048
CLEN = 256
CONT_DEV = 2
FF = 512
QTILE = 128
KV_WIDTH = KEY_VALUE_HEADS * HEAD_SIZE
ALL = ("ctx", "wt")

att_scale = 0.015625
resid_scale = 0.22
norm_eps = 1e-06
rope_base = 10000.0
masked_score = -1e30

bf16 = jnp.bfloat16
f32 = jnp.float32
VMEM_LIMIT = 60 * 1024 * 1024
SMALL = pl.CostEstimate(flops=1_000_000_000, bytes_accessed=1_000_000, transcendentals=0)

NT = (((1,), (1,)), ((), ()))
TN = (((0,), (0,)), ((), ()))


def dot(a, b):
    return jnp.dot(a, b, preferred_element_type=f32)


def dot_nt(a, b):
    return lax.dot_general(a, b, NT, preferred_element_type=f32)


def dot_tn(a, b):
    return lax.dot_general(a, b, TN, preferred_element_type=f32)


def turn_tile(values, cosine, sine, direction):
    middle = HEAD_SIZE // 2
    first = lax.broadcasted_iota(jnp.int32, values.shape, 1) % HEAD_SIZE < middle
    turned = jnp.where(first, -pltpu.roll(values, 128 - middle, 1), pltpu.roll(values, middle, 1))
    return values * cosine + direction * turned * sine


def project_kernel(places, x_ref, cos_ref, sin_ref, *refs, counts):
    pieces = refs[: len(counts)]
    normed_ref, q_ref, kv_ref, qkv_ref, out_ref, rest_ref, gains_ref = refs[len(counts) :]
    rows = MODEL_WIDTH // sum(counts)
    at = 0
    for piece, count in zip(pieces, counts):
        for i in range(count):
            source = slice(i * rows, (i + 1) * rows)
            target = pl.ds(pl.multiple_of(places[at] * rows, rows), rows)
            qkv_ref[target, :] = piece[source, :2048]
            out_ref[target, :] = piece[source, 2048:3072]
            rest_ref[target, :] = piece[source, 3072:]
            at += 1
    gains = rest_ref[...].astype(f32).T[EXPERTS : EXPERTS + 8]
    gains_ref[...] = gains
    x = x_ref[...].astype(f32)
    inverse = lax.rsqrt(jnp.mean(x * x, -1, keepdims=True) + norm_eps)
    normed_ref[...] = (x * inverse * gains[:1]).astype(bf16)
    for c in range(8):
        raw = dot(normed_ref[...], qkv_ref[:, 256 * c : 256 * (c + 1)])
        for h in range(2):
            part = raw[:, 128 * h : 128 * (h + 1)]
            if c < 6:
                part = turn_tile(part, cos_ref[...], sin_ref[...], 1.0)
            column = 256 * c + 128 * h
            if column < 1024:
                q_ref[:, column : column + 128] = part.astype(bf16)
            else:
                column -= 1024
                at = column % KV_WIDTH // 256 * 512 + column // KV_WIDTH * 256 + column % 256
                kv_ref[:, at : at + 128] = part.astype(bf16)


def project(x, cosine, sine, pieces, counts, places):
    tok = x.shape[0]
    shape = jax.ShapeDtypeStruct
    whole = pl.BlockSpec(memory_space=pltpu.VMEM)
    return pl.pallas_call(
        functools.partial(project_kernel, counts=counts),
        in_specs=[pl.BlockSpec(memory_space=pltpu.SMEM)] + [whole] * (3 + len(pieces)),
        out_specs=[whole] * 7,
        out_shape=[
            shape((tok, MODEL_WIDTH), bf16),
            shape((tok, HQ * HEAD_SIZE), bf16),
            shape((tok, 2 * KV_WIDTH), bf16),
            shape((MODEL_WIDTH, 2048), bf16),
            shape((MODEL_WIDTH, 1024), bf16),
            shape((MODEL_WIDTH, 128), bf16),
            shape((8, MODEL_WIDTH), f32),
        ],
        compiler_params=pltpu.CompilerParams(vmem_limit_bytes=VMEM_LIMIT),
        cost_estimate=SMALL,
        name="project",
    )(places, x, cosine, sine, *pieces)


def outer_kernel(mine, *refs):
    out_ref = refs[-1]
    at = 0
    for n in range(len(refs) // 2):
        columns = refs[2 * n + 1].shape[1]
        out_ref[:, at : at + columns] = dot_tn(refs[2 * n][...], refs[2 * n + 1][...]).astype(bf16)
        at += columns


def outer(*pairs):
    tok = pairs[0][0].shape[0]
    mine = lax.axis_index("ctx").astype(jnp.int32).reshape(1)
    specs = []
    for _, b in pairs:
        specs.append(pl.BlockSpec((tok, 128), lambda m, mine: (0, m ^ mine[0])))
        specs.append(pl.BlockSpec(b.shape, lambda m, mine: (0, 0)))
    columns = sum(b.shape[1] for _, b in pairs)
    return pl.pallas_call(
        outer_kernel,
        grid_spec=pltpu.PrefetchScalarGridSpec(
            num_scalar_prefetch=1,
            grid=(8,),
            in_specs=specs,
            out_specs=pl.BlockSpec((128, columns), lambda m, mine: (m, 0)),
        ),
        out_shape=jax.ShapeDtypeStruct((MODEL_WIDTH, columns), bf16),
        compiler_params=pltpu.CompilerParams(vmem_limit_bytes=VMEM_LIMIT),
        cost_estimate=SMALL,
        name="outer",
    )(mine, *[x for pair in pairs for x in pair])


def gather_keys(pieces, scratch, places, block_rows):
    at = 0
    for piece in pieces:
        for b in range(piece.shape[0] // block_rows):
            start = pl.multiple_of(places[at] * block_rows, block_rows)
            scratch[pl.ds(start, block_rows), :] = piece[b * block_rows : (b + 1) * block_rows, :]
            at += 1


def pair_rows(ref, start, rows, j):
    both = ref[pl.ds(start, rows), 2 * HEAD_SIZE * j : 2 * HEAD_SIZE * (j + 1)]
    return jnp.concatenate([both[:, :HEAD_SIZE], both[:, HEAD_SIZE:]], 0)


def attention_forward_kernel(places, starts, q_ref, *refs, block_rows, pieces):
    k_refs, v_refs = refs[:pieces], refs[pieces : 2 * pieces]
    kc_ref, vc_ref, o_ref, lse_ref, k_scr, v_scr = refs[2 * pieces :]
    prompt_local = 2 * block_rows
    gather_keys(k_refs, k_scr, places, block_rows)
    gather_keys(v_refs, v_scr, places, block_rows)

    def store(start, rows, j, out, m, total, at):
        out = (out / total).astype(bf16)
        lse = m + jnp.log(total)
        o_ref[pl.ds(start, rows), 2 * HEAD_SIZE * j : 2 * HEAD_SIZE * (j + 1)] = jnp.concatenate(
            [out[:rows], out[rows:]], 1
        )
        row = jnp.broadcast_to(lse, (2 * rows, 128)).T[:1]
        lse_ref[0, 2 * j : 2 * j + 2, pl.ds(at, rows)] = jnp.concatenate(
            [row[:, :rows], row[:, rows:]], 0
        )

    def tile(i, _):
        start = pl.multiple_of(prompt_local + i * QTILE, 64)
        per = CLEN // QTILE
        seg = pl.multiple_of((i // per) * CLEN, CLEN)
        for j in range(2):
            lanes = slice(HEAD_SIZE * j, HEAD_SIZE * (j + 1))
            q = pair_rows(q_ref, start, QTILE, j) * bf16(att_scale)
            s1 = dot_nt(q, k_scr[:, lanes])
            s2 = dot_nt(q, kc_ref[pl.ds(seg, CLEN), lanes])
            place = lax.broadcasted_iota(jnp.int32, s2.shape, 0) % QTILE + (i % per) * QTILE
            s2 = jnp.where(lax.broadcasted_iota(jnp.int32, s2.shape, 1) <= place, s2, masked_score)
            m = jnp.maximum(jnp.max(s1, 1, keepdims=True), jnp.max(s2, 1, keepdims=True))
            e1 = jnp.exp(s1 - m)
            e2 = jnp.exp(s2 - m)
            total = jnp.sum(e1, 1, keepdims=True) + jnp.sum(e2, 1, keepdims=True)
            out = dot(e1.astype(bf16), v_scr[:, lanes])
            out = out + dot(e2.astype(bf16), vc_ref[pl.ds(seg, CLEN), lanes])
            store(start, QTILE, j, out, m, total, pl.multiple_of(i * QTILE, QTILE))
        return 0

    lax.fori_loop(0, CONT_DEV * CLEN // QTILE, tile, 0)

    for half, keys in enumerate((PROMPT // 2, PROMPT)):
        start = pl.multiple_of(starts[half], block_rows)
        for j in range(2):
            lanes = slice(HEAD_SIZE * j, HEAD_SIZE * (j + 1))
            q = pair_rows(q_ref, start, block_rows, j) * bf16(att_scale)
            s = dot_nt(q, k_scr[:keys, lanes])
            place = lax.broadcasted_iota(jnp.int32, s.shape, 0) % block_rows + starts[2 + half]
            s = jnp.where(lax.broadcasted_iota(jnp.int32, s.shape, 1) <= place, s, masked_score)
            m = jnp.max(s, 1, keepdims=True)
            e = jnp.exp(s - m)
            total = jnp.sum(e, 1, keepdims=True)
            out = dot(e.astype(bf16), v_scr[:keys, lanes])
            store(start, block_rows, j, out, m, total, CONT_DEV * CLEN + half * block_rows)


def key_specs(pieces, own, half):
    spec = pl.BlockSpec
    key, value = (lambda g, *_: (0, 4 * half + g)), (lambda g, *_: (0, 4 * half + 2 + g))
    keys = [spec((p.shape[0], 128), key) for p in pieces]
    values = [spec((p.shape[0], 128), value) for p in pieces]
    return keys + values + [spec((own, 128), key), spec((own, 128), value)]


def attention_forward(q, pieces, kv_own, places, starts, block_rows, half):
    tok = q.shape[0]
    spec = pl.BlockSpec
    return pl.pallas_call(
        functools.partial(
            attention_forward_kernel, block_rows=block_rows, pieces=len(pieces)
        ),
        grid_spec=pltpu.PrefetchScalarGridSpec(
            num_scalar_prefetch=2,
            grid=(2,),
            in_specs=[spec((tok, 256), lambda g, *_: (0, 2 * half + g))]
            + key_specs(pieces, kv_own.shape[0], half),
            out_specs=[
                spec((tok, 256), lambda g, *_: (0, g)),
                spec((1, 4, tok), lambda g, *_: (g, 0, 0)),
            ],
            scratch_shapes=[
                pltpu.VMEM((PROMPT, 2 * HEAD_SIZE), bf16),
                pltpu.VMEM((PROMPT, 2 * HEAD_SIZE), bf16),
            ],
        ),
        out_shape=[
            jax.ShapeDtypeStruct((tok, HQ * HEAD_SIZE // 2), bf16),
            jax.ShapeDtypeStruct((2, 4, tok), f32),
        ],
        compiler_params=pltpu.CompilerParams(vmem_limit_bytes=VMEM_LIMIT),
        cost_estimate=SMALL,
        name="attention_forward",
    )(places, starts, q, *pieces, *pieces, kv_own, kv_own)


def attention_backward_kernel(
    places, starts, q_ref, do_ref, lse_ref, o_ref, cos_ref, sin_ref, *refs, block_rows, pieces
):
    k_refs, v_refs = refs[:pieces], refs[pieces : 2 * pieces]
    kc_ref, vc_ref, dq_ref, dkv_ref, dkc_ref, dvc_ref = refs[2 * pieces : 2 * pieces + 6]
    k_scr, v_scr, dk_acc, dv_acc, dq_acc = refs[2 * pieces + 6 :]
    prompt_local = 2 * block_rows
    gather_keys(k_refs, k_scr, places, block_rows)
    gather_keys(v_refs, v_scr, places, block_rows)
    dk_acc[...] = jnp.zeros_like(dk_acc)
    dv_acc[...] = jnp.zeros_like(dv_acc)
    dkc_ref[...] = jnp.zeros_like(dkc_ref)
    dvc_ref[...] = jnp.zeros_like(dvc_ref)

    def row_pair(ref, start, rows, j):
        both = ref[0, 2 * j : 2 * j + 2, pl.ds(start, rows)]
        return jnp.concatenate([both[:1], both[1:]], 1)

    def centre(start, rows, j, d_out):
        product = d_out.astype(f32) * pair_rows(o_ref, start, rows, j).astype(f32)
        ones = jnp.ones((8, HEAD_SIZE), f32)
        return lax.dot_general(
            ones, product, NT, precision=lax.Precision.HIGHEST, preferred_element_type=f32
        )[:1]

    def part(k, v, q, d_out, lse, delta, allowed):
        s = dot_nt(k, q)
        if allowed is not None:
            s = jnp.where(allowed(s.shape), s, masked_score)
        p = jnp.exp(s - lse)
        d_p = dot_nt(v, d_out)
        d_s = (p * (d_p - delta)).astype(bf16)
        return dot_tn(d_s, k), dot(d_s, q), dot(p.astype(bf16), d_out)

    def store(start, rows, j, d_q):
        d_q = d_q * att_scale
        dq_acc[pl.ds(start, rows), 2 * HEAD_SIZE * j : 2 * HEAD_SIZE * (j + 1)] = jnp.concatenate(
            [d_q[:rows], d_q[rows:]], 1
        )

    def tile(i, _):
        start = pl.multiple_of(prompt_local + i * QTILE, 64)
        per = CLEN // QTILE
        seg = pl.multiple_of((i // per) * CLEN, CLEN)
        own = pl.ds(seg, CLEN)
        lane_start = pl.multiple_of(i * QTILE, QTILE)

        def allowed(shape):
            place = lax.broadcasted_iota(jnp.int32, shape, 1) % QTILE + (i % per) * QTILE
            return lax.broadcasted_iota(jnp.int32, shape, 0) <= place

        for j in range(2):
            lanes = slice(HEAD_SIZE * j, HEAD_SIZE * (j + 1))
            q = pair_rows(q_ref, start, QTILE, j) * bf16(att_scale)
            d_out = pair_rows(do_ref, start, QTILE, j)
            lse = row_pair(lse_ref, lane_start, QTILE, j)
            delta = centre(start, QTILE, j, d_out)
            a, b, c = part(k_scr[:, lanes], v_scr[:, lanes], q, d_out, lse, delta, None)
            dk_acc[:, lanes] += b
            dv_acc[:, lanes] += c
            d_q = a
            a, b, c = part(
                kc_ref[own, lanes], vc_ref[own, lanes], q, d_out, lse, delta, allowed
            )
            dkc_ref[own, lanes] += b
            dvc_ref[own, lanes] += c
            store(start, QTILE, j, d_q + a)
        return 0

    lax.fori_loop(0, CONT_DEV * CLEN // QTILE, tile, 0)

    for half, keys in enumerate((PROMPT // 2, PROMPT)):
        start = pl.multiple_of(starts[half], block_rows)
        at = CONT_DEV * CLEN + half * block_rows

        def allowed(shape):
            place = lax.broadcasted_iota(jnp.int32, shape, 1) % block_rows + starts[2 + half]
            return lax.broadcasted_iota(jnp.int32, shape, 0) <= place

        for j in range(2):
            lanes = slice(HEAD_SIZE * j, HEAD_SIZE * (j + 1))
            q = pair_rows(q_ref, start, block_rows, j) * bf16(att_scale)
            d_out = pair_rows(do_ref, start, block_rows, j)
            lse = row_pair(lse_ref, at, block_rows, j)
            delta = centre(start, block_rows, j, d_out)
            a, b, c = part(
                k_scr[:keys, lanes], v_scr[:keys, lanes], q, d_out, lse, delta, allowed
            )
            dk_acc[:keys, lanes] += b
            dv_acc[:keys, lanes] += c
            store(start, block_rows, j, a)

    g = pl.program_id(0)
    key_lanes = pl.ds(pl.multiple_of(g * 128, 128), 128)
    value_lanes = pl.ds(pl.multiple_of(256 + g * 128, 128), 128)
    for b in range(PROMPT // block_rows):
        source = pl.ds(pl.multiple_of(places[b] * block_rows, block_rows), block_rows)
        rows = slice(b * block_rows, (b + 1) * block_rows)
        dkv_ref[rows, key_lanes] = dk_acc[source, :].astype(bf16)
        dkv_ref[rows, value_lanes] = dv_acc[source, :].astype(bf16)
    for c in range(2):
        lanes = slice(128 * c, 128 * (c + 1))
        dq_ref[:, lanes] = turn_tile(dq_acc[:, lanes], cos_ref[...], sin_ref[...], -1.0).astype(
            bf16
        )


def attention_backward(
    q, d_out, lse, attended, cosine, sine, pieces, kv_own, places, starts, block_rows, half
):
    tok = q.shape[0]
    own = kv_own.shape[0]
    spec = pl.BlockSpec
    wide = spec((tok, 256), lambda g, *_: (0, 2 * half + g))
    ours = spec((own, 128), lambda g, *_: (0, g))
    table = spec((tok, 128), lambda g, *_: (0, 0))
    return pl.pallas_call(
        functools.partial(
            attention_backward_kernel, block_rows=block_rows, pieces=len(pieces)
        ),
        grid_spec=pltpu.PrefetchScalarGridSpec(
            num_scalar_prefetch=2,
            grid=(2,),
            in_specs=[wide, wide, spec((1, 4, tok), lambda g, *_: (g, 0, 0)), wide, table, table]
            + key_specs(pieces, own, half),
            out_specs=[
                spec((tok, 256), lambda g, *_: (0, g)),
                spec((PROMPT, KV_WIDTH), lambda g, *_: (0, 0)),
                ours,
                ours,
            ],
            scratch_shapes=[
                pltpu.VMEM((PROMPT, 2 * HEAD_SIZE), bf16),
                pltpu.VMEM((PROMPT, 2 * HEAD_SIZE), bf16),
                pltpu.VMEM((PROMPT, 2 * HEAD_SIZE), f32),
                pltpu.VMEM((PROMPT, 2 * HEAD_SIZE), f32),
                pltpu.VMEM((tok, 4 * HEAD_SIZE), f32),
            ],
        ),
        out_shape=[
            jax.ShapeDtypeStruct((tok, HQ * HEAD_SIZE // 2), bf16),
            jax.ShapeDtypeStruct((PROMPT, KV_WIDTH), bf16),
            jax.ShapeDtypeStruct((own, KV_WIDTH // 2), f32),
            jax.ShapeDtypeStruct((own, KV_WIDTH // 2), f32),
        ],
        compiler_params=pltpu.CompilerParams(vmem_limit_bytes=VMEM_LIMIT),
        cost_estimate=SMALL,
        name="attention_backward",
    )(places, starts, q, d_out, lse, attended, cosine, sine, *pieces, *pieces, kv_own, kv_own)


def expert_kernel(
    counts,
    a2_ref,
    df_ref,
    rank_ref,
    gate_ref,
    *refs,
    sizes,
    pieces,
):
    weights, refs = refs[: 3 * pieces], refs[3 * pieces :]
    wg_refs, wu_refs, wd_refs = (weights[n * pieces : (n + 1) * pieces] for n in range(3))
    mix_ref, da_ref, dg_ref, x_ref, dy_ref, z_ref, dgate_ref, dup_ref, mix_acc, da_acc = refs
    e = pl.program_id(0)

    @pl.when(e == 0)
    def _():
        mix_acc[...] = jnp.zeros_like(mix_acc)
        da_acc[...] = jnp.zeros_like(da_acc)

    def body(size):
        rank = rank_ref[0]
        gates = gate_ref[0]
        tok = rank.shape[1]
        slot = lax.broadcasted_iota(jnp.int32, (size, tok), 0).astype(f32)
        hit = slot == rank
        chosen = hit.astype(f32).astype(bf16)
        gate = jnp.sum(jnp.where(hit, gates, 0.0), 1, keepdims=True)
        x = dot(chosen, a2_ref[...]).astype(bf16)
        d_mix = resid_scale * dot(chosen, df_ref[...])
        wg = jnp.concatenate([ref[:, 0].reshape(-1, FF) for ref in wg_refs], 0)
        wu = jnp.concatenate([ref[:, 0].reshape(-1, FF) for ref in wu_refs], 0)
        wd = jnp.concatenate([ref[c, 0] for ref in wd_refs for c in range(ref.shape[0])], 1)
        g = dot(x, wg)
        u = dot(x, wu)
        sig = jax.nn.sigmoid(g)
        z = (g * sig * u).astype(bf16)
        y = dot(z, wd).astype(bf16).astype(f32)
        d_gate_value = jnp.sum(d_mix * y, 1, keepdims=True)
        dg_ref[0] = jnp.sum(jnp.where(hit, d_gate_value, 0.0), 0, keepdims=True)
        mix_acc[...] += dot_tn(chosen, (gate * y).astype(bf16))
        d_y = (gate * d_mix).astype(bf16)
        d_z = dot_nt(d_y, wd)
        d_g = (d_z * u * sig * (1.0 + g * (1.0 - sig))).astype(bf16)
        d_u = (d_z * g * sig).astype(bf16)
        d_r = (dot_nt(d_g, wg) + dot_nt(d_u, wu)).astype(bf16)
        da_acc[...] += dot_tn(chosen, d_r)
        for ref, value in (
            (x_ref, x),
            (dy_ref, d_y),
            (z_ref, z),
            (dgate_ref, d_g),
            (dup_ref, d_u),
        ):
            ref[0, :size] = value
            if size < ref.shape[1]:
                ref[0, size:] = jnp.zeros((ref.shape[1] - size, ref.shape[2]), bf16)

    least = -1
    for size in sizes:
        pl.when((counts[e] > least) & (counts[e] <= size))(functools.partial(body, size))
        least = size

    @pl.when(e == pl.num_programs(0) - 1)
    def _():
        mix_ref[...] = mix_acc[...].astype(bf16)
        da_ref[...] = da_acc[...].astype(bf16)


def expert_pass(a2, df, rank, gates, wg, wu, wd, capacity):
    tok = a2.shape[0]
    parts, experts = wg[0].shape[0], wg[0].shape[1]
    pieces = len(wg)
    sizes = sorted({min(size, capacity) for size in (128, 192, 256, capacity)})
    counts = (jnp.max(rank, 1) + 1.0).astype(jnp.int32)
    spec = pl.BlockSpec
    whole = spec((tok, MODEL_WIDTH), lambda e, *_: (0, 0))
    row = spec((1, 1, tok), lambda e, *_: (e, 0, 0))
    width = wg[0].shape[2]
    up = spec((parts, 1, width, FF), lambda e, *_: (0, e, 0, 0))
    down = spec((parts, 1, FF, width), lambda e, *_: (0, e, 0, 0))
    rows_wide = spec((1, capacity, MODEL_WIDTH), lambda e, *_: (e, 0, 0))
    rows_thin = spec((1, capacity, FF), lambda e, *_: (e, 0, 0))
    shape = jax.ShapeDtypeStruct
    return pl.pallas_call(
        functools.partial(expert_kernel, sizes=sizes, pieces=pieces),
        grid_spec=pltpu.PrefetchScalarGridSpec(
            num_scalar_prefetch=1,
            grid=(experts,),
            in_specs=[whole, whole, row, row] + [up] * (2 * pieces) + [down] * pieces,
            out_specs=[whole, whole, row, rows_wide, rows_wide, rows_thin, rows_thin, rows_thin],
            scratch_shapes=[
                pltpu.VMEM((tok, MODEL_WIDTH), f32),
                pltpu.VMEM((tok, MODEL_WIDTH), f32),
            ],
        ),
        out_shape=[
            shape((tok, MODEL_WIDTH), bf16),
            shape((tok, MODEL_WIDTH), bf16),
            shape((experts, 1, tok), f32),
            shape((experts, capacity, MODEL_WIDTH), bf16),
            shape((experts, capacity, MODEL_WIDTH), bf16),
            shape((experts, capacity, FF), bf16),
            shape((experts, capacity, FF), bf16),
            shape((experts, capacity, FF), bf16),
        ],
        compiler_params=pltpu.CompilerParams(vmem_limit_bytes=VMEM_LIMIT),
        cost_estimate=SMALL,
        name="expert_pass",
    )(counts, a2, df, rank.reshape(experts, 1, tok), gates.reshape(experts, 1, tok), *wg, *wu, *wd)


def up_grad_kernel(order, *refs, sources):
    rows = refs[: 3 * sources]
    gate_ref, up_ref = refs[3 * sources :]
    width = gate_ref.shape[2]
    for n, out_ref in ((1, gate_ref), (2, up_ref)):
        total = None
        for s in range(sources):
            term = dot_tn(rows[3 * s][0], rows[3 * s + n][0])
            total = term if total is None else total + term
        total = total.astype(bf16)
        for c in range(out_ref.shape[0]):
            out_ref[order[c], 0] = total[c * width : (c + 1) * width]


def down_grad_kernel(order, *refs, sources, parts):
    rows, down_ref = refs[: 2 * sources], refs[-1]
    width = MODEL_WIDTH // parts
    total = None
    for s in range(sources):
        term = dot_tn(rows[2 * s][0], rows[2 * s + 1][0])
        total = term if total is None else total + term
    total = total.astype(bf16)
    for c in range(parts):
        down_ref[order[c], 0] = total[:, c * width : (c + 1) * width]


def row_specs(rows):
    return [pl.BlockSpec((1,) + a.shape[1:], lambda e, *_: (e, 0, 0)) for r in rows for a in r]


def up_weight_grads(rows, order):
    parts = order.shape[0]
    experts = rows[0][0].shape[0]
    shape = (parts, experts, MODEL_WIDTH // parts, FF)
    out = pl.BlockSpec((parts, 1) + shape[2:], lambda e, *_: (0, e, 0, 0))
    return pl.pallas_call(
        functools.partial(up_grad_kernel, sources=len(rows)),
        grid_spec=pltpu.PrefetchScalarGridSpec(
            num_scalar_prefetch=1,
            grid=(experts,),
            in_specs=row_specs(rows),
            out_specs=[out, out],
        ),
        out_shape=[jax.ShapeDtypeStruct(shape, bf16)] * 2,
        compiler_params=pltpu.CompilerParams(vmem_limit_bytes=VMEM_LIMIT),
        cost_estimate=SMALL,
        name="up_weight_grads",
    )(order, *[a for r in rows for a in r])


def down_weight_grads(rows, order):
    parts = order.shape[0]
    experts = rows[0][0].shape[0]
    shape = (parts, experts, FF, MODEL_WIDTH // parts)
    return pl.pallas_call(
        functools.partial(down_grad_kernel, sources=len(rows), parts=parts),
        grid_spec=pltpu.PrefetchScalarGridSpec(
            num_scalar_prefetch=1,
            grid=(experts,),
            in_specs=row_specs(rows),
            out_specs=pl.BlockSpec((parts, 1) + shape[2:], lambda e, *_: (0, e, 0, 0)),
        ),
        out_shape=jax.ShapeDtypeStruct(shape, bf16),
        compiler_params=pltpu.CompilerParams(vmem_limit_bytes=VMEM_LIMIT),
        cost_estimate=SMALL,
        name="down_weight_grads",
    )(order, *[a for r in rows for a in r])


def swap(x, mask):
    return lax.ppermute(x, "ctx", [(i, i ^ mask) for i in range(lax.axis_size("ctx"))])


def gather_ctx(x, rows):
    if lax.axis_size("ctx") != 8:
        return lax.all_gather(x[:rows], "ctx", axis=0, tiled=True)
    return plane_gather(x, rows)


def scatter_ctx(x):
    if lax.axis_size("ctx") != 8:
        return lax.psum_scatter(x, "ctx", scatter_dimension=0, tiled=True).astype(f32)
    rows = x.shape[0] // 8
    half = rows // 2
    block = [x[m * rows : (m + 1) * rows] for m in range(8)]
    diagonal, near, far, own = (
        block[m].astype(f32) + swap(block[m + 1], 1).astype(f32) for m in (6, 2, 4, 0)
    )
    diagonal = diagonal.astype(bf16)
    near_top = near[:half] + swap(diagonal[:half], 4).astype(f32)
    far_end = far[half:] + swap(diagonal[half:], 2).astype(f32)
    near = jnp.concatenate([near_top.astype(bf16), near[half:].astype(bf16)], 0)
    far = jnp.concatenate([far[:half].astype(bf16), far_end.astype(bf16)], 0)
    return own + swap(near, 2).astype(f32) + swap(far, 4).astype(f32)


MESH = pl.DeviceIdType.MESH
ANY = pl.BlockSpec(memory_space=pl.ANY)


def partner(mask):
    me = lax.axis_index("ctx")
    return me + mask - 2 * mask * ((me // mask) % 2)


def ahead(distance):
    return (lax.axis_index("wt") + distance) % lax.axis_size("wt")


class Copies:
    def __init__(self, send, recv):
        self.send, self.recv, self.made = send, recv, {}

    def start(self, name, source, target, device):
        n = len(self.made)
        self.made[name] = copy = pltpu.make_async_remote_copy(
            src_ref=source,
            dst_ref=target,
            send_sem=self.send.at[n],
            recv_sem=self.recv.at[n],
            device_id=device,
            device_id_type=MESH,
        )
        copy.start()

    def arrived(self, name):
        self.made[name].wait_recv()

    def close(self):
        for copy in self.made.values():
            copy.wait_send()


def greet(devices):
    barrier = pltpu.get_barrier_semaphore()
    for device in devices:
        pl.semaphore_signal(barrier, inc=1, device_id=device, device_id_type=MESH)
    pl.semaphore_wait(barrier, len(devices))


def plane_steps(copies, block, half, key):
    side, near, far = ({"ctx": partner(m)} for m in (1, 2, 4))
    top, end = (lambda m: block(m, 0, half)), (lambda m: block(m, half, half))

    def first():
        copies.start((key, 2), block(0), block(2), near)
        copies.start((key, 4), block(0), block(4), far)
        copies.start((key, 1), block(0), block(1), side)

    def second():
        copies.arrived((key, 2))
        copies.start((key, 6), top(2), top(6), far)
        copies.start((key, 3), block(2), block(3), side)

    def third():
        copies.arrived((key, 4))
        copies.start((key, 7), end(4), end(6), near)
        copies.start((key, 5), block(4), block(5), side)

    def fourth():
        copies.arrived((key, 6))
        copies.arrived((key, 7))
        copies.start((key, 8), block(6), block(7), side)

    def last():
        for m in (1, 3, 5, 8):
            copies.arrived((key, m))

    return [first, second, third, fourth, last]


def plane_gather_kernel(x_ref, out_ref, send, recv, own_sem):
    rows = out_ref.shape[0] // 8
    greet([{"ctx": partner(m)} for m in (1, 2, 4)])
    own = pltpu.make_async_copy(x_ref.at[pl.ds(0, rows)], out_ref.at[pl.ds(0, rows)], own_sem)
    own.start()
    copies = Copies(send, recv)

    def block(m, start=0, count=rows):
        if m == 0:
            return x_ref.at[pl.ds(start, count)]
        return out_ref.at[pl.ds(m * rows + start, count)]

    for step in plane_steps(copies, block, rows // 2, 0):
        step()
    own.wait()
    copies.close()


def plane_gather(x, rows):
    return pl.pallas_call(
        plane_gather_kernel,
        in_specs=[ANY],
        out_specs=ANY,
        out_shape=jax.ShapeDtypeStruct((8 * rows, x.shape[1]), x.dtype),
        scratch_shapes=[
            pltpu.SemaphoreType.DMA((8,)),
            pltpu.SemaphoreType.DMA((8,)),
            pltpu.SemaphoreType.DMA,
        ],
        compiler_params=pltpu.CompilerParams(collective_id=1, has_side_effects=True),
        cost_estimate=SMALL,
        name="plane_gather",
    )(x)


def packed_gather_kernel(x_ref, out_ref, send, recv, own_sem):
    rows = x_ref.shape[0]
    greet(
        [{"ctx": partner(m)} for m in (1, 2, 4)] + [{"wt": ahead(d)} for d in (1, 2, 3)]
    )
    own = pltpu.make_async_copy(x_ref, out_ref.at[pl.ds(0, rows)], own_sem)
    own.start()
    copies = Copies(send, recv)

    def block_of(d):
        def block(m, start=0, count=rows):
            if m == 0 and d == 0:
                return x_ref.at[pl.ds(start, count)]
            return out_ref.at[pl.ds((4 * m + d) * rows + start, count)]

        return block

    for d in (1, 3, 2):
        copies.start(d, x_ref, block_of(d)(0), {"wt": ahead(d)})
    steps = {d: plane_steps(copies, block_of(d), rows // 2, ("plane", d)) for d in range(4)}
    steps[0][0]()
    for d, before in ((1, 0), (3, 1), (2, 3)):
        copies.arrived(d)
        steps[d][0]()
        steps[before][1]()
        steps[before][2]()
        if d != 1:
            steps[{3: 0, 2: 1}[d]][3]()
    steps[2][1]()
    steps[2][2]()
    steps[3][3]()
    steps[2][3]()
    for d in range(4):
        steps[d][4]()
    own.wait()
    copies.close()


def packed_gather(x):
    return pl.pallas_call(
        packed_gather_kernel,
        in_specs=[ANY],
        out_specs=ANY,
        out_shape=jax.ShapeDtypeStruct((32 * x.shape[0], x.shape[1]), x.dtype),
        scratch_shapes=[
            pltpu.SemaphoreType.DMA((35,)),
            pltpu.SemaphoreType.DMA((35,)),
            pltpu.SemaphoreType.DMA,
        ],
        compiler_params=pltpu.CompilerParams(collective_id=2, has_side_effects=True),
        cost_estimate=SMALL,
        name="packed_gather",
    )(x)


def shift(x, distance):
    n = lax.axis_size("wt")
    return lax.ppermute(x, "wt", [(i, (i + distance) % n) for i in range(n)])


def beside(results, *arrivals):
    out = lax.optimization_barrier((results, arrivals))
    return (out[0],) + tuple(out[1])


def gather_all(x):
    ctx, wt = lax.axis_size("ctx"), lax.axis_size("wt")
    if ctx != 8 or wt != 4:
        return [lax.all_gather(x, ALL, axis=0, tiled=True)], [1], jnp.zeros((1,), jnp.int32)
    ctx_index, wt_index = lax.axis_index("ctx"), lax.axis_index("wt")
    m = jnp.arange(8, dtype=jnp.int32)
    d = jnp.arange(4, dtype=jnp.int32)
    places = ((ctx_index ^ m) * wt)[:, None] + ((wt_index - d) % wt)[None, :]
    return [packed_gather(x)], [32], places.reshape(-1).astype(jnp.int32)


def outer_part(*pairs):
    if lax.axis_size("ctx") != 8 or lax.axis_size("wt") != 4:
        return jnp.concatenate([dot_tn(a, b) for a, b in pairs], 1)
    return scatter_ctx(outer(*pairs))


def row_sum(part):
    wt = lax.axis_size("wt")
    if lax.axis_size("ctx") != 8 or wt != 4:
        return lax.psum_scatter(
            part.astype(bf16), ALL, scatter_dimension=0, tiled=True
        ).astype(f32)
    rows = part.shape[0] // wt
    low = part.astype(bf16)
    at = lambda d: ((lax.axis_index("wt") + d) % wt) * rows
    total = lax.dynamic_slice_in_dim(part, at(0), rows, 0)
    for d in range(1, wt):
        total = total + shift(lax.dynamic_slice_in_dim(low, at(d), rows, 0), d).astype(f32)
    return total


def spread_sum(x):
    return jnp.sum(lax.all_to_all(x, ALL, 0, 0, tiled=True), 0)


def after(x, *others):
    return lax.optimization_barrier((x,) + others)[0]


def rope_tables(positions, width):
    middle = HEAD_SIZE // 2
    frequency = jnp.power(
        jnp.float32(rope_base), -2.0 * jnp.arange(middle, dtype=f32) / HEAD_SIZE
    )
    angles = positions.astype(f32)[:, None] * frequency[None, :]
    times = width // middle
    return jnp.tile(jnp.cos(angles), (1, times)), jnp.tile(jnp.sin(angles), (1, times))


def turn(values, cosine, sine, direction):
    middle = HEAD_SIZE // 2
    first = lax.broadcasted_iota(jnp.int32, values.shape, 1) % HEAD_SIZE < middle
    turned = jnp.where(first, -jnp.roll(values, -middle, 1), jnp.roll(values, middle, 1))
    width = values.shape[1]
    return values * cosine[:, :width] + direction * turned * sine[:, :width]


def norm_forward(values, gain):
    inverse = lax.rsqrt(jnp.mean(values * values, -1, keepdims=True) + norm_eps)
    return (values * inverse * gain, inverse)


def norm_backward(values, inverse, gain, grad_out):
    scaled = gain * grad_out
    gain_grad = jnp.sum(grad_out * values * inverse, 0)
    projection = jnp.mean(scaled * values, -1, keepdims=True)
    return (inverse * scaled - values * inverse * inverse * inverse * projection, gain_grad)


def per_device(
    layer_input,
    attention_gain,
    query_weight,
    key_matrix,
    value_matrix,
    output_weight,
    mixture_gain,
    router_weight,
    gate_weight,
    up_weight,
    down_weight,
    expert_routes,
    prompt_deal,
    output_grad,
):
    tok = layer_input.shape[1]
    prompt_local = tok - CONT_DEV * CLEN
    block_rows = prompt_local // 2
    context_size = lax.axis_size("ctx")
    shard_count = lax.axis_size("wt")
    expert_count = gate_weight.shape[0]
    capacity = 8 * ((tok * TOP * 7 // (4 * EXPERTS) + 7) // 8)
    ctx_index = lax.axis_index("ctx")
    wt_index = lax.axis_index("wt")
    inputs = layer_input[0].astype(f32)
    routes = expert_routes[0]
    deal_row = prompt_deal[0]
    out_low = output_grad[0]
    out_grad = out_low.astype(f32)

    own_rows = query_weight.shape[0]
    packed = jnp.concatenate(
        [
            query_weight,
            key_matrix,
            value_matrix,
            output_weight.T,
            router_weight,
            attention_gain[:, None],
            mixture_gain[:, None],
            jnp.zeros((own_rows, 94), bf16),
        ],
        1,
    )
    pieces, counts, block_places = gather_all(packed)

    core = ctx_index % 2
    if context_size == 8:
        chips = [[0, 2, 4, 6], [1, 3, 5, 7]]
        expert_weights = [
            [lax.all_gather(w, "ctx", axis=0, tiled=False, axis_index_groups=chips)]
            for w in (gate_weight, up_weight, down_weight)
        ]
        four = 2 * jnp.arange(4, dtype=jnp.int32)
        width_order = jnp.concatenate([four + core, four + 1 - core]).astype(jnp.int32)
    else:
        expert_weights = [
            [lax.all_gather(w, "ctx", axis=0, tiled=False)]
            for w in (gate_weight, up_weight, down_weight)
        ]
        width_order = jnp.arange(context_size, dtype=jnp.int32)

    def to_line(x):
        if context_size != 8:
            return x
        x = x.reshape(tok, 4, 2, 128)
        ours, others = (x[:, :, n].reshape(tok, 512) for n in range(2))
        return jnp.where(
            core == 0, jnp.concatenate([ours, others], 1), jnp.concatenate([others, ours], 1)
        )

    def from_line(x):
        if context_size != 8:
            return x
        ours, others = (x[:, 512 * n : 512 * n + 512].reshape(tok, 4, 128) for n in range(2))
        return jnp.where(
            core == 0, jnp.stack([ours, others], 2), jnp.stack([others, ours], 2)
        ).reshape(tok, MODEL_WIDTH)

    mask = jnp.any(
        routes[:, :, None] == jnp.arange(EXPERTS, dtype=jnp.int32)[None, None, :], 1
    )
    order = jnp.arange(tok, dtype=jnp.int32)
    before = (order[None, :] < order[:, None]).astype(bf16)
    rank = jnp.where(mask, dot(before, mask.astype(bf16)), -1.0)
    ranks = lax.all_to_all(
        rank.T.reshape(shard_count, expert_count, tok), "wt", 0, 0, tiled=True
    )
    last = shard_count - 1
    out_line = to_line(out_low)
    grads_in = {0: out_line, last: shift(after(out_line, pieces[0]), -1)}

    pieces, ranks = beside(pieces, ranks)
    local_rows = jnp.arange(tok, dtype=jnp.int32)
    mine = lax.dynamic_slice_in_dim(deal_row, 2 * ctx_index, 2, 0)
    prompt_place = (
        jnp.where(local_rows < block_rows, mine[0], mine[1]) * block_rows
        + local_rows % block_rows
    )
    positions = jnp.where(
        local_rows < prompt_local, prompt_place, PROMPT + (local_rows - prompt_local) % CLEN
    )
    cosine, sine = rope_tables(positions, 128)
    normed_one, turned_query, kv_low, qkv_full, output_t, rest, gain_rows = project(
        layer_input[0], cosine, sine, pieces, counts, block_places
    )
    router_full = rest[:, :EXPERTS]
    first_gain, second_gain = gain_rows[0], gain_rows[1]
    inverse_one = lax.rsqrt(jnp.mean(inputs * inputs, -1, keepdims=True) + norm_eps)
    kv_own = kv_low[prompt_local:]
    kv_pieces, grads_in[last] = beside([gather_ctx(kv_low, prompt_local)], grads_in[last])

    places = deal_row
    if context_size == 8:
        pairs = deal_row.reshape(2, 2, 2, 2)
        for axis, bit in ((0, 4), (1, 2), (2, 1)):
            pairs = jnp.where(ctx_index & bit > 0, jnp.flip(pairs, axis), pairs)
        places = pairs.reshape(-1)
    low = (mine[0] > mine[1]).astype(jnp.int32)
    starts = jnp.stack(
        [
            low * block_rows,
            (1 - low) * block_rows,
            jnp.min(mine) * block_rows,
            jnp.max(mine) * block_rows,
        ]
    ).astype(jnp.int32)
    heads = []
    for half in range(2):
        result = attention_forward(
            turned_query, kv_pieces, kv_own, places, starts, block_rows, half
        )
        d = last - 1 - half
        grads_in[d] = shift(grads_in[d + 1], -1)
        result, grads_in[d] = beside(result, grads_in[d])
        if context_size == 8:
            for weights in expert_weights[half : 2 * half + 1]:
                result, sibling = beside(
                    result, swap(after(weights[0], turned_query, *kv_pieces), 1)
                )
                weights.append(sibling)
        if half == 0:
            turned_query = after(turned_query, result[0])
        heads.append(result)
    for d in range(last - 3, 0, -1):
        grads_in[d] = shift(grads_in[d + 1], -1)
    attended = jnp.concatenate([out for out, _ in heads], 1)
    lse = [row for _, row in heads]

    branch = dot_nt(attended, output_t)
    middle = inputs + resid_scale * branch
    normed_mid, inverse_two = norm_forward(middle, second_gain)
    normed_two = normed_mid.astype(bf16)
    logits = dot(normed_two, router_full)
    top = jnp.max(jnp.where(mask, logits, masked_score), -1, keepdims=True)
    raised = jnp.where(mask, jnp.exp(jnp.where(mask, logits - top, 0.0)), 0.0)
    gates = raised / jnp.sum(raised, -1, keepdims=True)

    gates_out = gates.T.reshape(shard_count, expert_count, tok)
    gates_in = []
    for d in range(shard_count):
        piece = lax.dynamic_index_in_dim(gates_out, (wt_index + d) % shard_count, 0, False)
        gates_in.append(shift(piece, d) if d else piece)
    got = {0: to_line(normed_two)}
    partial, mixed, gate_grads, rows = {}, {}, {}, []
    carried = None

    def add(a, b):
        return b if a is None else (a.astype(f32) + b.astype(f32)).astype(bf16)

    for d in [0] + list(range(last, 0, -1)):
        source = (wt_index - d) % shard_count
        rank_in = lax.dynamic_index_in_dim(ranks, source, 0, False)
        result = expert_pass(
            got[d], grads_in[d], rank_in, gates_in[d], *expert_weights, capacity
        )
        coming = d - 1 if d else last
        if coming:
            result, got[coming] = beside(result, shift(got[(coming + 1) % shard_count], -1))
        if d == 0:
            result, gates_in = beside(result, gates_in)
        if 0 < d <= last - 2:
            carried = shift(after(add(carried, partial[d + 2]), got[d]), -1)
            result, carried = beside(result, carried)
        mixed[d], partial[d], d_gate, *kept = result
        rows.append(kept)
        d_gate = d_gate.reshape(expert_count, tok)
        gate_grads[d] = shift(d_gate, shard_count - d) if d else d_gate
        if coming:
            got[coming] = after(got[coming], partial[d])
    carried = shift(add(carried, partial[2]), -1)
    (gate_grad, up_grad), carried = beside(
        up_weight_grads([(after(r[0], partial[1]), r[3], r[4]) for r in rows], width_order),
        carried,
    )
    carried = shift(add(carried, partial[1]), -1)
    down_grad, home = beside(
        down_weight_grads([(after(r[2], gate_grad), r[1]) for r in rows], width_order), carried
    )

    stacked = jnp.stack([gate_grads[d] for d in range(shard_count)], 0)
    stacked = jnp.roll(stacked, wt_index, 0).reshape(EXPERTS, tok).T
    grad_logits = (gates * (stacked - jnp.sum(gates * stacked, -1, keepdims=True))).astype(bf16)
    grad_normed_two = from_line(partial[0].astype(f32) + home.astype(f32))
    grad_normed_two = grad_normed_two + dot_nt(grad_logits, router_full)
    grad_mid_norm, second_gain_grad = norm_backward(
        middle, inverse_two, second_gain, grad_normed_two
    )
    grad_middle = out_grad + grad_mid_norm
    grad_branch = (resid_scale * grad_middle).astype(bf16)
    grad_attended = dot(grad_branch, output_t).astype(bf16)
    gate_share, up_share, down_share = (
        lax.psum_scatter(grad, "ctx", scatter_dimension=0, tiled=False).astype(f32)
        for grad in (gate_grad, up_grad, down_grad)
    )
    devices = context_size * shard_count
    small = jnp.concatenate(
        [
            dot_tn(normed_two, grad_logits).reshape(devices, own_rows * EXPERTS),
            second_gain_grad.reshape(devices, own_rows),
        ],
        1,
    )

    carried = shift(after(mixed[last], home), -1)
    query, carried = beside(after(turned_query, grad_attended), carried)
    d_query, owned, ours = [], [], []
    for half in range(2):
        result = attention_backward(
            query,
            grad_attended,
            lse[half],
            attended,
            cosine,
            sine,
            kv_pieces,
            kv_own,
            places,
            starts,
            block_rows,
            half,
        )
        carried = shift(add(carried, mixed[last - 1 - half]), -1)
        result, carried = beside(result, carried)
        d_q, d_kv, d_key_own, d_value_own = result
        query = after(query, d_q)
        if half == 0:
            small = spread_sum(after(small, d_q))
        d_query.append(d_q)
        owned.append(scatter_ctx(d_kv))
        ours.append((d_key_own, d_value_own))
    for d in range(last - 3, 0, -1):
        carried = shift(add(carried, mixed[d]), -1)
    mixture = from_line(mixed[0].astype(f32) + carried.astype(f32))
    layer_output = (middle + resid_scale * mixture).astype(bf16)
    d_query = jnp.concatenate(d_query, 1)
    query_part = outer_part((normed_one, d_query), (after(grad_branch, d_query), attended))
    d_key, d_value = (
        jnp.concatenate(
            [
                jnp.concatenate([owned[half][:, 256 * n : 256 * n + 256], ours[half][n]], 0)
                for half in range(2)
            ],
            1,
        )
        for n in range(2)
    )
    grad_key_low = turn(d_key, jnp.tile(cosine, (1, 4)), jnp.tile(sine, (1, 4)), -1.0).astype(
        bf16
    )
    grad_kv = jnp.concatenate([grad_key_low, d_value.astype(bf16)], 1)
    grad_kv, query_part = beside(grad_kv, query_part)
    kv_share = row_sum(outer_part((normed_one, grad_kv)))
    query_share, output_share = jnp.split(row_sum(query_part), 2, 1)
    grad_normed_one = dot_nt(d_query, qkv_full[:, :1024]) + dot_nt(grad_kv, qkv_full[:, 1024:])
    grad_input_norm, first_gain_grad = norm_backward(
        inputs, inverse_one, first_gain, grad_normed_one
    )
    input_grad = (grad_middle + grad_input_norm).astype(bf16)

    first_gain_share = spread_sum(first_gain_grad.reshape(devices, own_rows))
    return (
        layer_output[None],
        input_grad[None],
        first_gain_share,
        query_share,
        kv_share[:, :KV_WIDTH],
        kv_share[:, KV_WIDTH:],
        output_share.T,
        small[own_rows * EXPERTS :],
        small[: own_rows * EXPERTS].reshape(own_rows, EXPERTS),
        gate_share,
        up_share,
        down_share,
    )


def solution(mesh):
    return jax.shard_map(
        per_device,
        mesh=mesh,
        in_specs=(
            P("wt", "ctx", None),
            P(("ctx", "wt")),
            P(("ctx", "wt"), None),
            P(("ctx", "wt"), None),
            P(("ctx", "wt"), None),
            P(None, ("ctx", "wt")),
            P(("ctx", "wt")),
            P(("ctx", "wt"), None),
            P("wt", "ctx", None),
            P("wt", "ctx", None),
            P("wt", None, "ctx"),
            P("wt", "ctx", None),
            P("wt", None),
            P("wt", "ctx", None),
        ),
        out_specs=(
            P("wt", "ctx", None),
            P("wt", "ctx", None),
            P(("ctx", "wt")),
            P(("ctx", "wt"), None),
            P(("ctx", "wt"), None),
            P(("ctx", "wt"), None),
            P(None, ("ctx", "wt")),
            P(("ctx", "wt")),
            P(("ctx", "wt"), None),
            P("wt", "ctx", None),
            P("wt", "ctx", None),
            P("wt", None, "ctx"),
        ),
        check_vma=False,
    )
```

```python
import functools

import jax
import jax.numpy as jnp
from jax import lax
from jax.experimental import pallas as pl
from jax.experimental.pallas import tpu as pltpu
from jax.sharding import PartitionSpec as P

MODEL_WIDTH = 1024
HQ = 16
KEY_VALUE_HEADS = 8
HEAD_SIZE = 64
EXPERTS = 32
TOP = 8
PROMPT = 2048
CLEN = 256
CONT_DEV = 2
FF = 512
QTILE = 128
KV_WIDTH = KEY_VALUE_HEADS * HEAD_SIZE
ALL = ("ctx", "wt")

att_scale = 0.015625
resid_scale = 0.22
norm_eps = 1e-06
rope_base = 10000.0
masked_score = -1e30

bf16 = jnp.bfloat16
f32 = jnp.float32
VMEM_LIMIT = 60 * 1024 * 1024
SMALL = pl.CostEstimate(flops=1_000_000_000, bytes_accessed=1_000_000, transcendentals=0)

NT = (((1,), (1,)), ((), ()))
TN = (((0,), (0,)), ((), ()))


def dot(a, b):
    return jnp.dot(a, b, preferred_element_type=f32)


def dot_nt(a, b):
    return lax.dot_general(a, b, NT, preferred_element_type=f32)


def dot_tn(a, b):
    return lax.dot_general(a, b, TN, preferred_element_type=f32)


def turn_tile(values, cosine, sine, direction):
    middle = HEAD_SIZE // 2
    first = lax.broadcasted_iota(jnp.int32, values.shape, 1) % HEAD_SIZE < middle
    turned = jnp.where(first, -pltpu.roll(values, 128 - middle, 1), pltpu.roll(values, middle, 1))
    return values * cosine + direction * turned * sine


def project_kernel(places, x_ref, cos_ref, sin_ref, *refs, counts):
    pieces = refs[: len(counts)]
    normed_ref, q_ref, kv_ref, qkv_ref, out_ref, rest_ref, gains_ref = refs[len(counts) :]
    rows = MODEL_WIDTH // sum(counts)
    at = 0
    for piece, count in zip(pieces, counts):
        for i in range(count):
            source = slice(i * rows, (i + 1) * rows)
            target = pl.ds(pl.multiple_of(places[at] * rows, rows), rows)
            qkv_ref[target, :] = piece[source, :2048]
            out_ref[target, :] = piece[source, 2048:3072]
            rest_ref[target, :] = piece[source, 3072:]
            at += 1
    gains = rest_ref[...].astype(f32).T[EXPERTS : EXPERTS + 8]
    gains_ref[...] = gains
    x = x_ref[...].astype(f32)
    inverse = lax.rsqrt(jnp.mean(x * x, -1, keepdims=True) + norm_eps)
    normed_ref[...] = (x * inverse * gains[:1]).astype(bf16)
    for c in range(8):
        raw = dot(normed_ref[...], qkv_ref[:, 256 * c : 256 * (c + 1)])
        for h in range(2):
            part = raw[:, 128 * h : 128 * (h + 1)]
            if c < 6:
                part = turn_tile(part, cos_ref[...], sin_ref[...], 1.0)
            column = 256 * c + 128 * h
            if column < 1024:
                q_ref[:, column : column + 128] = part.astype(bf16)
            else:
                column -= 1024
                at = column % KV_WIDTH // 256 * 512 + column // KV_WIDTH * 256 + column % 256
                kv_ref[:, at : at + 128] = part.astype(bf16)


def project(x, cosine, sine, pieces, counts, places):
    tok = x.shape[0]
    shape = jax.ShapeDtypeStruct
    whole = pl.BlockSpec(memory_space=pltpu.VMEM)
    return pl.pallas_call(
        functools.partial(project_kernel, counts=counts),
        in_specs=[pl.BlockSpec(memory_space=pltpu.SMEM)] + [whole] * (3 + len(pieces)),
        out_specs=[whole] * 7,
        out_shape=[
            shape((tok, MODEL_WIDTH), bf16),
            shape((tok, HQ * HEAD_SIZE), bf16),
            shape((tok, 2 * KV_WIDTH), bf16),
            shape((MODEL_WIDTH, 2048), bf16),
            shape((MODEL_WIDTH, 1024), bf16),
            shape((MODEL_WIDTH, 128), bf16),
            shape((8, MODEL_WIDTH), f32),
        ],
        compiler_params=pltpu.CompilerParams(vmem_limit_bytes=VMEM_LIMIT),
        cost_estimate=SMALL,
        name="project",
    )(places, x, cosine, sine, *pieces)


def outer_kernel(mine, *refs, count):
    out_ref = refs[-1]
    pairs = [(refs[n], refs[n + 1]) for n in range(0, len(refs) - 1, 2)]
    at = 0
    for a_ref, b_ref in pairs[:count]:
        columns = b_ref.shape[1]
        out_ref[:, at : at + columns] = dot_tn(a_ref[...], b_ref[...]).astype(bf16)
        at += columns
    out_ref[:, at:] = sum(dot_tn(a[...], b[...]) for a, b in pairs[count:]).astype(bf16)


def outer(pairs, extra):
    tok = pairs[0][0].shape[0]
    mine = lax.axis_index("ctx").astype(jnp.int32).reshape(1)
    specs = []
    for _, b in pairs + extra:
        specs.append(pl.BlockSpec((tok, 128), lambda m, mine: (0, m ^ mine[0])))
        specs.append(pl.BlockSpec(b.shape, lambda m, mine: (0, 0)))
    columns = sum(b.shape[1] for _, b in pairs) + extra[0][1].shape[1]
    return pl.pallas_call(
        functools.partial(outer_kernel, count=len(pairs)),
        grid_spec=pltpu.PrefetchScalarGridSpec(
            num_scalar_prefetch=1,
            grid=(8,),
            in_specs=specs,
            out_specs=pl.BlockSpec((128, columns), lambda m, mine: (m, 0)),
        ),
        out_shape=jax.ShapeDtypeStruct((MODEL_WIDTH, columns), bf16),
        compiler_params=pltpu.CompilerParams(vmem_limit_bytes=VMEM_LIMIT),
        cost_estimate=SMALL,
        name="outer",
    )(mine, *[x for pair in pairs + extra for x in pair])


def gather_keys(pieces, scratch, places, block_rows):
    at = 0
    for piece in pieces:
        for b in range(piece.shape[0] // block_rows):
            start = pl.multiple_of(places[at] * block_rows, block_rows)
            scratch[pl.ds(start, block_rows), :] = piece[b * block_rows : (b + 1) * block_rows, :]
            at += 1


def pair_rows(ref, start, rows, j):
    both = ref[pl.ds(start, rows), 2 * HEAD_SIZE * j : 2 * HEAD_SIZE * (j + 1)]
    return jnp.concatenate([both[:, :HEAD_SIZE], both[:, HEAD_SIZE:]], 0)


def attention_forward_kernel(places, starts, q_ref, *refs, block_rows, pieces):
    k_refs, v_refs = refs[:pieces], refs[pieces : 2 * pieces]
    kc_ref, vc_ref, o_ref, lse_ref, k_scr, v_scr = refs[2 * pieces :]
    prompt_local = 2 * block_rows
    gather_keys(k_refs, k_scr, places, block_rows)
    gather_keys(v_refs, v_scr, places, block_rows)

    def store(start, rows, j, out, m, total, at):
        out = (out / total).astype(bf16)
        lse = m + jnp.log(total)
        o_ref[pl.ds(start, rows), 2 * HEAD_SIZE * j : 2 * HEAD_SIZE * (j + 1)] = jnp.concatenate(
            [out[:rows], out[rows:]], 1
        )
        row = jnp.broadcast_to(lse, (2 * rows, 128)).T[:1]
        lse_ref[0, 2 * j : 2 * j + 2, pl.ds(at, rows)] = jnp.concatenate(
            [row[:, :rows], row[:, rows:]], 0
        )

    def tile(i, _):
        start = pl.multiple_of(prompt_local + i * QTILE, 64)
        per = CLEN // QTILE
        seg = pl.multiple_of((i // per) * CLEN, CLEN)
        for j in range(2):
            lanes = slice(HEAD_SIZE * j, HEAD_SIZE * (j + 1))
            q = pair_rows(q_ref, start, QTILE, j) * bf16(att_scale)
            s1 = dot_nt(q, k_scr[:, lanes])
            s2 = dot_nt(q, kc_ref[pl.ds(seg, CLEN), lanes])
            place = lax.broadcasted_iota(jnp.int32, s2.shape, 0) % QTILE + (i % per) * QTILE
            s2 = jnp.where(lax.broadcasted_iota(jnp.int32, s2.shape, 1) <= place, s2, masked_score)
            m = jnp.maximum(jnp.max(s1, 1, keepdims=True), jnp.max(s2, 1, keepdims=True))
            e1 = jnp.exp(s1 - m)
            e2 = jnp.exp(s2 - m)
            total = jnp.sum(e1, 1, keepdims=True) + jnp.sum(e2, 1, keepdims=True)
            out = dot(e1.astype(bf16), v_scr[:, lanes])
            out = out + dot(e2.astype(bf16), vc_ref[pl.ds(seg, CLEN), lanes])
            store(start, QTILE, j, out, m, total, pl.multiple_of(i * QTILE, QTILE))
        return 0

    lax.fori_loop(0, CONT_DEV * CLEN // QTILE, tile, 0)

    for half, keys in enumerate((PROMPT // 2, PROMPT)):
        start = pl.multiple_of(starts[half], block_rows)
        for j in range(2):
            lanes = slice(HEAD_SIZE * j, HEAD_SIZE * (j + 1))
            q = pair_rows(q_ref, start, block_rows, j) * bf16(att_scale)
            s = dot_nt(q, k_scr[:keys, lanes])
            place = lax.broadcasted_iota(jnp.int32, s.shape, 0) % block_rows + starts[2 + half]
            s = jnp.where(lax.broadcasted_iota(jnp.int32, s.shape, 1) <= place, s, masked_score)
            m = jnp.max(s, 1, keepdims=True)
            e = jnp.exp(s - m)
            total = jnp.sum(e, 1, keepdims=True)
            out = dot(e.astype(bf16), v_scr[:keys, lanes])
            store(start, block_rows, j, out, m, total, CONT_DEV * CLEN + half * block_rows)


def key_specs(pieces, own, half):
    spec = pl.BlockSpec
    key, value = (lambda g, *_: (0, 4 * half + g)), (lambda g, *_: (0, 4 * half + 2 + g))
    keys = [spec((p.shape[0], 128), key) for p in pieces]
    values = [spec((p.shape[0], 128), value) for p in pieces]
    return keys + values + [spec((own, 128), key), spec((own, 128), value)]


def attention_forward(q, pieces, kv_own, places, starts, block_rows, half):
    tok = q.shape[0]
    spec = pl.BlockSpec
    return pl.pallas_call(
        functools.partial(
            attention_forward_kernel, block_rows=block_rows, pieces=len(pieces)
        ),
        grid_spec=pltpu.PrefetchScalarGridSpec(
            num_scalar_prefetch=2,
            grid=(2,),
            in_specs=[spec((tok, 256), lambda g, *_: (0, 2 * half + g))]
            + key_specs(pieces, kv_own.shape[0], half),
            out_specs=[
                spec((tok, 256), lambda g, *_: (0, g)),
                spec((1, 4, tok), lambda g, *_: (g, 0, 0)),
            ],
            scratch_shapes=[
                pltpu.VMEM((PROMPT, 2 * HEAD_SIZE), bf16),
                pltpu.VMEM((PROMPT, 2 * HEAD_SIZE), bf16),
            ],
        ),
        out_shape=[
            jax.ShapeDtypeStruct((tok, HQ * HEAD_SIZE // 2), bf16),
            jax.ShapeDtypeStruct((2, 4, tok), f32),
        ],
        compiler_params=pltpu.CompilerParams(vmem_limit_bytes=VMEM_LIMIT),
        cost_estimate=SMALL,
        name="attention_forward",
    )(places, starts, q, *pieces, *pieces, kv_own, kv_own)


def attention_backward_kernel(
    places, starts, q_ref, do_ref, lse_ref, o_ref, cos_ref, sin_ref, *refs, block_rows, pieces
):
    k_refs, v_refs = refs[:pieces], refs[pieces : 2 * pieces]
    kc_ref, vc_ref, dq_ref, dkv_ref, dkc_ref, dvc_ref = refs[2 * pieces : 2 * pieces + 6]
    k_scr, v_scr, dk_acc, dv_acc, dq_acc = refs[2 * pieces + 6 :]
    prompt_local = 2 * block_rows
    gather_keys(k_refs, k_scr, places, block_rows)
    gather_keys(v_refs, v_scr, places, block_rows)
    dk_acc[...] = jnp.zeros_like(dk_acc)
    dv_acc[...] = jnp.zeros_like(dv_acc)
    dkc_ref[...] = jnp.zeros_like(dkc_ref)
    dvc_ref[...] = jnp.zeros_like(dvc_ref)

    def row_pair(ref, start, rows, j):
        both = ref[0, 2 * j : 2 * j + 2, pl.ds(start, rows)]
        return jnp.concatenate([both[:1], both[1:]], 1)

    def centre(start, rows, j, d_out):
        product = d_out.astype(f32) * pair_rows(o_ref, start, rows, j).astype(f32)
        ones = jnp.ones((8, HEAD_SIZE), f32)
        return lax.dot_general(
            ones, product, NT, precision=lax.Precision.HIGHEST, preferred_element_type=f32
        )[:1]

    def part(k, v, q, d_out, lse, delta, allowed):
        s = dot_nt(k, q)
        if allowed is not None:
            s = jnp.where(allowed(s.shape), s, masked_score)
        p = jnp.exp(s - lse)
        d_p = dot_nt(v, d_out)
        d_s = (p * (d_p - delta)).astype(bf16)
        return dot_tn(d_s, k), dot(d_s, q), dot(p.astype(bf16), d_out)

    def store(start, rows, j, d_q):
        d_q = d_q * att_scale
        dq_acc[pl.ds(start, rows), 2 * HEAD_SIZE * j : 2 * HEAD_SIZE * (j + 1)] = jnp.concatenate(
            [d_q[:rows], d_q[rows:]], 1
        )

    def tile(i, _):
        start = pl.multiple_of(prompt_local + i * QTILE, 64)
        per = CLEN // QTILE
        seg = pl.multiple_of((i // per) * CLEN, CLEN)
        own = pl.ds(seg, CLEN)
        lane_start = pl.multiple_of(i * QTILE, QTILE)

        def allowed(shape):
            place = lax.broadcasted_iota(jnp.int32, shape, 1) % QTILE + (i % per) * QTILE
            return lax.broadcasted_iota(jnp.int32, shape, 0) <= place

        for j in range(2):
            lanes = slice(HEAD_SIZE * j, HEAD_SIZE * (j + 1))
            q = pair_rows(q_ref, start, QTILE, j) * bf16(att_scale)
            d_out = pair_rows(do_ref, start, QTILE, j)
            lse = row_pair(lse_ref, lane_start, QTILE, j)
            delta = centre(start, QTILE, j, d_out)
            a, b, c = part(k_scr[:, lanes], v_scr[:, lanes], q, d_out, lse, delta, None)
            dk_acc[:, lanes] += b
            dv_acc[:, lanes] += c
            d_q = a
            a, b, c = part(
                kc_ref[own, lanes], vc_ref[own, lanes], q, d_out, lse, delta, allowed
            )
            dkc_ref[own, lanes] += b
            dvc_ref[own, lanes] += c
            store(start, QTILE, j, d_q + a)
        return 0

    lax.fori_loop(0, CONT_DEV * CLEN // QTILE, tile, 0)

    for half, keys in enumerate((PROMPT // 2, PROMPT)):
        start = pl.multiple_of(starts[half], block_rows)
        at = CONT_DEV * CLEN + half * block_rows

        def allowed(shape):
            place = lax.broadcasted_iota(jnp.int32, shape, 1) % block_rows + starts[2 + half]
            return lax.broadcasted_iota(jnp.int32, shape, 0) <= place

        for j in range(2):
            lanes = slice(HEAD_SIZE * j, HEAD_SIZE * (j + 1))
            q = pair_rows(q_ref, start, block_rows, j) * bf16(att_scale)
            d_out = pair_rows(do_ref, start, block_rows, j)
            lse = row_pair(lse_ref, at, block_rows, j)
            delta = centre(start, block_rows, j, d_out)
            a, b, c = part(
                k_scr[:keys, lanes], v_scr[:keys, lanes], q, d_out, lse, delta, allowed
            )
            dk_acc[:keys, lanes] += b
            dv_acc[:keys, lanes] += c
            store(start, block_rows, j, a)

    g = pl.program_id(0)
    key_lanes = pl.ds(pl.multiple_of(g * 128, 128), 128)
    value_lanes = pl.ds(pl.multiple_of(256 + g * 128, 128), 128)
    for b in range(PROMPT // block_rows):
        source = pl.ds(pl.multiple_of(places[b] * block_rows, block_rows), block_rows)
        rows = slice(b * block_rows, (b + 1) * block_rows)
        dkv_ref[rows, key_lanes] = dk_acc[source, :].astype(bf16)
        dkv_ref[rows, value_lanes] = dv_acc[source, :].astype(bf16)
    for c in range(2):
        lanes = slice(128 * c, 128 * (c + 1))
        dq_ref[:, lanes] = turn_tile(dq_acc[:, lanes], cos_ref[...], sin_ref[...], -1.0).astype(
            bf16
        )


def attention_backward(
    q, d_out, lse, attended, cosine, sine, pieces, kv_own, places, starts, block_rows, half
):
    tok = q.shape[0]
    own = kv_own.shape[0]
    spec = pl.BlockSpec
    wide = spec((tok, 256), lambda g, *_: (0, 2 * half + g))
    ours = spec((own, 128), lambda g, *_: (0, g))
    table = spec((tok, 128), lambda g, *_: (0, 0))
    return pl.pallas_call(
        functools.partial(
            attention_backward_kernel, block_rows=block_rows, pieces=len(pieces)
        ),
        grid_spec=pltpu.PrefetchScalarGridSpec(
            num_scalar_prefetch=2,
            grid=(2,),
            in_specs=[wide, wide, spec((1, 4, tok), lambda g, *_: (g, 0, 0)), wide, table, table]
            + key_specs(pieces, own, half),
            out_specs=[
                spec((tok, 256), lambda g, *_: (0, g)),
                spec((PROMPT, KV_WIDTH), lambda g, *_: (0, 0)),
                ours,
                ours,
            ],
            scratch_shapes=[
                pltpu.VMEM((PROMPT, 2 * HEAD_SIZE), bf16),
                pltpu.VMEM((PROMPT, 2 * HEAD_SIZE), bf16),
                pltpu.VMEM((PROMPT, 2 * HEAD_SIZE), f32),
                pltpu.VMEM((PROMPT, 2 * HEAD_SIZE), f32),
                pltpu.VMEM((tok, 4 * HEAD_SIZE), f32),
            ],
        ),
        out_shape=[
            jax.ShapeDtypeStruct((tok, HQ * HEAD_SIZE // 2), bf16),
            jax.ShapeDtypeStruct((PROMPT, KV_WIDTH), bf16),
            jax.ShapeDtypeStruct((own, KV_WIDTH // 2), f32),
            jax.ShapeDtypeStruct((own, KV_WIDTH // 2), f32),
        ],
        compiler_params=pltpu.CompilerParams(vmem_limit_bytes=VMEM_LIMIT),
        cost_estimate=SMALL,
        name="attention_backward",
    )(places, starts, q, d_out, lse, attended, cosine, sine, *pieces, *pieces, kv_own, kv_own)


def expert_kernel(
    counts,
    a2_ref,
    df_ref,
    rank_ref,
    gate_ref,
    wg_ref,
    wu_ref,
    wd_ref,
    mix_ref,
    da_ref,
    dg_ref,
    x_ref,
    dy_ref,
    z_ref,
    dgate_ref,
    dup_ref,
    mix_acc,
    da_acc,
    *,
    sizes,
):
    e = pl.program_id(0)

    @pl.when(e == 0)
    def _():
        mix_acc[...] = jnp.zeros_like(mix_acc)
        da_acc[...] = jnp.zeros_like(da_acc)

    def body(size):
        rank = rank_ref[0]
        gates = gate_ref[0]
        tok = rank.shape[1]
        slot = lax.broadcasted_iota(jnp.int32, (size, tok), 0).astype(f32)
        hit = slot == rank
        chosen = hit.astype(f32).astype(bf16)
        gate = jnp.sum(jnp.where(hit, gates, 0.0), 1, keepdims=True)
        x = dot(chosen, a2_ref[...]).astype(bf16)
        d_mix = resid_scale * dot(chosen, df_ref[...])
        wg = wg_ref[:, 0].reshape(MODEL_WIDTH, FF)
        wu = wu_ref[:, 0].reshape(MODEL_WIDTH, FF)
        wd = jnp.concatenate([wd_ref[c, 0] for c in range(wd_ref.shape[0])], 1)
        g = dot(x, wg)
        u = dot(x, wu)
        sig = jax.nn.sigmoid(g)
        z = (g * sig * u).astype(bf16)
        y = dot(z, wd).astype(bf16).astype(f32)
        d_gate_value = jnp.sum(d_mix * y, 1, keepdims=True)
        dg_ref[0] = jnp.sum(jnp.where(hit, d_gate_value, 0.0), 0, keepdims=True)
        mix_acc[...] += dot_tn(chosen, (gate * y).astype(bf16))
        d_y = (gate * d_mix).astype(bf16)
        d_z = dot_nt(d_y, wd)
        d_g = (d_z * u * sig * (1.0 + g * (1.0 - sig))).astype(bf16)
        d_u = (d_z * g * sig).astype(bf16)
        d_r = (dot_nt(d_g, wg) + dot_nt(d_u, wu)).astype(bf16)
        da_acc[...] += dot_tn(chosen, d_r)
        for ref, value in (
            (x_ref, x),
            (dy_ref, d_y),
            (z_ref, z),
            (dgate_ref, d_g),
            (dup_ref, d_u),
        ):
            ref[0, :size] = value
            if size < ref.shape[1]:
                ref[0, size:] = jnp.zeros((ref.shape[1] - size, ref.shape[2]), bf16)

    least = -1
    for size in sizes:
        pl.when((counts[e] > least) & (counts[e] <= size))(functools.partial(body, size))
        least = size

    @pl.when(e == pl.num_programs(0) - 1)
    def _():
        mix_ref[...] = mix_acc[...].astype(bf16)
        da_ref[...] = da_acc[...].astype(bf16)


def expert_pass(a2, df, rank, gates, wg, wu, wd, capacity):
    tok = a2.shape[0]
    parts, experts = wg.shape[0], wg.shape[1]
    sizes = sorted({min(size, capacity) for size in (128, 192, 256, capacity)})
    counts = (jnp.max(rank, 1) + 1.0).astype(jnp.int32)
    spec = pl.BlockSpec
    whole = spec((tok, MODEL_WIDTH), lambda e, *_: (0, 0))
    row = spec((1, 1, tok), lambda e, *_: (e, 0, 0))
    up = spec((parts, 1, MODEL_WIDTH // parts, FF), lambda e, *_: (0, e, 0, 0))
    down = spec((parts, 1, FF, MODEL_WIDTH // parts), lambda e, *_: (0, e, 0, 0))
    rows_wide = spec((1, capacity, MODEL_WIDTH), lambda e, *_: (e, 0, 0))
    rows_thin = spec((1, capacity, FF), lambda e, *_: (e, 0, 0))
    shape = jax.ShapeDtypeStruct
    return pl.pallas_call(
        functools.partial(expert_kernel, sizes=sizes),
        grid_spec=pltpu.PrefetchScalarGridSpec(
            num_scalar_prefetch=1,
            grid=(experts,),
            in_specs=[whole, whole, row, row, up, up, down],
            out_specs=[whole, whole, row, rows_wide, rows_wide, rows_thin, rows_thin, rows_thin],
            scratch_shapes=[
                pltpu.VMEM((tok, MODEL_WIDTH), f32),
                pltpu.VMEM((tok, MODEL_WIDTH), f32),
            ],
        ),
        out_shape=[
            shape((tok, MODEL_WIDTH), bf16),
            shape((tok, MODEL_WIDTH), bf16),
            shape((experts, 1, tok), f32),
            shape((experts, capacity, MODEL_WIDTH), bf16),
            shape((experts, capacity, MODEL_WIDTH), bf16),
            shape((experts, capacity, FF), bf16),
            shape((experts, capacity, FF), bf16),
            shape((experts, capacity, FF), bf16),
        ],
        compiler_params=pltpu.CompilerParams(vmem_limit_bytes=VMEM_LIMIT),
        cost_estimate=SMALL,
        name="expert_pass",
    )(counts, a2, df, rank.reshape(experts, 1, tok), gates.reshape(experts, 1, tok), wg, wu, wd)


def up_grad_kernel(*refs, sources):
    rows = refs[: 3 * sources]
    gate_ref, up_ref = refs[3 * sources :]
    for n, out_ref in ((1, gate_ref), (2, up_ref)):
        total = None
        for s in range(sources):
            term = dot_tn(rows[3 * s][0], rows[3 * s + n][0])
            total = term if total is None else total + term
        out_ref[...] = total.astype(bf16).reshape(out_ref.shape)


def down_grad_kernel(*refs, sources, parts):
    rows, down_ref = refs[: 2 * sources], refs[-1]
    width = MODEL_WIDTH // parts
    total = None
    for s in range(sources):
        term = dot_tn(rows[2 * s][0], rows[2 * s + 1][0])
        total = term if total is None else total + term
    total = total.astype(bf16)
    for c in range(parts):
        down_ref[c, 0] = total[:, c * width : (c + 1) * width]


def row_specs(rows):
    return [pl.BlockSpec((1,) + a.shape[1:], lambda e: (e, 0, 0)) for r in rows for a in r]


def up_weight_grads(rows, parts):
    experts = rows[0][0].shape[0]
    shape = (parts, experts, MODEL_WIDTH // parts, FF)
    out = pl.BlockSpec((parts, 1) + shape[2:], lambda e: (0, e, 0, 0))
    return pl.pallas_call(
        functools.partial(up_grad_kernel, sources=len(rows)),
        grid=(experts,),
        in_specs=row_specs(rows),
        out_specs=[out, out],
        out_shape=[jax.ShapeDtypeStruct(shape, bf16)] * 2,
        compiler_params=pltpu.CompilerParams(vmem_limit_bytes=VMEM_LIMIT),
        cost_estimate=SMALL,
        name="up_weight_grads",
    )(*[a for r in rows for a in r])


def down_weight_grads(rows, parts):
    experts = rows[0][0].shape[0]
    shape = (parts, experts, FF, MODEL_WIDTH // parts)
    return pl.pallas_call(
        functools.partial(down_grad_kernel, sources=len(rows), parts=parts),
        grid=(experts,),
        in_specs=row_specs(rows),
        out_specs=pl.BlockSpec((parts, 1) + shape[2:], lambda e: (0, e, 0, 0)),
        out_shape=jax.ShapeDtypeStruct(shape, bf16),
        compiler_params=pltpu.CompilerParams(vmem_limit_bytes=VMEM_LIMIT),
        cost_estimate=SMALL,
        name="down_weight_grads",
    )(*[a for r in rows for a in r])


def swap(x, mask):
    return lax.ppermute(x, "ctx", [(i, i ^ mask) for i in range(lax.axis_size("ctx"))])


def gather_ctx(x, rows):
    if lax.axis_size("ctx") != 8:
        return lax.all_gather(x[:rows], "ctx", axis=0, tiled=True)
    return plane_gather(x, rows)


MESH = pl.DeviceIdType.MESH
ANY = pl.BlockSpec(memory_space=pl.ANY)


def partner(mask):
    me = lax.axis_index("ctx")
    return me + mask - 2 * mask * ((me // mask) % 2)


def ahead(distance):
    return (lax.axis_index("wt") + distance) % lax.axis_size("wt")


class Copies:
    def __init__(self, send, recv):
        self.send, self.recv, self.made = send, recv, {}

    def start(self, name, source, target, device):
        n = len(self.made)
        self.made[name] = copy = pltpu.make_async_remote_copy(
            src_ref=source,
            dst_ref=target,
            send_sem=self.send.at[n],
            recv_sem=self.recv.at[n],
            device_id=device,
            device_id_type=MESH,
        )
        copy.start()

    def arrived(self, name):
        self.made[name].wait_recv()

    def close(self):
        for copy in self.made.values():
            copy.wait_send()


def greet(devices):
    barrier = pltpu.get_barrier_semaphore()
    for device in devices:
        pl.semaphore_signal(barrier, inc=1, device_id=device, device_id_type=MESH)
    pl.semaphore_wait(barrier, len(devices))


def plane_steps(copies, block, half, key):
    side, near, far = ({"ctx": partner(m)} for m in (1, 2, 4))
    top, end = (lambda m: block(m, 0, half)), (lambda m: block(m, half, half))

    def first():
        copies.start((key, 2), block(0), block(2), near)
        copies.start((key, 4), block(0), block(4), far)
        copies.start((key, 1), block(0), block(1), side)

    def second():
        copies.arrived((key, 2))
        copies.start((key, 6), top(2), top(6), far)
        copies.start((key, 3), block(2), block(3), side)

    def third():
        copies.arrived((key, 4))
        copies.start((key, 7), end(4), end(6), near)
        copies.start((key, 5), block(4), block(5), side)

    def fourth():
        copies.arrived((key, 6))
        copies.arrived((key, 7))
        copies.start((key, 8), block(6), block(7), side)

    def last():
        for m in (1, 3, 5, 8):
            copies.arrived((key, m))

    return [first, second, third, fourth, last]


def plane_gather_kernel(x_ref, out_ref, send, recv, own_sem):
    rows = out_ref.shape[0] // 8
    greet([{"ctx": partner(m)} for m in (1, 2, 4)])
    own = pltpu.make_async_copy(x_ref.at[pl.ds(0, rows)], out_ref.at[pl.ds(0, rows)], own_sem)
    own.start()
    copies = Copies(send, recv)

    def block(m, start=0, count=rows):
        if m == 0:
            return x_ref.at[pl.ds(start, count)]
        return out_ref.at[pl.ds(m * rows + start, count)]

    for step in plane_steps(copies, block, rows // 2, 0):
        step()
    own.wait()
    copies.close()


def plane_gather(x, rows):
    return pl.pallas_call(
        plane_gather_kernel,
        in_specs=[ANY],
        out_specs=ANY,
        out_shape=jax.ShapeDtypeStruct((8 * rows, x.shape[1]), x.dtype),
        scratch_shapes=[
            pltpu.SemaphoreType.DMA((8,)),
            pltpu.SemaphoreType.DMA((8,)),
            pltpu.SemaphoreType.DMA,
        ],
        compiler_params=pltpu.CompilerParams(collective_id=1, has_side_effects=True),
        cost_estimate=SMALL,
        name="plane_gather",
    )(x)


def packed_gather_kernel(x_ref, out_ref, send, recv, own_sem):
    rows = x_ref.shape[0]
    greet(
        [{"ctx": partner(m)} for m in (1, 2, 4)] + [{"wt": ahead(d)} for d in (1, 2, 3)]
    )
    own = pltpu.make_async_copy(x_ref, out_ref.at[pl.ds(0, rows)], own_sem)
    own.start()
    copies = Copies(send, recv)

    def block_of(d):
        def block(m, start=0, count=rows):
            if m == 0 and d == 0:
                return x_ref.at[pl.ds(start, count)]
            return out_ref.at[pl.ds((4 * m + d) * rows + start, count)]

        return block

    for d in (1, 3, 2):
        copies.start(d, x_ref, block_of(d)(0), {"wt": ahead(d)})
    steps = {d: plane_steps(copies, block_of(d), rows // 2, ("plane", d)) for d in range(4)}
    steps[0][0]()
    for d, before in ((1, 0), (3, 1), (2, 3)):
        copies.arrived(d)
        steps[d][0]()
        steps[before][1]()
        steps[before][2]()
        if d != 1:
            steps[{3: 0, 2: 1}[d]][3]()
    steps[2][1]()
    steps[2][2]()
    steps[3][3]()
    steps[2][3]()
    for d in range(4):
        steps[d][4]()
    own.wait()
    copies.close()


def packed_gather(x):
    return pl.pallas_call(
        packed_gather_kernel,
        in_specs=[ANY],
        out_specs=ANY,
        out_shape=jax.ShapeDtypeStruct((32 * x.shape[0], x.shape[1]), x.dtype),
        scratch_shapes=[
            pltpu.SemaphoreType.DMA((35,)),
            pltpu.SemaphoreType.DMA((35,)),
            pltpu.SemaphoreType.DMA,
        ],
        compiler_params=pltpu.CompilerParams(collective_id=2, has_side_effects=True),
        cost_estimate=SMALL,
        name="packed_gather",
    )(x)


def sum_steps(copies, x_ref, key, sib, low, recv, out_ref):
    rows = x_ref.shape[0] // 8
    half = rows // 2
    side, near, far = ({"ctx": partner(m)} for m in (1, 2, 4))

    def blocks(ref, m, start=0, count=rows):
        return ref.at[pl.ds(m * rows + start, count)]

    def added(m, start, count):
        ours = x_ref[m * rows + start : m * rows + start + count, :].astype(f32)
        at = m // 2 * rows + start
        return ours + sib[at : at + count, :].astype(f32)

    def put(place, start, value, device):
        at = place * rows + start
        low[at : at + half, :] = value.astype(bf16)
        copies.start(
            (key, "low", place, start),
            blocks(low, place, start, half),
            blocks(recv, place, start, half),
            device,
        )

    def first():
        for m in (7, 3, 5, 1):
            copies.start((key, m), blocks(x_ref, m), blocks(sib, m // 2), side)

    def second():
        copies.arrived((key, 7))
        put(0, 0, added(6, 0, half), far)
        put(0, half, added(6, half, half), near)

    def third():
        copies.arrived((key, 3))
        put(1, half, added(2, half, half), near)
        copies.arrived((key, 5))
        put(2, 0, added(4, 0, half), far)

    def fourth():
        copies.arrived((key, "low", 0, 0))
        put(1, 0, added(2, 0, half) + recv[0:half, :].astype(f32), near)
        copies.arrived((key, "low", 0, half))
        put(2, half, added(4, half, half) + recv[half:rows, :].astype(f32), far)

    def last():
        copies.arrived((key, 1))
        for place in (1, 2):
            for start in (0, half):
                copies.arrived((key, "low", place, start))
        out_ref[...] = (
            added(0, 0, rows)
            + recv[rows : 2 * rows, :].astype(f32)
            + recv[2 * rows :, :].astype(f32)
        )

    return [first, second, third, fourth, last]


def plane_sum_kernel(*refs, sets):
    x_refs, out_refs = refs[:sets], refs[sets : 2 * sets]
    sibs, lows, recvs = (refs[(2 + n) * sets : (3 + n) * sets] for n in range(3))
    send, recv_sem = refs[5 * sets :]
    greet([{"ctx": partner(m)} for m in (1, 2, 4)])
    copies = Copies(send, recv_sem)
    steps = [
        sum_steps(copies, x_refs[n], n, sibs[n], lows[n], recvs[n], out_refs[n])
        for n in range(sets)
    ]
    for n in range(5):
        for one in steps:
            one[n]()
    copies.close()


def plane_sum(arrays):
    if lax.axis_size("ctx") != 8:
        return [
            lax.psum_scatter(x, "ctx", scatter_dimension=0, tiled=True).astype(f32)
            for x in arrays
        ]
    sets = len(arrays)
    rows, columns = arrays[0].shape[0] // 8, arrays[0].shape[1]
    vmem = pl.BlockSpec(memory_space=pltpu.VMEM)
    return pl.pallas_call(
        functools.partial(plane_sum_kernel, sets=sets),
        in_specs=[vmem] * sets,
        out_specs=[vmem] * sets,
        out_shape=[jax.ShapeDtypeStruct((rows, columns), f32)] * sets,
        scratch_shapes=[pltpu.VMEM((4 * rows, columns), bf16)] * sets
        + [pltpu.VMEM((3 * rows, columns), bf16)] * (2 * sets)
        + [pltpu.SemaphoreType.DMA((10 * sets,)), pltpu.SemaphoreType.DMA((10 * sets,))],
        compiler_params=pltpu.CompilerParams(
            collective_id=3, has_side_effects=True, vmem_limit_bytes=VMEM_LIMIT
        ),
        cost_estimate=SMALL,
        name="plane_sum",
    )(*arrays)


def full_sum_kernel(x_ref, out_ref, sib, low, recv, total, total_low, arrived, send, recv_sem):
    rows = out_ref.shape[0]
    greet(
        [{"ctx": partner(m)} for m in (1, 2, 4)] + [{"wt": ahead(d)} for d in (1, 2, 3)]
    )
    copies = Copies(send, recv_sem)
    for step in sum_steps(copies, x_ref, 0, sib, low, recv, total):
        step()
    total_low[...] = total[...].astype(bf16)
    for d in (2, 1, 3):
        copies.start(
            d,
            total_low.at[pl.ds(pl.multiple_of(ahead(d) * rows, rows), rows)],
            arrived.at[pl.ds((d - 1) * rows, rows)],
            {"wt": ahead(d)},
        )
    result = total[pl.ds(pl.multiple_of(ahead(0) * rows, rows), rows), :]
    for d in (1, 3, 2):
        copies.arrived(d)
        result = result + arrived[(d - 1) * rows : d * rows, :].astype(f32)
    out_ref[...] = result
    copies.close()


def full_sum(x):
    rows, columns = x.shape[0] // 32, x.shape[1]
    vmem = pl.BlockSpec(memory_space=pltpu.VMEM)
    return pl.pallas_call(
        full_sum_kernel,
        in_specs=[vmem],
        out_specs=vmem,
        out_shape=jax.ShapeDtypeStruct((rows, columns), f32),
        scratch_shapes=[
            pltpu.VMEM((16 * rows, columns), bf16),
            pltpu.VMEM((12 * rows, columns), bf16),
            pltpu.VMEM((12 * rows, columns), bf16),
            pltpu.VMEM((4 * rows, columns), f32),
            pltpu.VMEM((4 * rows, columns), bf16),
            pltpu.VMEM((3 * rows, columns), bf16),
            pltpu.SemaphoreType.DMA((13,)),
            pltpu.SemaphoreType.DMA((13,)),
        ],
        compiler_params=pltpu.CompilerParams(
            collective_id=4, has_side_effects=True, vmem_limit_bytes=VMEM_LIMIT
        ),
        cost_estimate=SMALL,
        name="full_sum",
    )(x)


def shift(x, distance):
    n = lax.axis_size("wt")
    return lax.ppermute(x, "wt", [(i, (i + distance) % n) for i in range(n)])


def beside(results, *arrivals):
    out = lax.optimization_barrier((results, arrivals))
    return (out[0],) + tuple(out[1])


def gather_all(x):
    ctx, wt = lax.axis_size("ctx"), lax.axis_size("wt")
    if ctx != 8 or wt != 4:
        return [lax.all_gather(x, ALL, axis=0, tiled=True)], [1], jnp.zeros((1,), jnp.int32)
    ctx_index, wt_index = lax.axis_index("ctx"), lax.axis_index("wt")
    m = jnp.arange(8, dtype=jnp.int32)
    d = jnp.arange(4, dtype=jnp.int32)
    places = ((ctx_index ^ m) * wt)[:, None] + ((wt_index - d) % wt)[None, :]
    return [packed_gather(x)], [32], places.reshape(-1).astype(jnp.int32)


def outer_sum(pairs, extra):
    if lax.axis_size("ctx") != 8 or lax.axis_size("wt") != 4:
        parts = [dot_tn(a, b) for a, b in pairs] + [sum(dot_tn(a, b) for a, b in extra)]
        return lax.psum_scatter(
            jnp.concatenate(parts, 1).astype(bf16), ALL, scatter_dimension=0, tiled=True
        ).astype(f32)
    return full_sum(outer(pairs, extra))


def after(x, *others):
    return lax.optimization_barrier((x,) + others)[0]


def rope_tables(positions, width):
    middle = HEAD_SIZE // 2
    frequency = jnp.power(
        jnp.float32(rope_base), -2.0 * jnp.arange(middle, dtype=f32) / HEAD_SIZE
    )
    angles = positions.astype(f32)[:, None] * frequency[None, :]
    times = width // middle
    return jnp.tile(jnp.cos(angles), (1, times)), jnp.tile(jnp.sin(angles), (1, times))


def turn(values, cosine, sine, direction):
    middle = HEAD_SIZE // 2
    first = lax.broadcasted_iota(jnp.int32, values.shape, 1) % HEAD_SIZE < middle
    turned = jnp.where(first, -jnp.roll(values, -middle, 1), jnp.roll(values, middle, 1))
    width = values.shape[1]
    return values * cosine[:, :width] + direction * turned * sine[:, :width]


def norm_forward(values, gain):
    inverse = lax.rsqrt(jnp.mean(values * values, -1, keepdims=True) + norm_eps)
    return (values * inverse * gain, inverse)


def norm_backward(values, inverse, gain, grad_out):
    scaled = gain * grad_out
    gain_grad = (grad_out * values * inverse).astype(bf16)
    projection = jnp.mean(scaled * values, -1, keepdims=True)
    return (inverse * scaled - values * inverse * inverse * inverse * projection, gain_grad)


def per_device(
    layer_input,
    attention_gain,
    query_weight,
    key_matrix,
    value_matrix,
    output_weight,
    mixture_gain,
    router_weight,
    gate_weight,
    up_weight,
    down_weight,
    expert_routes,
    prompt_deal,
    output_grad,
):
    tok = layer_input.shape[1]
    prompt_local = tok - CONT_DEV * CLEN
    block_rows = prompt_local // 2
    context_size = lax.axis_size("ctx")
    shard_count = lax.axis_size("wt")
    expert_count = gate_weight.shape[0]
    capacity = 8 * ((tok * TOP * 7 // (4 * EXPERTS) + 7) // 8)
    ctx_index = lax.axis_index("ctx")
    wt_index = lax.axis_index("wt")
    inputs = layer_input[0].astype(f32)
    routes = expert_routes[0]
    deal_row = prompt_deal[0]
    out_low = output_grad[0]
    out_grad = out_low.astype(f32)

    own_rows = query_weight.shape[0]
    packed = jnp.concatenate(
        [
            query_weight,
            key_matrix,
            value_matrix,
            output_weight.T,
            router_weight,
            attention_gain[:, None],
            mixture_gain[:, None],
            jnp.zeros((own_rows, 94), bf16),
        ],
        1,
    )
    pieces, counts, block_places = gather_all(packed)

    gate_full = lax.all_gather(gate_weight, "ctx", axis=0, tiled=False)
    up_full = lax.all_gather(up_weight, "ctx", axis=0, tiled=False)
    down_full = lax.all_gather(down_weight, "ctx", axis=0, tiled=False)

    mask = jnp.any(
        routes[:, :, None] == jnp.arange(EXPERTS, dtype=jnp.int32)[None, None, :], 1
    )
    order = jnp.arange(tok, dtype=jnp.int32)
    before = (order[None, :] < order[:, None]).astype(bf16)
    rank = jnp.where(mask, dot(before, mask.astype(bf16)), -1.0)
    ranks = lax.all_to_all(
        rank.T.reshape(shard_count, expert_count, tok), "wt", 0, 0, tiled=True
    )
    last = shard_count - 1
    grads_in = {0: out_low, last: shift(after(out_low, pieces[0], ranks), -1)}

    pieces, ranks = beside(pieces, ranks)
    local_rows = jnp.arange(tok, dtype=jnp.int32)
    mine = lax.dynamic_slice_in_dim(deal_row, 2 * ctx_index, 2, 0)
    prompt_place = (
        jnp.where(local_rows < block_rows, mine[0], mine[1]) * block_rows
        + local_rows % block_rows
    )
    positions = jnp.where(
        local_rows < prompt_local, prompt_place, PROMPT + (local_rows - prompt_local) % CLEN
    )
    cosine, sine = rope_tables(positions, 128)
    normed_one, turned_query, kv_low, qkv_full, output_t, rest, gain_rows = project(
        layer_input[0], cosine, sine, pieces, counts, block_places
    )
    router_full = rest[:, :EXPERTS]
    first_gain, second_gain = gain_rows[0], gain_rows[1]
    inverse_one = lax.rsqrt(jnp.mean(inputs * inputs, -1, keepdims=True) + norm_eps)
    kv_own = kv_low[prompt_local:]
    kv_pieces, grads_in[last] = beside([gather_ctx(kv_low, prompt_local)], grads_in[last])

    places = deal_row
    if context_size == 8:
        pairs = deal_row.reshape(2, 2, 2, 2)
        for axis, bit in ((0, 4), (1, 2), (2, 1)):
            pairs = jnp.where(ctx_index & bit > 0, jnp.flip(pairs, axis), pairs)
        places = pairs.reshape(-1)
    low = (mine[0] > mine[1]).astype(jnp.int32)
    starts = jnp.stack(
        [
            low * block_rows,
            (1 - low) * block_rows,
            jnp.min(mine) * block_rows,
            jnp.max(mine) * block_rows,
        ]
    ).astype(jnp.int32)
    heads = []
    for half in range(2):
        result = attention_forward(
            turned_query, kv_pieces, kv_own, places, starts, block_rows, half
        )
        d = last - 1 - half
        grads_in[d] = shift(grads_in[d + 1], -1)
        result, grads_in[d] = beside(result, grads_in[d])
        if half == 0:
            turned_query = after(turned_query, result[0])
        heads.append(result)
    for d in range(last - 3, 0, -1):
        grads_in[d] = shift(grads_in[d + 1], -1)
    attended = jnp.concatenate([out for out, _ in heads], 1)
    lse = [row for _, row in heads]

    branch = dot_nt(attended, output_t)
    middle = inputs + resid_scale * branch
    normed_mid, inverse_two = norm_forward(middle, second_gain)
    normed_two = normed_mid.astype(bf16)
    logits = dot(normed_two, router_full)
    top = jnp.max(jnp.where(mask, logits, masked_score), -1, keepdims=True)
    raised = jnp.where(mask, jnp.exp(jnp.where(mask, logits - top, 0.0)), 0.0)
    gates = raised / jnp.sum(raised, -1, keepdims=True)

    gates_out = gates.T.reshape(shard_count, expert_count, tok)
    gates_in = []
    for d in range(shard_count):
        piece = lax.dynamic_index_in_dim(gates_out, (wt_index + d) % shard_count, 0, False)
        gates_in.append(shift(piece, d) if d else piece)
    got = {0: normed_two}
    partial, mixed, gate_grads, rows = {}, {}, {}, []
    carried = None

    def add(a, b):
        return b if a is None else (a.astype(f32) + b.astype(f32)).astype(bf16)

    for d in [0] + list(range(last, 0, -1)):
        source = (wt_index - d) % shard_count
        rank_in = lax.dynamic_index_in_dim(ranks, source, 0, False)
        result = expert_pass(
            got[d], grads_in[d], rank_in, gates_in[d], gate_full, up_full, down_full, capacity
        )
        coming = d - 1 if d else last
        if coming:
            result, got[coming] = beside(result, shift(got[(coming + 1) % shard_count], -1))
        if d == 0:
            result, gates_in = beside(result, gates_in)
        if 0 < d <= last - 2:
            carried = shift(after(add(carried, partial[d + 2]), got[d]), -1)
            result, carried = beside(result, carried)
        mixed[d], partial[d], d_gate, *kept = result
        rows.append(kept)
        d_gate = d_gate.reshape(expert_count, tok)
        gate_grads[d] = shift(d_gate, shard_count - d) if d else d_gate
        if coming:
            got[coming] = after(got[coming], partial[d])
    carried = shift(add(carried, partial[2]), -1)
    (gate_grad, up_grad), carried = beside(
        up_weight_grads([(after(r[0], partial[1]), r[3], r[4]) for r in rows], context_size),
        carried,
    )
    carried = shift(add(carried, partial[1]), -1)
    down_grad, home = beside(
        down_weight_grads([(after(r[2], gate_grad), r[1]) for r in rows], context_size), carried
    )

    stacked = jnp.stack([gate_grads[d] for d in range(shard_count)], 0)
    stacked = jnp.roll(stacked, wt_index, 0).reshape(EXPERTS, tok).T
    grad_logits = (gates * (stacked - jnp.sum(gates * stacked, -1, keepdims=True))).astype(bf16)
    grad_normed_two = partial[0].astype(f32) + home.astype(f32)
    grad_normed_two = grad_normed_two + dot_nt(grad_logits, router_full)
    grad_mid_norm, second_gain_grad = norm_backward(
        middle, inverse_two, second_gain, grad_normed_two
    )
    grad_middle = out_grad + grad_mid_norm
    grad_branch = (resid_scale * grad_middle).astype(bf16)
    grad_attended = dot(grad_branch, output_t).astype(bf16)
    gate_share, up_share, down_share = (
        lax.psum_scatter(grad, "ctx", scatter_dimension=0, tiled=False).astype(f32)
        for grad in (gate_grad, up_grad, down_grad)
    )
    carried = None
    query = after(turned_query, grad_attended)
    d_query, d_kv, ours = [], [], []
    for half in range(2):
        result = attention_backward(
            query,
            grad_attended,
            lse[half],
            attended,
            cosine,
            sine,
            kv_pieces,
            kv_own,
            places,
            starts,
            block_rows,
            half,
        )
        carried = shift(after(add(carried, mixed[last - half]), home), -1)
        result, carried = beside(result, carried)
        query = after(query, result[0])
        d_query.append(result[0])
        d_kv.append(result[1])
        ours.append(result[2:])
    carried = shift(add(carried, mixed[last - 2]), -1)
    owned, carried = beside(plane_sum(d_kv), carried)
    for d in range(last - 3, 0, -1):
        carried = shift(add(carried, mixed[d]), -1)
    mixture = mixed[0].astype(f32) + carried.astype(f32)
    layer_output = (middle + resid_scale * mixture).astype(bf16)
    d_query = jnp.concatenate(d_query, 1)
    d_key, d_value = (
        jnp.concatenate(
            [
                jnp.concatenate([owned[half][:, 256 * n : 256 * n + 256], ours[half][n]], 0)
                for half in range(2)
            ],
            1,
        )
        for n in range(2)
    )
    grad_key_low = turn(d_key, jnp.tile(cosine, (1, 4)), jnp.tile(sine, (1, 4)), -1.0).astype(
        bf16
    )
    grad_kv = jnp.concatenate([grad_key_low, d_value.astype(bf16)], 1)
    grad_normed_one = dot_nt(d_query, qkv_full[:, :1024]) + dot_nt(grad_kv, qkv_full[:, 1024:])
    grad_input_norm, first_gain_grad = norm_backward(
        inputs, inverse_one, first_gain, grad_normed_one
    )
    input_grad = (grad_middle + grad_input_norm).astype(bf16)

    column = lax.broadcasted_iota(jnp.int32, (tok, 128), 1)
    shares = outer_sum(
        [(normed_one, d_query), (grad_branch, attended), (normed_one, grad_kv)],
        [
            (normed_two, jnp.pad(grad_logits, ((0, 0), (0, 128 - EXPERTS)))),
            (second_gain_grad, (column == EXPERTS).astype(bf16)),
            (first_gain_grad, (column == EXPERTS + 1).astype(bf16)),
        ],
    )
    return (
        layer_output[None],
        input_grad[None],
        shares[:, 3073 + EXPERTS],
        shares[:, :1024],
        shares[:, 2048 : 2048 + KV_WIDTH],
        shares[:, 2048 + KV_WIDTH : 3072],
        shares[:, 1024:2048].T,
        shares[:, 3072 + EXPERTS],
        shares[:, 3072 : 3072 + EXPERTS],
        gate_share,
        up_share,
        down_share,
    )


def solution(mesh):
    return jax.shard_map(
        per_device,
        mesh=mesh,
        in_specs=(
            P("wt", "ctx", None),
            P(("ctx", "wt")),
            P(("ctx", "wt"), None),
            P(("ctx", "wt"), None),
            P(("ctx", "wt"), None),
            P(None, ("ctx", "wt")),
            P(("ctx", "wt")),
            P(("ctx", "wt"), None),
            P("wt", "ctx", None),
            P("wt", "ctx", None),
            P("wt", None, "ctx"),
            P("wt", "ctx", None),
            P("wt", None),
            P("wt", "ctx", None),
        ),
        out_specs=(
            P("wt", "ctx", None),
            P("wt", "ctx", None),
            P(("ctx", "wt")),
            P(("ctx", "wt"), None),
            P(("ctx", "wt"), None),
            P(("ctx", "wt"), None),
            P(None, ("ctx", "wt")),
            P(("ctx", "wt")),
            P(("ctx", "wt"), None),
            P("wt", "ctx", None),
            P("wt", "ctx", None),
            P("wt", None, "ctx"),
        ),
        check_vma=False,
    )
```

```python
import functools

import jax
import jax.numpy as jnp
from jax import lax
from jax.experimental import pallas as pl
from jax.experimental.pallas import tpu as pltpu
from jax.sharding import PartitionSpec as P

MODEL_WIDTH = 1024
HQ = 16
KEY_VALUE_HEADS = 8
HEAD_SIZE = 64
EXPERTS = 32
TOP = 8
PROMPT = 2048
CLEN = 256
CONT_DEV = 2
FF = 512
QTILE = 128
PARTS = 4
KV_WIDTH = KEY_VALUE_HEADS * HEAD_SIZE
ALL = ("ctx", "wt")

att_scale = 0.015625
resid_scale = 0.22
norm_eps = 1e-06
rope_base = 10000.0
masked_score = -1e30

bf16 = jnp.bfloat16
f32 = jnp.float32
VMEM_LIMIT = 60 * 1024 * 1024
SMALL = pl.CostEstimate(flops=1_000_000_000, bytes_accessed=1_000_000, transcendentals=0)

NT = (((1,), (1,)), ((), ()))
TN = (((0,), (0,)), ((), ()))


def dot(a, b):
    return jnp.dot(a, b, preferred_element_type=f32)


def dot_nt(a, b):
    return lax.dot_general(a, b, NT, preferred_element_type=f32)


def dot_tn(a, b):
    return lax.dot_general(a, b, TN, preferred_element_type=f32)


def turn_tile(values, cosine, sine, direction):
    middle = HEAD_SIZE // 2
    first = lax.broadcasted_iota(jnp.int32, values.shape, 1) % HEAD_SIZE < middle
    turned = jnp.where(first, -pltpu.roll(values, 128 - middle, 1), pltpu.roll(values, middle, 1))
    return values * cosine + direction * turned * sine


def project_kernel(places, x_ref, cos_ref, sin_ref, *refs, counts):
    pieces = refs[: len(counts)]
    normed_ref, q_ref, kv_ref, qkv_ref, out_ref, rest_ref, gains_ref = refs[len(counts) :]
    rows = MODEL_WIDTH // sum(counts)
    at = 0
    for piece, count in zip(pieces, counts):
        for i in range(count):
            source = slice(i * rows, (i + 1) * rows)
            target = pl.ds(pl.multiple_of(places[at] * rows, rows), rows)
            qkv_ref[target, :] = piece[source, :2048]
            out_ref[target, :] = piece[source, 2048:3072]
            rest_ref[target, :] = piece[source, 3072:]
            at += 1
    gains = rest_ref[...].astype(f32).T[EXPERTS : EXPERTS + 8]
    gains_ref[...] = gains
    x = x_ref[...].astype(f32)
    inverse = lax.rsqrt(jnp.mean(x * x, -1, keepdims=True) + norm_eps)
    normed_ref[...] = (x * inverse * gains[:1]).astype(bf16)
    for c in range(8):
        raw = dot(normed_ref[...], qkv_ref[:, 256 * c : 256 * (c + 1)])
        for h in range(2):
            part = raw[:, 128 * h : 128 * (h + 1)]
            if c < 6:
                part = turn_tile(part, cos_ref[...], sin_ref[...], 1.0)
            column = 256 * c + 128 * h
            if column < 1024:
                q_ref[:, column : column + 128] = part.astype(bf16)
            else:
                column -= 1024
                at = column % KV_WIDTH // 256 * 512 + column // KV_WIDTH * 256 + column % 256
                kv_ref[:, at : at + 128] = part.astype(bf16)


def project(x, cosine, sine, pieces, counts, places):
    tok = x.shape[0]
    shape = jax.ShapeDtypeStruct
    whole = pl.BlockSpec(memory_space=pltpu.VMEM)
    return pl.pallas_call(
        functools.partial(project_kernel, counts=counts),
        in_specs=[pl.BlockSpec(memory_space=pltpu.SMEM)] + [whole] * (3 + len(pieces)),
        out_specs=[whole] * 7,
        out_shape=[
            shape((tok, MODEL_WIDTH), bf16),
            shape((tok, HQ * HEAD_SIZE), bf16),
            shape((tok, 2 * KV_WIDTH), bf16),
            shape((MODEL_WIDTH, 2048), bf16),
            shape((MODEL_WIDTH, 1024), bf16),
            shape((MODEL_WIDTH, 128), bf16),
            shape((8, MODEL_WIDTH), f32),
        ],
        compiler_params=pltpu.CompilerParams(vmem_limit_bytes=VMEM_LIMIT),
        cost_estimate=SMALL,
        name="project",
    )(places, x, cosine, sine, *pieces)


def outer_kernel(mine, *refs, count):
    out_ref = refs[-1]
    pairs = [(refs[n], refs[n + 1]) for n in range(0, len(refs) - 1, 2)]
    at = 0
    for a_ref, b_ref in pairs[:count]:
        columns = b_ref.shape[1]
        out_ref[:, at : at + columns] = dot_tn(a_ref[...], b_ref[...]).astype(bf16)
        at += columns
    out_ref[:, at:] = sum(dot_tn(a[...], b[...]) for a, b in pairs[count:]).astype(bf16)


def outer(pairs, extra):
    tok = pairs[0][0].shape[0]
    mine = lax.axis_index("ctx").astype(jnp.int32).reshape(1)
    specs = []
    for _, b in pairs + extra:
        specs.append(pl.BlockSpec((tok, 128), lambda m, mine: (0, m ^ mine[0])))
        specs.append(pl.BlockSpec(b.shape, lambda m, mine: (0, 0)))
    columns = sum(b.shape[1] for _, b in pairs) + extra[0][1].shape[1]
    return pl.pallas_call(
        functools.partial(outer_kernel, count=len(pairs)),
        grid_spec=pltpu.PrefetchScalarGridSpec(
            num_scalar_prefetch=1,
            grid=(8,),
            in_specs=specs,
            out_specs=pl.BlockSpec((128, columns), lambda m, mine: (m, 0)),
        ),
        out_shape=jax.ShapeDtypeStruct((MODEL_WIDTH, columns), bf16),
        compiler_params=pltpu.CompilerParams(vmem_limit_bytes=VMEM_LIMIT),
        cost_estimate=SMALL,
        name="outer",
    )(mine, *[x for pair in pairs + extra for x in pair])


def gather_keys(pieces, scratch, places, block_rows):
    at = 0
    for piece in pieces:
        for b in range(piece.shape[0] // block_rows):
            start = pl.multiple_of(places[at] * block_rows, block_rows)
            scratch[pl.ds(start, block_rows), :] = piece[b * block_rows : (b + 1) * block_rows, :]
            at += 1


def pair_rows(ref, start, rows, j):
    both = ref[pl.ds(start, rows), 2 * HEAD_SIZE * j : 2 * HEAD_SIZE * (j + 1)]
    return jnp.concatenate([both[:, :HEAD_SIZE], both[:, HEAD_SIZE:]], 0)


def attention_forward_kernel(places, starts, q_ref, *refs, block_rows, pieces):
    k_refs, v_refs = refs[:pieces], refs[pieces : 2 * pieces]
    kc_ref, vc_ref, o_ref, lse_ref, k_scr, v_scr = refs[2 * pieces :]
    prompt_local = 2 * block_rows
    gather_keys(k_refs, k_scr, places, block_rows)
    gather_keys(v_refs, v_scr, places, block_rows)

    def store(start, rows, j, out, m, total, at):
        out = (out / total).astype(bf16)
        lse = m + jnp.log(total)
        o_ref[pl.ds(start, rows), 2 * HEAD_SIZE * j : 2 * HEAD_SIZE * (j + 1)] = jnp.concatenate(
            [out[:rows], out[rows:]], 1
        )
        row = jnp.broadcast_to(lse, (2 * rows, 128)).T[:1]
        lse_ref[0, 2 * j : 2 * j + 2, pl.ds(at, rows)] = jnp.concatenate(
            [row[:, :rows], row[:, rows:]], 0
        )

    def tile(i, _):
        start = pl.multiple_of(prompt_local + i * QTILE, 64)
        per = CLEN // QTILE
        seg = pl.multiple_of((i // per) * CLEN, CLEN)
        for j in range(2):
            lanes = slice(HEAD_SIZE * j, HEAD_SIZE * (j + 1))
            q = pair_rows(q_ref, start, QTILE, j) * bf16(att_scale)
            s1 = dot_nt(q, k_scr[:, lanes])
            s2 = dot_nt(q, kc_ref[pl.ds(seg, CLEN), lanes])
            place = lax.broadcasted_iota(jnp.int32, s2.shape, 0) % QTILE + (i % per) * QTILE
            s2 = jnp.where(lax.broadcasted_iota(jnp.int32, s2.shape, 1) <= place, s2, masked_score)
            m = jnp.maximum(jnp.max(s1, 1, keepdims=True), jnp.max(s2, 1, keepdims=True))
            e1 = jnp.exp(s1 - m)
            e2 = jnp.exp(s2 - m)
            total = jnp.sum(e1, 1, keepdims=True) + jnp.sum(e2, 1, keepdims=True)
            out = dot(e1.astype(bf16), v_scr[:, lanes])
            out = out + dot(e2.astype(bf16), vc_ref[pl.ds(seg, CLEN), lanes])
            store(start, QTILE, j, out, m, total, pl.multiple_of(i * QTILE, QTILE))
        return 0

    lax.fori_loop(0, CONT_DEV * CLEN // QTILE, tile, 0)

    for half, keys in enumerate((PROMPT // 2, PROMPT)):
        start = pl.multiple_of(starts[half], block_rows)
        for j in range(2):
            lanes = slice(HEAD_SIZE * j, HEAD_SIZE * (j + 1))
            q = pair_rows(q_ref, start, block_rows, j) * bf16(att_scale)
            s = dot_nt(q, k_scr[:keys, lanes])
            place = lax.broadcasted_iota(jnp.int32, s.shape, 0) % block_rows + starts[2 + half]
            s = jnp.where(lax.broadcasted_iota(jnp.int32, s.shape, 1) <= place, s, masked_score)
            m = jnp.max(s, 1, keepdims=True)
            e = jnp.exp(s - m)
            total = jnp.sum(e, 1, keepdims=True)
            out = dot(e.astype(bf16), v_scr[:keys, lanes])
            store(start, block_rows, j, out, m, total, CONT_DEV * CLEN + half * block_rows)


def key_specs(pieces, own, half):
    spec = pl.BlockSpec
    key, value = (lambda g, *_: (0, 4 * half + g)), (lambda g, *_: (0, 4 * half + 2 + g))
    keys = [spec((p.shape[0], 128), key) for p in pieces]
    values = [spec((p.shape[0], 128), value) for p in pieces]
    return keys + values + [spec((own, 128), key), spec((own, 128), value)]


def attention_forward(q, pieces, kv_own, places, starts, block_rows, half):
    tok = q.shape[0]
    spec = pl.BlockSpec
    return pl.pallas_call(
        functools.partial(
            attention_forward_kernel, block_rows=block_rows, pieces=len(pieces)
        ),
        grid_spec=pltpu.PrefetchScalarGridSpec(
            num_scalar_prefetch=2,
            grid=(2,),
            in_specs=[spec((tok, 256), lambda g, *_: (0, 2 * half + g))]
            + key_specs(pieces, kv_own.shape[0], half),
            out_specs=[
                spec((tok, 256), lambda g, *_: (0, g)),
                spec((1, 4, tok), lambda g, *_: (g, 0, 0)),
            ],
            scratch_shapes=[
                pltpu.VMEM((PROMPT, 2 * HEAD_SIZE), bf16),
                pltpu.VMEM((PROMPT, 2 * HEAD_SIZE), bf16),
            ],
        ),
        out_shape=[
            jax.ShapeDtypeStruct((tok, HQ * HEAD_SIZE // 2), bf16),
            jax.ShapeDtypeStruct((2, 4, tok), f32),
        ],
        compiler_params=pltpu.CompilerParams(vmem_limit_bytes=VMEM_LIMIT),
        cost_estimate=SMALL,
        name="attention_forward",
    )(places, starts, q, *pieces, *pieces, kv_own, kv_own)


def attention_backward_kernel(
    places, starts, q_ref, do_ref, lse_ref, o_ref, cos_ref, sin_ref, *refs, block_rows, pieces
):
    k_refs, v_refs = refs[:pieces], refs[pieces : 2 * pieces]
    kc_ref, vc_ref, dq_ref, dkv_ref, dkc_ref, dvc_ref = refs[2 * pieces : 2 * pieces + 6]
    k_scr, v_scr, dk_acc, dv_acc, dq_acc = refs[2 * pieces + 6 :]
    prompt_local = 2 * block_rows
    gather_keys(k_refs, k_scr, places, block_rows)
    gather_keys(v_refs, v_scr, places, block_rows)
    dk_acc[...] = jnp.zeros_like(dk_acc)
    dv_acc[...] = jnp.zeros_like(dv_acc)
    dkc_ref[...] = jnp.zeros_like(dkc_ref)
    dvc_ref[...] = jnp.zeros_like(dvc_ref)

    def row_pair(ref, start, rows, j):
        both = ref[0, 2 * j : 2 * j + 2, pl.ds(start, rows)]
        return jnp.concatenate([both[:1], both[1:]], 1)

    def centre(start, rows, j, d_out):
        product = d_out.astype(f32) * pair_rows(o_ref, start, rows, j).astype(f32)
        ones = jnp.ones((8, HEAD_SIZE), f32)
        return lax.dot_general(
            ones, product, NT, precision=lax.Precision.HIGHEST, preferred_element_type=f32
        )[:1]

    def part(k, v, q, d_out, lse, delta, allowed):
        s = dot_nt(k, q)
        if allowed is not None:
            s = jnp.where(allowed(s.shape), s, masked_score)
        p = jnp.exp(s - lse)
        d_p = dot_nt(v, d_out)
        d_s = (p * (d_p - delta)).astype(bf16)
        return dot_tn(d_s, k), dot(d_s, q), dot(p.astype(bf16), d_out)

    def store(start, rows, j, d_q):
        d_q = d_q * att_scale
        dq_acc[pl.ds(start, rows), 2 * HEAD_SIZE * j : 2 * HEAD_SIZE * (j + 1)] = jnp.concatenate(
            [d_q[:rows], d_q[rows:]], 1
        )

    def tile(i, _):
        start = pl.multiple_of(prompt_local + i * QTILE, 64)
        per = CLEN // QTILE
        seg = pl.multiple_of((i // per) * CLEN, CLEN)
        own = pl.ds(seg, CLEN)
        lane_start = pl.multiple_of(i * QTILE, QTILE)

        def allowed(shape):
            place = lax.broadcasted_iota(jnp.int32, shape, 1) % QTILE + (i % per) * QTILE
            return lax.broadcasted_iota(jnp.int32, shape, 0) <= place

        for j in range(2):
            lanes = slice(HEAD_SIZE * j, HEAD_SIZE * (j + 1))
            q = pair_rows(q_ref, start, QTILE, j) * bf16(att_scale)
            d_out = pair_rows(do_ref, start, QTILE, j)
            lse = row_pair(lse_ref, lane_start, QTILE, j)
            delta = centre(start, QTILE, j, d_out)
            a, b, c = part(k_scr[:, lanes], v_scr[:, lanes], q, d_out, lse, delta, None)
            dk_acc[:, lanes] += b
            dv_acc[:, lanes] += c
            d_q = a
            a, b, c = part(
                kc_ref[own, lanes], vc_ref[own, lanes], q, d_out, lse, delta, allowed
            )
            dkc_ref[own, lanes] += b
            dvc_ref[own, lanes] += c
            store(start, QTILE, j, d_q + a)
        return 0

    lax.fori_loop(0, CONT_DEV * CLEN // QTILE, tile, 0)

    for half, keys in enumerate((PROMPT // 2, PROMPT)):
        start = pl.multiple_of(starts[half], block_rows)
        at = CONT_DEV * CLEN + half * block_rows

        def allowed(shape):
            place = lax.broadcasted_iota(jnp.int32, shape, 1) % block_rows + starts[2 + half]
            return lax.broadcasted_iota(jnp.int32, shape, 0) <= place

        for j in range(2):
            lanes = slice(HEAD_SIZE * j, HEAD_SIZE * (j + 1))
            q = pair_rows(q_ref, start, block_rows, j) * bf16(att_scale)
            d_out = pair_rows(do_ref, start, block_rows, j)
            lse = row_pair(lse_ref, at, block_rows, j)
            delta = centre(start, block_rows, j, d_out)
            a, b, c = part(
                k_scr[:keys, lanes], v_scr[:keys, lanes], q, d_out, lse, delta, allowed
            )
            dk_acc[:keys, lanes] += b
            dv_acc[:keys, lanes] += c
            store(start, block_rows, j, a)

    g = pl.program_id(0)
    key_lanes = pl.ds(pl.multiple_of(g * 128, 128), 128)
    value_lanes = pl.ds(pl.multiple_of(256 + g * 128, 128), 128)
    for b in range(PROMPT // block_rows):
        source = pl.ds(pl.multiple_of(places[b] * block_rows, block_rows), block_rows)
        rows = slice(b * block_rows, (b + 1) * block_rows)
        dkv_ref[rows, key_lanes] = dk_acc[source, :].astype(bf16)
        dkv_ref[rows, value_lanes] = dv_acc[source, :].astype(bf16)
    for c in range(2):
        lanes = slice(128 * c, 128 * (c + 1))
        dq_ref[:, lanes] = turn_tile(dq_acc[:, lanes], cos_ref[...], sin_ref[...], -1.0).astype(
            bf16
        )


def attention_backward(
    q, d_out, lse, attended, cosine, sine, pieces, kv_own, places, starts, block_rows, half
):
    tok = q.shape[0]
    own = kv_own.shape[0]
    spec = pl.BlockSpec
    wide = spec((tok, 256), lambda g, *_: (0, 2 * half + g))
    ours = spec((own, 128), lambda g, *_: (0, g))
    table = spec((tok, 128), lambda g, *_: (0, 0))
    return pl.pallas_call(
        functools.partial(
            attention_backward_kernel, block_rows=block_rows, pieces=len(pieces)
        ),
        grid_spec=pltpu.PrefetchScalarGridSpec(
            num_scalar_prefetch=2,
            grid=(2,),
            in_specs=[wide, wide, spec((1, 4, tok), lambda g, *_: (g, 0, 0)), wide, table, table]
            + key_specs(pieces, own, half),
            out_specs=[
                spec((tok, 256), lambda g, *_: (0, g)),
                spec((PROMPT, KV_WIDTH), lambda g, *_: (0, 0)),
                ours,
                ours,
            ],
            scratch_shapes=[
                pltpu.VMEM((PROMPT, 2 * HEAD_SIZE), bf16),
                pltpu.VMEM((PROMPT, 2 * HEAD_SIZE), bf16),
                pltpu.VMEM((PROMPT, 2 * HEAD_SIZE), f32),
                pltpu.VMEM((PROMPT, 2 * HEAD_SIZE), f32),
                pltpu.VMEM((tok, 4 * HEAD_SIZE), f32),
            ],
        ),
        out_shape=[
            jax.ShapeDtypeStruct((tok, HQ * HEAD_SIZE // 2), bf16),
            jax.ShapeDtypeStruct((PROMPT, KV_WIDTH), bf16),
            jax.ShapeDtypeStruct((own, KV_WIDTH // 2), f32),
            jax.ShapeDtypeStruct((own, KV_WIDTH // 2), f32),
        ],
        compiler_params=pltpu.CompilerParams(vmem_limit_bytes=VMEM_LIMIT),
        cost_estimate=SMALL,
        name="attention_backward",
    )(places, starts, q, d_out, lse, attended, cosine, sine, *pieces, *pieces, kv_own, kv_own)


def expert_kernel(
    counts,
    a2_ref,
    df_ref,
    rank_ref,
    gate_ref,
    wg_ref,
    wu_ref,
    wd_ref,
    mix_ref,
    da_ref,
    dg_ref,
    x_ref,
    dy_ref,
    z_ref,
    dgate_ref,
    dup_ref,
    mix_acc,
    da_acc,
    *,
    sizes,
):
    e = pl.program_id(0)

    @pl.when(e == 0)
    def _():
        mix_acc[...] = jnp.zeros_like(mix_acc)
        da_acc[...] = jnp.zeros_like(da_acc)

    def body(size):
        rank = rank_ref[0]
        gates = gate_ref[0]
        tok = rank.shape[1]
        slot = lax.broadcasted_iota(jnp.int32, (size, tok), 0).astype(f32)
        hit = slot == rank
        chosen = hit.astype(f32).astype(bf16)
        gate = jnp.sum(jnp.where(hit, gates, 0.0), 1, keepdims=True)
        x = dot(chosen, a2_ref[...]).astype(bf16)
        d_mix = resid_scale * dot(chosen, df_ref[...])
        wg = wg_ref[:, 0].reshape(MODEL_WIDTH, FF)
        wu = wu_ref[:, 0].reshape(MODEL_WIDTH, FF)
        wd = jnp.concatenate([wd_ref[c, 0] for c in range(wd_ref.shape[0])], 1)
        g = dot(x, wg)
        u = dot(x, wu)
        sig = jax.nn.sigmoid(g)
        z = (g * sig * u).astype(bf16)
        y = dot(z, wd).astype(bf16).astype(f32)
        d_gate_value = jnp.sum(d_mix * y, 1, keepdims=True)
        dg_ref[0] = jnp.sum(jnp.where(hit, d_gate_value, 0.0), 0, keepdims=True)
        mix_acc[...] += dot_tn(chosen, (gate * y).astype(bf16))
        d_y = (gate * d_mix).astype(bf16)
        d_z = dot_nt(d_y, wd)
        d_g = (d_z * u * sig * (1.0 + g * (1.0 - sig))).astype(bf16)
        d_u = (d_z * g * sig).astype(bf16)
        d_r = (dot_nt(d_g, wg) + dot_nt(d_u, wu)).astype(bf16)
        da_acc[...] += dot_tn(chosen, d_r)
        for ref, value in (
            (x_ref, x),
            (dy_ref, d_y),
            (z_ref, z),
            (dgate_ref, d_g),
            (dup_ref, d_u),
        ):
            ref[0, :size] = value
            if size < ref.shape[1]:
                ref[0, size:] = jnp.zeros((ref.shape[1] - size, ref.shape[2]), bf16)

    least = -1
    for size in sizes:
        pl.when((counts[e] > least) & (counts[e] <= size))(functools.partial(body, size))
        least = size

    @pl.when(e == pl.num_programs(0) - 1)
    def _():
        mix_ref[...] = mix_acc[...].astype(bf16)
        da_ref[...] = da_acc[...].astype(bf16)


def expert_pass(a2, df, rank, gates, wg, wu, wd, capacity):
    tok = a2.shape[0]
    parts, experts = wg.shape[0], wg.shape[1]
    sizes = sorted({min(size, capacity) for size in (128, 192, 256, capacity)})
    counts = (jnp.max(rank, (1, 2)) + 1.0).astype(jnp.int32)
    spec = pl.BlockSpec
    whole = spec((tok, MODEL_WIDTH), lambda e, *_: (0, 0))
    row = spec((1, 1, tok), lambda e, *_: (e, 0, 0))
    up = spec((parts, 1, MODEL_WIDTH // parts, FF), lambda e, *_: (0, e, 0, 0))
    down = spec((parts, 1, FF, MODEL_WIDTH // parts), lambda e, *_: (0, e, 0, 0))
    rows_wide = spec((1, capacity, MODEL_WIDTH), lambda e, *_: (e, 0, 0))
    rows_thin = spec((1, capacity, FF), lambda e, *_: (e, 0, 0))
    shape = jax.ShapeDtypeStruct
    return pl.pallas_call(
        functools.partial(expert_kernel, sizes=sizes),
        grid_spec=pltpu.PrefetchScalarGridSpec(
            num_scalar_prefetch=1,
            grid=(experts,),
            in_specs=[whole, whole, row, row, up, up, down],
            out_specs=[whole, whole, row, rows_wide, rows_wide, rows_thin, rows_thin, rows_thin],
            scratch_shapes=[
                pltpu.VMEM((tok, MODEL_WIDTH), f32),
                pltpu.VMEM((tok, MODEL_WIDTH), f32),
            ],
        ),
        out_shape=[
            shape((tok, MODEL_WIDTH), bf16),
            shape((tok, MODEL_WIDTH), bf16),
            shape((experts, 1, tok), f32),
            shape((experts, capacity, MODEL_WIDTH), bf16),
            shape((experts, capacity, MODEL_WIDTH), bf16),
            shape((experts, capacity, FF), bf16),
            shape((experts, capacity, FF), bf16),
            shape((experts, capacity, FF), bf16),
        ],
        compiler_params=pltpu.CompilerParams(vmem_limit_bytes=VMEM_LIMIT),
        cost_estimate=SMALL,
        name="expert_pass",
    )(counts, a2, df, rank, gates, wg, wu, wd)


def up_grad_kernel(*refs, sources):
    rows = refs[: 3 * sources]
    gate_ref, up_ref = refs[3 * sources :]
    for n, out_ref in ((1, gate_ref), (2, up_ref)):
        total = None
        for s in range(sources):
            term = dot_tn(rows[3 * s][0], rows[3 * s + n][0])
            total = term if total is None else total + term
        out_ref[...] = total.astype(bf16).reshape(out_ref.shape)


def down_grad_kernel(*refs, sources, parts):
    rows, down_ref = refs[: 2 * sources], refs[-1]
    width = MODEL_WIDTH // parts
    total = None
    for s in range(sources):
        term = dot_tn(rows[2 * s][0], rows[2 * s + 1][0])
        total = term if total is None else total + term
    total = total.astype(bf16)
    for c in range(parts):
        down_ref[c, 0] = total[:, c * width : (c + 1) * width]


def row_specs(rows):
    return [pl.BlockSpec((1,) + a.shape[1:], lambda e: (e, 0, 0)) for r in rows for a in r]


def up_weight_grads(rows, parts):
    experts = rows[0][0].shape[0]
    shape = (parts, experts, MODEL_WIDTH // parts, FF)
    out = pl.BlockSpec((parts, 1) + shape[2:], lambda e: (0, e, 0, 0))
    return pl.pallas_call(
        functools.partial(up_grad_kernel, sources=len(rows)),
        grid=(experts,),
        in_specs=row_specs(rows),
        out_specs=[out, out],
        out_shape=[jax.ShapeDtypeStruct(shape, bf16)] * 2,
        compiler_params=pltpu.CompilerParams(vmem_limit_bytes=VMEM_LIMIT),
        cost_estimate=SMALL,
        name="up_weight_grads",
    )(*[a for r in rows for a in r])


def down_weight_grads(rows, parts):
    experts = rows[0][0].shape[0]
    shape = (parts, experts, FF, MODEL_WIDTH // parts)
    return pl.pallas_call(
        functools.partial(down_grad_kernel, sources=len(rows), parts=parts),
        grid=(experts,),
        in_specs=row_specs(rows),
        out_specs=pl.BlockSpec((parts, 1) + shape[2:], lambda e: (0, e, 0, 0)),
        out_shape=jax.ShapeDtypeStruct(shape, bf16),
        compiler_params=pltpu.CompilerParams(vmem_limit_bytes=VMEM_LIMIT),
        cost_estimate=SMALL,
        name="down_weight_grads",
    )(*[a for r in rows for a in r])


def swap(x, mask):
    return lax.ppermute(x, "ctx", [(i, i ^ mask) for i in range(lax.axis_size("ctx"))])


def gather_ctx(x, rows):
    if lax.axis_size("ctx") != 8:
        return lax.all_gather(x[:rows], "ctx", axis=0, tiled=True)
    return plane_gather(x, rows)


MESH = pl.DeviceIdType.MESH
ANY = pl.BlockSpec(memory_space=pl.ANY)


def partner(mask):
    me = lax.axis_index("ctx")
    return me + mask - 2 * mask * ((me // mask) % 2)


def ahead(distance):
    return (lax.axis_index("wt") + distance) % lax.axis_size("wt")


class Copies:
    def __init__(self, send, recv):
        self.send, self.recv, self.made = send, recv, {}

    def start(self, name, source, target, device):
        n = len(self.made)
        self.made[name] = copy = pltpu.make_async_remote_copy(
            src_ref=source,
            dst_ref=target,
            send_sem=self.send.at[n],
            recv_sem=self.recv.at[n],
            device_id=device,
            device_id_type=MESH,
        )
        copy.start()

    def arrived(self, name):
        self.made[name].wait_recv()

    def close(self):
        for copy in self.made.values():
            copy.wait_send()


def greet(devices):
    barrier = pltpu.get_barrier_semaphore()
    for device in devices:
        pl.semaphore_signal(barrier, inc=1, device_id=device, device_id_type=MESH)
    pl.semaphore_wait(barrier, len(devices))


def plane_steps(copies, block, half, key):
    side, near, far = ({"ctx": partner(m)} for m in (1, 2, 4))
    top, end = (lambda m: block(m, 0, half)), (lambda m: block(m, half, half))

    def first():
        copies.start((key, 2), block(0), block(2), near)
        copies.start((key, 4), block(0), block(4), far)
        copies.start((key, 1), block(0), block(1), side)

    def second():
        copies.arrived((key, 2))
        copies.start((key, 6), top(2), top(6), far)
        copies.start((key, 3), block(2), block(3), side)

    def third():
        copies.arrived((key, 4))
        copies.start((key, 7), end(4), end(6), near)
        copies.start((key, 5), block(4), block(5), side)

    def fourth():
        copies.arrived((key, 6))
        copies.arrived((key, 7))
        copies.start((key, 8), block(6), block(7), side)

    def last():
        for m in (1, 3, 5, 8):
            copies.arrived((key, m))

    return [first, second, third, fourth, last]


def plane_gather_kernel(x_ref, out_ref, send, recv, own_sem):
    rows = out_ref.shape[0] // 8
    greet([{"ctx": partner(m)} for m in (1, 2, 4)])
    own = pltpu.make_async_copy(x_ref.at[pl.ds(0, rows)], out_ref.at[pl.ds(0, rows)], own_sem)
    own.start()
    copies = Copies(send, recv)

    def block(m, start=0, count=rows):
        if m == 0:
            return x_ref.at[pl.ds(start, count)]
        return out_ref.at[pl.ds(m * rows + start, count)]

    for step in plane_steps(copies, block, rows // 2, 0):
        step()
    own.wait()
    copies.close()


def plane_gather(x, rows):
    return pl.pallas_call(
        plane_gather_kernel,
        in_specs=[ANY],
        out_specs=ANY,
        out_shape=jax.ShapeDtypeStruct((8 * rows, x.shape[1]), x.dtype),
        scratch_shapes=[
            pltpu.SemaphoreType.DMA((8,)),
            pltpu.SemaphoreType.DMA((8,)),
            pltpu.SemaphoreType.DMA,
        ],
        compiler_params=pltpu.CompilerParams(collective_id=1, has_side_effects=True),
        cost_estimate=SMALL,
        name="plane_gather",
    )(x)


def packed_gather_kernel(x_ref, out_ref, send, recv, own_sem):
    rows = x_ref.shape[0]
    greet(
        [{"ctx": partner(m)} for m in (1, 2, 4)] + [{"wt": ahead(d)} for d in (1, 2, 3)]
    )
    own = pltpu.make_async_copy(x_ref, out_ref.at[pl.ds(0, rows)], own_sem)
    own.start()
    copies = Copies(send, recv)

    def block_of(d):
        def block(m, start=0, count=rows):
            if m == 0 and d == 0:
                return x_ref.at[pl.ds(start, count)]
            return out_ref.at[pl.ds((4 * m + d) * rows + start, count)]

        return block

    for d in (1, 3, 2):
        copies.start(d, x_ref, block_of(d)(0), {"wt": ahead(d)})
    steps = {d: plane_steps(copies, block_of(d), rows // 2, ("plane", d)) for d in range(4)}
    steps[0][0]()
    for d, before in ((1, 0), (3, 1), (2, 3)):
        copies.arrived(d)
        steps[d][0]()
        steps[before][1]()
        steps[before][2]()
        if d != 1:
            steps[{3: 0, 2: 1}[d]][3]()
    steps[2][1]()
    steps[2][2]()
    steps[3][3]()
    steps[2][3]()
    for d in range(4):
        steps[d][4]()
    own.wait()
    copies.close()


def packed_gather(x):
    return pl.pallas_call(
        packed_gather_kernel,
        in_specs=[ANY],
        out_specs=ANY,
        out_shape=jax.ShapeDtypeStruct((32 * x.shape[0], x.shape[1]), x.dtype),
        scratch_shapes=[
            pltpu.SemaphoreType.DMA((35,)),
            pltpu.SemaphoreType.DMA((35,)),
            pltpu.SemaphoreType.DMA,
        ],
        compiler_params=pltpu.CompilerParams(collective_id=2, has_side_effects=True),
        cost_estimate=SMALL,
        name="packed_gather",
    )(x)


def sum_steps(copies, x_ref, key, sib, low, recv, out_ref, columns):
    rows = x_ref.shape[0] // 8
    half = rows // 2
    side, near, far = ({"ctx": partner(m)} for m in (1, 2, 4))

    def blocks(ref, m, start=0, count=rows):
        return ref.at[pl.ds(m * rows + start, count), columns]

    def added(m, start, count):
        ours = x_ref[m * rows + start : m * rows + start + count, columns].astype(f32)
        at = m // 2 * rows + start
        return ours + sib[at : at + count, columns].astype(f32)

    def put(place, start, value, device):
        at = place * rows + start
        low[at : at + half, columns] = value.astype(bf16)
        copies.start(
            (key, "low", place, start),
            blocks(low, place, start, half),
            blocks(recv, place, start, half),
            device,
        )

    def first():
        for m in (7, 3, 5, 1):
            copies.start((key, m), blocks(x_ref, m), blocks(sib, m // 2), side)

    def second():
        copies.arrived((key, 7))
        put(0, 0, added(6, 0, half), far)
        put(0, half, added(6, half, half), near)

    def third():
        copies.arrived((key, 3))
        put(1, half, added(2, half, half), near)
        copies.arrived((key, 5))
        put(2, 0, added(4, 0, half), far)

    def fourth():
        copies.arrived((key, "low", 0, 0))
        put(1, 0, added(2, 0, half) + recv[0:half, columns].astype(f32), near)
        copies.arrived((key, "low", 0, half))
        put(2, half, added(4, half, half) + recv[half:rows, columns].astype(f32), far)

    def last():
        copies.arrived((key, 1))
        for place in (1, 2):
            for start in (0, half):
                copies.arrived((key, "low", place, start))
        out_ref[:, columns] = (
            added(0, 0, rows)
            + recv[rows : 2 * rows, columns].astype(f32)
            + recv[2 * rows :, columns].astype(f32)
        )

    return [first, second, third, fourth, last]


def plane_sum_kernel(*refs, sets):
    x_refs, out_refs = refs[:sets], refs[sets : 2 * sets]
    sibs, lows, recvs = (refs[(2 + n) * sets : (3 + n) * sets] for n in range(3))
    send, recv_sem = refs[5 * sets :]
    greet([{"ctx": partner(m)} for m in (1, 2, 4)])
    copies = Copies(send, recv_sem)
    steps = [
        sum_steps(copies, x_refs[n], n, sibs[n], lows[n], recvs[n], out_refs[n], slice(None))
        for n in range(sets)
    ]
    for n in range(5):
        for one in steps:
            one[n]()
    copies.close()


def plane_sum(arrays):
    if lax.axis_size("ctx") != 8:
        return [
            lax.psum_scatter(x, "ctx", scatter_dimension=0, tiled=True).astype(f32)
            for x in arrays
        ]
    sets = len(arrays)
    rows, columns = arrays[0].shape[0] // 8, arrays[0].shape[1]
    vmem = pl.BlockSpec(memory_space=pltpu.VMEM)
    return pl.pallas_call(
        functools.partial(plane_sum_kernel, sets=sets),
        in_specs=[vmem] * sets,
        out_specs=[vmem] * sets,
        out_shape=[jax.ShapeDtypeStruct((rows, columns), f32)] * sets,
        scratch_shapes=[pltpu.VMEM((4 * rows, columns), bf16)] * sets
        + [pltpu.VMEM((3 * rows, columns), bf16)] * (2 * sets)
        + [pltpu.SemaphoreType.DMA((10 * sets,)), pltpu.SemaphoreType.DMA((10 * sets,))],
        compiler_params=pltpu.CompilerParams(
            collective_id=3, has_side_effects=True, vmem_limit_bytes=VMEM_LIMIT
        ),
        cost_estimate=SMALL,
        name="plane_sum",
    )(*arrays)


def full_sum_kernel(x_ref, out_ref, sib, low, recv, total, total_low, arrived, send, recv_sem):
    rows = out_ref.shape[0]
    greet(
        [{"ctx": partner(m)} for m in (1, 2, 4)] + [{"wt": ahead(d)} for d in (1, 2, 3)]
    )
    copies = Copies(send, recv_sem)
    wide = x_ref.shape[1]
    edges = [128 * (n * (wide // 128) // PARTS) for n in range(PARTS + 1)]
    parts = [slice(a, b) for a, b in zip(edges, edges[1:])]
    steps = [
        sum_steps(copies, x_ref, n, sib, low, recv, total, columns)
        for n, columns in enumerate(parts)
    ]

    def leave(n):
        total_low[:, parts[n]] = total[:, parts[n]].astype(bf16)
        for d in (2, 1, 3):
            copies.start(
                ("wt", n, d),
                total_low.at[pl.ds(pl.multiple_of(ahead(d) * rows, rows), rows), parts[n]],
                arrived.at[pl.ds((d - 1) * rows, rows), parts[n]],
                {"wt": ahead(d)},
            )

    def finish(n):
        own = pl.ds(pl.multiple_of(ahead(0) * rows, rows), rows)
        result = total[own, parts[n]]
        for d in (1, 3, 2):
            copies.arrived(("wt", n, d))
            result = result + arrived[(d - 1) * rows : d * rows, parts[n]].astype(f32)
        out_ref[:, parts[n]] = result

    for one in steps:
        one[0]()
    for n in range(PARTS + 2):
        if n < PARTS:
            steps[n][1]()
            steps[n][2]()
        if 1 <= n <= PARTS:
            steps[n - 1][3]()
        if n >= 2:
            steps[n - 2][4]()
            leave(n - 2)
    for n in range(PARTS):
        finish(n)
    copies.close()


def full_sum(x):
    rows, columns = x.shape[0] // 32, x.shape[1]
    vmem = pl.BlockSpec(memory_space=pltpu.VMEM)
    return pl.pallas_call(
        full_sum_kernel,
        in_specs=[vmem],
        out_specs=vmem,
        out_shape=jax.ShapeDtypeStruct((rows, columns), f32),
        scratch_shapes=[
            pltpu.VMEM((16 * rows, columns), bf16),
            pltpu.VMEM((12 * rows, columns), bf16),
            pltpu.VMEM((12 * rows, columns), bf16),
            pltpu.VMEM((4 * rows, columns), f32),
            pltpu.VMEM((4 * rows, columns), bf16),
            pltpu.VMEM((3 * rows, columns), bf16),
            pltpu.SemaphoreType.DMA((13 * PARTS,)),
            pltpu.SemaphoreType.DMA((13 * PARTS,)),
        ],
        compiler_params=pltpu.CompilerParams(
            collective_id=4, has_side_effects=True, vmem_limit_bytes=VMEM_LIMIT
        ),
        cost_estimate=SMALL,
        name="full_sum",
    )(x)


def shift(x, distance):
    n = lax.axis_size("wt")
    return lax.ppermute(x, "wt", [(i, (i + distance) % n) for i in range(n)])


def beside(results, *arrivals):
    out = lax.optimization_barrier((results, arrivals))
    return (out[0],) + tuple(out[1])


def gather_all(x):
    ctx, wt = lax.axis_size("ctx"), lax.axis_size("wt")
    if ctx != 8 or wt != 4:
        return [lax.all_gather(x, ALL, axis=0, tiled=True)], [1], jnp.zeros((1,), jnp.int32)
    ctx_index, wt_index = lax.axis_index("ctx"), lax.axis_index("wt")
    m = jnp.arange(8, dtype=jnp.int32)
    d = jnp.arange(4, dtype=jnp.int32)
    places = ((ctx_index ^ m) * wt)[:, None] + ((wt_index - d) % wt)[None, :]
    return [packed_gather(x)], [32], places.reshape(-1).astype(jnp.int32)


def outer_sum(pairs, extra):
    if lax.axis_size("ctx") != 8 or lax.axis_size("wt") != 4:
        parts = [dot_tn(a, b) for a, b in pairs] + [sum(dot_tn(a, b) for a, b in extra)]
        return lax.psum_scatter(
            jnp.concatenate(parts, 1).astype(bf16), ALL, scatter_dimension=0, tiled=True
        ).astype(f32)
    return full_sum(outer(pairs, extra))


def after(x, *others):
    return lax.optimization_barrier((x,) + others)[0]


def rope_tables(positions, width):
    middle = HEAD_SIZE // 2
    frequency = jnp.power(
        jnp.float32(rope_base), -2.0 * jnp.arange(middle, dtype=f32) / HEAD_SIZE
    )
    angles = positions.astype(f32)[:, None] * frequency[None, :]
    times = width // middle
    return jnp.tile(jnp.cos(angles), (1, times)), jnp.tile(jnp.sin(angles), (1, times))


def turn(values, cosine, sine, direction):
    middle = HEAD_SIZE // 2
    first = lax.broadcasted_iota(jnp.int32, values.shape, 1) % HEAD_SIZE < middle
    turned = jnp.where(first, -jnp.roll(values, -middle, 1), jnp.roll(values, middle, 1))
    width = values.shape[1]
    return values * cosine[:, :width] + direction * turned * sine[:, :width]


def norm_forward(values, gain):
    inverse = lax.rsqrt(jnp.mean(values * values, -1, keepdims=True) + norm_eps)
    return (values * inverse * gain, inverse)


def norm_backward(values, inverse, gain, grad_out):
    scaled = gain * grad_out
    gain_grad = (grad_out * values * inverse).astype(bf16)
    projection = jnp.mean(scaled * values, -1, keepdims=True)
    return (inverse * scaled - values * inverse * inverse * inverse * projection, gain_grad)


def per_device(
    layer_input,
    attention_gain,
    query_weight,
    key_matrix,
    value_matrix,
    output_weight,
    mixture_gain,
    router_weight,
    gate_weight,
    up_weight,
    down_weight,
    expert_routes,
    prompt_deal,
    output_grad,
):
    tok = layer_input.shape[1]
    prompt_local = tok - CONT_DEV * CLEN
    block_rows = prompt_local // 2
    context_size = lax.axis_size("ctx")
    shard_count = lax.axis_size("wt")
    expert_count = gate_weight.shape[0]
    capacity = 8 * ((tok * TOP * 7 // (4 * EXPERTS) + 7) // 8)
    ctx_index = lax.axis_index("ctx")
    wt_index = lax.axis_index("wt")
    inputs = layer_input[0].astype(f32)
    routes = expert_routes[0]
    deal_row = prompt_deal[0]
    out_low = output_grad[0]
    out_grad = out_low.astype(f32)

    own_rows = query_weight.shape[0]
    packed = jnp.concatenate(
        [
            query_weight,
            key_matrix,
            value_matrix,
            output_weight.T,
            router_weight,
            attention_gain[:, None],
            mixture_gain[:, None],
            jnp.zeros((own_rows, 94), bf16),
        ],
        1,
    )
    pieces, counts, block_places = gather_all(packed)

    gate_full = lax.all_gather(gate_weight, "ctx", axis=0, tiled=False)
    up_full = lax.all_gather(up_weight, "ctx", axis=0, tiled=False)
    down_full = lax.all_gather(down_weight, "ctx", axis=0, tiled=False)

    mask = jnp.any(
        routes[:, :, None] == jnp.arange(EXPERTS, dtype=jnp.int32)[None, None, :], 1
    )
    order = jnp.arange(tok, dtype=jnp.int32)
    before = (order[None, :] < order[:, None]).astype(bf16)
    rank = jnp.where(mask, dot(before, mask.astype(bf16)), -1.0)
    ranks = lax.all_to_all(
        rank.T.reshape(shard_count, expert_count, 1, tok), "wt", 0, 0, tiled=True
    )
    last = shard_count - 1
    grads_in = {0: out_low, last: shift(after(out_low, pieces[0], ranks), -1)}

    pieces, ranks = beside(pieces, ranks)
    local_rows = jnp.arange(tok, dtype=jnp.int32)
    mine = lax.dynamic_slice_in_dim(deal_row, 2 * ctx_index, 2, 0)
    prompt_place = (
        jnp.where(local_rows < block_rows, mine[0], mine[1]) * block_rows
        + local_rows % block_rows
    )
    positions = jnp.where(
        local_rows < prompt_local, prompt_place, PROMPT + (local_rows - prompt_local) % CLEN
    )
    cosine, sine = rope_tables(positions, 128)
    normed_one, turned_query, kv_low, qkv_full, output_t, rest, gain_rows = project(
        layer_input[0], cosine, sine, pieces, counts, block_places
    )
    router_full = rest[:, :EXPERTS]
    first_gain, second_gain = gain_rows[0], gain_rows[1]
    inverse_one = lax.rsqrt(jnp.mean(inputs * inputs, -1, keepdims=True) + norm_eps)
    kv_own = kv_low[prompt_local:]
    kv_pieces, grads_in[last] = beside([gather_ctx(kv_low, prompt_local)], grads_in[last])

    places = deal_row
    if context_size == 8:
        pairs = deal_row.reshape(2, 2, 2, 2)
        for axis, bit in ((0, 4), (1, 2), (2, 1)):
            pairs = jnp.where(ctx_index & bit > 0, jnp.flip(pairs, axis), pairs)
        places = pairs.reshape(-1)
    low = (mine[0] > mine[1]).astype(jnp.int32)
    starts = jnp.stack(
        [
            low * block_rows,
            (1 - low) * block_rows,
            jnp.min(mine) * block_rows,
            jnp.max(mine) * block_rows,
        ]
    ).astype(jnp.int32)
    heads = []
    for half in range(2):
        result = attention_forward(
            turned_query, kv_pieces, kv_own, places, starts, block_rows, half
        )
        d = last - 1 - half
        grads_in[d] = shift(grads_in[d + 1], -1)
        result, grads_in[d] = beside(result, grads_in[d])
        if half == 0:
            turned_query = after(turned_query, result[0])
        heads.append(result)
    for d in range(last - 3, 0, -1):
        grads_in[d] = shift(grads_in[d + 1], -1)
    attended = jnp.concatenate([out for out, _ in heads], 1)
    lse = [row for _, row in heads]

    branch = dot_nt(attended, output_t)
    middle = inputs + resid_scale * branch
    normed_mid, inverse_two = norm_forward(middle, second_gain)
    normed_two = normed_mid.astype(bf16)
    logits = dot(normed_two, router_full)
    top = jnp.max(jnp.where(mask, logits, masked_score), -1, keepdims=True)
    raised = jnp.where(mask, jnp.exp(jnp.where(mask, logits - top, 0.0)), 0.0)
    gates = raised / jnp.sum(raised, -1, keepdims=True)

    gates_out = gates.T.reshape(shard_count, expert_count, 1, tok)
    gates_in = []
    for d in range(shard_count):
        piece = lax.dynamic_index_in_dim(gates_out, (wt_index + d) % shard_count, 0, False)
        gates_in.append(shift(piece, d) if d else piece)
    got = {0: normed_two}
    partial, mixed, gate_grads, rows = {}, {}, {}, []
    carried = None

    def add(a, b):
        return b if a is None else (a.astype(f32) + b.astype(f32)).astype(bf16)

    for d in [0] + list(range(last, 0, -1)):
        source = (wt_index - d) % shard_count
        rank_in = lax.dynamic_index_in_dim(ranks, source, 0, False)
        result = expert_pass(
            got[d], grads_in[d], rank_in, gates_in[d], gate_full, up_full, down_full, capacity
        )
        coming = d - 1 if d else last
        if coming:
            result, got[coming] = beside(result, shift(got[(coming + 1) % shard_count], -1))
        if d == 0:
            result, gates_in = beside(result, gates_in)
        if 0 < d <= last - 2:
            carried = shift(after(add(carried, partial[d + 2]), got[d]), -1)
            result, carried = beside(result, carried)
        mixed[d], partial[d], d_gate, *kept = result
        rows.append(kept)
        gate_grads[d] = shift(d_gate, shard_count - d) if d else d_gate
        if coming:
            got[coming] = after(got[coming], partial[d])
    carried = shift(add(carried, partial[2]), -1)
    (gate_grad, up_grad), carried, gate_grads = beside(
        up_weight_grads([(after(r[0], partial[1]), r[3], r[4]) for r in rows], context_size),
        carried,
        gate_grads,
    )
    stacked = jnp.stack([gate_grads[d] for d in range(shard_count)], 0)
    for bit in (1, 2, 4):
        if bit < shard_count:
            stacked = jnp.where(wt_index & bit > 0, jnp.roll(stacked, bit, 0), stacked)
    stacked = stacked.reshape(EXPERTS, tok).T
    grad_logits = (gates * (stacked - jnp.sum(gates * stacked, -1, keepdims=True))).astype(bf16)
    carried = shift(add(carried, partial[1]), -1)
    down_grad, home = beside(
        down_weight_grads([(after(r[2], gate_grad, grad_logits), r[1]) for r in rows], context_size), carried
    )

    grad_normed_two = partial[0].astype(f32) + home.astype(f32)
    grad_normed_two = grad_normed_two + dot_nt(grad_logits, router_full)
    grad_mid_norm, second_gain_grad = norm_backward(
        middle, inverse_two, second_gain, grad_normed_two
    )
    grad_middle = out_grad + grad_mid_norm
    grad_branch = (resid_scale * grad_middle).astype(bf16)
    grad_attended = dot(grad_branch, output_t).astype(bf16)
    gate_share, up_share, down_share = (
        lax.psum_scatter(grad, "ctx", scatter_dimension=0, tiled=False).astype(f32)
        for grad in (gate_grad, up_grad, down_grad)
    )
    carried = None
    query = after(turned_query, grad_attended)
    d_query, d_kv, ours = [], [], []
    for half in range(2):
        result = attention_backward(
            query,
            grad_attended,
            lse[half],
            attended,
            cosine,
            sine,
            kv_pieces,
            kv_own,
            places,
            starts,
            block_rows,
            half,
        )
        carried = shift(after(add(carried, mixed[last - half]), home), -1)
        result, carried = beside(result, carried)
        query = after(query, result[0])
        d_query.append(result[0])
        d_kv.append(result[1])
        ours.append(result[2:])
    carried = shift(add(carried, mixed[last - 2]), -1)
    owned, carried = beside(plane_sum(d_kv), carried)
    for d in range(last - 3, 0, -1):
        carried = shift(add(carried, mixed[d]), -1)
    mixture = mixed[0].astype(f32) + carried.astype(f32)
    layer_output = (middle + resid_scale * mixture).astype(bf16)
    d_query = jnp.concatenate(d_query, 1)
    d_key, d_value = (
        jnp.concatenate(
            [
                jnp.concatenate([owned[half][:, 256 * n : 256 * n + 256], ours[half][n]], 0)
                for half in range(2)
            ],
            1,
        )
        for n in range(2)
    )
    grad_key_low = turn(d_key, jnp.tile(cosine, (1, 4)), jnp.tile(sine, (1, 4)), -1.0).astype(
        bf16
    )
    grad_kv = jnp.concatenate([grad_key_low, d_value.astype(bf16)], 1)
    grad_normed_one = dot_nt(d_query, qkv_full[:, :1024]) + dot_nt(grad_kv, qkv_full[:, 1024:])
    grad_input_norm, first_gain_grad = norm_backward(
        inputs, inverse_one, first_gain, grad_normed_one
    )
    input_grad = (grad_middle + grad_input_norm).astype(bf16)

    column = lax.broadcasted_iota(jnp.int32, (tok, 128), 1)
    shares = outer_sum(
        [(normed_one, d_query), (grad_branch, attended), (normed_one, grad_kv)],
        [
            (normed_two, jnp.pad(grad_logits, ((0, 0), (0, 128 - EXPERTS)))),
            (second_gain_grad, (column == EXPERTS).astype(bf16)),
            (first_gain_grad, (column == EXPERTS + 1).astype(bf16)),
        ],
    )
    return (
        layer_output[None],
        input_grad[None],
        shares[:, 3073 + EXPERTS],
        shares[:, :1024],
        shares[:, 2048 : 2048 + KV_WIDTH],
        shares[:, 2048 + KV_WIDTH : 3072],
        shares[:, 1024:2048].T,
        shares[:, 3072 + EXPERTS],
        shares[:, 3072 : 3072 + EXPERTS],
        gate_share,
        up_share,
        down_share,
    )


def solution(mesh):
    return jax.shard_map(
        per_device,
        mesh=mesh,
        in_specs=(
            P("wt", "ctx", None),
            P(("ctx", "wt")),
            P(("ctx", "wt"), None),
            P(("ctx", "wt"), None),
            P(("ctx", "wt"), None),
            P(None, ("ctx", "wt")),
            P(("ctx", "wt")),
            P(("ctx", "wt"), None),
            P("wt", "ctx", None),
            P("wt", "ctx", None),
            P("wt", None, "ctx"),
            P("wt", "ctx", None),
            P("wt", None),
            P("wt", "ctx", None),
        ),
        out_specs=(
            P("wt", "ctx", None),
            P("wt", "ctx", None),
            P(("ctx", "wt")),
            P(("ctx", "wt"), None),
            P(("ctx", "wt"), None),
            P(("ctx", "wt"), None),
            P(None, ("ctx", "wt")),
            P(("ctx", "wt")),
            P(("ctx", "wt"), None),
            P("wt", "ctx", None),
            P("wt", "ctx", None),
            P("wt", None, "ctx"),
        ),
        check_vma=False,
    )
```

```python
import functools

import jax
import jax.numpy as jnp
from jax import lax
from jax.experimental import pallas as pl
from jax.experimental.pallas import tpu as pltpu
from jax.sharding import PartitionSpec as P

MODEL_WIDTH = 1024
HQ = 16
KEY_VALUE_HEADS = 8
HEAD_SIZE = 64
EXPERTS = 32
TOP = 8
PROMPT = 2048
CLEN = 256
CONT_DEV = 2
FF = 512
QTILE = 128
PARTS = 2
KV_WIDTH = KEY_VALUE_HEADS * HEAD_SIZE
ALL = ("ctx", "wt")

att_scale = 0.015625
resid_scale = 0.22
norm_eps = 1e-06
rope_base = 10000.0
masked_score = -1e30

bf16 = jnp.bfloat16
f32 = jnp.float32
VMEM_LIMIT = 60 * 1024 * 1024
SMALL = pl.CostEstimate(flops=1_000_000_000, bytes_accessed=1_000_000, transcendentals=0)

NT = (((1,), (1,)), ((), ()))
TN = (((0,), (0,)), ((), ()))


def dot(a, b):
    return jnp.dot(a, b, preferred_element_type=f32)


def dot_nt(a, b):
    return lax.dot_general(a, b, NT, preferred_element_type=f32)


def dot_tn(a, b):
    return lax.dot_general(a, b, TN, preferred_element_type=f32)


def turn_tile(values, cosine, sine, direction):
    middle = HEAD_SIZE // 2
    first = lax.broadcasted_iota(jnp.int32, values.shape, 1) % HEAD_SIZE < middle
    turned = jnp.where(first, -pltpu.roll(values, 128 - middle, 1), pltpu.roll(values, middle, 1))
    return values * cosine + direction * turned * sine


def project_kernel(places, x_ref, cos_ref, sin_ref, *refs, counts):
    pieces = refs[: len(counts)]
    normed_ref, q_ref, kv_ref, qkv_ref, out_ref, rest_ref, gains_ref = refs[len(counts) :]
    rows = MODEL_WIDTH // sum(counts)
    at = 0
    for piece, count in zip(pieces, counts):
        for i in range(count):
            source = slice(i * rows, (i + 1) * rows)
            target = pl.ds(pl.multiple_of(places[at] * rows, rows), rows)
            qkv_ref[target, :] = piece[source, :2048]
            out_ref[target, :] = piece[source, 2048:3072]
            rest_ref[target, :] = piece[source, 3072:]
            at += 1
    gains = rest_ref[...].astype(f32).T[EXPERTS : EXPERTS + 8]
    gains_ref[...] = gains
    x = x_ref[...].astype(f32)
    inverse = lax.rsqrt(jnp.mean(x * x, -1, keepdims=True) + norm_eps)
    normed_ref[...] = (x * inverse * gains[:1]).astype(bf16)
    for c in range(8):
        raw = dot(normed_ref[...], qkv_ref[:, 256 * c : 256 * (c + 1)])
        for h in range(2):
            part = raw[:, 128 * h : 128 * (h + 1)]
            if c < 6:
                part = turn_tile(part, cos_ref[...], sin_ref[...], 1.0)
            column = 256 * c + 128 * h
            if column < 1024:
                q_ref[:, column : column + 128] = part.astype(bf16)
            else:
                column -= 1024
                at = column % KV_WIDTH // 256 * 512 + column // KV_WIDTH * 256 + column % 256
                kv_ref[:, at : at + 128] = part.astype(bf16)


def project(x, cosine, sine, pieces, counts, places):
    tok = x.shape[0]
    shape = jax.ShapeDtypeStruct
    whole = pl.BlockSpec(memory_space=pltpu.VMEM)
    return pl.pallas_call(
        functools.partial(project_kernel, counts=counts),
        in_specs=[pl.BlockSpec(memory_space=pltpu.SMEM)] + [whole] * (3 + len(pieces)),
        out_specs=[whole] * 7,
        out_shape=[
            shape((tok, MODEL_WIDTH), bf16),
            shape((tok, HQ * HEAD_SIZE), bf16),
            shape((tok, 2 * KV_WIDTH), bf16),
            shape((MODEL_WIDTH, 2048), bf16),
            shape((MODEL_WIDTH, 1024), bf16),
            shape((MODEL_WIDTH, 128), bf16),
            shape((8, MODEL_WIDTH), f32),
        ],
        compiler_params=pltpu.CompilerParams(vmem_limit_bytes=VMEM_LIMIT),
        cost_estimate=SMALL,
        name="project",
    )(places, x, cosine, sine, *pieces)


def middle_kernel(
    a_ref, b_ref, x_ref, out_ref, rest_ref, gains_ref, mask_ref, middle_ref, normed_ref, inv_ref, gates_ref
):
    half = a_ref.shape[1]
    branch = dot_nt(a_ref[...], out_ref[:, :half]) + dot_nt(b_ref[...], out_ref[:, half:])
    middle = x_ref[...].astype(f32) + resid_scale * branch
    middle_ref[...] = middle
    inverse = lax.rsqrt(jnp.mean(middle * middle, -1, keepdims=True) + norm_eps)
    inv_ref[...] = inverse
    normed = (middle * inverse * gains_ref[1:2]).astype(bf16)
    normed_ref[...] = normed
    mask = mask_ref[...] > 0.0
    logits = jnp.where(mask, dot(normed, rest_ref[...]), masked_score)
    top = jnp.max(logits, -1, keepdims=True)
    raised = jnp.where(mask, jnp.exp(logits - top), 0.0)
    gates_ref[...] = (raised / jnp.sum(raised, -1, keepdims=True)).T[:EXPERTS]


def to_gates(halves, x, output_t, rest, gain_rows, mask):
    tok = x.shape[0]
    shape = jax.ShapeDtypeStruct
    whole = pl.BlockSpec(memory_space=pltpu.VMEM)
    return pl.pallas_call(
        middle_kernel,
        in_specs=[whole] * 7,
        out_specs=[whole] * 4,
        out_shape=[
            shape((tok, MODEL_WIDTH), f32),
            shape((tok, MODEL_WIDTH), bf16),
            shape((tok, 1), f32),
            shape((EXPERTS, tok), f32),
        ],
        compiler_params=pltpu.CompilerParams(vmem_limit_bytes=VMEM_LIMIT),
        cost_estimate=SMALL,
        name="to_gates",
    )(*halves, x, output_t, rest, gain_rows, mask)


def outer_kernel(mine, *refs, count):
    out_ref = refs[-1]
    pairs = [(refs[n], refs[n + 1]) for n in range(0, len(refs) - 1, 2)]
    at = 0
    for a_ref, b_ref in pairs[:count]:
        columns = b_ref.shape[1]
        out_ref[:, at : at + columns] = dot_tn(a_ref[...], b_ref[...]).astype(bf16)
        at += columns
    if pairs[count:]:
        out_ref[:, at:] = sum(dot_tn(a[...], b[...]) for a, b in pairs[count:]).astype(bf16)


def outer(pairs, extra=()):
    tok = pairs[0][0].shape[0]
    mine = lax.axis_index("ctx").astype(jnp.int32).reshape(1)
    specs = []
    everything = [*pairs, *extra]
    for _, b in everything:
        specs.append(pl.BlockSpec((tok, 128), lambda m, mine: (0, m ^ mine[0])))
        specs.append(pl.BlockSpec(b.shape, lambda m, mine: (0, 0)))
    columns = sum(b.shape[1] for _, b in [*pairs, *extra[:1]])
    return pl.pallas_call(
        functools.partial(outer_kernel, count=len(pairs)),
        grid_spec=pltpu.PrefetchScalarGridSpec(
            num_scalar_prefetch=1,
            grid=(8,),
            in_specs=specs,
            out_specs=pl.BlockSpec((128, columns), lambda m, mine: (m, 0)),
        ),
        out_shape=jax.ShapeDtypeStruct((MODEL_WIDTH, columns), bf16),
        compiler_params=pltpu.CompilerParams(vmem_limit_bytes=VMEM_LIMIT),
        cost_estimate=SMALL,
        name="outer",
    )(mine, *[x for pair in everything for x in pair])


def gather_keys(pieces, scratch, places, block_rows):
    at = 0
    for piece in pieces:
        for b in range(piece.shape[0] // block_rows):
            start = pl.multiple_of(places[at] * block_rows, block_rows)
            scratch[pl.ds(start, block_rows), :] = piece[b * block_rows : (b + 1) * block_rows, :]
            at += 1


def pair_rows(ref, start, rows, j):
    both = ref[pl.ds(start, rows), 2 * HEAD_SIZE * j : 2 * HEAD_SIZE * (j + 1)]
    return jnp.concatenate([both[:, :HEAD_SIZE], both[:, HEAD_SIZE:]], 0)


def attention_forward_kernel(places, starts, q_ref, *refs, block_rows, pieces):
    k_refs, v_refs = refs[:pieces], refs[pieces : 2 * pieces]
    kc_ref, vc_ref, o_ref, lse_ref, k_scr, v_scr = refs[2 * pieces :]
    prompt_local = 2 * block_rows
    gather_keys(k_refs, k_scr, places, block_rows)
    gather_keys(v_refs, v_scr, places, block_rows)

    def store(start, rows, j, out, m, total, at):
        out = (out / total).astype(bf16)
        lse = m + jnp.log(total)
        o_ref[pl.ds(start, rows), 2 * HEAD_SIZE * j : 2 * HEAD_SIZE * (j + 1)] = jnp.concatenate(
            [out[:rows], out[rows:]], 1
        )
        row = jnp.broadcast_to(lse, (2 * rows, 128)).T[:1]
        lse_ref[0, 2 * j : 2 * j + 2, pl.ds(at, rows)] = jnp.concatenate(
            [row[:, :rows], row[:, rows:]], 0
        )

    def tile(i, _):
        start = pl.multiple_of(prompt_local + i * QTILE, 64)
        per = CLEN // QTILE
        seg = pl.multiple_of((i // per) * CLEN, CLEN)
        for j in range(2):
            lanes = slice(HEAD_SIZE * j, HEAD_SIZE * (j + 1))
            q = pair_rows(q_ref, start, QTILE, j) * bf16(att_scale)
            s1 = dot_nt(q, k_scr[:, lanes])
            s2 = dot_nt(q, kc_ref[pl.ds(seg, CLEN), lanes])
            place = lax.broadcasted_iota(jnp.int32, s2.shape, 0) % QTILE + (i % per) * QTILE
            s2 = jnp.where(lax.broadcasted_iota(jnp.int32, s2.shape, 1) <= place, s2, masked_score)
            m = jnp.maximum(jnp.max(s1, 1, keepdims=True), jnp.max(s2, 1, keepdims=True))
            e1 = jnp.exp(s1 - m)
            e2 = jnp.exp(s2 - m)
            total = jnp.sum(e1, 1, keepdims=True) + jnp.sum(e2, 1, keepdims=True)
            out = dot(e1.astype(bf16), v_scr[:, lanes])
            out = out + dot(e2.astype(bf16), vc_ref[pl.ds(seg, CLEN), lanes])
            store(start, QTILE, j, out, m, total, pl.multiple_of(i * QTILE, QTILE))
        return 0

    lax.fori_loop(0, CONT_DEV * CLEN // QTILE, tile, 0)

    for half, keys in enumerate((PROMPT // 2, PROMPT)):
        start = pl.multiple_of(starts[half], block_rows)
        for j in range(2):
            lanes = slice(HEAD_SIZE * j, HEAD_SIZE * (j + 1))
            q = pair_rows(q_ref, start, block_rows, j) * bf16(att_scale)
            s = dot_nt(q, k_scr[:keys, lanes])
            place = lax.broadcasted_iota(jnp.int32, s.shape, 0) % block_rows + starts[2 + half]
            s = jnp.where(lax.broadcasted_iota(jnp.int32, s.shape, 1) <= place, s, masked_score)
            m = jnp.max(s, 1, keepdims=True)
            e = jnp.exp(s - m)
            total = jnp.sum(e, 1, keepdims=True)
            out = dot(e.astype(bf16), v_scr[:keys, lanes])
            store(start, block_rows, j, out, m, total, CONT_DEV * CLEN + half * block_rows)


def key_specs(pieces, own, half):
    spec = pl.BlockSpec
    key, value = (lambda g, *_: (0, 4 * half + g)), (lambda g, *_: (0, 4 * half + 2 + g))
    keys = [spec((p.shape[0], 128), key) for p in pieces]
    values = [spec((p.shape[0], 128), value) for p in pieces]
    return keys + values + [spec((own, 128), key), spec((own, 128), value)]


def attention_forward(q, pieces, kv_own, places, starts, block_rows, half):
    tok = q.shape[0]
    spec = pl.BlockSpec
    return pl.pallas_call(
        functools.partial(
            attention_forward_kernel, block_rows=block_rows, pieces=len(pieces)
        ),
        grid_spec=pltpu.PrefetchScalarGridSpec(
            num_scalar_prefetch=2,
            grid=(2,),
            in_specs=[spec((tok, 256), lambda g, *_: (0, 2 * half + g))]
            + key_specs(pieces, kv_own.shape[0], half),
            out_specs=[
                spec((tok, 256), lambda g, *_: (0, g)),
                spec((1, 4, tok), lambda g, *_: (g, 0, 0)),
            ],
            scratch_shapes=[
                pltpu.VMEM((PROMPT, 2 * HEAD_SIZE), bf16),
                pltpu.VMEM((PROMPT, 2 * HEAD_SIZE), bf16),
            ],
        ),
        out_shape=[
            jax.ShapeDtypeStruct((tok, HQ * HEAD_SIZE // 2), bf16),
            jax.ShapeDtypeStruct((2, 4, tok), f32),
        ],
        compiler_params=pltpu.CompilerParams(vmem_limit_bytes=VMEM_LIMIT),
        cost_estimate=SMALL,
        name="attention_forward",
    )(places, starts, q, *pieces, *pieces, kv_own, kv_own)


def attention_backward_kernel(
    places, starts, q_ref, do_ref, lse_ref, o_ref, cos_ref, sin_ref, *refs, block_rows, pieces
):
    k_refs, v_refs = refs[:pieces], refs[pieces : 2 * pieces]
    kc_ref, vc_ref, dq_ref, dkv_ref, dkc_ref, dvc_ref = refs[2 * pieces : 2 * pieces + 6]
    k_scr, v_scr, dk_acc, dv_acc, dq_acc = refs[2 * pieces + 6 :]
    prompt_local = 2 * block_rows
    gather_keys(k_refs, k_scr, places, block_rows)
    gather_keys(v_refs, v_scr, places, block_rows)
    dk_acc[...] = jnp.zeros_like(dk_acc)
    dv_acc[...] = jnp.zeros_like(dv_acc)
    dkc_ref[...] = jnp.zeros_like(dkc_ref)
    dvc_ref[...] = jnp.zeros_like(dvc_ref)

    def row_pair(ref, start, rows, j):
        both = ref[0, 2 * j : 2 * j + 2, pl.ds(start, rows)]
        return jnp.concatenate([both[:1], both[1:]], 1)

    def centre(start, rows, j, d_out):
        product = d_out.astype(f32) * pair_rows(o_ref, start, rows, j).astype(f32)
        ones = jnp.ones((8, HEAD_SIZE), f32)
        return lax.dot_general(
            ones, product, NT, precision=lax.Precision.HIGHEST, preferred_element_type=f32
        )[:1]

    def part(k, v, q, d_out, lse, delta, allowed):
        s = dot_nt(k, q)
        if allowed is not None:
            s = jnp.where(allowed(s.shape), s, masked_score)
        p = jnp.exp(s - lse)
        d_p = dot_nt(v, d_out)
        d_s = (p * (d_p - delta)).astype(bf16)
        return dot_tn(d_s, k), dot(d_s, q), dot(p.astype(bf16), d_out)

    def store(start, rows, j, d_q):
        d_q = d_q * att_scale
        dq_acc[pl.ds(start, rows), 2 * HEAD_SIZE * j : 2 * HEAD_SIZE * (j + 1)] = jnp.concatenate(
            [d_q[:rows], d_q[rows:]], 1
        )

    def tile(i, _):
        start = pl.multiple_of(prompt_local + i * QTILE, 64)
        per = CLEN // QTILE
        seg = pl.multiple_of((i // per) * CLEN, CLEN)
        own = pl.ds(seg, CLEN)
        lane_start = pl.multiple_of(i * QTILE, QTILE)

        def allowed(shape):
            place = lax.broadcasted_iota(jnp.int32, shape, 1) % QTILE + (i % per) * QTILE
            return lax.broadcasted_iota(jnp.int32, shape, 0) <= place

        for j in range(2):
            lanes = slice(HEAD_SIZE * j, HEAD_SIZE * (j + 1))
            q = pair_rows(q_ref, start, QTILE, j) * bf16(att_scale)
            d_out = pair_rows(do_ref, start, QTILE, j)
            lse = row_pair(lse_ref, lane_start, QTILE, j)
            delta = centre(start, QTILE, j, d_out)
            a, b, c = part(k_scr[:, lanes], v_scr[:, lanes], q, d_out, lse, delta, None)
            dk_acc[:, lanes] += b
            dv_acc[:, lanes] += c
            d_q = a
            a, b, c = part(
                kc_ref[own, lanes], vc_ref[own, lanes], q, d_out, lse, delta, allowed
            )
            dkc_ref[own, lanes] += b
            dvc_ref[own, lanes] += c
            store(start, QTILE, j, d_q + a)
        return 0

    lax.fori_loop(0, CONT_DEV * CLEN // QTILE, tile, 0)

    for half, keys in enumerate((PROMPT // 2, PROMPT)):
        start = pl.multiple_of(starts[half], block_rows)
        at = CONT_DEV * CLEN + half * block_rows

        def allowed(shape):
            place = lax.broadcasted_iota(jnp.int32, shape, 1) % block_rows + starts[2 + half]
            return lax.broadcasted_iota(jnp.int32, shape, 0) <= place

        for j in range(2):
            lanes = slice(HEAD_SIZE * j, HEAD_SIZE * (j + 1))
            q = pair_rows(q_ref, start, block_rows, j) * bf16(att_scale)
            d_out = pair_rows(do_ref, start, block_rows, j)
            lse = row_pair(lse_ref, at, block_rows, j)
            delta = centre(start, block_rows, j, d_out)
            a, b, c = part(
                k_scr[:keys, lanes], v_scr[:keys, lanes], q, d_out, lse, delta, allowed
            )
            dk_acc[:keys, lanes] += b
            dv_acc[:keys, lanes] += c
            store(start, block_rows, j, a)

    g = pl.program_id(0)
    key_lanes = pl.ds(pl.multiple_of(g * 128, 128), 128)
    value_lanes = pl.ds(pl.multiple_of(256 + g * 128, 128), 128)
    for b in range(PROMPT // block_rows):
        source = pl.ds(pl.multiple_of(places[b] * block_rows, block_rows), block_rows)
        rows = slice(b * block_rows, (b + 1) * block_rows)
        dkv_ref[rows, key_lanes] = dk_acc[source, :].astype(bf16)
        dkv_ref[rows, value_lanes] = dv_acc[source, :].astype(bf16)
    for c in range(2):
        lanes = slice(128 * c, 128 * (c + 1))
        dq_ref[:, lanes] = turn_tile(dq_acc[:, lanes], cos_ref[...], sin_ref[...], -1.0).astype(
            bf16
        )


def attention_backward(
    q, d_out, lse, attended, cosine, sine, pieces, kv_own, places, starts, block_rows, half
):
    tok = q.shape[0]
    own = kv_own.shape[0]
    spec = pl.BlockSpec
    wide = spec((tok, 256), lambda g, *_: (0, 2 * half + g))
    narrow = spec((tok, 256), lambda g, *_: (0, g))
    ours = spec((own, 128), lambda g, *_: (0, g))
    table = spec((tok, 128), lambda g, *_: (0, 0))
    return pl.pallas_call(
        functools.partial(
            attention_backward_kernel, block_rows=block_rows, pieces=len(pieces)
        ),
        grid_spec=pltpu.PrefetchScalarGridSpec(
            num_scalar_prefetch=2,
            grid=(2,),
            in_specs=[wide, wide, spec((1, 4, tok), lambda g, *_: (g, 0, 0)), narrow, table, table]
            + key_specs(pieces, own, half),
            out_specs=[
                spec((tok, 256), lambda g, *_: (0, g)),
                spec((PROMPT, KV_WIDTH), lambda g, *_: (0, 0)),
                ours,
                ours,
            ],
            scratch_shapes=[
                pltpu.VMEM((PROMPT, 2 * HEAD_SIZE), bf16),
                pltpu.VMEM((PROMPT, 2 * HEAD_SIZE), bf16),
                pltpu.VMEM((PROMPT, 2 * HEAD_SIZE), f32),
                pltpu.VMEM((PROMPT, 2 * HEAD_SIZE), f32),
                pltpu.VMEM((tok, 4 * HEAD_SIZE), f32),
            ],
        ),
        out_shape=[
            jax.ShapeDtypeStruct((tok, HQ * HEAD_SIZE // 2), bf16),
            jax.ShapeDtypeStruct((PROMPT, KV_WIDTH), bf16),
            jax.ShapeDtypeStruct((own, KV_WIDTH // 2), f32),
            jax.ShapeDtypeStruct((own, KV_WIDTH // 2), f32),
        ],
        compiler_params=pltpu.CompilerParams(vmem_limit_bytes=VMEM_LIMIT),
        cost_estimate=SMALL,
        name="attention_backward",
    )(places, starts, q, d_out, lse, attended, cosine, sine, *pieces, *pieces, kv_own, kv_own)


def expert_kernel(
    counts,
    a2_ref,
    df_ref,
    rank_ref,
    gate_ref,
    wg_ref,
    wu_ref,
    wd_ref,
    mix_ref,
    da_ref,
    dg_ref,
    x_ref,
    dy_ref,
    z_ref,
    dgate_ref,
    dup_ref,
    mix_acc,
    da_acc,
    *,
    sizes,
):
    e = pl.program_id(0)

    @pl.when(e == 0)
    def _():
        mix_acc[...] = jnp.zeros_like(mix_acc)
        da_acc[...] = jnp.zeros_like(da_acc)

    def body(size):
        rank = rank_ref[0]
        gates = gate_ref[0]
        tok = rank.shape[1]
        slot = lax.broadcasted_iota(jnp.int32, (size, tok), 0).astype(f32)
        hit = slot == rank
        chosen = hit.astype(f32).astype(bf16)
        gate = jnp.sum(jnp.where(hit, gates, 0.0), 1, keepdims=True)
        x = dot(chosen, a2_ref[...]).astype(bf16)
        d_mix = resid_scale * dot(chosen, df_ref[...])
        wg = wg_ref[:, 0].reshape(MODEL_WIDTH, FF)
        wu = wu_ref[:, 0].reshape(MODEL_WIDTH, FF)
        wd = jnp.concatenate([wd_ref[c, 0] for c in range(wd_ref.shape[0])], 1)
        g = dot(x, wg)
        u = dot(x, wu)
        sig = jax.nn.sigmoid(g)
        z = (g * sig * u).astype(bf16)
        y = dot(z, wd).astype(bf16).astype(f32)
        d_gate_value = jnp.sum(d_mix * y, 1, keepdims=True)
        dg_ref[0] = jnp.sum(jnp.where(hit, d_gate_value, 0.0), 0, keepdims=True)
        mix_acc[...] += dot_tn(chosen, (gate * y).astype(bf16))
        d_y = (gate * d_mix).astype(bf16)
        d_z = dot_nt(d_y, wd)
        d_g = (d_z * u * sig * (1.0 + g * (1.0 - sig))).astype(bf16)
        d_u = (d_z * g * sig).astype(bf16)
        d_r = (dot_nt(d_g, wg) + dot_nt(d_u, wu)).astype(bf16)
        da_acc[...] += dot_tn(chosen, d_r)
        for ref, value in (
            (x_ref, x),
            (dy_ref, d_y),
            (z_ref, z),
            (dgate_ref, d_g),
            (dup_ref, d_u),
        ):
            ref[0, :size] = value
            if size < ref.shape[1]:
                ref[0, size:] = jnp.zeros((ref.shape[1] - size, ref.shape[2]), bf16)

    least = -1
    for size in sizes:
        pl.when((counts[e] > least) & (counts[e] <= size))(functools.partial(body, size))
        least = size

    @pl.when(e == pl.num_programs(0) - 1)
    def _():
        mix_ref[...] = mix_acc[...].astype(bf16)
        da_ref[...] = da_acc[...].astype(bf16)


def expert_pass(a2, df, rank, gates, wg, wu, wd, capacity):
    tok = a2.shape[0]
    parts, experts = wg.shape[0], wg.shape[1]
    sizes = sorted({min(size, capacity) for size in (128, 192, 256, capacity)})
    counts = (jnp.max(rank, (1, 2)) + 1.0).astype(jnp.int32)
    spec = pl.BlockSpec
    whole = spec((tok, MODEL_WIDTH), lambda e, *_: (0, 0))
    row = spec((1, 1, tok), lambda e, *_: (e, 0, 0))
    up = spec((parts, 1, MODEL_WIDTH // parts, FF), lambda e, *_: (0, e, 0, 0))
    down = spec((parts, 1, FF, MODEL_WIDTH // parts), lambda e, *_: (0, e, 0, 0))
    rows_wide = spec((1, capacity, MODEL_WIDTH), lambda e, *_: (e, 0, 0))
    rows_thin = spec((1, capacity, FF), lambda e, *_: (e, 0, 0))
    shape = jax.ShapeDtypeStruct
    return pl.pallas_call(
        functools.partial(expert_kernel, sizes=sizes),
        grid_spec=pltpu.PrefetchScalarGridSpec(
            num_scalar_prefetch=1,
            grid=(experts,),
            in_specs=[whole, whole, row, row, up, up, down],
            out_specs=[whole, whole, row, rows_wide, rows_wide, rows_thin, rows_thin, rows_thin],
            scratch_shapes=[
                pltpu.VMEM((tok, MODEL_WIDTH), f32),
                pltpu.VMEM((tok, MODEL_WIDTH), f32),
            ],
        ),
        out_shape=[
            shape((tok, MODEL_WIDTH), bf16),
            shape((tok, MODEL_WIDTH), bf16),
            shape((experts, 1, tok), f32),
            shape((experts, capacity, MODEL_WIDTH), bf16),
            shape((experts, capacity, MODEL_WIDTH), bf16),
            shape((experts, capacity, FF), bf16),
            shape((experts, capacity, FF), bf16),
            shape((experts, capacity, FF), bf16),
        ],
        compiler_params=pltpu.CompilerParams(vmem_limit_bytes=VMEM_LIMIT),
        cost_estimate=SMALL,
        name="expert_pass",
    )(counts, a2, df, rank, gates, wg, wu, wd)


def up_grad_kernel(*refs, sources):
    rows = refs[: 3 * sources]
    gate_ref, up_ref = refs[3 * sources :]
    for n, out_ref in ((1, gate_ref), (2, up_ref)):
        total = None
        for s in range(sources):
            term = dot_tn(rows[3 * s][0], rows[3 * s + n][0])
            total = term if total is None else total + term
        out_ref[...] = total.astype(bf16).reshape(out_ref.shape)


def down_grad_kernel(*refs, sources, parts):
    rows, down_ref = refs[: 2 * sources], refs[-1]
    width = MODEL_WIDTH // parts
    total = None
    for s in range(sources):
        term = dot_tn(rows[2 * s][0], rows[2 * s + 1][0])
        total = term if total is None else total + term
    total = total.astype(bf16)
    for c in range(parts):
        down_ref[c, 0] = total[:, c * width : (c + 1) * width]


def row_specs(rows):
    return [pl.BlockSpec((1,) + a.shape[1:], lambda e: (e, 0, 0)) for r in rows for a in r]


def up_weight_grads(rows, parts):
    experts = rows[0][0].shape[0]
    shape = (parts, experts, MODEL_WIDTH // parts, FF)
    out = pl.BlockSpec((parts, 1) + shape[2:], lambda e: (0, e, 0, 0))
    return pl.pallas_call(
        functools.partial(up_grad_kernel, sources=len(rows)),
        grid=(experts,),
        in_specs=row_specs(rows),
        out_specs=[out, out],
        out_shape=[jax.ShapeDtypeStruct(shape, bf16)] * 2,
        compiler_params=pltpu.CompilerParams(vmem_limit_bytes=VMEM_LIMIT),
        cost_estimate=SMALL,
        name="up_weight_grads",
    )(*[a for r in rows for a in r])


def down_weight_grads(rows, parts):
    experts = rows[0][0].shape[0]
    shape = (parts, experts, FF, MODEL_WIDTH // parts)
    return pl.pallas_call(
        functools.partial(down_grad_kernel, sources=len(rows), parts=parts),
        grid=(experts,),
        in_specs=row_specs(rows),
        out_specs=pl.BlockSpec((parts, 1) + shape[2:], lambda e: (0, e, 0, 0)),
        out_shape=jax.ShapeDtypeStruct(shape, bf16),
        compiler_params=pltpu.CompilerParams(vmem_limit_bytes=VMEM_LIMIT),
        cost_estimate=SMALL,
        name="down_weight_grads",
    )(*[a for r in rows for a in r])


def swap(x, mask):
    return lax.ppermute(x, "ctx", [(i, i ^ mask) for i in range(lax.axis_size("ctx"))])


def gather_ctx(x, rows):
    if lax.axis_size("ctx") != 8:
        return lax.all_gather(x[:rows], "ctx", axis=0, tiled=True)
    return plane_gather(x, rows)


MESH = pl.DeviceIdType.MESH
ANY = pl.BlockSpec(memory_space=pl.ANY)


def partner(mask):
    me = lax.axis_index("ctx")
    return me + mask - 2 * mask * ((me // mask) % 2)


def ahead(distance):
    return (lax.axis_index("wt") + distance) % lax.axis_size("wt")


class Copies:
    def __init__(self, send, recv):
        self.send, self.recv, self.made = send, recv, {}

    def start(self, name, source, target, device):
        n = len(self.made)
        self.made[name] = copy = pltpu.make_async_remote_copy(
            src_ref=source,
            dst_ref=target,
            send_sem=self.send.at[n],
            recv_sem=self.recv.at[n],
            device_id=device,
            device_id_type=MESH,
        )
        copy.start()

    def arrived(self, name):
        self.made[name].wait_recv()

    def close(self):
        for copy in self.made.values():
            copy.wait_send()


def greet(devices):
    barrier = pltpu.get_barrier_semaphore()
    for device in devices:
        pl.semaphore_signal(barrier, inc=1, device_id=device, device_id_type=MESH)
    pl.semaphore_wait(barrier, len(devices))


def plane_steps(copies, block, half, key):
    side, near, far = ({"ctx": partner(m)} for m in (1, 2, 4))
    top, end = (lambda m: block(m, 0, half)), (lambda m: block(m, half, half))

    def first():
        copies.start((key, 2), block(0), block(2), near)
        copies.start((key, 4), block(0), block(4), far)
        copies.start((key, 1), block(0), block(1), side)

    def second():
        copies.arrived((key, 2))
        copies.start((key, 6), top(2), top(6), far)
        copies.start((key, 3), block(2), block(3), side)

    def third():
        copies.arrived((key, 4))
        copies.start((key, 7), end(4), end(6), near)
        copies.start((key, 5), block(4), block(5), side)

    def fourth():
        copies.arrived((key, 6))
        copies.arrived((key, 7))
        copies.start((key, 8), block(6), block(7), side)

    def last():
        for m in (1, 3, 5, 8):
            copies.arrived((key, m))

    return [first, second, third, fourth, last]


def plane_gather_kernel(x_ref, out_ref, send, recv, own_sem):
    rows = out_ref.shape[0] // 8
    greet([{"ctx": partner(m)} for m in (1, 2, 4)])
    own = pltpu.make_async_copy(x_ref.at[pl.ds(0, rows)], out_ref.at[pl.ds(0, rows)], own_sem)
    own.start()
    copies = Copies(send, recv)

    def block(m, start=0, count=rows):
        if m == 0:
            return x_ref.at[pl.ds(start, count)]
        return out_ref.at[pl.ds(m * rows + start, count)]

    for step in plane_steps(copies, block, rows // 2, 0):
        step()
    own.wait()
    copies.close()


def plane_gather(x, rows):
    return pl.pallas_call(
        plane_gather_kernel,
        in_specs=[ANY],
        out_specs=ANY,
        out_shape=jax.ShapeDtypeStruct((8 * rows, x.shape[1]), x.dtype),
        scratch_shapes=[
            pltpu.SemaphoreType.DMA((8,)),
            pltpu.SemaphoreType.DMA((8,)),
            pltpu.SemaphoreType.DMA,
        ],
        compiler_params=pltpu.CompilerParams(collective_id=1, has_side_effects=True),
        cost_estimate=SMALL,
        name="plane_gather",
    )(x)


def packed_gather_kernel(x_ref, out_ref, send, recv, own_sem):
    rows = x_ref.shape[0]
    greet(
        [{"ctx": partner(m)} for m in (1, 2, 4)] + [{"wt": ahead(d)} for d in (1, 2, 3)]
    )
    own = pltpu.make_async_copy(x_ref, out_ref.at[pl.ds(0, rows)], own_sem)
    own.start()
    copies = Copies(send, recv)

    def block_of(d):
        def block(m, start=0, count=rows):
            if m == 0 and d == 0:
                return x_ref.at[pl.ds(start, count)]
            return out_ref.at[pl.ds((4 * m + d) * rows + start, count)]

        return block

    for d in (1, 3, 2):
        copies.start(d, x_ref, block_of(d)(0), {"wt": ahead(d)})
    steps = {d: plane_steps(copies, block_of(d), rows // 2, ("plane", d)) for d in range(4)}
    steps[0][0]()
    for d, before in ((1, 0), (3, 1), (2, 3)):
        copies.arrived(d)
        steps[d][0]()
        steps[before][1]()
        steps[before][2]()
        if d != 1:
            steps[{3: 0, 2: 1}[d]][3]()
    steps[2][1]()
    steps[2][2]()
    steps[3][3]()
    steps[2][3]()
    for d in range(4):
        steps[d][4]()
    own.wait()
    copies.close()


def packed_gather(x):
    return pl.pallas_call(
        packed_gather_kernel,
        in_specs=[ANY],
        out_specs=ANY,
        out_shape=jax.ShapeDtypeStruct((32 * x.shape[0], x.shape[1]), x.dtype),
        scratch_shapes=[
            pltpu.SemaphoreType.DMA((35,)),
            pltpu.SemaphoreType.DMA((35,)),
            pltpu.SemaphoreType.DMA,
        ],
        compiler_params=pltpu.CompilerParams(collective_id=2, has_side_effects=True),
        cost_estimate=SMALL,
        name="packed_gather",
    )(x)


def sum_steps(copies, x_ref, key, sib, low, recv, out_ref, columns):
    rows = x_ref.shape[0] // 8
    half = rows // 2
    side, near, far = ({"ctx": partner(m)} for m in (1, 2, 4))

    def blocks(ref, m, start=0, count=rows):
        return ref.at[pl.ds(m * rows + start, count), columns]

    def added(m, start, count):
        ours = x_ref[m * rows + start : m * rows + start + count, columns].astype(f32)
        at = m // 2 * rows + start
        return ours + sib[at : at + count, columns].astype(f32)

    def put(place, start, value, device):
        at = place * rows + start
        low[at : at + half, columns] = value.astype(bf16)
        copies.start(
            (key, "low", place, start),
            blocks(low, place, start, half),
            blocks(recv, place, start, half),
            device,
        )

    def first():
        for m in (7, 3, 5, 1):
            copies.start((key, m), blocks(x_ref, m), blocks(sib, m // 2), side)

    def second():
        copies.arrived((key, 7))
        put(0, 0, added(6, 0, half), far)
        put(0, half, added(6, half, half), near)

    def third():
        copies.arrived((key, 3))
        put(1, half, added(2, half, half), near)
        copies.arrived((key, 5))
        put(2, 0, added(4, 0, half), far)

    def fourth():
        copies.arrived((key, "low", 0, 0))
        put(1, 0, added(2, 0, half) + recv[0:half, columns].astype(f32), near)
        copies.arrived((key, "low", 0, half))
        put(2, half, added(4, half, half) + recv[half:rows, columns].astype(f32), far)

    def last():
        copies.arrived((key, 1))
        for place in (1, 2):
            for start in (0, half):
                copies.arrived((key, "low", place, start))
        out_ref[:, columns] = (
            added(0, 0, rows)
            + recv[rows : 2 * rows, columns].astype(f32)
            + recv[2 * rows :, columns].astype(f32)
        )

    return [first, second, third, fourth, last]


def plane_sum_kernel(*refs, sets):
    x_refs, out_refs = refs[:sets], refs[sets : 2 * sets]
    sibs, lows, recvs = (refs[(2 + n) * sets : (3 + n) * sets] for n in range(3))
    send, recv_sem = refs[5 * sets :]
    greet([{"ctx": partner(m)} for m in (1, 2, 4)])
    copies = Copies(send, recv_sem)
    steps = [
        sum_steps(
            copies, x_refs[n], n, sibs[n], lows[n], recvs[n], out_refs[n], slice(None)
        )
        for n in range(sets)
    ]
    for n in range(5):
        for one in steps:
            one[n]()
    copies.close()


def plane_sum(arrays):
    sets = len(arrays)
    shapes = [(x.shape[0] // 8, x.shape[1]) for x in arrays]
    vmem = pl.BlockSpec(memory_space=pltpu.VMEM)
    return pl.pallas_call(
        functools.partial(plane_sum_kernel, sets=sets),
        in_specs=[vmem] * sets,
        out_specs=[vmem] * sets,
        out_shape=[jax.ShapeDtypeStruct(shape, f32) for shape in shapes],
        scratch_shapes=[
            pltpu.VMEM((times * rows, columns), bf16)
            for times in (4, 3, 3)
            for rows, columns in shapes
        ]
        + [pltpu.SemaphoreType.DMA((10 * sets,)), pltpu.SemaphoreType.DMA((10 * sets,))],
        compiler_params=pltpu.CompilerParams(
            collective_id=3, has_side_effects=True, vmem_limit_bytes=VMEM_LIMIT
        ),
        cost_estimate=SMALL,
        name="plane_sum",
    )(*arrays)


def full_sum_kernel(
    x_ref, ready_ref, out_ref, sib, low, recv, total, total_low, arrived, send, recv_sem
):
    rows = out_ref.shape[0]
    lead = ready_ref.shape[1]
    greet(
        [{"ctx": partner(m)} for m in (1, 2, 4)] + [{"wt": ahead(d)} for d in (1, 2, 3)]
    )
    copies = Copies(send, recv_sem)
    wide = x_ref.shape[1]
    edges = [128 * (n * (wide // 128) // PARTS) for n in range(PARTS + 1)]
    parts = [slice(a, b) for a, b in zip(edges, edges[1:])]
    places = [slice(lead + a, lead + b) for a, b in zip(edges, edges[1:])] + [slice(0, lead)]
    own = pl.ds(pl.multiple_of(ahead(0) * rows, rows), rows)
    steps = [
        sum_steps(copies, x_ref, n, sib, low, recv, total, columns)
        for n, columns in enumerate(parts)
    ]

    def leave(n, value):
        total_low[:, places[n]] = value.astype(bf16)
        for d in (2, 1, 3):
            copies.start(
                ("wt", n, d),
                total_low.at[pl.ds(pl.multiple_of(ahead(d) * rows, rows), rows), places[n]],
                arrived.at[pl.ds((d - 1) * rows, rows), places[n]],
                {"wt": ahead(d)},
            )

    def finish(n, result):
        for d in (1, 3, 2):
            copies.arrived(("wt", n, d))
            result = result + arrived[(d - 1) * rows : d * rows, places[n]].astype(f32)
        out_ref[:, places[n]] = result

    for one in steps:
        one[0]()
    leave(PARTS, ready_ref[...])
    for n in range(PARTS + 2):
        if n < PARTS:
            steps[n][1]()
            steps[n][2]()
        if 1 <= n <= PARTS:
            steps[n - 1][3]()
        if n >= 2:
            steps[n - 2][4]()
            leave(n - 2, total[:, parts[n - 2]])
    finish(PARTS, ready_ref[own, :])
    for n in range(PARTS):
        finish(n, total[own, parts[n]])
    copies.close()


def full_sum(x, ready):
    rows, columns = x.shape[0] // 32, x.shape[1]
    whole = ready.shape[1] + columns
    vmem = pl.BlockSpec(memory_space=pltpu.VMEM)
    count = 13 * PARTS + 3
    return pl.pallas_call(
        full_sum_kernel,
        in_specs=[vmem, vmem],
        out_specs=vmem,
        out_shape=jax.ShapeDtypeStruct((rows, whole), f32),
        scratch_shapes=[
            pltpu.VMEM((16 * rows, columns), bf16),
            pltpu.VMEM((12 * rows, columns), bf16),
            pltpu.VMEM((12 * rows, columns), bf16),
            pltpu.VMEM((4 * rows, columns), f32),
            pltpu.VMEM((4 * rows, whole), bf16),
            pltpu.VMEM((3 * rows, whole), bf16),
            pltpu.SemaphoreType.DMA((count,)),
            pltpu.SemaphoreType.DMA((count,)),
        ],
        compiler_params=pltpu.CompilerParams(
            collective_id=4, has_side_effects=True, vmem_limit_bytes=VMEM_LIMIT
        ),
        cost_estimate=SMALL,
        name="full_sum",
    )(x, ready)


def shift(x, distance):
    n = lax.axis_size("wt")
    return lax.ppermute(x, "wt", [(i, (i + distance) % n) for i in range(n)])


def beside(results, *arrivals):
    out = lax.optimization_barrier((results, arrivals))
    return (out[0],) + tuple(out[1])


def gather_all(x):
    ctx, wt = lax.axis_size("ctx"), lax.axis_size("wt")
    if ctx != 8 or wt != 4:
        return [lax.all_gather(x, ALL, axis=0, tiled=True)], [1], jnp.zeros((1,), jnp.int32)
    ctx_index, wt_index = lax.axis_index("ctx"), lax.axis_index("wt")
    m = jnp.arange(8, dtype=jnp.int32)
    d = jnp.arange(4, dtype=jnp.int32)
    places = ((ctx_index ^ m) * wt)[:, None] + ((wt_index - d) % wt)[None, :]
    return [packed_gather(x)], [32], places.reshape(-1).astype(jnp.int32)


def keys_and_early(d_kv, pairs):
    if lax.axis_size("ctx") != 8 or lax.axis_size("wt") != 4:
        owned = [
            lax.psum_scatter(x, "ctx", scatter_dimension=0, tiled=True).astype(f32)
            for x in d_kv
        ]
        return owned, jnp.concatenate([dot_tn(a, b) for a, b in pairs], 1)
    *owned, early = plane_sum(d_kv + [outer(pairs)])
    return owned, early


def last_sum(early, pairs, extra):
    if lax.axis_size("ctx") != 8 or lax.axis_size("wt") != 4:
        parts = [early] + [dot_tn(a, b) for a, b in pairs] + [sum(dot_tn(a, b) for a, b in extra)]
        return lax.psum_scatter(
            jnp.concatenate(parts, 1).astype(bf16), ALL, scatter_dimension=0, tiled=True
        ).astype(f32)
    return full_sum(outer(pairs, extra), early)


def after(x, *others):
    return lax.optimization_barrier((x,) + others)[0]


def rope_tables(positions, width):
    middle = HEAD_SIZE // 2
    frequency = jnp.power(
        jnp.float32(rope_base), -2.0 * jnp.arange(middle, dtype=f32) / HEAD_SIZE
    )
    angles = positions.astype(f32)[:, None] * frequency[None, :]
    times = width // middle
    return jnp.tile(jnp.cos(angles), (1, times)), jnp.tile(jnp.sin(angles), (1, times))


def turn(values, cosine, sine, direction):
    middle = HEAD_SIZE // 2
    first = lax.broadcasted_iota(jnp.int32, values.shape, 1) % HEAD_SIZE < middle
    turned = jnp.where(first, -jnp.roll(values, -middle, 1), jnp.roll(values, middle, 1))
    width = values.shape[1]
    return values * cosine[:, :width] + direction * turned * sine[:, :width]


def norm_forward(values, gain):
    inverse = lax.rsqrt(jnp.mean(values * values, -1, keepdims=True) + norm_eps)
    return (values * inverse * gain, inverse)


def norm_backward(values, inverse, gain, grad_out):
    scaled = gain * grad_out
    gain_grad = (grad_out * values * inverse).astype(bf16)
    projection = jnp.mean(scaled * values, -1, keepdims=True)
    return (inverse * scaled - values * inverse * inverse * inverse * projection, gain_grad)


def per_device(
    layer_input,
    attention_gain,
    query_weight,
    key_matrix,
    value_matrix,
    output_weight,
    mixture_gain,
    router_weight,
    gate_weight,
    up_weight,
    down_weight,
    expert_routes,
    prompt_deal,
    output_grad,
):
    tok = layer_input.shape[1]
    prompt_local = tok - CONT_DEV * CLEN
    block_rows = prompt_local // 2
    context_size = lax.axis_size("ctx")
    shard_count = lax.axis_size("wt")
    expert_count = gate_weight.shape[0]
    capacity = 8 * ((tok * TOP * 7 // (4 * EXPERTS) + 7) // 8)
    ctx_index = lax.axis_index("ctx")
    wt_index = lax.axis_index("wt")
    inputs = layer_input[0].astype(f32)
    routes = expert_routes[0]
    deal_row = prompt_deal[0]
    out_low = output_grad[0]
    out_grad = out_low.astype(f32)

    own_rows = query_weight.shape[0]
    packed = jnp.concatenate(
        [
            query_weight,
            key_matrix,
            value_matrix,
            output_weight.T,
            router_weight,
            attention_gain[:, None],
            mixture_gain[:, None],
            jnp.zeros((own_rows, 94), bf16),
        ],
        1,
    )
    pieces, counts, block_places = gather_all(packed)

    gate_full = lax.all_gather(gate_weight, "ctx", axis=0, tiled=False)
    up_full = lax.all_gather(up_weight, "ctx", axis=0, tiled=False)
    down_full = lax.all_gather(down_weight, "ctx", axis=0, tiled=False)

    mask = jnp.any(
        routes[:, :, None] == jnp.arange(EXPERTS, dtype=jnp.int32)[None, None, :], 1
    )
    order = jnp.arange(tok, dtype=jnp.int32)
    before = (order[None, :] < order[:, None]).astype(bf16)
    rank = jnp.where(mask, dot(before, mask.astype(bf16)), -1.0)
    ranks = lax.all_to_all(
        rank.T.reshape(shard_count, expert_count, 1, tok), "wt", 0, 0, tiled=True
    )
    last = shard_count - 1
    grads_in = {0: out_low, last: shift(after(out_low, pieces[0], ranks), -1)}

    pieces, ranks = beside(pieces, ranks)
    local_rows = jnp.arange(tok, dtype=jnp.int32)
    mine = lax.dynamic_slice_in_dim(deal_row, 2 * ctx_index, 2, 0)
    prompt_place = (
        jnp.where(local_rows < block_rows, mine[0], mine[1]) * block_rows
        + local_rows % block_rows
    )
    positions = jnp.where(
        local_rows < prompt_local, prompt_place, PROMPT + (local_rows - prompt_local) % CLEN
    )
    cosine, sine = rope_tables(positions, 128)
    normed_one, turned_query, kv_low, qkv_full, output_t, rest, gain_rows = project(
        layer_input[0], cosine, sine, pieces, counts, block_places
    )
    router_full = rest[:, :EXPERTS]
    first_gain, second_gain = gain_rows[0], gain_rows[1]
    inverse_one = lax.rsqrt(jnp.mean(inputs * inputs, -1, keepdims=True) + norm_eps)
    kv_own = kv_low[prompt_local:]
    kv_pieces, grads_in[last] = beside([gather_ctx(kv_low, prompt_local)], grads_in[last])

    places = deal_row
    if context_size == 8:
        pairs = deal_row.reshape(2, 2, 2, 2)
        for axis, bit in ((0, 4), (1, 2), (2, 1)):
            pairs = jnp.where(ctx_index & bit > 0, jnp.flip(pairs, axis), pairs)
        places = pairs.reshape(-1)
    low = (mine[0] > mine[1]).astype(jnp.int32)
    starts = jnp.stack(
        [
            low * block_rows,
            (1 - low) * block_rows,
            jnp.min(mine) * block_rows,
            jnp.max(mine) * block_rows,
        ]
    ).astype(jnp.int32)
    heads = []
    for half in range(2):
        result = attention_forward(
            turned_query, kv_pieces, kv_own, places, starts, block_rows, half
        )
        d = last - 1 - half
        grads_in[d] = shift(grads_in[d + 1], -1)
        result, grads_in[d] = beside(result, grads_in[d])
        if half == 0:
            turned_query = after(turned_query, result[0])
        heads.append(result)
    for d in range(last - 3, 0, -1):
        grads_in[d] = shift(grads_in[d + 1], -1)
    attended = [out for out, _ in heads]
    lse = [row for _, row in heads]

    middle, normed_two, inverse_two, gates = to_gates(
        attended,
        layer_input[0],
        output_t,
        rest,
        gain_rows,
        jnp.pad(mask.astype(f32), ((0, 0), (0, 128 - EXPERTS))),
    )

    gates_out = gates.reshape(shard_count, expert_count, 1, tok)
    gates_in = []
    for d in range(shard_count):
        piece = lax.dynamic_index_in_dim(gates_out, (wt_index + d) % shard_count, 0, False)
        gates_in.append(shift(piece, d) if d else piece)
    got = {0: normed_two}
    partial, mixed, gate_grads, rows = {}, {}, {}, []
    carried = None

    def add(a, b):
        return b if a is None else (a.astype(f32) + b.astype(f32)).astype(bf16)

    for d in [0] + list(range(last, 0, -1)):
        source = (wt_index - d) % shard_count
        rank_in = lax.dynamic_index_in_dim(ranks, source, 0, False)
        result = expert_pass(
            got[d], grads_in[d], rank_in, gates_in[d], gate_full, up_full, down_full, capacity
        )
        coming = d - 1 if d else last
        if coming:
            result, got[coming] = beside(result, shift(got[(coming + 1) % shard_count], -1))
        if d == 0:
            result, gates_in = beside(result, gates_in)
        if 0 < d <= last - 2:
            carried = shift(after(add(carried, partial[d + 2]), got[d]), -1)
            result, carried = beside(result, carried)
        mixed[d], partial[d], d_gate, *kept = result
        rows.append(kept)
        gate_grads[d] = shift(d_gate, shard_count - d) if d else d_gate
        if coming:
            got[coming] = after(got[coming], partial[d])
    carried = shift(add(carried, partial[2]), -1)
    (gate_grad, up_grad), carried, gate_grads = beside(
        up_weight_grads([(after(r[0], partial[1]), r[3], r[4]) for r in rows], context_size),
        carried,
        gate_grads,
    )
    stacked = jnp.stack([gate_grads[d] for d in range(shard_count)], 0)
    for bit in (1, 2, 4):
        if bit < shard_count:
            stacked = jnp.where(wt_index & bit > 0, jnp.roll(stacked, bit, 0), stacked)
    stacked = stacked.reshape(EXPERTS, tok)
    grad_logits = gates * (stacked - jnp.sum(gates * stacked, 0, keepdims=True))
    grad_logits = grad_logits.T.astype(bf16)
    carried = shift(add(carried, partial[1]), -1)
    down_grad, home = beside(
        down_weight_grads([(after(r[2], gate_grad, grad_logits), r[1]) for r in rows], context_size), carried
    )

    grad_normed_two = partial[0].astype(f32) + home.astype(f32)
    grad_normed_two = grad_normed_two + dot_nt(grad_logits, router_full)
    grad_mid_norm, second_gain_grad = norm_backward(
        middle, inverse_two, second_gain, grad_normed_two
    )
    grad_middle = out_grad + grad_mid_norm
    grad_branch = (resid_scale * grad_middle).astype(bf16)
    grad_attended = dot(grad_branch, output_t).astype(bf16)
    gate_share, up_share, down_share = (
        lax.psum_scatter(grad, "ctx", scatter_dimension=0, tiled=False).astype(f32)
        for grad in (gate_grad, up_grad, down_grad)
    )
    carried = None
    query = after(turned_query, grad_attended)
    d_query, d_kv, ours = [], [], []
    for half in range(2):
        result = attention_backward(
            query,
            grad_attended,
            lse[half],
            attended[half],
            cosine,
            sine,
            kv_pieces,
            kv_own,
            places,
            starts,
            block_rows,
            half,
        )
        carried = shift(after(add(carried, mixed[last - half]), home), -1)
        result, carried = beside(result, carried)
        query = after(query, result[0])
        d_query.append(result[0])
        d_kv.append(result[1])
        ours.append(result[2:])
    carried = shift(add(carried, mixed[last - 2]), -1)
    d_query = jnp.concatenate(d_query, 1)
    (owned, early), carried = beside(
        keys_and_early(
            d_kv,
            [(normed_one, d_query), (grad_branch, attended[0]), (grad_branch, attended[1])],
        ),
        carried,
    )
    for d in range(last - 3, 0, -1):
        carried = shift(add(carried, mixed[d]), -1)
    mixture = mixed[0].astype(f32) + carried.astype(f32)
    layer_output = (middle + resid_scale * mixture).astype(bf16)
    d_key, d_value = (
        jnp.concatenate(
            [
                jnp.concatenate([owned[half][:, 256 * n : 256 * n + 256], ours[half][n]], 0)
                for half in range(2)
            ],
            1,
        )
        for n in range(2)
    )
    grad_key_low = turn(d_key, jnp.tile(cosine, (1, 4)), jnp.tile(sine, (1, 4)), -1.0).astype(
        bf16
    )
    grad_kv = jnp.concatenate([grad_key_low, d_value.astype(bf16)], 1)
    grad_normed_one = dot_nt(d_query, qkv_full[:, :1024]) + dot_nt(grad_kv, qkv_full[:, 1024:])
    grad_input_norm, first_gain_grad = norm_backward(
        inputs, inverse_one, first_gain, grad_normed_one
    )
    input_grad = (grad_middle + grad_input_norm).astype(bf16)

    column = lax.broadcasted_iota(jnp.int32, (tok, 128), 1)
    shares = last_sum(
        early,
        [(normed_one, grad_kv)],
        [
            (normed_two, jnp.pad(grad_logits, ((0, 0), (0, 128 - EXPERTS)))),
            (second_gain_grad, (column == EXPERTS).astype(bf16)),
            (first_gain_grad, (column == EXPERTS + 1).astype(bf16)),
        ],
    )
    return (
        layer_output[None],
        input_grad[None],
        shares[:, 3073 + EXPERTS],
        shares[:, :1024],
        shares[:, 2048 : 2048 + KV_WIDTH],
        shares[:, 2048 + KV_WIDTH : 3072],
        shares[:, 1024:2048].T,
        shares[:, 3072 + EXPERTS],
        shares[:, 3072 : 3072 + EXPERTS],
        gate_share,
        up_share,
        down_share,
    )


def solution(mesh):
    return jax.shard_map(
        per_device,
        mesh=mesh,
        in_specs=(
            P("wt", "ctx", None),
            P(("ctx", "wt")),
            P(("ctx", "wt"), None),
            P(("ctx", "wt"), None),
            P(("ctx", "wt"), None),
            P(None, ("ctx", "wt")),
            P(("ctx", "wt")),
            P(("ctx", "wt"), None),
            P("wt", "ctx", None),
            P("wt", "ctx", None),
            P("wt", None, "ctx"),
            P("wt", "ctx", None),
            P("wt", None),
            P("wt", "ctx", None),
        ),
        out_specs=(
            P("wt", "ctx", None),
            P("wt", "ctx", None),
            P(("ctx", "wt")),
            P(("ctx", "wt"), None),
            P(("ctx", "wt"), None),
            P(("ctx", "wt"), None),
            P(None, ("ctx", "wt")),
            P(("ctx", "wt")),
            P(("ctx", "wt"), None),
            P("wt", "ctx", None),
            P("wt", "ctx", None),
            P("wt", None, "ctx"),
        ),
        check_vma=False,
    )
```

```python
import functools

import jax
import jax.numpy as jnp
from jax import lax
from jax.experimental import pallas as pl
from jax.experimental.pallas import tpu as pltpu
from jax.sharding import PartitionSpec as P

MODEL_WIDTH = 1024
HQ = 16
KEY_VALUE_HEADS = 8
HEAD_SIZE = 64
EXPERTS = 32
TOP = 8
PROMPT = 2048
CLEN = 256
CONT_DEV = 2
FF = 512
QTILE = 128
PARTS = 4
KV_WIDTH = KEY_VALUE_HEADS * HEAD_SIZE
ALL = ("ctx", "wt")

att_scale = 0.015625
resid_scale = 0.22
norm_eps = 1e-06
rope_base = 10000.0
masked_score = -1e30

bf16 = jnp.bfloat16
f32 = jnp.float32
VMEM_LIMIT = 60 * 1024 * 1024
SMALL = pl.CostEstimate(flops=1_000_000_000, bytes_accessed=1_000_000, transcendentals=0)

NT = (((1,), (1,)), ((), ()))
TN = (((0,), (0,)), ((), ()))


def dot(a, b):
    return jnp.dot(a, b, preferred_element_type=f32)


def dot_nt(a, b):
    return lax.dot_general(a, b, NT, preferred_element_type=f32)


def dot_tn(a, b):
    return lax.dot_general(a, b, TN, preferred_element_type=f32)


def turn_tile(values, cosine, sine, direction):
    middle = HEAD_SIZE // 2
    first = lax.broadcasted_iota(jnp.int32, values.shape, 1) % HEAD_SIZE < middle
    turned = jnp.where(first, -pltpu.roll(values, 128 - middle, 1), pltpu.roll(values, middle, 1))
    return values * cosine + direction * turned * sine


def project_kernel(places, x_ref, cos_ref, sin_ref, *refs, counts):
    pieces = refs[: len(counts)]
    normed_ref, q_ref, kv_ref, qkv_ref, out_ref, rest_ref, gains_ref = refs[len(counts) :]
    rows = MODEL_WIDTH // sum(counts)
    at = 0
    for piece, count in zip(pieces, counts):
        for i in range(count):
            source = slice(i * rows, (i + 1) * rows)
            target = pl.ds(pl.multiple_of(places[at] * rows, rows), rows)
            qkv_ref[target, :] = piece[source, :2048]
            out_ref[target, :] = piece[source, 2048:3072]
            rest_ref[target, :] = piece[source, 3072:]
            at += 1
    gains = rest_ref[...].astype(f32).T[EXPERTS : EXPERTS + 8]
    gains_ref[...] = gains
    x = x_ref[...].astype(f32)
    inverse = lax.rsqrt(jnp.mean(x * x, -1, keepdims=True) + norm_eps)
    normed_ref[...] = (x * inverse * gains[:1]).astype(bf16)
    for c in range(8):
        raw = dot(normed_ref[...], qkv_ref[:, 256 * c : 256 * (c + 1)])
        for h in range(2):
            part = raw[:, 128 * h : 128 * (h + 1)]
            if c < 6:
                part = turn_tile(part, cos_ref[...], sin_ref[...], 1.0)
            column = 256 * c + 128 * h
            if column < 1024:
                q_ref[:, column : column + 128] = part.astype(bf16)
            else:
                column -= 1024
                at = column % KV_WIDTH // 256 * 512 + column // KV_WIDTH * 256 + column % 256
                kv_ref[:, at : at + 128] = part.astype(bf16)


def project(x, cosine, sine, pieces, counts, places):
    tok = x.shape[0]
    shape = jax.ShapeDtypeStruct
    whole = pl.BlockSpec(memory_space=pltpu.VMEM)
    return pl.pallas_call(
        functools.partial(project_kernel, counts=counts),
        in_specs=[pl.BlockSpec(memory_space=pltpu.SMEM)] + [whole] * (3 + len(pieces)),
        out_specs=[whole] * 7,
        out_shape=[
            shape((tok, MODEL_WIDTH), bf16),
            shape((tok, HQ * HEAD_SIZE), bf16),
            shape((tok, 2 * KV_WIDTH), bf16),
            shape((MODEL_WIDTH, 2048), bf16),
            shape((MODEL_WIDTH, 1024), bf16),
            shape((MODEL_WIDTH, 128), bf16),
            shape((8, MODEL_WIDTH), f32),
        ],
        compiler_params=pltpu.CompilerParams(vmem_limit_bytes=VMEM_LIMIT),
        cost_estimate=SMALL,
        name="project",
    )(places, x, cosine, sine, *pieces)


def middle_kernel(
    a_ref, b_ref, x_ref, out_ref, rest_ref, gains_ref, mask_ref, middle_ref, normed_ref, inv_ref, gates_ref
):
    half = a_ref.shape[1]
    branch = dot_nt(a_ref[...], out_ref[:, :half]) + dot_nt(b_ref[...], out_ref[:, half:])
    middle = x_ref[...].astype(f32) + resid_scale * branch
    middle_ref[...] = middle
    inverse = lax.rsqrt(jnp.mean(middle * middle, -1, keepdims=True) + norm_eps)
    inv_ref[...] = inverse
    normed = (middle * inverse * gains_ref[1:2]).astype(bf16)
    normed_ref[...] = normed
    mask = mask_ref[...] > 0.0
    logits = jnp.where(mask, dot(normed, rest_ref[...]), masked_score)
    top = jnp.max(logits, -1, keepdims=True)
    raised = jnp.where(mask, jnp.exp(logits - top), 0.0)
    gates_ref[...] = (raised / jnp.sum(raised, -1, keepdims=True)).T[:EXPERTS]


def to_gates(halves, x, output_t, rest, gain_rows, mask):
    tok = x.shape[0]
    shape = jax.ShapeDtypeStruct
    whole = pl.BlockSpec(memory_space=pltpu.VMEM)
    return pl.pallas_call(
        middle_kernel,
        in_specs=[whole] * 7,
        out_specs=[whole] * 4,
        out_shape=[
            shape((tok, MODEL_WIDTH), f32),
            shape((tok, MODEL_WIDTH), bf16),
            shape((tok, 1), f32),
            shape((EXPERTS, tok), f32),
        ],
        compiler_params=pltpu.CompilerParams(vmem_limit_bytes=VMEM_LIMIT),
        cost_estimate=SMALL,
        name="to_gates",
    )(*halves, x, output_t, rest, gain_rows, mask)


def outer_kernel(mine, *refs, count):
    out_ref = refs[-1]
    pairs = [(refs[n], refs[n + 1]) for n in range(0, len(refs) - 1, 2)]
    at = 0
    for a_ref, b_ref in pairs[:count]:
        columns = b_ref.shape[1]
        out_ref[:, at : at + columns] = dot_tn(a_ref[...], b_ref[...]).astype(bf16)
        at += columns
    if pairs[count:]:
        out_ref[:, at:] = sum(dot_tn(a[...], b[...]) for a, b in pairs[count:]).astype(bf16)


def outer(pairs, extra=()):
    tok = pairs[0][0].shape[0]
    mine = lax.axis_index("ctx").astype(jnp.int32).reshape(1)
    specs = []
    everything = [*pairs, *extra]
    for _, b in everything:
        specs.append(pl.BlockSpec((tok, 128), lambda m, mine: (0, m ^ mine[0])))
        specs.append(pl.BlockSpec(b.shape, lambda m, mine: (0, 0)))
    columns = sum(b.shape[1] for _, b in [*pairs, *extra[:1]])
    return pl.pallas_call(
        functools.partial(outer_kernel, count=len(pairs)),
        grid_spec=pltpu.PrefetchScalarGridSpec(
            num_scalar_prefetch=1,
            grid=(8,),
            in_specs=specs,
            out_specs=pl.BlockSpec((128, columns), lambda m, mine: (m, 0)),
        ),
        out_shape=jax.ShapeDtypeStruct((MODEL_WIDTH, columns), bf16),
        compiler_params=pltpu.CompilerParams(vmem_limit_bytes=VMEM_LIMIT),
        cost_estimate=SMALL,
        name="outer",
    )(mine, *[x for pair in everything for x in pair])


def gather_keys(pieces, scratch, places, block_rows):
    at = 0
    for piece in pieces:
        for b in range(piece.shape[0] // block_rows):
            start = pl.multiple_of(places[at] * block_rows, block_rows)
            scratch[pl.ds(start, block_rows), :] = piece[b * block_rows : (b + 1) * block_rows, :]
            at += 1


def pair_rows(ref, start, rows, j):
    both = ref[pl.ds(start, rows), 2 * HEAD_SIZE * j : 2 * HEAD_SIZE * (j + 1)]
    return jnp.concatenate([both[:, :HEAD_SIZE], both[:, HEAD_SIZE:]], 0)


def attention_forward_kernel(places, starts, q_ref, *refs, block_rows, pieces):
    k_refs, v_refs = refs[:pieces], refs[pieces : 2 * pieces]
    kc_ref, vc_ref, o_ref, lse_ref, k_scr, v_scr = refs[2 * pieces :]
    prompt_local = 2 * block_rows
    gather_keys(k_refs, k_scr, places, block_rows)
    gather_keys(v_refs, v_scr, places, block_rows)

    def store(start, rows, j, out, m, total, at):
        out = (out / total).astype(bf16)
        lse = m + jnp.log(total)
        o_ref[pl.ds(start, rows), 2 * HEAD_SIZE * j : 2 * HEAD_SIZE * (j + 1)] = jnp.concatenate(
            [out[:rows], out[rows:]], 1
        )
        row = jnp.broadcast_to(lse, (2 * rows, 128)).T[:1]
        lse_ref[0, 2 * j : 2 * j + 2, pl.ds(at, rows)] = jnp.concatenate(
            [row[:, :rows], row[:, rows:]], 0
        )

    def tile(i, _):
        start = pl.multiple_of(prompt_local + i * QTILE, 64)
        per = CLEN // QTILE
        seg = pl.multiple_of((i // per) * CLEN, CLEN)
        for j in range(2):
            lanes = slice(HEAD_SIZE * j, HEAD_SIZE * (j + 1))
            q = pair_rows(q_ref, start, QTILE, j) * bf16(att_scale)
            s1 = dot_nt(q, k_scr[:, lanes])
            s2 = dot_nt(q, kc_ref[pl.ds(seg, CLEN), lanes])
            place = lax.broadcasted_iota(jnp.int32, s2.shape, 0) % QTILE + (i % per) * QTILE
            s2 = jnp.where(lax.broadcasted_iota(jnp.int32, s2.shape, 1) <= place, s2, masked_score)
            m = jnp.maximum(jnp.max(s1, 1, keepdims=True), jnp.max(s2, 1, keepdims=True))
            e1 = jnp.exp(s1 - m)
            e2 = jnp.exp(s2 - m)
            total = jnp.sum(e1, 1, keepdims=True) + jnp.sum(e2, 1, keepdims=True)
            out = dot(e1.astype(bf16), v_scr[:, lanes])
            out = out + dot(e2.astype(bf16), vc_ref[pl.ds(seg, CLEN), lanes])
            store(start, QTILE, j, out, m, total, pl.multiple_of(i * QTILE, QTILE))
        return 0

    lax.fori_loop(0, CONT_DEV * CLEN // QTILE, tile, 0)

    for half, keys in enumerate((PROMPT // 2, PROMPT)):
        start = pl.multiple_of(starts[half], block_rows)
        for j in range(2):
            lanes = slice(HEAD_SIZE * j, HEAD_SIZE * (j + 1))
            q = pair_rows(q_ref, start, block_rows, j) * bf16(att_scale)
            s = dot_nt(q, k_scr[:keys, lanes])
            place = lax.broadcasted_iota(jnp.int32, s.shape, 0) % block_rows + starts[2 + half]
            s = jnp.where(lax.broadcasted_iota(jnp.int32, s.shape, 1) <= place, s, masked_score)
            m = jnp.max(s, 1, keepdims=True)
            e = jnp.exp(s - m)
            total = jnp.sum(e, 1, keepdims=True)
            out = dot(e.astype(bf16), v_scr[:keys, lanes])
            store(start, block_rows, j, out, m, total, CONT_DEV * CLEN + half * block_rows)


def key_specs(pieces, own, half):
    spec = pl.BlockSpec
    key, value = (lambda g, *_: (0, 4 * half + g)), (lambda g, *_: (0, 4 * half + 2 + g))
    keys = [spec((p.shape[0], 128), key) for p in pieces]
    values = [spec((p.shape[0], 128), value) for p in pieces]
    return keys + values + [spec((own, 128), key), spec((own, 128), value)]


def attention_forward(q, pieces, kv_own, places, starts, block_rows, half):
    tok = q.shape[0]
    spec = pl.BlockSpec
    return pl.pallas_call(
        functools.partial(
            attention_forward_kernel, block_rows=block_rows, pieces=len(pieces)
        ),
        grid_spec=pltpu.PrefetchScalarGridSpec(
            num_scalar_prefetch=2,
            grid=(2,),
            in_specs=[spec((tok, 256), lambda g, *_: (0, 2 * half + g))]
            + key_specs(pieces, kv_own.shape[0], half),
            out_specs=[
                spec((tok, 256), lambda g, *_: (0, g)),
                spec((1, 4, tok), lambda g, *_: (g, 0, 0)),
            ],
            scratch_shapes=[
                pltpu.VMEM((PROMPT, 2 * HEAD_SIZE), bf16),
                pltpu.VMEM((PROMPT, 2 * HEAD_SIZE), bf16),
            ],
        ),
        out_shape=[
            jax.ShapeDtypeStruct((tok, HQ * HEAD_SIZE // 2), bf16),
            jax.ShapeDtypeStruct((2, 4, tok), f32),
        ],
        compiler_params=pltpu.CompilerParams(vmem_limit_bytes=VMEM_LIMIT),
        cost_estimate=SMALL,
        name="attention_forward",
    )(places, starts, q, *pieces, *pieces, kv_own, kv_own)


def attention_backward_kernel(
    places, starts, q_ref, do_ref, lse_ref, o_ref, cos_ref, sin_ref, *refs, block_rows, pieces
):
    k_refs, v_refs = refs[:pieces], refs[pieces : 2 * pieces]
    kc_ref, vc_ref, dq_ref, dkv_ref, dkc_ref, dvc_ref = refs[2 * pieces : 2 * pieces + 6]
    k_scr, v_scr, dk_acc, dv_acc, dq_acc = refs[2 * pieces + 6 :]
    prompt_local = 2 * block_rows
    gather_keys(k_refs, k_scr, places, block_rows)
    gather_keys(v_refs, v_scr, places, block_rows)
    dk_acc[...] = jnp.zeros_like(dk_acc)
    dv_acc[...] = jnp.zeros_like(dv_acc)
    dkc_ref[...] = jnp.zeros_like(dkc_ref)
    dvc_ref[...] = jnp.zeros_like(dvc_ref)

    def row_pair(ref, start, rows, j):
        both = ref[0, 2 * j : 2 * j + 2, pl.ds(start, rows)]
        return jnp.concatenate([both[:1], both[1:]], 1)

    def centre(start, rows, j, d_out):
        product = d_out.astype(f32) * pair_rows(o_ref, start, rows, j).astype(f32)
        ones = jnp.ones((8, HEAD_SIZE), f32)
        return lax.dot_general(
            ones, product, NT, precision=lax.Precision.HIGHEST, preferred_element_type=f32
        )[:1]

    def part(k, v, q, d_out, lse, delta, allowed):
        s = dot_nt(k, q)
        if allowed is not None:
            s = jnp.where(allowed(s.shape), s, masked_score)
        p = jnp.exp(s - lse)
        d_p = dot_nt(v, d_out)
        d_s = (p * (d_p - delta)).astype(bf16)
        return dot_tn(d_s, k), dot(d_s, q), dot(p.astype(bf16), d_out)

    def store(start, rows, j, d_q):
        d_q = d_q * att_scale
        dq_acc[pl.ds(start, rows), 2 * HEAD_SIZE * j : 2 * HEAD_SIZE * (j + 1)] = jnp.concatenate(
            [d_q[:rows], d_q[rows:]], 1
        )

    def tile(i, _):
        start = pl.multiple_of(prompt_local + i * QTILE, 64)
        per = CLEN // QTILE
        seg = pl.multiple_of((i // per) * CLEN, CLEN)
        own = pl.ds(seg, CLEN)
        lane_start = pl.multiple_of(i * QTILE, QTILE)

        def allowed(shape):
            place = lax.broadcasted_iota(jnp.int32, shape, 1) % QTILE + (i % per) * QTILE
            return lax.broadcasted_iota(jnp.int32, shape, 0) <= place

        for j in range(2):
            lanes = slice(HEAD_SIZE * j, HEAD_SIZE * (j + 1))
            q = pair_rows(q_ref, start, QTILE, j) * bf16(att_scale)
            d_out = pair_rows(do_ref, start, QTILE, j)
            lse = row_pair(lse_ref, lane_start, QTILE, j)
            delta = centre(start, QTILE, j, d_out)
            a, b, c = part(k_scr[:, lanes], v_scr[:, lanes], q, d_out, lse, delta, None)
            dk_acc[:, lanes] += b
            dv_acc[:, lanes] += c
            d_q = a
            a, b, c = part(
                kc_ref[own, lanes], vc_ref[own, lanes], q, d_out, lse, delta, allowed
            )
            dkc_ref[own, lanes] += b
            dvc_ref[own, lanes] += c
            store(start, QTILE, j, d_q + a)
        return 0

    lax.fori_loop(0, CONT_DEV * CLEN // QTILE, tile, 0)

    for half, keys in enumerate((PROMPT // 2, PROMPT)):
        start = pl.multiple_of(starts[half], block_rows)
        at = CONT_DEV * CLEN + half * block_rows

        def allowed(shape):
            place = lax.broadcasted_iota(jnp.int32, shape, 1) % block_rows + starts[2 + half]
            return lax.broadcasted_iota(jnp.int32, shape, 0) <= place

        for j in range(2):
            lanes = slice(HEAD_SIZE * j, HEAD_SIZE * (j + 1))
            q = pair_rows(q_ref, start, block_rows, j) * bf16(att_scale)
            d_out = pair_rows(do_ref, start, block_rows, j)
            lse = row_pair(lse_ref, at, block_rows, j)
            delta = centre(start, block_rows, j, d_out)
            a, b, c = part(
                k_scr[:keys, lanes], v_scr[:keys, lanes], q, d_out, lse, delta, allowed
            )
            dk_acc[:keys, lanes] += b
            dv_acc[:keys, lanes] += c
            store(start, block_rows, j, a)

    g = pl.program_id(0)
    key_lanes = pl.ds(pl.multiple_of(g * 128, 128), 128)
    value_lanes = pl.ds(pl.multiple_of(256 + g * 128, 128), 128)
    for b in range(PROMPT // block_rows):
        source = pl.ds(pl.multiple_of(places[b] * block_rows, block_rows), block_rows)
        rows = slice(b * block_rows, (b + 1) * block_rows)
        dkv_ref[rows, key_lanes] = dk_acc[source, :].astype(bf16)
        dkv_ref[rows, value_lanes] = dv_acc[source, :].astype(bf16)
    for c in range(2):
        lanes = slice(128 * c, 128 * (c + 1))
        dq_ref[:, lanes] = turn_tile(dq_acc[:, lanes], cos_ref[...], sin_ref[...], -1.0).astype(
            bf16
        )


def attention_backward(
    q, d_out, lse, attended, cosine, sine, pieces, kv_own, places, starts, block_rows, half
):
    tok = q.shape[0]
    own = kv_own.shape[0]
    spec = pl.BlockSpec
    wide = spec((tok, 256), lambda g, *_: (0, 2 * half + g))
    narrow = spec((tok, 256), lambda g, *_: (0, g))
    ours = spec((own, 128), lambda g, *_: (0, g))
    table = spec((tok, 128), lambda g, *_: (0, 0))
    return pl.pallas_call(
        functools.partial(
            attention_backward_kernel, block_rows=block_rows, pieces=len(pieces)
        ),
        grid_spec=pltpu.PrefetchScalarGridSpec(
            num_scalar_prefetch=2,
            grid=(2,),
            in_specs=[wide, wide, spec((1, 4, tok), lambda g, *_: (g, 0, 0)), narrow, table, table]
            + key_specs(pieces, own, half),
            out_specs=[
                spec((tok, 256), lambda g, *_: (0, g)),
                spec((PROMPT, KV_WIDTH), lambda g, *_: (0, 0)),
                ours,
                ours,
            ],
            scratch_shapes=[
                pltpu.VMEM((PROMPT, 2 * HEAD_SIZE), bf16),
                pltpu.VMEM((PROMPT, 2 * HEAD_SIZE), bf16),
                pltpu.VMEM((PROMPT, 2 * HEAD_SIZE), f32),
                pltpu.VMEM((PROMPT, 2 * HEAD_SIZE), f32),
                pltpu.VMEM((tok, 4 * HEAD_SIZE), f32),
            ],
        ),
        out_shape=[
            jax.ShapeDtypeStruct((tok, HQ * HEAD_SIZE // 2), bf16),
            jax.ShapeDtypeStruct((PROMPT, KV_WIDTH), bf16),
            jax.ShapeDtypeStruct((own, KV_WIDTH // 2), f32),
            jax.ShapeDtypeStruct((own, KV_WIDTH // 2), f32),
        ],
        compiler_params=pltpu.CompilerParams(vmem_limit_bytes=VMEM_LIMIT),
        cost_estimate=SMALL,
        name="attention_backward",
    )(places, starts, q, d_out, lse, attended, cosine, sine, *pieces, *pieces, kv_own, kv_own)


def expert_kernel(
    counts,
    a2_ref,
    df_ref,
    rank_ref,
    gate_ref,
    wg_ref,
    wu_ref,
    wd_ref,
    mix_ref,
    da_ref,
    dg_ref,
    x_ref,
    dy_ref,
    z_ref,
    dgate_ref,
    dup_ref,
    mix_acc,
    da_acc,
    *,
    sizes,
):
    e = pl.program_id(0)

    @pl.when(e == 0)
    def _():
        mix_acc[...] = jnp.zeros_like(mix_acc)
        da_acc[...] = jnp.zeros_like(da_acc)

    def body(size):
        rank = rank_ref[0]
        gates = gate_ref[0]
        tok = rank.shape[1]
        slot = lax.broadcasted_iota(jnp.int32, (size, tok), 0).astype(f32)
        hit = slot == rank
        chosen = hit.astype(f32).astype(bf16)
        gate = jnp.sum(jnp.where(hit, gates, 0.0), 1, keepdims=True)
        x = dot(chosen, a2_ref[...]).astype(bf16)
        d_mix = resid_scale * dot(chosen, df_ref[...])
        wg = wg_ref[:, 0].reshape(MODEL_WIDTH, FF)
        wu = wu_ref[:, 0].reshape(MODEL_WIDTH, FF)
        wd = jnp.concatenate([wd_ref[c, 0] for c in range(wd_ref.shape[0])], 1)
        g = dot(x, wg)
        u = dot(x, wu)
        sig = jax.nn.sigmoid(g)
        z = (g * sig * u).astype(bf16)
        y = dot(z, wd).astype(bf16).astype(f32)
        d_gate_value = jnp.sum(d_mix * y, 1, keepdims=True)
        dg_ref[0] = jnp.sum(jnp.where(hit, d_gate_value, 0.0), 0, keepdims=True)
        mix_acc[...] += dot_tn(chosen, (gate * y).astype(bf16))
        d_y = (gate * d_mix).astype(bf16)
        d_z = dot_nt(d_y, wd)
        d_g = (d_z * u * sig * (1.0 + g * (1.0 - sig))).astype(bf16)
        d_u = (d_z * g * sig).astype(bf16)
        d_r = (dot_nt(d_g, wg) + dot_nt(d_u, wu)).astype(bf16)
        da_acc[...] += dot_tn(chosen, d_r)
        for ref, value in (
            (x_ref, x),
            (dy_ref, d_y),
            (z_ref, z),
            (dgate_ref, d_g),
            (dup_ref, d_u),
        ):
            ref[0, :size] = value
            if size < ref.shape[1]:
                ref[0, size:] = jnp.zeros((ref.shape[1] - size, ref.shape[2]), bf16)

    least = -1
    for size in sizes:
        pl.when((counts[e] > least) & (counts[e] <= size))(functools.partial(body, size))
        least = size

    @pl.when(e == pl.num_programs(0) - 1)
    def _():
        mix_ref[...] = mix_acc[...].astype(bf16)
        da_ref[...] = da_acc[...].astype(bf16)


def expert_pass(a2, df, rank, gates, wg, wu, wd, capacity):
    tok = a2.shape[0]
    parts, experts = wg.shape[0], wg.shape[1]
    sizes = sorted({min(size, capacity) for size in (128, 192, 256, capacity)})
    counts = (jnp.max(rank, (1, 2)) + 1.0).astype(jnp.int32)
    spec = pl.BlockSpec
    whole = spec((tok, MODEL_WIDTH), lambda e, *_: (0, 0))
    row = spec((1, 1, tok), lambda e, *_: (e, 0, 0))
    up = spec((parts, 1, MODEL_WIDTH // parts, FF), lambda e, *_: (0, e, 0, 0))
    down = spec((parts, 1, FF, MODEL_WIDTH // parts), lambda e, *_: (0, e, 0, 0))
    rows_wide = spec((1, capacity, MODEL_WIDTH), lambda e, *_: (e, 0, 0))
    rows_thin = spec((1, capacity, FF), lambda e, *_: (e, 0, 0))
    shape = jax.ShapeDtypeStruct
    return pl.pallas_call(
        functools.partial(expert_kernel, sizes=sizes),
        grid_spec=pltpu.PrefetchScalarGridSpec(
            num_scalar_prefetch=1,
            grid=(experts,),
            in_specs=[whole, whole, row, row, up, up, down],
            out_specs=[whole, whole, row, rows_wide, rows_wide, rows_thin, rows_thin, rows_thin],
            scratch_shapes=[
                pltpu.VMEM((tok, MODEL_WIDTH), f32),
                pltpu.VMEM((tok, MODEL_WIDTH), f32),
            ],
        ),
        out_shape=[
            shape((tok, MODEL_WIDTH), bf16),
            shape((tok, MODEL_WIDTH), bf16),
            shape((experts, 1, tok), f32),
            shape((experts, capacity, MODEL_WIDTH), bf16),
            shape((experts, capacity, MODEL_WIDTH), bf16),
            shape((experts, capacity, FF), bf16),
            shape((experts, capacity, FF), bf16),
            shape((experts, capacity, FF), bf16),
        ],
        compiler_params=pltpu.CompilerParams(vmem_limit_bytes=VMEM_LIMIT),
        cost_estimate=SMALL,
        name="expert_pass",
    )(counts, a2, df, rank, gates, wg, wu, wd)


def up_grad_kernel(*refs, sources):
    rows = refs[: 3 * sources]
    gate_ref, up_ref = refs[3 * sources :]
    for n, out_ref in ((1, gate_ref), (2, up_ref)):
        total = None
        for s in range(sources):
            term = dot_tn(rows[3 * s][0], rows[3 * s + n][0])
            total = term if total is None else total + term
        out_ref[...] = total.astype(bf16).reshape(out_ref.shape)


def down_grad_kernel(*refs, sources, parts):
    rows, down_ref = refs[: 2 * sources], refs[-1]
    width = MODEL_WIDTH // parts
    total = None
    for s in range(sources):
        term = dot_tn(rows[2 * s][0], rows[2 * s + 1][0])
        total = term if total is None else total + term
    total = total.astype(bf16)
    for c in range(parts):
        down_ref[c, 0] = total[:, c * width : (c + 1) * width]


def row_specs(rows):
    return [pl.BlockSpec((1,) + a.shape[1:], lambda e: (e, 0, 0)) for r in rows for a in r]


def up_weight_grads(rows, parts):
    experts = rows[0][0].shape[0]
    shape = (parts, experts, MODEL_WIDTH // parts, FF)
    out = pl.BlockSpec((parts, 1) + shape[2:], lambda e: (0, e, 0, 0))
    return pl.pallas_call(
        functools.partial(up_grad_kernel, sources=len(rows)),
        grid=(experts,),
        in_specs=row_specs(rows),
        out_specs=[out, out],
        out_shape=[jax.ShapeDtypeStruct(shape, bf16)] * 2,
        compiler_params=pltpu.CompilerParams(vmem_limit_bytes=VMEM_LIMIT),
        cost_estimate=SMALL,
        name="up_weight_grads",
    )(*[a for r in rows for a in r])


def down_weight_grads(rows, parts):
    experts = rows[0][0].shape[0]
    shape = (parts, experts, FF, MODEL_WIDTH // parts)
    return pl.pallas_call(
        functools.partial(down_grad_kernel, sources=len(rows), parts=parts),
        grid=(experts,),
        in_specs=row_specs(rows),
        out_specs=pl.BlockSpec((parts, 1) + shape[2:], lambda e: (0, e, 0, 0)),
        out_shape=jax.ShapeDtypeStruct(shape, bf16),
        compiler_params=pltpu.CompilerParams(vmem_limit_bytes=VMEM_LIMIT),
        cost_estimate=SMALL,
        name="down_weight_grads",
    )(*[a for r in rows for a in r])


def swap(x, mask):
    return lax.ppermute(x, "ctx", [(i, i ^ mask) for i in range(lax.axis_size("ctx"))])


def gather_ctx(x, rows):
    if lax.axis_size("ctx") != 8:
        return lax.all_gather(x[:rows], "ctx", axis=0, tiled=True)
    return plane_gather(x, rows)


MESH = pl.DeviceIdType.MESH
ANY = pl.BlockSpec(memory_space=pl.ANY)


def partner(mask):
    me = lax.axis_index("ctx")
    return me + mask - 2 * mask * ((me // mask) % 2)


def ahead(distance):
    return (lax.axis_index("wt") + distance) % lax.axis_size("wt")


class Copies:
    def __init__(self, send, recv):
        self.send, self.recv, self.made = send, recv, {}

    def start(self, name, source, target, device):
        n = len(self.made)
        self.made[name] = copy = pltpu.make_async_remote_copy(
            src_ref=source,
            dst_ref=target,
            send_sem=self.send.at[n],
            recv_sem=self.recv.at[n],
            device_id=device,
            device_id_type=MESH,
        )
        copy.start()

    def arrived(self, name):
        self.made[name].wait_recv()

    def close(self):
        for copy in self.made.values():
            copy.wait_send()


def greet(devices):
    barrier = pltpu.get_barrier_semaphore()
    for device in devices:
        pl.semaphore_signal(barrier, inc=1, device_id=device, device_id_type=MESH)
    pl.semaphore_wait(barrier, len(devices))


def plane_steps(copies, block, half, key):
    side, near, far = ({"ctx": partner(m)} for m in (1, 2, 4))
    top, end = (lambda m: block(m, 0, half)), (lambda m: block(m, half, half))

    def first():
        copies.start((key, 2), block(0), block(2), near)
        copies.start((key, 4), block(0), block(4), far)
        copies.start((key, 1), block(0), block(1), side)

    def second():
        copies.arrived((key, 2))
        copies.start((key, 6), top(2), top(6), far)
        copies.start((key, 3), block(2), block(3), side)

    def third():
        copies.arrived((key, 4))
        copies.start((key, 7), end(4), end(6), near)
        copies.start((key, 5), block(4), block(5), side)

    def fourth():
        copies.arrived((key, 6))
        copies.arrived((key, 7))
        copies.start((key, 8), block(6), block(7), side)

    def last():
        for m in (1, 3, 5, 8):
            copies.arrived((key, m))

    return [first, second, third, fourth, last]


def plane_gather_kernel(x_ref, out_ref, send, recv, own_sem):
    rows = out_ref.shape[0] // 8
    greet([{"ctx": partner(m)} for m in (1, 2, 4)])
    own = pltpu.make_async_copy(x_ref.at[pl.ds(0, rows)], out_ref.at[pl.ds(0, rows)], own_sem)
    own.start()
    copies = Copies(send, recv)

    def block(m, start=0, count=rows):
        if m == 0:
            return x_ref.at[pl.ds(start, count)]
        return out_ref.at[pl.ds(m * rows + start, count)]

    for step in plane_steps(copies, block, rows // 2, 0):
        step()
    own.wait()
    copies.close()


def plane_gather(x, rows):
    return pl.pallas_call(
        plane_gather_kernel,
        in_specs=[ANY],
        out_specs=ANY,
        out_shape=jax.ShapeDtypeStruct((8 * rows, x.shape[1]), x.dtype),
        scratch_shapes=[
            pltpu.SemaphoreType.DMA((8,)),
            pltpu.SemaphoreType.DMA((8,)),
            pltpu.SemaphoreType.DMA,
        ],
        compiler_params=pltpu.CompilerParams(collective_id=1, has_side_effects=True),
        cost_estimate=SMALL,
        name="plane_gather",
    )(x)


def packed_gather_kernel(x_ref, out_ref, send, recv, own_sem):
    rows = x_ref.shape[0]
    greet(
        [{"ctx": partner(m)} for m in (1, 2, 4)] + [{"wt": ahead(d)} for d in (1, 2, 3)]
    )
    own = pltpu.make_async_copy(x_ref, out_ref.at[pl.ds(0, rows)], own_sem)
    own.start()
    copies = Copies(send, recv)

    def block_of(d):
        def block(m, start=0, count=rows):
            if m == 0 and d == 0:
                return x_ref.at[pl.ds(start, count)]
            return out_ref.at[pl.ds((4 * m + d) * rows + start, count)]

        return block

    for d in (1, 3, 2):
        copies.start(d, x_ref, block_of(d)(0), {"wt": ahead(d)})
    steps = {d: plane_steps(copies, block_of(d), rows // 2, ("plane", d)) for d in range(4)}
    steps[0][0]()
    for d, before in ((1, 0), (3, 1), (2, 3)):
        copies.arrived(d)
        steps[d][0]()
        steps[before][1]()
        steps[before][2]()
        if d != 1:
            steps[{3: 0, 2: 1}[d]][3]()
    steps[2][1]()
    steps[2][2]()
    steps[3][3]()
    steps[2][3]()
    for d in range(4):
        steps[d][4]()
    own.wait()
    copies.close()


def packed_gather(x):
    return pl.pallas_call(
        packed_gather_kernel,
        in_specs=[ANY],
        out_specs=ANY,
        out_shape=jax.ShapeDtypeStruct((32 * x.shape[0], x.shape[1]), x.dtype),
        scratch_shapes=[
            pltpu.SemaphoreType.DMA((35,)),
            pltpu.SemaphoreType.DMA((35,)),
            pltpu.SemaphoreType.DMA,
        ],
        compiler_params=pltpu.CompilerParams(collective_id=2, has_side_effects=True),
        cost_estimate=SMALL,
        name="packed_gather",
    )(x)


def sum_steps(copies, x_ref, key, sib, low, recv, out_ref, columns):
    rows = x_ref.shape[0] // 8
    half = rows // 2
    side, near, far = ({"ctx": partner(m)} for m in (1, 2, 4))

    def blocks(ref, m, start=0, count=rows):
        return ref.at[pl.ds(m * rows + start, count), columns]

    def added(m, start, count):
        ours = x_ref[m * rows + start : m * rows + start + count, columns].astype(f32)
        at = m // 2 * rows + start
        return ours + sib[at : at + count, columns].astype(f32)

    def put(place, start, value, device):
        at = place * rows + start
        low[at : at + half, columns] = value.astype(bf16)
        copies.start(
            (key, "low", place, start),
            blocks(low, place, start, half),
            blocks(recv, place, start, half),
            device,
        )

    def first():
        for m in (7, 3, 5, 1):
            copies.start((key, m), blocks(x_ref, m), blocks(sib, m // 2), side)

    def second():
        copies.arrived((key, 7))
        put(0, 0, added(6, 0, half), far)
        put(0, half, added(6, half, half), near)

    def third():
        copies.arrived((key, 3))
        put(1, half, added(2, half, half), near)
        copies.arrived((key, 5))
        put(2, 0, added(4, 0, half), far)

    def fourth():
        copies.arrived((key, "low", 0, 0))
        put(1, 0, added(2, 0, half) + recv[0:half, columns].astype(f32), near)
        copies.arrived((key, "low", 0, half))
        put(2, half, added(4, half, half) + recv[half:rows, columns].astype(f32), far)

    def last():
        copies.arrived((key, 1))
        for place in (1, 2):
            for start in (0, half):
                copies.arrived((key, "low", place, start))
        out_ref[:, columns] = (
            added(0, 0, rows)
            + recv[rows : 2 * rows, columns].astype(f32)
            + recv[2 * rows :, columns].astype(f32)
        )

    return [first, second, third, fourth, last]


def plane_sum_kernel(*refs, sets):
    x_refs, out_refs = refs[:sets], refs[sets : 2 * sets]
    sibs, lows, recvs = (refs[(2 + n) * sets : (3 + n) * sets] for n in range(3))
    send, recv_sem = refs[5 * sets :]
    greet([{"ctx": partner(m)} for m in (1, 2, 4)])
    copies = Copies(send, recv_sem)
    steps = [
        sum_steps(copies, x_refs[n], n, sibs[n], lows[n], recvs[n], out_refs[n], slice(None))
        for n in range(sets)
    ]
    for n in range(5):
        for one in steps:
            one[n]()
    copies.close()


def plane_sum(arrays):
    if lax.axis_size("ctx") != 8:
        return [
            lax.psum_scatter(x, "ctx", scatter_dimension=0, tiled=True).astype(f32)
            for x in arrays
        ]
    sets = len(arrays)
    rows, columns = arrays[0].shape[0] // 8, arrays[0].shape[1]
    vmem = pl.BlockSpec(memory_space=pltpu.VMEM)
    return pl.pallas_call(
        functools.partial(plane_sum_kernel, sets=sets),
        in_specs=[vmem] * sets,
        out_specs=[vmem] * sets,
        out_shape=[jax.ShapeDtypeStruct((rows, columns), f32)] * sets,
        scratch_shapes=[pltpu.VMEM((4 * rows, columns), bf16)] * sets
        + [pltpu.VMEM((3 * rows, columns), bf16)] * (2 * sets)
        + [pltpu.SemaphoreType.DMA((10 * sets,)), pltpu.SemaphoreType.DMA((10 * sets,))],
        compiler_params=pltpu.CompilerParams(
            collective_id=3, has_side_effects=True, vmem_limit_bytes=VMEM_LIMIT
        ),
        cost_estimate=SMALL,
        name="plane_sum",
    )(*arrays)


def full_sum_kernel(x_ref, *refs, widths):
    out_refs, refs = refs[: len(widths)], refs[len(widths) :]
    sib, low, recv, total, total_low, arrived, result_ref, send, recv_sem = refs
    rows = result_ref.shape[0]
    greet(
        [{"ctx": partner(m)} for m in (1, 2, 4)] + [{"wt": ahead(d)} for d in (1, 2, 3)]
    )
    copies = Copies(send, recv_sem)
    wide = x_ref.shape[1]
    edges = [128 * (n * (wide // 128) // PARTS) for n in range(PARTS + 1)]
    parts = [slice(a, b) for a, b in zip(edges, edges[1:])]
    steps = [
        sum_steps(copies, x_ref, n, sib, low, recv, total, columns)
        for n, columns in enumerate(parts)
    ]

    def leave(n):
        total_low[:, parts[n]] = total[:, parts[n]].astype(bf16)
        for d in (2, 1, 3):
            copies.start(
                ("wt", n, d),
                total_low.at[pl.ds(pl.multiple_of(ahead(d) * rows, rows), rows), parts[n]],
                arrived.at[pl.ds((d - 1) * rows, rows), parts[n]],
                {"wt": ahead(d)},
            )

    def finish(n):
        own = pl.ds(pl.multiple_of(ahead(0) * rows, rows), rows)
        result = total[own, parts[n]]
        for d in (1, 3, 2):
            copies.arrived(("wt", n, d))
            result = result + arrived[(d - 1) * rows : d * rows, parts[n]].astype(f32)
        result_ref[:, parts[n]] = result

    for one in steps:
        one[0]()
    for n in range(PARTS + 2):
        if n < PARTS:
            steps[n][1]()
            steps[n][2]()
        if 1 <= n <= PARTS:
            steps[n - 1][3]()
        if n >= 2:
            steps[n - 2][4]()
            leave(n - 2)
    for n in range(PARTS):
        finish(n)
    at = 0
    for out_ref, width in zip(out_refs, widths):
        out_ref[...] = result_ref[:, at : at + width]
        at += width
    copies.close()


def full_sum(x, widths):
    rows, columns = x.shape[0] // 32, x.shape[1]
    vmem = pl.BlockSpec(memory_space=pltpu.VMEM)
    return pl.pallas_call(
        functools.partial(full_sum_kernel, widths=widths),
        in_specs=[vmem],
        out_specs=[vmem] * len(widths),
        out_shape=[jax.ShapeDtypeStruct((rows, width), f32) for width in widths],
        scratch_shapes=[
            pltpu.VMEM((16 * rows, columns), bf16),
            pltpu.VMEM((12 * rows, columns), bf16),
            pltpu.VMEM((12 * rows, columns), bf16),
            pltpu.VMEM((4 * rows, columns), f32),
            pltpu.VMEM((4 * rows, columns), bf16),
            pltpu.VMEM((3 * rows, columns), bf16),
            pltpu.VMEM((rows, columns), f32),
            pltpu.SemaphoreType.DMA((13 * PARTS,)),
            pltpu.SemaphoreType.DMA((13 * PARTS,)),
        ],
        compiler_params=pltpu.CompilerParams(
            collective_id=4, has_side_effects=True, vmem_limit_bytes=VMEM_LIMIT
        ),
        cost_estimate=SMALL,
        name="full_sum",
    )(x)


def shift(x, distance):
    n = lax.axis_size("wt")
    return lax.ppermute(x, "wt", [(i, (i + distance) % n) for i in range(n)])


def beside(results, *arrivals):
    out = lax.optimization_barrier((results, arrivals))
    return (out[0],) + tuple(out[1])


def gather_all(x):
    ctx, wt = lax.axis_size("ctx"), lax.axis_size("wt")
    if ctx != 8 or wt != 4:
        return [lax.all_gather(x, ALL, axis=0, tiled=True)], [1], jnp.zeros((1,), jnp.int32)
    ctx_index, wt_index = lax.axis_index("ctx"), lax.axis_index("wt")
    m = jnp.arange(8, dtype=jnp.int32)
    d = jnp.arange(4, dtype=jnp.int32)
    places = ((ctx_index ^ m) * wt)[:, None] + ((wt_index - d) % wt)[None, :]
    return [packed_gather(x)], [32], places.reshape(-1).astype(jnp.int32)


def outer_sum(pairs, extra, widths):
    if lax.axis_size("ctx") != 8 or lax.axis_size("wt") != 4:
        parts = [dot_tn(a, b) for a, b in pairs] + [sum(dot_tn(a, b) for a, b in extra)]
        result = lax.psum_scatter(
            jnp.concatenate(parts, 1).astype(bf16), ALL, scatter_dimension=0, tiled=True
        ).astype(f32)
        edges = [sum(widths[: n + 1]) for n in range(len(widths) - 1)]
        return jnp.split(result, edges, 1)
    return full_sum(outer(pairs, extra), widths)


def after(x, *others):
    return lax.optimization_barrier((x,) + others)[0]


def rope_tables(positions, width):
    middle = HEAD_SIZE // 2
    frequency = jnp.power(
        jnp.float32(rope_base), -2.0 * jnp.arange(middle, dtype=f32) / HEAD_SIZE
    )
    angles = positions.astype(f32)[:, None] * frequency[None, :]
    times = width // middle
    return jnp.tile(jnp.cos(angles), (1, times)), jnp.tile(jnp.sin(angles), (1, times))


def turn(values, cosine, sine, direction):
    middle = HEAD_SIZE // 2
    first = lax.broadcasted_iota(jnp.int32, values.shape, 1) % HEAD_SIZE < middle
    turned = jnp.where(first, -jnp.roll(values, -middle, 1), jnp.roll(values, middle, 1))
    width = values.shape[1]
    return values * cosine[:, :width] + direction * turned * sine[:, :width]


def norm_forward(values, gain):
    inverse = lax.rsqrt(jnp.mean(values * values, -1, keepdims=True) + norm_eps)
    return (values * inverse * gain, inverse)


def norm_backward(values, inverse, gain, grad_out):
    scaled = gain * grad_out
    gain_grad = (grad_out * values * inverse).astype(bf16)
    projection = jnp.mean(scaled * values, -1, keepdims=True)
    return (inverse * scaled - values * inverse * inverse * inverse * projection, gain_grad)


def per_device(
    layer_input,
    attention_gain,
    query_weight,
    key_matrix,
    value_matrix,
    output_weight,
    mixture_gain,
    router_weight,
    gate_weight,
    up_weight,
    down_weight,
    expert_routes,
    prompt_deal,
    output_grad,
):
    tok = layer_input.shape[1]
    prompt_local = tok - CONT_DEV * CLEN
    block_rows = prompt_local // 2
    context_size = lax.axis_size("ctx")
    shard_count = lax.axis_size("wt")
    expert_count = gate_weight.shape[0]
    capacity = 8 * ((tok * TOP * 7 // (4 * EXPERTS) + 7) // 8)
    ctx_index = lax.axis_index("ctx")
    wt_index = lax.axis_index("wt")
    inputs = layer_input[0].astype(f32)
    routes = expert_routes[0]
    deal_row = prompt_deal[0]
    out_low = output_grad[0]
    out_grad = out_low.astype(f32)

    own_rows = query_weight.shape[0]
    packed = jnp.concatenate(
        [
            query_weight,
            key_matrix,
            value_matrix,
            output_weight.T,
            router_weight,
            attention_gain[:, None],
            mixture_gain[:, None],
            jnp.zeros((own_rows, 94), bf16),
        ],
        1,
    )
    pieces, counts, block_places = gather_all(packed)

    gate_full = lax.all_gather(gate_weight, "ctx", axis=0, tiled=False)
    up_full = lax.all_gather(up_weight, "ctx", axis=0, tiled=False)
    down_full = lax.all_gather(down_weight, "ctx", axis=0, tiled=False)

    mask = jnp.any(
        routes[:, :, None] == jnp.arange(EXPERTS, dtype=jnp.int32)[None, None, :], 1
    )
    order = jnp.arange(tok, dtype=jnp.int32)
    before = (order[None, :] < order[:, None]).astype(bf16)
    rank = jnp.where(mask, dot(before, mask.astype(bf16)), -1.0)
    ranks = lax.all_to_all(
        rank.T.reshape(shard_count, expert_count, 1, tok), "wt", 0, 0, tiled=True
    )
    last = shard_count - 1
    grads_in = {0: out_low, last: shift(after(out_low, pieces[0], ranks), -1)}

    pieces, ranks = beside(pieces, ranks)
    local_rows = jnp.arange(tok, dtype=jnp.int32)
    mine = lax.dynamic_slice_in_dim(deal_row, 2 * ctx_index, 2, 0)
    prompt_place = (
        jnp.where(local_rows < block_rows, mine[0], mine[1]) * block_rows
        + local_rows % block_rows
    )
    positions = jnp.where(
        local_rows < prompt_local, prompt_place, PROMPT + (local_rows - prompt_local) % CLEN
    )
    cosine, sine = rope_tables(positions, 128)
    normed_one, turned_query, kv_low, qkv_full, output_t, rest, gain_rows = project(
        layer_input[0], cosine, sine, pieces, counts, block_places
    )
    router_full = rest[:, :EXPERTS]
    first_gain, second_gain = gain_rows[0], gain_rows[1]
    inverse_one = lax.rsqrt(jnp.mean(inputs * inputs, -1, keepdims=True) + norm_eps)
    kv_own = kv_low[prompt_local:]
    kv_pieces, grads_in[last] = beside([gather_ctx(kv_low, prompt_local)], grads_in[last])

    places = deal_row
    if context_size == 8:
        pairs = deal_row.reshape(2, 2, 2, 2)
        for axis, bit in ((0, 4), (1, 2), (2, 1)):
            pairs = jnp.where(ctx_index & bit > 0, jnp.flip(pairs, axis), pairs)
        places = pairs.reshape(-1)
    low = (mine[0] > mine[1]).astype(jnp.int32)
    starts = jnp.stack(
        [
            low * block_rows,
            (1 - low) * block_rows,
            jnp.min(mine) * block_rows,
            jnp.max(mine) * block_rows,
        ]
    ).astype(jnp.int32)
    heads = []
    for half in range(2):
        result = attention_forward(
            turned_query, kv_pieces, kv_own, places, starts, block_rows, half
        )
        d = last - 1 - half
        grads_in[d] = shift(grads_in[d + 1], -1)
        result, grads_in[d] = beside(result, grads_in[d])
        if half == 0:
            turned_query = after(turned_query, result[0])
        heads.append(result)
    for d in range(last - 3, 0, -1):
        grads_in[d] = shift(grads_in[d + 1], -1)
    attended = [out for out, _ in heads]
    lse = [row for _, row in heads]

    middle, normed_two, inverse_two, gates = to_gates(
        attended,
        layer_input[0],
        output_t,
        rest,
        gain_rows,
        jnp.pad(mask.astype(f32), ((0, 0), (0, 128 - EXPERTS))),
    )

    gates_out = gates.reshape(shard_count, expert_count, 1, tok)
    gates_in = []
    for d in range(shard_count):
        piece = lax.dynamic_index_in_dim(gates_out, (wt_index + d) % shard_count, 0, False)
        gates_in.append(shift(piece, d) if d else piece)
    got = {0: normed_two}
    partial, mixed, gate_grads, rows = {}, {}, {}, []
    carried = None

    def add(a, b):
        return b if a is None else (a.astype(f32) + b.astype(f32)).astype(bf16)

    for d in [0] + list(range(last, 0, -1)):
        source = (wt_index - d) % shard_count
        rank_in = lax.dynamic_index_in_dim(ranks, source, 0, False)
        result = expert_pass(
            got[d], grads_in[d], rank_in, gates_in[d], gate_full, up_full, down_full, capacity
        )
        coming = d - 1 if d else last
        if coming:
            result, got[coming] = beside(result, shift(got[(coming + 1) % shard_count], -1))
        if d == 0:
            result, gates_in = beside(result, gates_in)
        if 0 < d <= last - 2:
            carried = shift(after(add(carried, partial[d + 2]), got[d]), -1)
            result, carried = beside(result, carried)
        mixed[d], partial[d], d_gate, *kept = result
        rows.append(kept)
        gate_grads[d] = shift(d_gate, shard_count - d) if d else d_gate
        if coming:
            got[coming] = after(got[coming], partial[d])
    carried = shift(add(carried, partial[2]), -1)
    (gate_grad, up_grad), carried, gate_grads = beside(
        up_weight_grads([(after(r[0], partial[1]), r[3], r[4]) for r in rows], context_size),
        carried,
        gate_grads,
    )
    stacked = jnp.stack([gate_grads[d] for d in range(shard_count)], 0)
    for bit in (1, 2, 4):
        if bit < shard_count:
            stacked = jnp.where(wt_index & bit > 0, jnp.roll(stacked, bit, 0), stacked)
    stacked = stacked.reshape(EXPERTS, tok)
    grad_logits = gates * (stacked - jnp.sum(gates * stacked, 0, keepdims=True))
    grad_logits = grad_logits.T.astype(bf16)
    carried = shift(add(carried, partial[1]), -1)
    down_grad, home = beside(
        down_weight_grads([(after(r[2], gate_grad, grad_logits), r[1]) for r in rows], context_size), carried
    )

    grad_normed_two = partial[0].astype(f32) + home.astype(f32)
    grad_normed_two = grad_normed_two + dot_nt(grad_logits, router_full)
    grad_mid_norm, second_gain_grad = norm_backward(
        middle, inverse_two, second_gain, grad_normed_two
    )
    grad_middle = out_grad + grad_mid_norm
    grad_branch = (resid_scale * grad_middle).astype(bf16)
    grad_attended = dot(grad_branch, output_t).astype(bf16)
    gate_share, up_share, down_share = (
        lax.psum_scatter(grad, "ctx", scatter_dimension=0, tiled=False).astype(f32)
        for grad in (gate_grad, up_grad, down_grad)
    )
    carried = None
    query = after(turned_query, grad_attended)
    d_query, d_kv, ours = [], [], []
    for half in range(2):
        result = attention_backward(
            query,
            grad_attended,
            lse[half],
            attended[half],
            cosine,
            sine,
            kv_pieces,
            kv_own,
            places,
            starts,
            block_rows,
            half,
        )
        carried = shift(after(add(carried, mixed[last - half]), home), -1)
        result, carried = beside(result, carried)
        query = after(query, result[0])
        d_query.append(result[0])
        d_kv.append(result[1])
        ours.append(result[2:])
    carried = shift(add(carried, mixed[last - 2]), -1)
    owned, carried = beside(plane_sum(d_kv), carried)
    for d in range(last - 3, 0, -1):
        carried = shift(add(carried, mixed[d]), -1)
    mixture = mixed[0].astype(f32) + carried.astype(f32)
    layer_output = (middle + resid_scale * mixture).astype(bf16)
    d_query = jnp.concatenate(d_query, 1)
    d_key, d_value = (
        jnp.concatenate(
            [
                jnp.concatenate([owned[half][:, 256 * n : 256 * n + 256], ours[half][n]], 0)
                for half in range(2)
            ],
            1,
        )
        for n in range(2)
    )
    grad_key_low = turn(d_key, jnp.tile(cosine, (1, 4)), jnp.tile(sine, (1, 4)), -1.0).astype(
        bf16
    )
    grad_kv = jnp.concatenate([grad_key_low, d_value.astype(bf16)], 1)
    grad_normed_one = dot_nt(d_query, qkv_full[:, :1024]) + dot_nt(grad_kv, qkv_full[:, 1024:])
    grad_input_norm, first_gain_grad = norm_backward(
        inputs, inverse_one, first_gain, grad_normed_one
    )
    input_grad = (grad_middle + grad_input_norm).astype(bf16)

    column = lax.broadcasted_iota(jnp.int32, (tok, 128), 1)
    query_share, output_share, key_share, value_share, small = outer_sum(
        [(normed_one, d_query), (grad_branch, attended[0]), (grad_branch, attended[1]), (normed_one, grad_kv)],
        [
            (normed_two, jnp.pad(grad_logits, ((0, 0), (0, 128 - EXPERTS)))),
            (second_gain_grad, (column == EXPERTS).astype(bf16)),
            (first_gain_grad, (column == EXPERTS + 1).astype(bf16)),
        ],
        (1024, 1024, KV_WIDTH, KV_WIDTH, 128),
    )
    return (
        layer_output[None],
        input_grad[None],
        small[:, EXPERTS + 1],
        query_share,
        key_share,
        value_share,
        output_share.T,
        small[:, EXPERTS],
        small[:, :EXPERTS],
        gate_share,
        up_share,
        down_share,
    )


def solution(mesh):
    return jax.shard_map(
        per_device,
        mesh=mesh,
        in_specs=(
            P("wt", "ctx", None),
            P(("ctx", "wt")),
            P(("ctx", "wt"), None),
            P(("ctx", "wt"), None),
            P(("ctx", "wt"), None),
            P(None, ("ctx", "wt")),
            P(("ctx", "wt")),
            P(("ctx", "wt"), None),
            P("wt", "ctx", None),
            P("wt", "ctx", None),
            P("wt", None, "ctx"),
            P("wt", "ctx", None),
            P("wt", None),
            P("wt", "ctx", None),
        ),
        out_specs=(
            P("wt", "ctx", None),
            P("wt", "ctx", None),
            P(("ctx", "wt")),
            P(("ctx", "wt"), None),
            P(("ctx", "wt"), None),
            P(("ctx", "wt"), None),
            P(None, ("ctx", "wt")),
            P(("ctx", "wt")),
            P(("ctx", "wt"), None),
            P("wt", "ctx", None),
            P("wt", "ctx", None),
            P("wt", None, "ctx"),
        ),
        check_vma=False,
    )
```

```python
import functools

import jax
import jax.numpy as jnp
from jax import lax
from jax.experimental import pallas as pl
from jax.experimental.pallas import tpu as pltpu
from jax.sharding import PartitionSpec as P

MODEL_WIDTH = 1024
HQ = 16
KEY_VALUE_HEADS = 8
HEAD_SIZE = 64
EXPERTS = 32
TOP = 8
PROMPT = 2048
CLEN = 256
CONT_DEV = 2
FF = 512
QTILE = 128
PARTS = 4
KV_WIDTH = KEY_VALUE_HEADS * HEAD_SIZE
ALL = ("ctx", "wt")

att_scale = 0.015625
resid_scale = 0.22
norm_eps = 1e-06
rope_base = 10000.0
masked_score = -1e30

bf16 = jnp.bfloat16
f32 = jnp.float32
VMEM_LIMIT = 60 * 1024 * 1024
SMALL = pl.CostEstimate(flops=1_000_000_000, bytes_accessed=1_000_000, transcendentals=0)

NT = (((1,), (1,)), ((), ()))
TN = (((0,), (0,)), ((), ()))


def dot(a, b):
    return jnp.dot(a, b, preferred_element_type=f32)


def dot_nt(a, b):
    return lax.dot_general(a, b, NT, preferred_element_type=f32)


def dot_tn(a, b):
    return lax.dot_general(a, b, TN, preferred_element_type=f32)


def turn_tile(values, cosine, sine, direction):
    middle = HEAD_SIZE // 2
    first = lax.broadcasted_iota(jnp.int32, values.shape, 1) % HEAD_SIZE < middle
    turned = jnp.where(first, -pltpu.roll(values, 128 - middle, 1), pltpu.roll(values, middle, 1))
    return values * cosine + direction * turned * sine


def project_kernel(places, x_ref, cos_ref, sin_ref, *refs, counts):
    pieces = refs[: len(counts)]
    normed_ref, q_ref, kv_ref, qkv_ref, out_ref, rest_ref, gains_ref = refs[len(counts) :]
    rows = MODEL_WIDTH // sum(counts)
    at = 0
    for piece, count in zip(pieces, counts):
        for i in range(count):
            source = slice(i * rows, (i + 1) * rows)
            target = pl.ds(pl.multiple_of(places[at] * rows, rows), rows)
            qkv_ref[target, :] = piece[source, :2048]
            out_ref[target, :] = piece[source, 2048:3072]
            rest_ref[target, :] = piece[source, 3072:]
            at += 1
    gains = rest_ref[...].astype(f32).T[EXPERTS : EXPERTS + 8]
    gains_ref[...] = gains
    x = x_ref[...].astype(f32)
    inverse = lax.rsqrt(jnp.mean(x * x, -1, keepdims=True) + norm_eps)
    normed_ref[...] = (x * inverse * gains[:1]).astype(bf16)
    for c in range(8):
        raw = dot(normed_ref[...], qkv_ref[:, 256 * c : 256 * (c + 1)])
        for h in range(2):
            part = raw[:, 128 * h : 128 * (h + 1)]
            if c < 6:
                part = turn_tile(part, cos_ref[...], sin_ref[...], 1.0)
            column = 256 * c + 128 * h
            if column < 1024:
                q_ref[:, column : column + 128] = part.astype(bf16)
            else:
                column -= 1024
                at = column % KV_WIDTH // 256 * 512 + column // KV_WIDTH * 256 + column % 256
                kv_ref[:, at : at + 128] = part.astype(bf16)


def project(x, cosine, sine, pieces, counts, places):
    tok = x.shape[0]
    shape = jax.ShapeDtypeStruct
    whole = pl.BlockSpec(memory_space=pltpu.VMEM)
    return pl.pallas_call(
        functools.partial(project_kernel, counts=counts),
        in_specs=[pl.BlockSpec(memory_space=pltpu.SMEM)] + [whole] * (3 + len(pieces)),
        out_specs=[whole] * 7,
        out_shape=[
            shape((tok, MODEL_WIDTH), bf16),
            shape((tok, HQ * HEAD_SIZE), bf16),
            shape((tok, 2 * KV_WIDTH), bf16),
            shape((MODEL_WIDTH, 2048), bf16),
            shape((MODEL_WIDTH, 1024), bf16),
            shape((MODEL_WIDTH, 128), bf16),
            shape((8, MODEL_WIDTH), f32),
        ],
        compiler_params=pltpu.CompilerParams(vmem_limit_bytes=VMEM_LIMIT),
        cost_estimate=SMALL,
        name="project",
    )(places, x, cosine, sine, *pieces)


def middle_kernel(
    a_ref, b_ref, x_ref, out_ref, rest_ref, gains_ref, mask_ref, middle_ref, normed_ref, inv_ref, gates_ref
):
    half = a_ref.shape[1]
    branch = dot_nt(a_ref[...], out_ref[:, :half]) + dot_nt(b_ref[...], out_ref[:, half:])
    middle = x_ref[...].astype(f32) + resid_scale * branch
    middle_ref[...] = middle
    inverse = lax.rsqrt(jnp.mean(middle * middle, -1, keepdims=True) + norm_eps)
    inv_ref[...] = inverse
    normed = (middle * inverse * gains_ref[1:2]).astype(bf16)
    normed_ref[...] = normed
    mask = mask_ref[...] > 0.0
    logits = jnp.where(mask, dot(normed, rest_ref[...]), masked_score)
    top = jnp.max(logits, -1, keepdims=True)
    raised = jnp.where(mask, jnp.exp(logits - top), 0.0)
    gates_ref[...] = (raised / jnp.sum(raised, -1, keepdims=True)).T[:EXPERTS]


def to_gates(halves, x, output_t, rest, gain_rows, mask):
    tok = x.shape[0]
    shape = jax.ShapeDtypeStruct
    whole = pl.BlockSpec(memory_space=pltpu.VMEM)
    return pl.pallas_call(
        middle_kernel,
        in_specs=[whole] * 7,
        out_specs=[whole] * 4,
        out_shape=[
            shape((tok, MODEL_WIDTH), f32),
            shape((tok, MODEL_WIDTH), bf16),
            shape((tok, 1), f32),
            shape((EXPERTS, tok), f32),
        ],
        compiler_params=pltpu.CompilerParams(vmem_limit_bytes=VMEM_LIMIT),
        cost_estimate=SMALL,
        name="to_gates",
    )(*halves, x, output_t, rest, gain_rows, mask)


def gather_keys(pieces, scratch, places, block_rows):
    at = 0
    for piece in pieces:
        for b in range(piece.shape[0] // block_rows):
            start = pl.multiple_of(places[at] * block_rows, block_rows)
            scratch[pl.ds(start, block_rows), :] = piece[b * block_rows : (b + 1) * block_rows, :]
            at += 1


def pair_rows(ref, start, rows, j):
    both = ref[pl.ds(start, rows), 2 * HEAD_SIZE * j : 2 * HEAD_SIZE * (j + 1)]
    return jnp.concatenate([both[:, :HEAD_SIZE], both[:, HEAD_SIZE:]], 0)


def attention_forward_kernel(places, starts, q_ref, *refs, block_rows, pieces):
    k_refs, v_refs = refs[:pieces], refs[pieces : 2 * pieces]
    kc_ref, vc_ref, o_ref, lse_ref, k_scr, v_scr = refs[2 * pieces :]
    prompt_local = 2 * block_rows
    gather_keys(k_refs, k_scr, places, block_rows)
    gather_keys(v_refs, v_scr, places, block_rows)

    def store(start, rows, j, out, m, total, at):
        out = (out / total).astype(bf16)
        lse = m + jnp.log(total)
        o_ref[pl.ds(start, rows), 2 * HEAD_SIZE * j : 2 * HEAD_SIZE * (j + 1)] = jnp.concatenate(
            [out[:rows], out[rows:]], 1
        )
        row = jnp.broadcast_to(lse, (2 * rows, 128)).T[:1]
        lse_ref[0, 2 * j : 2 * j + 2, pl.ds(at, rows)] = jnp.concatenate(
            [row[:, :rows], row[:, rows:]], 0
        )

    def tile(i, _):
        start = pl.multiple_of(prompt_local + i * QTILE, 64)
        per = CLEN // QTILE
        seg = pl.multiple_of((i // per) * CLEN, CLEN)
        for j in range(2):
            lanes = slice(HEAD_SIZE * j, HEAD_SIZE * (j + 1))
            q = pair_rows(q_ref, start, QTILE, j) * bf16(att_scale)
            s1 = dot_nt(q, k_scr[:, lanes])
            s2 = dot_nt(q, kc_ref[pl.ds(seg, CLEN), lanes])
            place = lax.broadcasted_iota(jnp.int32, s2.shape, 0) % QTILE + (i % per) * QTILE
            s2 = jnp.where(lax.broadcasted_iota(jnp.int32, s2.shape, 1) <= place, s2, masked_score)
            m = jnp.maximum(jnp.max(s1, 1, keepdims=True), jnp.max(s2, 1, keepdims=True))
            e1 = jnp.exp(s1 - m)
            e2 = jnp.exp(s2 - m)
            total = jnp.sum(e1, 1, keepdims=True) + jnp.sum(e2, 1, keepdims=True)
            out = dot(e1.astype(bf16), v_scr[:, lanes])
            out = out + dot(e2.astype(bf16), vc_ref[pl.ds(seg, CLEN), lanes])
            store(start, QTILE, j, out, m, total, pl.multiple_of(i * QTILE, QTILE))
        return 0

    lax.fori_loop(0, CONT_DEV * CLEN // QTILE, tile, 0)

    for half, keys in enumerate((PROMPT // 2, PROMPT)):
        start = pl.multiple_of(starts[half], block_rows)
        for j in range(2):
            lanes = slice(HEAD_SIZE * j, HEAD_SIZE * (j + 1))
            q = pair_rows(q_ref, start, block_rows, j) * bf16(att_scale)
            s = dot_nt(q, k_scr[:keys, lanes])
            place = lax.broadcasted_iota(jnp.int32, s.shape, 0) % block_rows + starts[2 + half]
            s = jnp.where(lax.broadcasted_iota(jnp.int32, s.shape, 1) <= place, s, masked_score)
            m = jnp.max(s, 1, keepdims=True)
            e = jnp.exp(s - m)
            total = jnp.sum(e, 1, keepdims=True)
            out = dot(e.astype(bf16), v_scr[:keys, lanes])
            store(start, block_rows, j, out, m, total, CONT_DEV * CLEN + half * block_rows)


def key_specs(pieces, own, half):
    spec = pl.BlockSpec
    key, value = (lambda g, *_: (0, 4 * half + g)), (lambda g, *_: (0, 4 * half + 2 + g))
    keys = [spec((p.shape[0], 128), key) for p in pieces]
    values = [spec((p.shape[0], 128), value) for p in pieces]
    return keys + values + [spec((own, 128), key), spec((own, 128), value)]


def attention_forward(q, pieces, kv_own, places, starts, block_rows, half):
    tok = q.shape[0]
    spec = pl.BlockSpec
    return pl.pallas_call(
        functools.partial(
            attention_forward_kernel, block_rows=block_rows, pieces=len(pieces)
        ),
        grid_spec=pltpu.PrefetchScalarGridSpec(
            num_scalar_prefetch=2,
            grid=(2,),
            in_specs=[spec((tok, 256), lambda g, *_: (0, 2 * half + g))]
            + key_specs(pieces, kv_own.shape[0], half),
            out_specs=[
                spec((tok, 256), lambda g, *_: (0, g)),
                spec((1, 4, tok), lambda g, *_: (g, 0, 0)),
            ],
            scratch_shapes=[
                pltpu.VMEM((PROMPT, 2 * HEAD_SIZE), bf16),
                pltpu.VMEM((PROMPT, 2 * HEAD_SIZE), bf16),
            ],
        ),
        out_shape=[
            jax.ShapeDtypeStruct((tok, HQ * HEAD_SIZE // 2), bf16),
            jax.ShapeDtypeStruct((2, 4, tok), f32),
        ],
        compiler_params=pltpu.CompilerParams(vmem_limit_bytes=VMEM_LIMIT),
        cost_estimate=SMALL,
        name="attention_forward",
    )(places, starts, q, *pieces, *pieces, kv_own, kv_own)


def attention_backward_kernel(
    places, starts, q_ref, do_ref, lse_ref, o_ref, cos_ref, sin_ref, *refs, block_rows, pieces
):
    k_refs, v_refs = refs[:pieces], refs[pieces : 2 * pieces]
    kc_ref, vc_ref, dq_ref, dkv_ref, dkc_ref, dvc_ref = refs[2 * pieces : 2 * pieces + 6]
    k_scr, v_scr, dk_acc, dv_acc, dq_acc = refs[2 * pieces + 6 :]
    prompt_local = 2 * block_rows
    gather_keys(k_refs, k_scr, places, block_rows)
    gather_keys(v_refs, v_scr, places, block_rows)
    dk_acc[...] = jnp.zeros_like(dk_acc)
    dv_acc[...] = jnp.zeros_like(dv_acc)
    dkc_ref[...] = jnp.zeros_like(dkc_ref)
    dvc_ref[...] = jnp.zeros_like(dvc_ref)

    def row_pair(ref, start, rows, j):
        both = ref[0, 2 * j : 2 * j + 2, pl.ds(start, rows)]
        return jnp.concatenate([both[:1], both[1:]], 1)

    def centre(start, rows, j, d_out):
        product = d_out.astype(f32) * pair_rows(o_ref, start, rows, j).astype(f32)
        ones = jnp.ones((8, HEAD_SIZE), f32)
        return lax.dot_general(
            ones, product, NT, precision=lax.Precision.HIGHEST, preferred_element_type=f32
        )[:1]

    def part(k, v, q, d_out, lse, delta, allowed):
        s = dot_nt(k, q)
        if allowed is not None:
            s = jnp.where(allowed(s.shape), s, masked_score)
        p = jnp.exp(s - lse)
        d_p = dot_nt(v, d_out)
        d_s = (p * (d_p - delta)).astype(bf16)
        return dot_tn(d_s, k), dot(d_s, q), dot(p.astype(bf16), d_out)

    def store(start, rows, j, d_q):
        d_q = d_q * att_scale
        dq_acc[pl.ds(start, rows), 2 * HEAD_SIZE * j : 2 * HEAD_SIZE * (j + 1)] = jnp.concatenate(
            [d_q[:rows], d_q[rows:]], 1
        )

    def tile(i, _):
        start = pl.multiple_of(prompt_local + i * QTILE, 64)
        per = CLEN // QTILE
        seg = pl.multiple_of((i // per) * CLEN, CLEN)
        own = pl.ds(seg, CLEN)
        lane_start = pl.multiple_of(i * QTILE, QTILE)

        def allowed(shape):
            place = lax.broadcasted_iota(jnp.int32, shape, 1) % QTILE + (i % per) * QTILE
            return lax.broadcasted_iota(jnp.int32, shape, 0) <= place

        for j in range(2):
            lanes = slice(HEAD_SIZE * j, HEAD_SIZE * (j + 1))
            q = pair_rows(q_ref, start, QTILE, j) * bf16(att_scale)
            d_out = pair_rows(do_ref, start, QTILE, j)
            lse = row_pair(lse_ref, lane_start, QTILE, j)
            delta = centre(start, QTILE, j, d_out)
            a, b, c = part(k_scr[:, lanes], v_scr[:, lanes], q, d_out, lse, delta, None)
            dk_acc[:, lanes] += b
            dv_acc[:, lanes] += c
            d_q = a
            a, b, c = part(
                kc_ref[own, lanes], vc_ref[own, lanes], q, d_out, lse, delta, allowed
            )
            dkc_ref[own, lanes] += b
            dvc_ref[own, lanes] += c
            store(start, QTILE, j, d_q + a)
        return 0

    lax.fori_loop(0, CONT_DEV * CLEN // QTILE, tile, 0)

    for half, keys in enumerate((PROMPT // 2, PROMPT)):
        start = pl.multiple_of(starts[half], block_rows)
        at = CONT_DEV * CLEN + half * block_rows

        def allowed(shape):
            place = lax.broadcasted_iota(jnp.int32, shape, 1) % block_rows + starts[2 + half]
            return lax.broadcasted_iota(jnp.int32, shape, 0) <= place

        for j in range(2):
            lanes = slice(HEAD_SIZE * j, HEAD_SIZE * (j + 1))
            q = pair_rows(q_ref, start, block_rows, j) * bf16(att_scale)
            d_out = pair_rows(do_ref, start, block_rows, j)
            lse = row_pair(lse_ref, at, block_rows, j)
            delta = centre(start, block_rows, j, d_out)
            a, b, c = part(
                k_scr[:keys, lanes], v_scr[:keys, lanes], q, d_out, lse, delta, allowed
            )
            dk_acc[:keys, lanes] += b
            dv_acc[:keys, lanes] += c
            store(start, block_rows, j, a)

    g = pl.program_id(0)
    key_lanes = pl.ds(pl.multiple_of(g * 128, 128), 128)
    value_lanes = pl.ds(pl.multiple_of(256 + g * 128, 128), 128)
    for b in range(PROMPT // block_rows):
        source = pl.ds(pl.multiple_of(places[b] * block_rows, block_rows), block_rows)
        rows = slice(b * block_rows, (b + 1) * block_rows)
        dkv_ref[rows, key_lanes] = dk_acc[source, :].astype(bf16)
        dkv_ref[rows, value_lanes] = dv_acc[source, :].astype(bf16)
    for c in range(2):
        lanes = slice(128 * c, 128 * (c + 1))
        dq_ref[:, lanes] = turn_tile(dq_acc[:, lanes], cos_ref[...], sin_ref[...], -1.0).astype(
            bf16
        )


def attention_backward(
    q, d_out, lse, attended, cosine, sine, pieces, kv_own, places, starts, block_rows, half
):
    tok = q.shape[0]
    own = kv_own.shape[0]
    spec = pl.BlockSpec
    wide = spec((tok, 256), lambda g, *_: (0, 2 * half + g))
    narrow = spec((tok, 256), lambda g, *_: (0, g))
    ours = spec((own, 128), lambda g, *_: (0, g))
    table = spec((tok, 128), lambda g, *_: (0, 0))
    return pl.pallas_call(
        functools.partial(
            attention_backward_kernel, block_rows=block_rows, pieces=len(pieces)
        ),
        grid_spec=pltpu.PrefetchScalarGridSpec(
            num_scalar_prefetch=2,
            grid=(2,),
            in_specs=[wide, wide, spec((1, 4, tok), lambda g, *_: (g, 0, 0)), narrow, table, table]
            + key_specs(pieces, own, half),
            out_specs=[
                spec((tok, 256), lambda g, *_: (0, g)),
                spec((PROMPT, KV_WIDTH), lambda g, *_: (0, 0)),
                ours,
                ours,
            ],
            scratch_shapes=[
                pltpu.VMEM((PROMPT, 2 * HEAD_SIZE), bf16),
                pltpu.VMEM((PROMPT, 2 * HEAD_SIZE), bf16),
                pltpu.VMEM((PROMPT, 2 * HEAD_SIZE), f32),
                pltpu.VMEM((PROMPT, 2 * HEAD_SIZE), f32),
                pltpu.VMEM((tok, 4 * HEAD_SIZE), f32),
            ],
        ),
        out_shape=[
            jax.ShapeDtypeStruct((tok, HQ * HEAD_SIZE // 2), bf16),
            jax.ShapeDtypeStruct((PROMPT, KV_WIDTH), bf16),
            jax.ShapeDtypeStruct((own, KV_WIDTH // 2), f32),
            jax.ShapeDtypeStruct((own, KV_WIDTH // 2), f32),
        ],
        compiler_params=pltpu.CompilerParams(vmem_limit_bytes=VMEM_LIMIT),
        cost_estimate=SMALL,
        name="attention_backward",
    )(places, starts, q, d_out, lse, attended, cosine, sine, *pieces, *pieces, kv_own, kv_own)


def expert_kernel(
    counts,
    a2_ref,
    df_ref,
    rank_ref,
    gate_ref,
    wg_ref,
    wu_ref,
    wd_ref,
    mix_ref,
    da_ref,
    dg_ref,
    x_ref,
    dy_ref,
    z_ref,
    dgate_ref,
    dup_ref,
    mix_acc,
    da_acc,
    *,
    sizes,
):
    e = pl.program_id(0)

    @pl.when(e == 0)
    def _():
        mix_acc[...] = jnp.zeros_like(mix_acc)
        da_acc[...] = jnp.zeros_like(da_acc)

    def body(size):
        rank = rank_ref[0]
        gates = gate_ref[0]
        tok = rank.shape[1]
        slot = lax.broadcasted_iota(jnp.int32, (size, tok), 0).astype(f32)
        hit = slot == rank
        chosen = hit.astype(f32).astype(bf16)
        gate = jnp.sum(jnp.where(hit, gates, 0.0), 1, keepdims=True)
        x = dot(chosen, a2_ref[...]).astype(bf16)
        d_mix = resid_scale * dot(chosen, df_ref[...])
        wg = wg_ref[:, 0].reshape(MODEL_WIDTH, FF)
        wu = wu_ref[:, 0].reshape(MODEL_WIDTH, FF)
        wd = jnp.concatenate([wd_ref[c, 0] for c in range(wd_ref.shape[0])], 1)
        g = dot(x, wg)
        u = dot(x, wu)
        sig = jax.nn.sigmoid(g)
        z = (g * sig * u).astype(bf16)
        y = dot(z, wd).astype(bf16).astype(f32)
        d_gate_value = jnp.sum(d_mix * y, 1, keepdims=True)
        dg_ref[0] = jnp.sum(jnp.where(hit, d_gate_value, 0.0), 0, keepdims=True)
        mix_acc[...] += dot_tn(chosen, (gate * y).astype(bf16))
        d_y = (gate * d_mix).astype(bf16)
        d_z = dot_nt(d_y, wd)
        d_g = (d_z * u * sig * (1.0 + g * (1.0 - sig))).astype(bf16)
        d_u = (d_z * g * sig).astype(bf16)
        d_r = (dot_nt(d_g, wg) + dot_nt(d_u, wu)).astype(bf16)
        da_acc[...] += dot_tn(chosen, d_r)
        for ref, value in (
            (x_ref, x),
            (dy_ref, d_y),
            (z_ref, z),
            (dgate_ref, d_g),
            (dup_ref, d_u),
        ):
            ref[0, :size] = value
            if size < ref.shape[1]:
                ref[0, size:] = jnp.zeros((ref.shape[1] - size, ref.shape[2]), bf16)

    least = -1
    for size in sizes:
        pl.when((counts[e] > least) & (counts[e] <= size))(functools.partial(body, size))
        least = size

    @pl.when(e == pl.num_programs(0) - 1)
    def _():
        mix_ref[...] = mix_acc[...].astype(bf16)
        da_ref[...] = da_acc[...].astype(bf16)


def expert_pass(a2, df, rank, gates, wg, wu, wd, capacity):
    tok = a2.shape[0]
    parts, experts = wg.shape[0], wg.shape[1]
    sizes = sorted({min(size, capacity) for size in (128, 192, 256, capacity)})
    counts = (jnp.max(rank, (1, 2)) + 1.0).astype(jnp.int32)
    spec = pl.BlockSpec
    whole = spec((tok, MODEL_WIDTH), lambda e, *_: (0, 0))
    row = spec((1, 1, tok), lambda e, *_: (e, 0, 0))
    up = spec((parts, 1, MODEL_WIDTH // parts, FF), lambda e, *_: (0, e, 0, 0))
    down = spec((parts, 1, FF, MODEL_WIDTH // parts), lambda e, *_: (0, e, 0, 0))
    rows_wide = spec((1, capacity, MODEL_WIDTH), lambda e, *_: (e, 0, 0))
    rows_thin = spec((1, capacity, FF), lambda e, *_: (e, 0, 0))
    shape = jax.ShapeDtypeStruct
    return pl.pallas_call(
        functools.partial(expert_kernel, sizes=sizes),
        grid_spec=pltpu.PrefetchScalarGridSpec(
            num_scalar_prefetch=1,
            grid=(experts,),
            in_specs=[whole, whole, row, row, up, up, down],
            out_specs=[whole, whole, row, rows_wide, rows_wide, rows_thin, rows_thin, rows_thin],
            scratch_shapes=[
                pltpu.VMEM((tok, MODEL_WIDTH), f32),
                pltpu.VMEM((tok, MODEL_WIDTH), f32),
            ],
        ),
        out_shape=[
            shape((tok, MODEL_WIDTH), bf16),
            shape((tok, MODEL_WIDTH), bf16),
            shape((experts, 1, tok), f32),
            shape((experts, capacity, MODEL_WIDTH), bf16),
            shape((experts, capacity, MODEL_WIDTH), bf16),
            shape((experts, capacity, FF), bf16),
            shape((experts, capacity, FF), bf16),
            shape((experts, capacity, FF), bf16),
        ],
        compiler_params=pltpu.CompilerParams(vmem_limit_bytes=VMEM_LIMIT),
        cost_estimate=SMALL,
        name="expert_pass",
    )(counts, a2, df, rank, gates, wg, wu, wd)


def up_grad_kernel(*refs, sources):
    rows = refs[: 3 * sources]
    gate_ref, up_ref = refs[3 * sources :]
    for n, out_ref in ((1, gate_ref), (2, up_ref)):
        total = None
        for s in range(sources):
            term = dot_tn(rows[3 * s][0], rows[3 * s + n][0])
            total = term if total is None else total + term
        out_ref[...] = total.astype(bf16).reshape(out_ref.shape)


def down_grad_kernel(*refs, sources, parts):
    rows, down_ref = refs[: 2 * sources], refs[-1]
    width = MODEL_WIDTH // parts
    total = None
    for s in range(sources):
        term = dot_tn(rows[2 * s][0], rows[2 * s + 1][0])
        total = term if total is None else total + term
    total = total.astype(bf16)
    for c in range(parts):
        down_ref[c, 0] = total[:, c * width : (c + 1) * width]


def row_specs(rows):
    return [pl.BlockSpec((1,) + a.shape[1:], lambda e: (e, 0, 0)) for r in rows for a in r]


def up_weight_grads(rows, parts):
    experts = rows[0][0].shape[0]
    shape = (parts, experts, MODEL_WIDTH // parts, FF)
    out = pl.BlockSpec((parts, 1) + shape[2:], lambda e: (0, e, 0, 0))
    return pl.pallas_call(
        functools.partial(up_grad_kernel, sources=len(rows)),
        grid=(experts,),
        in_specs=row_specs(rows),
        out_specs=[out, out],
        out_shape=[jax.ShapeDtypeStruct(shape, bf16)] * 2,
        compiler_params=pltpu.CompilerParams(vmem_limit_bytes=VMEM_LIMIT),
        cost_estimate=SMALL,
        name="up_weight_grads",
    )(*[a for r in rows for a in r])


def down_weight_grads(rows, parts):
    experts = rows[0][0].shape[0]
    shape = (parts, experts, FF, MODEL_WIDTH // parts)
    return pl.pallas_call(
        functools.partial(down_grad_kernel, sources=len(rows), parts=parts),
        grid=(experts,),
        in_specs=row_specs(rows),
        out_specs=pl.BlockSpec((parts, 1) + shape[2:], lambda e: (0, e, 0, 0)),
        out_shape=jax.ShapeDtypeStruct(shape, bf16),
        compiler_params=pltpu.CompilerParams(vmem_limit_bytes=VMEM_LIMIT),
        cost_estimate=SMALL,
        name="down_weight_grads",
    )(*[a for r in rows for a in r])


def swap(x, mask):
    return lax.ppermute(x, "ctx", [(i, i ^ mask) for i in range(lax.axis_size("ctx"))])


def gather_ctx(x, rows):
    if lax.axis_size("ctx") != 8:
        return lax.all_gather(x[:rows], "ctx", axis=0, tiled=True)
    return plane_gather(x, rows)


MESH = pl.DeviceIdType.MESH
ANY = pl.BlockSpec(memory_space=pl.ANY)


def partner(mask):
    me = lax.axis_index("ctx")
    other = me
    for bit in (1, 2, 4):
        if mask & bit:
            other = other + bit - 2 * bit * ((me // bit) % 2)
    return other


def ahead(distance):
    return (lax.axis_index("wt") + distance) % lax.axis_size("wt")


class Copies:
    def __init__(self, send, recv):
        self.send, self.recv, self.made = send, recv, {}

    def start(self, name, source, target, device):
        n = len(self.made)
        self.made[name] = copy = pltpu.make_async_remote_copy(
            src_ref=source,
            dst_ref=target,
            send_sem=self.send.at[n],
            recv_sem=self.recv.at[n],
            device_id=device,
            device_id_type=MESH,
        )
        copy.start()

    def arrived(self, name):
        self.made[name].wait_recv()

    def close(self):
        for copy in self.made.values():
            copy.wait_send()


def greet(devices):
    barrier = pltpu.get_barrier_semaphore()
    for device in devices:
        pl.semaphore_signal(barrier, inc=1, device_id=device, device_id_type=MESH)
    pl.semaphore_wait(barrier, len(devices))


def plane_steps(copies, block, half, key):
    side, near, far = ({"ctx": partner(m)} for m in (1, 2, 4))
    top, end = (lambda m: block(m, 0, half)), (lambda m: block(m, half, half))

    def first():
        copies.start((key, 2), block(0), block(2), near)
        copies.start((key, 4), block(0), block(4), far)
        copies.start((key, 1), block(0), block(1), side)

    def second():
        copies.arrived((key, 2))
        copies.start((key, 6), top(2), top(6), far)
        copies.start((key, 3), block(2), block(3), side)

    def third():
        copies.arrived((key, 4))
        copies.start((key, 7), end(4), end(6), near)
        copies.start((key, 5), block(4), block(5), side)

    def fourth():
        copies.arrived((key, 6))
        copies.arrived((key, 7))
        copies.start((key, 8), block(6), block(7), side)

    def last():
        for m in (1, 3, 5, 8):
            copies.arrived((key, m))

    return [first, second, third, fourth, last]


def plane_gather_kernel(x_ref, out_ref, send, recv, own_sem):
    rows = out_ref.shape[0] // 8
    greet([{"ctx": partner(m)} for m in (1, 2, 4)])
    own = pltpu.make_async_copy(x_ref.at[pl.ds(0, rows)], out_ref.at[pl.ds(0, rows)], own_sem)
    own.start()
    copies = Copies(send, recv)

    def block(m, start=0, count=rows):
        if m == 0:
            return x_ref.at[pl.ds(start, count)]
        return out_ref.at[pl.ds(m * rows + start, count)]

    for step in plane_steps(copies, block, rows // 2, 0):
        step()
    own.wait()
    copies.close()


def plane_gather(x, rows):
    return pl.pallas_call(
        plane_gather_kernel,
        in_specs=[ANY],
        out_specs=ANY,
        out_shape=jax.ShapeDtypeStruct((8 * rows, x.shape[1]), x.dtype),
        scratch_shapes=[
            pltpu.SemaphoreType.DMA((8,)),
            pltpu.SemaphoreType.DMA((8,)),
            pltpu.SemaphoreType.DMA,
        ],
        compiler_params=pltpu.CompilerParams(collective_id=1, has_side_effects=True),
        cost_estimate=SMALL,
        name="plane_gather",
    )(x)


def packed_gather_kernel(x_ref, out_ref, send, recv, own_sem):
    rows = x_ref.shape[0]
    greet(
        [{"ctx": partner(m)} for m in (1, 2, 4)] + [{"wt": ahead(d)} for d in (1, 2, 3)]
    )
    own = pltpu.make_async_copy(x_ref, out_ref.at[pl.ds(0, rows)], own_sem)
    own.start()
    copies = Copies(send, recv)

    def block_of(d):
        def block(m, start=0, count=rows):
            if m == 0 and d == 0:
                return x_ref.at[pl.ds(start, count)]
            return out_ref.at[pl.ds((4 * m + d) * rows + start, count)]

        return block

    for d in (1, 3, 2):
        copies.start(d, x_ref, block_of(d)(0), {"wt": ahead(d)})
    steps = {d: plane_steps(copies, block_of(d), rows // 2, ("plane", d)) for d in range(4)}
    steps[0][0]()
    for d, before in ((1, 0), (3, 1), (2, 3)):
        copies.arrived(d)
        steps[d][0]()
        steps[before][1]()
        steps[before][2]()
        if d != 1:
            steps[{3: 0, 2: 1}[d]][3]()
    steps[2][1]()
    steps[2][2]()
    steps[3][3]()
    steps[2][3]()
    for d in range(4):
        steps[d][4]()
    own.wait()
    copies.close()


def packed_gather(x):
    return pl.pallas_call(
        packed_gather_kernel,
        in_specs=[ANY],
        out_specs=ANY,
        out_shape=jax.ShapeDtypeStruct((32 * x.shape[0], x.shape[1]), x.dtype),
        scratch_shapes=[
            pltpu.SemaphoreType.DMA((35,)),
            pltpu.SemaphoreType.DMA((35,)),
            pltpu.SemaphoreType.DMA,
        ],
        compiler_params=pltpu.CompilerParams(collective_id=2, has_side_effects=True),
        cost_estimate=SMALL,
        name="packed_gather",
    )(x)


def sum_steps(copies, x_ref, key, sib, low, recv, out_ref, columns):
    rows = x_ref.shape[0] // 8
    half = rows // 2
    side, near, far = ({"ctx": partner(m)} for m in (1, 2, 4))

    def blocks(ref, m, start=0, count=rows):
        return ref.at[pl.ds(m * rows + start, count), columns]

    def added(m, start, count):
        ours = x_ref[m * rows + start : m * rows + start + count, columns].astype(f32)
        at = m // 2 * rows + start
        return ours + sib[at : at + count, columns].astype(f32)

    def put(place, start, value, device):
        at = place * rows + start
        low[at : at + half, columns] = value.astype(bf16)
        copies.start(
            (key, "low", place, start),
            blocks(low, place, start, half),
            blocks(recv, place, start, half),
            device,
        )

    def send_one(m):
        copies.start((key, m), blocks(x_ref, m), blocks(sib, m // 2), side)

    def first():
        for m in (7, 3, 5, 1):
            send_one(m)

    def second():
        copies.arrived((key, 7))
        put(0, 0, added(6, 0, half), far)
        put(0, half, added(6, half, half), near)

    def third():
        copies.arrived((key, 3))
        put(1, half, added(2, half, half), near)
        copies.arrived((key, 5))
        put(2, 0, added(4, 0, half), far)

    def fourth():
        copies.arrived((key, "low", 0, 0))
        put(1, 0, added(2, 0, half) + recv[0:half, columns].astype(f32), near)
        copies.arrived((key, "low", 0, half))
        put(2, half, added(4, half, half) + recv[half:rows, columns].astype(f32), far)

    def last():
        copies.arrived((key, 1))
        for place in (1, 2):
            for start in (0, half):
                copies.arrived((key, "low", place, start))
        out_ref[:, columns] = (
            added(0, 0, rows)
            + recv[rows : 2 * rows, columns].astype(f32)
            + recv[2 * rows :, columns].astype(f32)
        )

    return [first, second, third, fourth, last, send_one]


def plane_sum_kernel(*refs, sets):
    x_refs, out_refs = refs[:sets], refs[sets : 2 * sets]
    sibs, lows, recvs = (refs[(2 + n) * sets : (3 + n) * sets] for n in range(3))
    send, recv_sem = refs[5 * sets :]
    greet([{"ctx": partner(m)} for m in (1, 2, 4)])
    copies = Copies(send, recv_sem)
    steps = [
        sum_steps(copies, x_refs[n], n, sibs[n], lows[n], recvs[n], out_refs[n], slice(None))
        for n in range(sets)
    ]
    for n in range(5):
        for one in steps:
            one[n]()
    copies.close()


def plane_sum(arrays):
    if lax.axis_size("ctx") != 8:
        return [
            lax.psum_scatter(x, "ctx", scatter_dimension=0, tiled=True).astype(f32)
            for x in arrays
        ]
    sets = len(arrays)
    rows, columns = arrays[0].shape[0] // 8, arrays[0].shape[1]
    vmem = pl.BlockSpec(memory_space=pltpu.VMEM)
    return pl.pallas_call(
        functools.partial(plane_sum_kernel, sets=sets),
        in_specs=[vmem] * sets,
        out_specs=[vmem] * sets,
        out_shape=[jax.ShapeDtypeStruct((rows, columns), f32)] * sets,
        scratch_shapes=[pltpu.VMEM((4 * rows, columns), bf16)] * sets
        + [pltpu.VMEM((3 * rows, columns), bf16)] * (2 * sets)
        + [pltpu.SemaphoreType.DMA((10 * sets,)), pltpu.SemaphoreType.DMA((10 * sets,))],
        compiler_params=pltpu.CompilerParams(
            collective_id=3, has_side_effects=True, vmem_limit_bytes=VMEM_LIMIT
        ),
        cost_estimate=SMALL,
        name="plane_sum",
    )(*arrays)


def full_sum_kernel(*refs, sides, count, widths):
    arrays = sum(sides)
    out_refs = refs[arrays : arrays + len(widths)]
    a_refs, b_refs = refs[: sides[0]], refs[sides[0] : arrays]
    x_ref, sib, low, recv, total, total_low, arrived, result_ref, send, recv_sem = refs[
        arrays + len(widths) :
    ]
    rows = result_ref.shape[0]
    greet(
        [{"ctx": partner(m)} for m in (1, 2, 4)] + [{"wt": ahead(d)} for d in (1, 2, 3)]
    )
    copies = Copies(send, recv_sem)
    wide = x_ref.shape[1]
    edges = [128 * (n * (wide // 128) // PARTS) for n in range(PARTS + 1)]
    parts = [slice(a, b) for a, b in zip(edges, edges[1:])]
    steps = [
        sum_steps(copies, x_ref, n, sib, low, recv, total, columns)
        for n, columns in enumerate(parts)
    ]

    def leave(n):
        total_low[:, parts[n]] = total[:, parts[n]].astype(bf16)
        for d in (2, 1, 3):
            copies.start(
                ("wt", n, d),
                total_low.at[pl.ds(pl.multiple_of(ahead(d) * rows, rows), rows), parts[n]],
                arrived.at[pl.ds((d - 1) * rows, rows), parts[n]],
                {"wt": ahead(d)},
            )

    def finish(n):
        own = pl.ds(pl.multiple_of(ahead(0) * rows, rows), rows)
        result = total[own, parts[n]]
        for d in (1, 3, 2):
            copies.arrived(("wt", n, d))
            result = result + arrived[(d - 1) * rows : d * rows, parts[n]].astype(f32)
        result_ref[:, parts[n]] = result

    def make(m):
        lanes = pl.ds(pl.multiple_of(partner(m) * 128, 128), 128)
        block = slice(m * 4 * rows, (m + 1) * 4 * rows)
        terms = [dot_tn(a[:, lanes], b[...]) for a, b in zip(a_refs, b_refs)]
        at = 0
        for term in terms[:count] + [sum(terms[count:])]:
            x_ref[block, at : at + term.shape[1]] = term.astype(bf16)
            at += term.shape[1]

    for m in (7, 3, 5, 1):
        make(m)
        for one in steps:
            one[5](m)
    make(6)
    for one in steps:
        one[1]()
    make(2)
    make(4)
    for one in steps:
        one[2]()
    make(0)
    for one in steps:
        one[3]()
    for n in range(PARTS):
        steps[n][4]()
        leave(n)
    for n in range(PARTS):
        finish(n)
    at = 0
    for out_ref, width in zip(out_refs, widths):
        out_ref[...] = result_ref[:, at : at + width]
        at += width
    copies.close()


def full_sum(pairs, extra, widths):
    rows, columns = MODEL_WIDTH // 32, sum(widths)
    vmem = pl.BlockSpec(memory_space=pltpu.VMEM)
    lefts = [a for a, _ in [*pairs, *extra]]
    rights = [b for _, b in [*pairs, *extra]]
    return pl.pallas_call(
        functools.partial(
            full_sum_kernel, sides=(len(lefts), len(rights)), count=len(pairs), widths=widths
        ),
        in_specs=[vmem] * (len(lefts) + len(rights)),
        out_specs=[vmem] * len(widths),
        out_shape=[jax.ShapeDtypeStruct((rows, width), f32) for width in widths],
        scratch_shapes=[
            pltpu.VMEM((32 * rows, columns), bf16),
            pltpu.VMEM((16 * rows, columns), bf16),
            pltpu.VMEM((12 * rows, columns), bf16),
            pltpu.VMEM((12 * rows, columns), bf16),
            pltpu.VMEM((4 * rows, columns), f32),
            pltpu.VMEM((4 * rows, columns), bf16),
            pltpu.VMEM((3 * rows, columns), bf16),
            pltpu.VMEM((rows, columns), f32),
            pltpu.SemaphoreType.DMA((13 * PARTS,)),
            pltpu.SemaphoreType.DMA((13 * PARTS,)),
        ],
        compiler_params=pltpu.CompilerParams(
            collective_id=4, has_side_effects=True, vmem_limit_bytes=VMEM_LIMIT
        ),
        cost_estimate=SMALL,
        name="full_sum",
    )(*lefts, *rights)


def shift(x, distance):
    n = lax.axis_size("wt")
    return lax.ppermute(x, "wt", [(i, (i + distance) % n) for i in range(n)])


def beside(results, *arrivals):
    out = lax.optimization_barrier((results, arrivals))
    return (out[0],) + tuple(out[1])


def gather_all(x):
    ctx, wt = lax.axis_size("ctx"), lax.axis_size("wt")
    if ctx != 8 or wt != 4:
        return [lax.all_gather(x, ALL, axis=0, tiled=True)], [1], jnp.zeros((1,), jnp.int32)
    ctx_index, wt_index = lax.axis_index("ctx"), lax.axis_index("wt")
    m = jnp.arange(8, dtype=jnp.int32)
    d = jnp.arange(4, dtype=jnp.int32)
    places = ((ctx_index ^ m) * wt)[:, None] + ((wt_index - d) % wt)[None, :]
    return [packed_gather(x)], [32], places.reshape(-1).astype(jnp.int32)


def outer_sum(pairs, extra, widths):
    if lax.axis_size("ctx") != 8 or lax.axis_size("wt") != 4:
        parts = [dot_tn(a, b) for a, b in pairs] + [sum(dot_tn(a, b) for a, b in extra)]
        result = lax.psum_scatter(
            jnp.concatenate(parts, 1).astype(bf16), ALL, scatter_dimension=0, tiled=True
        ).astype(f32)
        edges = [sum(widths[: n + 1]) for n in range(len(widths) - 1)]
        return jnp.split(result, edges, 1)
    return full_sum(pairs, extra, widths)


def after(x, *others):
    return lax.optimization_barrier((x,) + others)[0]


def rope_tables(positions, width):
    middle = HEAD_SIZE // 2
    frequency = jnp.power(
        jnp.float32(rope_base), -2.0 * jnp.arange(middle, dtype=f32) / HEAD_SIZE
    )
    angles = positions.astype(f32)[:, None] * frequency[None, :]
    times = width // middle
    return jnp.tile(jnp.cos(angles), (1, times)), jnp.tile(jnp.sin(angles), (1, times))


def turn(values, cosine, sine, direction):
    middle = HEAD_SIZE // 2
    first = lax.broadcasted_iota(jnp.int32, values.shape, 1) % HEAD_SIZE < middle
    turned = jnp.where(first, -jnp.roll(values, -middle, 1), jnp.roll(values, middle, 1))
    width = values.shape[1]
    return values * cosine[:, :width] + direction * turned * sine[:, :width]


def norm_forward(values, gain):
    inverse = lax.rsqrt(jnp.mean(values * values, -1, keepdims=True) + norm_eps)
    return (values * inverse * gain, inverse)


def norm_backward(values, inverse, gain, grad_out):
    scaled = gain * grad_out
    gain_grad = (grad_out * values * inverse).astype(bf16)
    projection = jnp.mean(scaled * values, -1, keepdims=True)
    return (inverse * scaled - values * inverse * inverse * inverse * projection, gain_grad)


def per_device(
    layer_input,
    attention_gain,
    query_weight,
    key_matrix,
    value_matrix,
    output_weight,
    mixture_gain,
    router_weight,
    gate_weight,
    up_weight,
    down_weight,
    expert_routes,
    prompt_deal,
    output_grad,
):
    tok = layer_input.shape[1]
    prompt_local = tok - CONT_DEV * CLEN
    block_rows = prompt_local // 2
    context_size = lax.axis_size("ctx")
    shard_count = lax.axis_size("wt")
    expert_count = gate_weight.shape[0]
    capacity = 8 * ((tok * TOP * 7 // (4 * EXPERTS) + 7) // 8)
    ctx_index = lax.axis_index("ctx")
    wt_index = lax.axis_index("wt")
    inputs = layer_input[0].astype(f32)
    routes = expert_routes[0]
    deal_row = prompt_deal[0]
    out_low = output_grad[0]
    out_grad = out_low.astype(f32)

    own_rows = query_weight.shape[0]
    packed = jnp.concatenate(
        [
            query_weight,
            key_matrix,
            value_matrix,
            output_weight.T,
            router_weight,
            attention_gain[:, None],
            mixture_gain[:, None],
            jnp.zeros((own_rows, 94), bf16),
        ],
        1,
    )
    pieces, counts, block_places = gather_all(packed)

    gate_full = lax.all_gather(gate_weight, "ctx", axis=0, tiled=False)
    up_full = lax.all_gather(up_weight, "ctx", axis=0, tiled=False)
    down_full = lax.all_gather(down_weight, "ctx", axis=0, tiled=False)

    mask = jnp.any(
        routes[:, :, None] == jnp.arange(EXPERTS, dtype=jnp.int32)[None, None, :], 1
    )
    order = jnp.arange(tok, dtype=jnp.int32)
    before = (order[None, :] < order[:, None]).astype(bf16)
    rank = jnp.where(mask, dot(before, mask.astype(bf16)), -1.0)
    ranks = lax.all_to_all(
        rank.T.reshape(shard_count, expert_count, 1, tok), "wt", 0, 0, tiled=True
    )
    last = shard_count - 1
    grads_in = {0: out_low, last: shift(after(out_low, pieces[0], ranks), -1)}

    pieces, ranks = beside(pieces, ranks)
    local_rows = jnp.arange(tok, dtype=jnp.int32)
    mine = lax.dynamic_slice_in_dim(deal_row, 2 * ctx_index, 2, 0)
    prompt_place = (
        jnp.where(local_rows < block_rows, mine[0], mine[1]) * block_rows
        + local_rows % block_rows
    )
    positions = jnp.where(
        local_rows < prompt_local, prompt_place, PROMPT + (local_rows - prompt_local) % CLEN
    )
    cosine, sine = rope_tables(positions, 128)
    normed_one, turned_query, kv_low, qkv_full, output_t, rest, gain_rows = project(
        layer_input[0], cosine, sine, pieces, counts, block_places
    )
    router_full = rest[:, :EXPERTS]
    first_gain, second_gain = gain_rows[0], gain_rows[1]
    inverse_one = lax.rsqrt(jnp.mean(inputs * inputs, -1, keepdims=True) + norm_eps)
    kv_own = kv_low[prompt_local:]
    kv_pieces, grads_in[last] = beside([gather_ctx(kv_low, prompt_local)], grads_in[last])

    places = deal_row
    if context_size == 8:
        pairs = deal_row.reshape(2, 2, 2, 2)
        for axis, bit in ((0, 4), (1, 2), (2, 1)):
            pairs = jnp.where(ctx_index & bit > 0, jnp.flip(pairs, axis), pairs)
        places = pairs.reshape(-1)
    low = (mine[0] > mine[1]).astype(jnp.int32)
    starts = jnp.stack(
        [
            low * block_rows,
            (1 - low) * block_rows,
            jnp.min(mine) * block_rows,
            jnp.max(mine) * block_rows,
        ]
    ).astype(jnp.int32)
    heads = []
    for half in range(2):
        result = attention_forward(
            turned_query, kv_pieces, kv_own, places, starts, block_rows, half
        )
        d = last - 1 - half
        grads_in[d] = shift(grads_in[d + 1], -1)
        result, grads_in[d] = beside(result, grads_in[d])
        if half == 0:
            turned_query = after(turned_query, result[0])
        heads.append(result)
    for d in range(last - 3, 0, -1):
        grads_in[d] = shift(grads_in[d + 1], -1)
    attended = [out for out, _ in heads]
    lse = [row for _, row in heads]

    middle, normed_two, inverse_two, gates = to_gates(
        attended,
        layer_input[0],
        output_t,
        rest,
        gain_rows,
        jnp.pad(mask.astype(f32), ((0, 0), (0, 128 - EXPERTS))),
    )

    gates_out = gates.reshape(shard_count, expert_count, 1, tok)
    gates_in = []
    for d in range(shard_count):
        piece = lax.dynamic_index_in_dim(gates_out, (wt_index + d) % shard_count, 0, False)
        gates_in.append(shift(piece, d) if d else piece)
    got = {0: normed_two}
    partial, mixed, gate_grads, rows = {}, {}, {}, []
    carried = None

    def add(a, b):
        return b if a is None else (a.astype(f32) + b.astype(f32)).astype(bf16)

    for d in [0] + list(range(last, 0, -1)):
        source = (wt_index - d) % shard_count
        rank_in = lax.dynamic_index_in_dim(ranks, source, 0, False)
        result = expert_pass(
            got[d], grads_in[d], rank_in, gates_in[d], gate_full, up_full, down_full, capacity
        )
        coming = d - 1 if d else last
        if coming:
            result, got[coming] = beside(result, shift(got[(coming + 1) % shard_count], -1))
        if d == 0:
            result, gates_in = beside(result, gates_in)
        if 0 < d <= last - 2:
            carried = shift(after(add(carried, partial[d + 2]), got[d]), -1)
            result, carried = beside(result, carried)
        mixed[d], partial[d], d_gate, *kept = result
        rows.append(kept)
        gate_grads[d] = shift(d_gate, shard_count - d) if d else d_gate
        if coming:
            got[coming] = after(got[coming], partial[d])
    carried = shift(add(carried, partial[2]), -1)
    (gate_grad, up_grad), carried, gate_grads = beside(
        up_weight_grads([(after(r[0], partial[1]), r[3], r[4]) for r in rows], context_size),
        carried,
        gate_grads,
    )
    stacked = jnp.stack([gate_grads[d] for d in range(shard_count)], 0)
    for bit in (1, 2, 4):
        if bit < shard_count:
            stacked = jnp.where(wt_index & bit > 0, jnp.roll(stacked, bit, 0), stacked)
    stacked = stacked.reshape(EXPERTS, tok)
    grad_logits = gates * (stacked - jnp.sum(gates * stacked, 0, keepdims=True))
    grad_logits = grad_logits.T.astype(bf16)
    carried = shift(add(carried, partial[1]), -1)
    down_grad, home = beside(
        down_weight_grads([(after(r[2], gate_grad, grad_logits), r[1]) for r in rows], context_size), carried
    )

    grad_normed_two = partial[0].astype(f32) + home.astype(f32)
    grad_normed_two = grad_normed_two + dot_nt(grad_logits, router_full)
    grad_mid_norm, second_gain_grad = norm_backward(
        middle, inverse_two, second_gain, grad_normed_two
    )
    grad_middle = out_grad + grad_mid_norm
    grad_branch = (resid_scale * grad_middle).astype(bf16)
    grad_attended = dot(grad_branch, output_t).astype(bf16)
    gate_share, up_share, down_share = (
        lax.psum_scatter(grad, "ctx", scatter_dimension=0, tiled=False).astype(f32)
        for grad in (gate_grad, up_grad, down_grad)
    )
    carried = None
    query = after(turned_query, grad_attended)
    d_query, d_kv, ours = [], [], []
    for half in range(2):
        result = attention_backward(
            query,
            grad_attended,
            lse[half],
            attended[half],
            cosine,
            sine,
            kv_pieces,
            kv_own,
            places,
            starts,
            block_rows,
            half,
        )
        carried = shift(after(add(carried, mixed[last - half]), home), -1)
        result, carried = beside(result, carried)
        query = after(query, result[0])
        d_query.append(result[0])
        d_kv.append(result[1])
        ours.append(result[2:])
    carried = shift(add(carried, mixed[last - 2]), -1)
    owned, carried = beside(plane_sum(d_kv), carried)
    for d in range(last - 3, 0, -1):
        carried = shift(add(carried, mixed[d]), -1)
    mixture = mixed[0].astype(f32) + carried.astype(f32)
    layer_output = (middle + resid_scale * mixture).astype(bf16)
    d_query = jnp.concatenate(d_query, 1)
    d_key, d_value = (
        jnp.concatenate(
            [
                jnp.concatenate([owned[half][:, 256 * n : 256 * n + 256], ours[half][n]], 0)
                for half in range(2)
            ],
            1,
        )
        for n in range(2)
    )
    grad_key_low = turn(d_key, jnp.tile(cosine, (1, 4)), jnp.tile(sine, (1, 4)), -1.0).astype(
        bf16
    )
    grad_kv = jnp.concatenate([grad_key_low, d_value.astype(bf16)], 1)
    grad_normed_one = dot_nt(d_query, qkv_full[:, :1024]) + dot_nt(grad_kv, qkv_full[:, 1024:])
    grad_input_norm, first_gain_grad = norm_backward(
        inputs, inverse_one, first_gain, grad_normed_one
    )
    input_grad = (grad_middle + grad_input_norm).astype(bf16)

    column = lax.broadcasted_iota(jnp.int32, (tok, 128), 1)
    query_share, output_share, key_share, value_share, small = outer_sum(
        [(normed_one, d_query), (grad_branch, attended[0]), (grad_branch, attended[1]), (normed_one, grad_kv)],
        [
            (normed_two, jnp.pad(grad_logits, ((0, 0), (0, 128 - EXPERTS)))),
            (second_gain_grad, (column == EXPERTS).astype(bf16)),
            (first_gain_grad, (column == EXPERTS + 1).astype(bf16)),
        ],
        (1024, 1024, KV_WIDTH, KV_WIDTH, 128),
    )
    return (
        layer_output[None],
        input_grad[None],
        small[:, EXPERTS + 1],
        query_share,
        key_share,
        value_share,
        output_share.T,
        small[:, EXPERTS],
        small[:, :EXPERTS],
        gate_share,
        up_share,
        down_share,
    )


def solution(mesh):
    return jax.shard_map(
        per_device,
        mesh=mesh,
        in_specs=(
            P("wt", "ctx", None),
            P(("ctx", "wt")),
            P(("ctx", "wt"), None),
            P(("ctx", "wt"), None),
            P(("ctx", "wt"), None),
            P(None, ("ctx", "wt")),
            P(("ctx", "wt")),
            P(("ctx", "wt"), None),
            P("wt", "ctx", None),
            P("wt", "ctx", None),
            P("wt", None, "ctx"),
            P("wt", "ctx", None),
            P("wt", None),
            P("wt", "ctx", None),
        ),
        out_specs=(
            P("wt", "ctx", None),
            P("wt", "ctx", None),
            P(("ctx", "wt")),
            P(("ctx", "wt"), None),
            P(("ctx", "wt"), None),
            P(("ctx", "wt"), None),
            P(None, ("ctx", "wt")),
            P(("ctx", "wt")),
            P(("ctx", "wt"), None),
            P("wt", "ctx", None),
            P("wt", "ctx", None),
            P("wt", None, "ctx"),
        ),
        check_vma=False,
    )
```

```python
import functools

import jax
import jax.numpy as jnp
from jax import lax
from jax.experimental import pallas as pl
from jax.experimental.pallas import tpu as pltpu
from jax.sharding import PartitionSpec as P

MODEL_WIDTH = 1024
HQ = 16
KEY_VALUE_HEADS = 8
HEAD_SIZE = 64
EXPERTS = 32
TOP = 8
PROMPT = 2048
CLEN = 256
CONT_DEV = 2
FF = 512
QTILE = 128
PARTS = 4
KV_WIDTH = KEY_VALUE_HEADS * HEAD_SIZE
ALL = ("ctx", "wt")

att_scale = 0.015625
resid_scale = 0.22
norm_eps = 1e-06
rope_base = 10000.0
masked_score = -1e30

bf16 = jnp.bfloat16
f32 = jnp.float32
VMEM_LIMIT = 60 * 1024 * 1024
SMALL = pl.CostEstimate(flops=1_000_000_000, bytes_accessed=1_000_000, transcendentals=0)

NT = (((1,), (1,)), ((), ()))
TN = (((0,), (0,)), ((), ()))


def dot(a, b):
    return jnp.dot(a, b, preferred_element_type=f32)


def dot_nt(a, b):
    return lax.dot_general(a, b, NT, preferred_element_type=f32)


def dot_tn(a, b):
    return lax.dot_general(a, b, TN, preferred_element_type=f32)


def turn_tile(values, cosine, sine, direction):
    middle = HEAD_SIZE // 2
    first = lax.broadcasted_iota(jnp.int32, values.shape, 1) % HEAD_SIZE < middle
    turned = jnp.where(first, -pltpu.roll(values, 128 - middle, 1), pltpu.roll(values, middle, 1))
    return values * cosine + direction * turned * sine


def project_kernel(places, x_ref, cos_ref, sin_ref, *refs, counts):
    pieces = refs[: len(counts)]
    normed_ref, q_ref, kv_ref, qkv_ref, out_ref, rest_ref, gains_ref = refs[len(counts) :]
    rows = MODEL_WIDTH // sum(counts)
    at = 0
    for piece, count in zip(pieces, counts):
        for i in range(count):
            source = slice(i * rows, (i + 1) * rows)
            target = pl.ds(pl.multiple_of(places[at] * rows, rows), rows)
            qkv_ref[target, :] = piece[source, :2048]
            out_ref[target, :] = piece[source, 2048:3072]
            rest_ref[target, :] = piece[source, 3072:]
            at += 1
    gains = rest_ref[...].astype(f32).T[EXPERTS : EXPERTS + 8]
    gains_ref[...] = gains
    x = x_ref[...].astype(f32)
    inverse = lax.rsqrt(jnp.mean(x * x, -1, keepdims=True) + norm_eps)
    normed_ref[...] = (x * inverse * gains[:1]).astype(bf16)
    for c in range(8):
        raw = dot(normed_ref[...], qkv_ref[:, 256 * c : 256 * (c + 1)])
        for h in range(2):
            part = raw[:, 128 * h : 128 * (h + 1)]
            if c < 6:
                part = turn_tile(part, cos_ref[...], sin_ref[...], 1.0)
            column = 256 * c + 128 * h
            if column < 1024:
                q_ref[:, column : column + 128] = part.astype(bf16)
            else:
                column -= 1024
                at = column % KV_WIDTH // 256 * 512 + column // KV_WIDTH * 256 + column % 256
                kv_ref[:, at : at + 128] = part.astype(bf16)


def project(x, cosine, sine, pieces, counts, places):
    tok = x.shape[0]
    shape = jax.ShapeDtypeStruct
    whole = pl.BlockSpec(memory_space=pltpu.VMEM)
    return pl.pallas_call(
        functools.partial(project_kernel, counts=counts),
        in_specs=[pl.BlockSpec(memory_space=pltpu.SMEM)] + [whole] * (3 + len(pieces)),
        out_specs=[whole] * 7,
        out_shape=[
            shape((tok, MODEL_WIDTH), bf16),
            shape((tok, HQ * HEAD_SIZE), bf16),
            shape((tok, 2 * KV_WIDTH), bf16),
            shape((MODEL_WIDTH, 2048), bf16),
            shape((MODEL_WIDTH, 1024), bf16),
            shape((MODEL_WIDTH, 128), bf16),
            shape((8, MODEL_WIDTH), f32),
        ],
        compiler_params=pltpu.CompilerParams(vmem_limit_bytes=VMEM_LIMIT),
        cost_estimate=SMALL,
        name="project",
    )(places, x, cosine, sine, *pieces)


def middle_kernel(
    a_ref, b_ref, x_ref, out_ref, rest_ref, gains_ref, mask_ref, middle_ref, normed_ref, inv_ref, gates_ref
):
    half = a_ref.shape[1]
    branch = dot_nt(a_ref[...], out_ref[:, :half]) + dot_nt(b_ref[...], out_ref[:, half:])
    middle = x_ref[...].astype(f32) + resid_scale * branch
    middle_ref[...] = middle
    inverse = lax.rsqrt(jnp.mean(middle * middle, -1, keepdims=True) + norm_eps)
    inv_ref[...] = inverse
    normed = (middle * inverse * gains_ref[1:2]).astype(bf16)
    normed_ref[...] = normed
    mask = mask_ref[...] > 0.0
    logits = jnp.where(mask, dot(normed, rest_ref[...]), masked_score)
    top = jnp.max(logits, -1, keepdims=True)
    raised = jnp.where(mask, jnp.exp(logits - top), 0.0)
    gates_ref[...] = (raised / jnp.sum(raised, -1, keepdims=True)).T[:EXPERTS]


def to_gates(halves, x, output_t, rest, gain_rows, mask):
    tok = x.shape[0]
    shape = jax.ShapeDtypeStruct
    whole = pl.BlockSpec(memory_space=pltpu.VMEM)
    return pl.pallas_call(
        middle_kernel,
        in_specs=[whole] * 7,
        out_specs=[whole] * 4,
        out_shape=[
            shape((tok, MODEL_WIDTH), f32),
            shape((tok, MODEL_WIDTH), bf16),
            shape((tok, 1), f32),
            shape((EXPERTS, tok), f32),
        ],
        compiler_params=pltpu.CompilerParams(vmem_limit_bytes=VMEM_LIMIT),
        cost_estimate=SMALL,
        name="to_gates",
    )(*halves, x, output_t, rest, gain_rows, mask)


def outer_kernel(mine, *refs, count):
    out_ref = refs[-1]
    pairs = [(refs[n], refs[n + 1]) for n in range(0, len(refs) - 1, 2)]
    at = 0
    for a_ref, b_ref in pairs[:count]:
        columns = b_ref.shape[1]
        out_ref[:, at : at + columns] = dot_tn(a_ref[...], b_ref[...]).astype(bf16)
        at += columns
    if pairs[count:]:
        out_ref[:, at:] = sum(dot_tn(a[...], b[...]) for a, b in pairs[count:]).astype(bf16)


def outer(pairs, extra=()):
    tok = pairs[0][0].shape[0]
    mine = lax.axis_index("ctx").astype(jnp.int32).reshape(1)
    specs = []
    everything = [*pairs, *extra]
    for _, b in everything:
        specs.append(pl.BlockSpec((tok, 128), lambda m, mine: (0, m ^ mine[0])))
        specs.append(pl.BlockSpec(b.shape, lambda m, mine: (0, 0)))
    columns = sum(b.shape[1] for _, b in [*pairs, *extra[:1]])
    return pl.pallas_call(
        functools.partial(outer_kernel, count=len(pairs)),
        grid_spec=pltpu.PrefetchScalarGridSpec(
            num_scalar_prefetch=1,
            grid=(8,),
            in_specs=specs,
            out_specs=pl.BlockSpec((128, columns), lambda m, mine: (m, 0)),
        ),
        out_shape=jax.ShapeDtypeStruct((MODEL_WIDTH, columns), bf16),
        compiler_params=pltpu.CompilerParams(vmem_limit_bytes=VMEM_LIMIT),
        cost_estimate=SMALL,
        name="outer",
    )(mine, *[x for pair in everything for x in pair])


def gather_keys(pieces, scratch, places, block_rows):
    at = 0
    for piece in pieces:
        for b in range(piece.shape[0] // block_rows):
            start = pl.multiple_of(places[at] * block_rows, block_rows)
            scratch[pl.ds(start, block_rows), :] = piece[b * block_rows : (b + 1) * block_rows, :]
            at += 1


def pair_rows(ref, start, rows, j):
    both = ref[pl.ds(start, rows), 2 * HEAD_SIZE * j : 2 * HEAD_SIZE * (j + 1)]
    return jnp.concatenate([both[:, :HEAD_SIZE], both[:, HEAD_SIZE:]], 0)


def attention_forward_kernel(places, starts, q_ref, *refs, block_rows, pieces):
    k_refs, v_refs = refs[:pieces], refs[pieces : 2 * pieces]
    kc_ref, vc_ref, o_ref, lse_ref, k_scr, v_scr = refs[2 * pieces :]
    prompt_local = 2 * block_rows
    gather_keys(k_refs, k_scr, places, block_rows)
    gather_keys(v_refs, v_scr, places, block_rows)

    def store(start, rows, j, out, m, total, at):
        out = (out / total).astype(bf16)
        lse = m + jnp.log(total)
        o_ref[pl.ds(start, rows), 2 * HEAD_SIZE * j : 2 * HEAD_SIZE * (j + 1)] = jnp.concatenate(
            [out[:rows], out[rows:]], 1
        )
        row = jnp.broadcast_to(lse, (2 * rows, 128)).T[:1]
        lse_ref[0, 2 * j : 2 * j + 2, pl.ds(at, rows)] = jnp.concatenate(
            [row[:, :rows], row[:, rows:]], 0
        )

    def tile(i, _):
        start = pl.multiple_of(prompt_local + i * QTILE, 64)
        per = CLEN // QTILE
        seg = pl.multiple_of((i // per) * CLEN, CLEN)
        for j in range(2):
            lanes = slice(HEAD_SIZE * j, HEAD_SIZE * (j + 1))
            q = pair_rows(q_ref, start, QTILE, j) * bf16(att_scale)
            s1 = dot_nt(q, k_scr[:, lanes])
            s2 = dot_nt(q, kc_ref[pl.ds(seg, CLEN), lanes])
            place = lax.broadcasted_iota(jnp.int32, s2.shape, 0) % QTILE + (i % per) * QTILE
            s2 = jnp.where(lax.broadcasted_iota(jnp.int32, s2.shape, 1) <= place, s2, masked_score)
            m = jnp.maximum(jnp.max(s1, 1, keepdims=True), jnp.max(s2, 1, keepdims=True))
            e1 = jnp.exp(s1 - m)
            e2 = jnp.exp(s2 - m)
            total = jnp.sum(e1, 1, keepdims=True) + jnp.sum(e2, 1, keepdims=True)
            out = dot(e1.astype(bf16), v_scr[:, lanes])
            out = out + dot(e2.astype(bf16), vc_ref[pl.ds(seg, CLEN), lanes])
            store(start, QTILE, j, out, m, total, pl.multiple_of(i * QTILE, QTILE))
        return 0

    lax.fori_loop(0, CONT_DEV * CLEN // QTILE, tile, 0)

    for half, keys in enumerate((PROMPT // 2, PROMPT)):
        start = pl.multiple_of(starts[half], block_rows)
        for j in range(2):
            lanes = slice(HEAD_SIZE * j, HEAD_SIZE * (j + 1))
            q = pair_rows(q_ref, start, block_rows, j) * bf16(att_scale)
            s = dot_nt(q, k_scr[:keys, lanes])
            place = lax.broadcasted_iota(jnp.int32, s.shape, 0) % block_rows + starts[2 + half]
            s = jnp.where(lax.broadcasted_iota(jnp.int32, s.shape, 1) <= place, s, masked_score)
            m = jnp.max(s, 1, keepdims=True)
            e = jnp.exp(s - m)
            total = jnp.sum(e, 1, keepdims=True)
            out = dot(e.astype(bf16), v_scr[:keys, lanes])
            store(start, block_rows, j, out, m, total, CONT_DEV * CLEN + half * block_rows)


def key_specs(pieces, own, half):
    spec = pl.BlockSpec
    key, value = (lambda g, *_: (0, 4 * half + g)), (lambda g, *_: (0, 4 * half + 2 + g))
    keys = [spec((p.shape[0], 128), key) for p in pieces]
    values = [spec((p.shape[0], 128), value) for p in pieces]
    return keys + values + [spec((own, 128), key), spec((own, 128), value)]


def attention_forward(q, pieces, kv_own, places, starts, block_rows, half):
    tok = q.shape[0]
    spec = pl.BlockSpec
    return pl.pallas_call(
        functools.partial(
            attention_forward_kernel, block_rows=block_rows, pieces=len(pieces)
        ),
        grid_spec=pltpu.PrefetchScalarGridSpec(
            num_scalar_prefetch=2,
            grid=(2,),
            in_specs=[spec((tok, 256), lambda g, *_: (0, 2 * half + g))]
            + key_specs(pieces, kv_own.shape[0], half),
            out_specs=[
                spec((tok, 256), lambda g, *_: (0, g)),
                spec((1, 4, tok), lambda g, *_: (g, 0, 0)),
            ],
            scratch_shapes=[
                pltpu.VMEM((PROMPT, 2 * HEAD_SIZE), bf16),
                pltpu.VMEM((PROMPT, 2 * HEAD_SIZE), bf16),
            ],
        ),
        out_shape=[
            jax.ShapeDtypeStruct((tok, HQ * HEAD_SIZE // 2), bf16),
            jax.ShapeDtypeStruct((2, 4, tok), f32),
        ],
        compiler_params=pltpu.CompilerParams(vmem_limit_bytes=VMEM_LIMIT),
        cost_estimate=SMALL,
        name="attention_forward",
    )(places, starts, q, *pieces, *pieces, kv_own, kv_own)


def attention_backward_kernel(
    places, starts, q_ref, do_ref, lse_ref, o_ref, cos_ref, sin_ref, *refs, block_rows, pieces
):
    k_refs, v_refs = refs[:pieces], refs[pieces : 2 * pieces]
    kc_ref, vc_ref, dq_ref, dkv_ref, dkc_ref, dvc_ref = refs[2 * pieces : 2 * pieces + 6]
    k_scr, v_scr, dk_acc, dv_acc, dq_acc = refs[2 * pieces + 6 :]
    prompt_local = 2 * block_rows
    gather_keys(k_refs, k_scr, places, block_rows)
    gather_keys(v_refs, v_scr, places, block_rows)
    dk_acc[...] = jnp.zeros_like(dk_acc)
    dv_acc[...] = jnp.zeros_like(dv_acc)
    dkc_ref[...] = jnp.zeros_like(dkc_ref)
    dvc_ref[...] = jnp.zeros_like(dvc_ref)

    def row_pair(ref, start, rows, j):
        both = ref[0, 2 * j : 2 * j + 2, pl.ds(start, rows)]
        return jnp.concatenate([both[:1], both[1:]], 1)

    def centre(start, rows, j, d_out):
        product = d_out.astype(f32) * pair_rows(o_ref, start, rows, j).astype(f32)
        ones = jnp.ones((8, HEAD_SIZE), f32)
        return lax.dot_general(
            ones, product, NT, precision=lax.Precision.HIGHEST, preferred_element_type=f32
        )[:1]

    def part(k, v, q, d_out, lse, delta, allowed):
        s = dot_nt(k, q)
        if allowed is not None:
            s = jnp.where(allowed(s.shape), s, masked_score)
        p = jnp.exp(s - lse)
        d_p = dot_nt(v, d_out)
        d_s = (p * (d_p - delta)).astype(bf16)
        return dot_tn(d_s, k), dot(d_s, q), dot(p.astype(bf16), d_out)

    def store(start, rows, j, d_q):
        d_q = d_q * att_scale
        dq_acc[pl.ds(start, rows), 2 * HEAD_SIZE * j : 2 * HEAD_SIZE * (j + 1)] = jnp.concatenate(
            [d_q[:rows], d_q[rows:]], 1
        )

    def tile(i, _):
        start = pl.multiple_of(prompt_local + i * QTILE, 64)
        per = CLEN // QTILE
        seg = pl.multiple_of((i // per) * CLEN, CLEN)
        own = pl.ds(seg, CLEN)
        lane_start = pl.multiple_of(i * QTILE, QTILE)

        def allowed(shape):
            place = lax.broadcasted_iota(jnp.int32, shape, 1) % QTILE + (i % per) * QTILE
            return lax.broadcasted_iota(jnp.int32, shape, 0) <= place

        for j in range(2):
            lanes = slice(HEAD_SIZE * j, HEAD_SIZE * (j + 1))
            q = pair_rows(q_ref, start, QTILE, j) * bf16(att_scale)
            d_out = pair_rows(do_ref, start, QTILE, j)
            lse = row_pair(lse_ref, lane_start, QTILE, j)
            delta = centre(start, QTILE, j, d_out)
            a, b, c = part(k_scr[:, lanes], v_scr[:, lanes], q, d_out, lse, delta, None)
            dk_acc[:, lanes] += b
            dv_acc[:, lanes] += c
            d_q = a
            a, b, c = part(
                kc_ref[own, lanes], vc_ref[own, lanes], q, d_out, lse, delta, allowed
            )
            dkc_ref[own, lanes] += b
            dvc_ref[own, lanes] += c
            store(start, QTILE, j, d_q + a)
        return 0

    lax.fori_loop(0, CONT_DEV * CLEN // QTILE, tile, 0)

    for half, keys in enumerate((PROMPT // 2, PROMPT)):
        start = pl.multiple_of(starts[half], block_rows)
        at = CONT_DEV * CLEN + half * block_rows

        def allowed(shape):
            place = lax.broadcasted_iota(jnp.int32, shape, 1) % block_rows + starts[2 + half]
            return lax.broadcasted_iota(jnp.int32, shape, 0) <= place

        for j in range(2):
            lanes = slice(HEAD_SIZE * j, HEAD_SIZE * (j + 1))
            q = pair_rows(q_ref, start, block_rows, j) * bf16(att_scale)
            d_out = pair_rows(do_ref, start, block_rows, j)
            lse = row_pair(lse_ref, at, block_rows, j)
            delta = centre(start, block_rows, j, d_out)
            a, b, c = part(
                k_scr[:keys, lanes], v_scr[:keys, lanes], q, d_out, lse, delta, allowed
            )
            dk_acc[:keys, lanes] += b
            dv_acc[:keys, lanes] += c
            store(start, block_rows, j, a)

    g = pl.program_id(0)
    key_lanes = pl.ds(pl.multiple_of(g * 128, 128), 128)
    value_lanes = pl.ds(pl.multiple_of(256 + g * 128, 128), 128)
    for b in range(PROMPT // block_rows):
        source = pl.ds(pl.multiple_of(places[b] * block_rows, block_rows), block_rows)
        rows = slice(b * block_rows, (b + 1) * block_rows)
        dkv_ref[rows, key_lanes] = dk_acc[source, :].astype(bf16)
        dkv_ref[rows, value_lanes] = dv_acc[source, :].astype(bf16)
    for c in range(2):
        lanes = slice(128 * c, 128 * (c + 1))
        dq_ref[:, lanes] = turn_tile(dq_acc[:, lanes], cos_ref[...], sin_ref[...], -1.0).astype(
            bf16
        )


def attention_backward(
    q, d_out, lse, attended, cosine, sine, pieces, kv_own, places, starts, block_rows, half
):
    tok = q.shape[0]
    own = kv_own.shape[0]
    spec = pl.BlockSpec
    wide = spec((tok, 256), lambda g, *_: (0, 2 * half + g))
    narrow = spec((tok, 256), lambda g, *_: (0, g))
    ours = spec((own, 128), lambda g, *_: (0, g))
    table = spec((tok, 128), lambda g, *_: (0, 0))
    return pl.pallas_call(
        functools.partial(
            attention_backward_kernel, block_rows=block_rows, pieces=len(pieces)
        ),
        grid_spec=pltpu.PrefetchScalarGridSpec(
            num_scalar_prefetch=2,
            grid=(2,),
            in_specs=[wide, wide, spec((1, 4, tok), lambda g, *_: (g, 0, 0)), narrow, table, table]
            + key_specs(pieces, own, half),
            out_specs=[
                spec((tok, 256), lambda g, *_: (0, g)),
                spec((PROMPT, KV_WIDTH), lambda g, *_: (0, 0)),
                ours,
                ours,
            ],
            scratch_shapes=[
                pltpu.VMEM((PROMPT, 2 * HEAD_SIZE), bf16),
                pltpu.VMEM((PROMPT, 2 * HEAD_SIZE), bf16),
                pltpu.VMEM((PROMPT, 2 * HEAD_SIZE), f32),
                pltpu.VMEM((PROMPT, 2 * HEAD_SIZE), f32),
                pltpu.VMEM((tok, 4 * HEAD_SIZE), f32),
            ],
        ),
        out_shape=[
            jax.ShapeDtypeStruct((tok, HQ * HEAD_SIZE // 2), bf16),
            jax.ShapeDtypeStruct((PROMPT, KV_WIDTH), bf16),
            jax.ShapeDtypeStruct((own, KV_WIDTH // 2), f32),
            jax.ShapeDtypeStruct((own, KV_WIDTH // 2), f32),
        ],
        compiler_params=pltpu.CompilerParams(vmem_limit_bytes=VMEM_LIMIT),
        cost_estimate=SMALL,
        name="attention_backward",
    )(places, starts, q, d_out, lse, attended, cosine, sine, *pieces, *pieces, kv_own, kv_own)


def expert_kernel(
    counts,
    a2_ref,
    df_ref,
    rank_ref,
    gate_ref,
    wg_ref,
    wu_ref,
    wd_ref,
    mix_ref,
    da_ref,
    dg_ref,
    x_ref,
    dy_ref,
    z_ref,
    dgate_ref,
    dup_ref,
    mix_acc,
    da_acc,
    *,
    sizes,
):
    e = pl.program_id(0)

    @pl.when(e == 0)
    def _():
        mix_acc[...] = jnp.zeros_like(mix_acc)
        da_acc[...] = jnp.zeros_like(da_acc)

    def body(size):
        rank = rank_ref[0]
        gates = gate_ref[0]
        tok = rank.shape[1]
        slot = lax.broadcasted_iota(jnp.int32, (size, tok), 0).astype(f32)
        hit = slot == rank
        chosen = hit.astype(f32).astype(bf16)
        gate = jnp.sum(jnp.where(hit, gates, 0.0), 1, keepdims=True)
        x = dot(chosen, a2_ref[...]).astype(bf16)
        d_mix = resid_scale * dot(chosen, df_ref[...])
        wg = wg_ref[:, 0].reshape(MODEL_WIDTH, FF)
        wu = wu_ref[:, 0].reshape(MODEL_WIDTH, FF)
        wd = jnp.concatenate([wd_ref[c, 0] for c in range(wd_ref.shape[0])], 1)
        g = dot(x, wg)
        u = dot(x, wu)
        sig = jax.nn.sigmoid(g)
        z = (g * sig * u).astype(bf16)
        y = dot(z, wd).astype(bf16).astype(f32)
        d_gate_value = jnp.sum(d_mix * y, 1, keepdims=True)
        dg_ref[0] = jnp.sum(jnp.where(hit, d_gate_value, 0.0), 0, keepdims=True)
        mix_acc[...] += dot_tn(chosen, (gate * y).astype(bf16))
        d_y = (gate * d_mix).astype(bf16)
        d_z = dot_nt(d_y, wd)
        d_g = (d_z * u * sig * (1.0 + g * (1.0 - sig))).astype(bf16)
        d_u = (d_z * g * sig).astype(bf16)
        d_r = (dot_nt(d_g, wg) + dot_nt(d_u, wu)).astype(bf16)
        da_acc[...] += dot_tn(chosen, d_r)
        for ref, value in (
            (x_ref, x),
            (dy_ref, d_y),
            (z_ref, z),
            (dgate_ref, d_g),
            (dup_ref, d_u),
        ):
            ref[0, :size] = value
            if size < ref.shape[1]:
                ref[0, size:] = jnp.zeros((ref.shape[1] - size, ref.shape[2]), bf16)

    least = -1
    for size in sizes:
        pl.when((counts[e] > least) & (counts[e] <= size))(functools.partial(body, size))
        least = size

    @pl.when(e == pl.num_programs(0) - 1)
    def _():
        mix_ref[...] = mix_acc[...].astype(bf16)
        da_ref[...] = da_acc[...].astype(bf16)


def expert_pass(a2, df, rank, gates, wg, wu, wd, capacity):
    tok = a2.shape[0]
    parts, experts = wg.shape[0], wg.shape[1]
    sizes = sorted({min(size, capacity) for size in (128, 192, 256, capacity)})
    counts = (jnp.max(rank, (1, 2)) + 1.0).astype(jnp.int32)
    spec = pl.BlockSpec
    whole = spec((tok, MODEL_WIDTH), lambda e, *_: (0, 0))
    row = spec((1, 1, tok), lambda e, *_: (e, 0, 0))
    up = spec((parts, 1, MODEL_WIDTH // parts, FF), lambda e, *_: (0, e, 0, 0))
    down = spec((parts, 1, FF, MODEL_WIDTH // parts), lambda e, *_: (0, e, 0, 0))
    rows_wide = spec((1, capacity, MODEL_WIDTH), lambda e, *_: (e, 0, 0))
    rows_thin = spec((1, capacity, FF), lambda e, *_: (e, 0, 0))
    shape = jax.ShapeDtypeStruct
    return pl.pallas_call(
        functools.partial(expert_kernel, sizes=sizes),
        grid_spec=pltpu.PrefetchScalarGridSpec(
            num_scalar_prefetch=1,
            grid=(experts,),
            in_specs=[whole, whole, row, row, up, up, down],
            out_specs=[whole, whole, row, rows_wide, rows_wide, rows_thin, rows_thin, rows_thin],
            scratch_shapes=[
                pltpu.VMEM((tok, MODEL_WIDTH), f32),
                pltpu.VMEM((tok, MODEL_WIDTH), f32),
            ],
        ),
        out_shape=[
            shape((tok, MODEL_WIDTH), bf16),
            shape((tok, MODEL_WIDTH), bf16),
            shape((experts, 1, tok), f32),
            shape((experts, capacity, MODEL_WIDTH), bf16),
            shape((experts, capacity, MODEL_WIDTH), bf16),
            shape((experts, capacity, FF), bf16),
            shape((experts, capacity, FF), bf16),
            shape((experts, capacity, FF), bf16),
        ],
        compiler_params=pltpu.CompilerParams(vmem_limit_bytes=VMEM_LIMIT),
        cost_estimate=SMALL,
        name="expert_pass",
    )(counts, a2, df, rank, gates, wg, wu, wd)


def up_grad_kernel(*refs, sources):
    rows = refs[: 3 * sources]
    gate_ref, up_ref = refs[3 * sources :]
    for n, out_ref in ((1, gate_ref), (2, up_ref)):
        total = None
        for s in range(sources):
            term = dot_tn(rows[3 * s][0], rows[3 * s + n][0])
            total = term if total is None else total + term
        out_ref[...] = total.astype(bf16).reshape(out_ref.shape)


def down_grad_kernel(*refs, sources, parts):
    rows, down_ref = refs[: 2 * sources], refs[-1]
    width = MODEL_WIDTH // parts
    total = None
    for s in range(sources):
        term = dot_tn(rows[2 * s][0], rows[2 * s + 1][0])
        total = term if total is None else total + term
    total = total.astype(bf16)
    for c in range(parts):
        down_ref[c, 0] = total[:, c * width : (c + 1) * width]


def row_specs(rows):
    return [pl.BlockSpec((1,) + a.shape[1:], lambda e: (e, 0, 0)) for r in rows for a in r]


def up_weight_grads(rows, parts):
    experts = rows[0][0].shape[0]
    shape = (parts, experts, MODEL_WIDTH // parts, FF)
    out = pl.BlockSpec((parts, 1) + shape[2:], lambda e: (0, e, 0, 0))
    return pl.pallas_call(
        functools.partial(up_grad_kernel, sources=len(rows)),
        grid=(experts,),
        in_specs=row_specs(rows),
        out_specs=[out, out],
        out_shape=[jax.ShapeDtypeStruct(shape, bf16)] * 2,
        compiler_params=pltpu.CompilerParams(vmem_limit_bytes=VMEM_LIMIT),
        cost_estimate=SMALL,
        name="up_weight_grads",
    )(*[a for r in rows for a in r])


def down_weight_grads(rows, parts):
    experts = rows[0][0].shape[0]
    shape = (parts, experts, FF, MODEL_WIDTH // parts)
    return pl.pallas_call(
        functools.partial(down_grad_kernel, sources=len(rows), parts=parts),
        grid=(experts,),
        in_specs=row_specs(rows),
        out_specs=pl.BlockSpec((parts, 1) + shape[2:], lambda e: (0, e, 0, 0)),
        out_shape=jax.ShapeDtypeStruct(shape, bf16),
        compiler_params=pltpu.CompilerParams(vmem_limit_bytes=VMEM_LIMIT),
        cost_estimate=SMALL,
        name="down_weight_grads",
    )(*[a for r in rows for a in r])


def swap(x, mask):
    return lax.ppermute(x, "ctx", [(i, i ^ mask) for i in range(lax.axis_size("ctx"))])


def gather_ctx(x, rows):
    if lax.axis_size("ctx") != 8:
        return lax.all_gather(x[:rows], "ctx", axis=0, tiled=True)
    return plane_gather(x, rows)


MESH = pl.DeviceIdType.MESH
ANY = pl.BlockSpec(memory_space=pl.ANY)


def partner(mask):
    me = lax.axis_index("ctx")
    return me + mask - 2 * mask * ((me // mask) % 2)


def ahead(distance):
    return (lax.axis_index("wt") + distance) % lax.axis_size("wt")


class Copies:
    def __init__(self, send, recv):
        self.send, self.recv, self.made = send, recv, {}

    def start(self, name, source, target, device):
        n = len(self.made)
        self.made[name] = copy = pltpu.make_async_remote_copy(
            src_ref=source,
            dst_ref=target,
            send_sem=self.send.at[n],
            recv_sem=self.recv.at[n],
            device_id=device,
            device_id_type=MESH,
        )
        copy.start()

    def arrived(self, name):
        self.made[name].wait_recv()

    def close(self):
        for copy in self.made.values():
            copy.wait_send()


def greet(devices):
    barrier = pltpu.get_barrier_semaphore()
    for device in devices:
        pl.semaphore_signal(barrier, inc=1, device_id=device, device_id_type=MESH)
    pl.semaphore_wait(barrier, len(devices))


def plane_steps(copies, block, half, key):
    side, near, far = ({"ctx": partner(m)} for m in (1, 2, 4))
    top, end = (lambda m: block(m, 0, half)), (lambda m: block(m, half, half))

    def first():
        copies.start((key, 2), block(0), block(2), near)
        copies.start((key, 4), block(0), block(4), far)
        copies.start((key, 1), block(0), block(1), side)

    def second():
        copies.arrived((key, 2))
        copies.start((key, 6), top(2), top(6), far)
        copies.start((key, 3), block(2), block(3), side)

    def third():
        copies.arrived((key, 4))
        copies.start((key, 7), end(4), end(6), near)
        copies.start((key, 5), block(4), block(5), side)

    def fourth():
        copies.arrived((key, 6))
        copies.arrived((key, 7))
        copies.start((key, 8), block(6), block(7), side)

    def last():
        for m in (1, 3, 5, 8):
            copies.arrived((key, m))

    return [first, second, third, fourth, last]


def plane_gather_kernel(x_ref, out_ref, send, recv, own_sem):
    rows = out_ref.shape[0] // 8
    greet([{"ctx": partner(m)} for m in (1, 2, 4)])
    own = pltpu.make_async_copy(x_ref.at[pl.ds(0, rows)], out_ref.at[pl.ds(0, rows)], own_sem)
    own.start()
    copies = Copies(send, recv)

    def block(m, start=0, count=rows):
        if m == 0:
            return x_ref.at[pl.ds(start, count)]
        return out_ref.at[pl.ds(m * rows + start, count)]

    for step in plane_steps(copies, block, rows // 2, 0):
        step()
    own.wait()
    copies.close()


def plane_gather(x, rows):
    return pl.pallas_call(
        plane_gather_kernel,
        in_specs=[ANY],
        out_specs=ANY,
        out_shape=jax.ShapeDtypeStruct((8 * rows, x.shape[1]), x.dtype),
        scratch_shapes=[
            pltpu.SemaphoreType.DMA((8,)),
            pltpu.SemaphoreType.DMA((8,)),
            pltpu.SemaphoreType.DMA,
        ],
        compiler_params=pltpu.CompilerParams(collective_id=1, has_side_effects=True),
        cost_estimate=SMALL,
        name="plane_gather",
    )(x)


def packed_gather_kernel(x_ref, out_ref, send, recv, own_sem):
    rows = x_ref.shape[0]
    greet(
        [{"ctx": partner(m)} for m in (1, 2, 4)] + [{"wt": ahead(d)} for d in (1, 2, 3)]
    )
    own = pltpu.make_async_copy(x_ref, out_ref.at[pl.ds(0, rows)], own_sem)
    own.start()
    copies = Copies(send, recv)

    def block_of(d):
        def block(m, start=0, count=rows):
            if m == 0 and d == 0:
                return x_ref.at[pl.ds(start, count)]
            return out_ref.at[pl.ds((4 * m + d) * rows + start, count)]

        return block

    for d in (1, 3, 2):
        copies.start(d, x_ref, block_of(d)(0), {"wt": ahead(d)})
    steps = {d: plane_steps(copies, block_of(d), rows // 2, ("plane", d)) for d in range(4)}
    steps[0][0]()
    for d, before in ((1, 0), (3, 1), (2, 3)):
        copies.arrived(d)
        steps[d][0]()
        steps[before][1]()
        steps[before][2]()
        if d != 1:
            steps[{3: 0, 2: 1}[d]][3]()
    steps[2][1]()
    steps[2][2]()
    steps[3][3]()
    steps[2][3]()
    for d in range(4):
        steps[d][4]()
    own.wait()
    copies.close()


def packed_gather(x):
    return pl.pallas_call(
        packed_gather_kernel,
        in_specs=[ANY],
        out_specs=ANY,
        out_shape=jax.ShapeDtypeStruct((32 * x.shape[0], x.shape[1]), x.dtype),
        scratch_shapes=[
            pltpu.SemaphoreType.DMA((35,)),
            pltpu.SemaphoreType.DMA((35,)),
            pltpu.SemaphoreType.DMA,
        ],
        compiler_params=pltpu.CompilerParams(collective_id=2, has_side_effects=True),
        cost_estimate=SMALL,
        name="packed_gather",
    )(x)


def sum_steps(copies, x_ref, key, sib, low, recv, out_ref, columns):
    rows = x_ref.shape[0] // 8
    half = rows // 2
    side, near, far = ({"ctx": partner(m)} for m in (1, 2, 4))

    def blocks(ref, m, start=0, count=rows):
        return ref.at[pl.ds(m * rows + start, count), columns]

    def added(m, start, count):
        ours = x_ref[m * rows + start : m * rows + start + count, columns].astype(f32)
        at = m // 2 * rows + start
        return ours + sib[at : at + count, columns].astype(f32)

    def put(place, start, value, device):
        at = place * rows + start
        low[at : at + half, columns] = value.astype(bf16)
        copies.start(
            (key, "low", place, start),
            blocks(low, place, start, half),
            blocks(recv, place, start, half),
            device,
        )

    def first():
        for m in (7, 3, 5, 1):
            copies.start((key, m), blocks(x_ref, m), blocks(sib, m // 2), side)

    def second():
        copies.arrived((key, 7))
        put(0, 0, added(6, 0, half), far)
        put(0, half, added(6, half, half), near)

    def third():
        copies.arrived((key, 3))
        put(1, half, added(2, half, half), near)
        copies.arrived((key, 5))
        put(2, 0, added(4, 0, half), far)

    def fourth():
        copies.arrived((key, "low", 0, 0))
        put(1, 0, added(2, 0, half) + recv[0:half, columns].astype(f32), near)
        copies.arrived((key, "low", 0, half))
        put(2, half, added(4, half, half) + recv[half:rows, columns].astype(f32), far)

    def last():
        copies.arrived((key, 1))
        for place in (1, 2):
            for start in (0, half):
                copies.arrived((key, "low", place, start))
        out_ref[:, columns] = (
            added(0, 0, rows)
            + recv[rows : 2 * rows, columns].astype(f32)
            + recv[2 * rows :, columns].astype(f32)
        )

    return [first, second, third, fourth, last]


def plane_sum_kernel(*refs, sets):
    x_refs, out_refs = refs[:sets], refs[sets : 2 * sets]
    sibs, lows, recvs = (refs[(2 + n) * sets : (3 + n) * sets] for n in range(3))
    send, recv_sem = refs[5 * sets :]
    greet([{"ctx": partner(m)} for m in (1, 2, 4)])
    copies = Copies(send, recv_sem)
    steps = [
        sum_steps(copies, x_refs[n], n, sibs[n], lows[n], recvs[n], out_refs[n], slice(None))
        for n in range(sets)
    ]
    for n in range(5):
        for one in steps:
            one[n]()
    copies.close()


def plane_sum(arrays):
    if lax.axis_size("ctx") != 8:
        return [
            lax.psum_scatter(x, "ctx", scatter_dimension=0, tiled=True).astype(f32)
            for x in arrays
        ]
    sets = len(arrays)
    rows, columns = arrays[0].shape[0] // 8, arrays[0].shape[1]
    vmem = pl.BlockSpec(memory_space=pltpu.VMEM)
    return pl.pallas_call(
        functools.partial(plane_sum_kernel, sets=sets),
        in_specs=[vmem] * sets,
        out_specs=[vmem] * sets,
        out_shape=[jax.ShapeDtypeStruct((rows, columns), f32)] * sets,
        scratch_shapes=[pltpu.VMEM((4 * rows, columns), bf16)] * sets
        + [pltpu.VMEM((3 * rows, columns), bf16)] * (2 * sets)
        + [pltpu.SemaphoreType.DMA((10 * sets,)), pltpu.SemaphoreType.DMA((10 * sets,))],
        compiler_params=pltpu.CompilerParams(
            collective_id=3, has_side_effects=True, vmem_limit_bytes=VMEM_LIMIT
        ),
        cost_estimate=SMALL,
        name="plane_sum",
    )(*arrays)


def full_sum_kernel(x_ref, *refs, widths):
    out_refs, refs = refs[: len(widths)], refs[len(widths) :]
    sib, low, recv, total, total_low, arrived, result_ref, send, recv_sem = refs
    rows = result_ref.shape[0]
    greet(
        [{"ctx": partner(m)} for m in (1, 2, 4)] + [{"wt": ahead(d)} for d in (1, 2, 3)]
    )
    copies = Copies(send, recv_sem)
    wide = x_ref.shape[1]
    edges = [128 * (n * (wide // 128) // PARTS) for n in range(PARTS + 1)]
    parts = [slice(a, b) for a, b in zip(edges, edges[1:])]
    steps = [
        sum_steps(copies, x_ref, n, sib, low, recv, total, columns)
        for n, columns in enumerate(parts)
    ]

    def leave(n):
        total_low[:, parts[n]] = total[:, parts[n]].astype(bf16)
        for d in (2, 1, 3):
            copies.start(
                ("wt", n, d),
                total_low.at[pl.ds(pl.multiple_of(ahead(d) * rows, rows), rows), parts[n]],
                arrived.at[pl.ds((d - 1) * rows, rows), parts[n]],
                {"wt": ahead(d)},
            )

    def finish(n):
        own = pl.ds(pl.multiple_of(ahead(0) * rows, rows), rows)
        result = total[own, parts[n]]
        for d in (1, 3, 2):
            copies.arrived(("wt", n, d))
            result = result + arrived[(d - 1) * rows : d * rows, parts[n]].astype(f32)
        result_ref[:, parts[n]] = result

    for one in steps:
        one[0]()
    for n in range(PARTS + 2):
        if n < PARTS:
            steps[n][1]()
            steps[n][2]()
        if 1 <= n <= PARTS:
            steps[n - 1][3]()
        if n >= 2:
            steps[n - 2][4]()
            leave(n - 2)
    for n in range(PARTS):
        finish(n)
    at = 0
    for out_ref, width in zip(out_refs, widths):
        out_ref[...] = result_ref[:, at : at + width]
        at += width
    copies.close()


def full_sum(x, widths):
    rows, columns = x.shape[0] // 32, x.shape[1]
    vmem = pl.BlockSpec(memory_space=pltpu.VMEM)
    return pl.pallas_call(
        functools.partial(full_sum_kernel, widths=widths),
        in_specs=[vmem],
        out_specs=[vmem] * len(widths),
        out_shape=[jax.ShapeDtypeStruct((rows, width), f32) for width in widths],
        scratch_shapes=[
            pltpu.VMEM((16 * rows, columns), bf16),
            pltpu.VMEM((12 * rows, columns), bf16),
            pltpu.VMEM((12 * rows, columns), bf16),
            pltpu.VMEM((4 * rows, columns), f32),
            pltpu.VMEM((4 * rows, columns), bf16),
            pltpu.VMEM((3 * rows, columns), bf16),
            pltpu.VMEM((rows, columns), f32),
            pltpu.SemaphoreType.DMA((13 * PARTS,)),
            pltpu.SemaphoreType.DMA((13 * PARTS,)),
        ],
        compiler_params=pltpu.CompilerParams(
            collective_id=4, has_side_effects=True, vmem_limit_bytes=VMEM_LIMIT
        ),
        cost_estimate=SMALL,
        name="full_sum",
    )(x)


def shift(x, distance):
    n = lax.axis_size("wt")
    return lax.ppermute(x, "wt", [(i, (i + distance) % n) for i in range(n)])


def beside(results, *arrivals):
    out = lax.optimization_barrier((results, arrivals))
    return (out[0],) + tuple(out[1])


def gather_all(x):
    ctx, wt = lax.axis_size("ctx"), lax.axis_size("wt")
    if ctx != 8 or wt != 4:
        return [lax.all_gather(x, ALL, axis=0, tiled=True)], [1], jnp.zeros((1,), jnp.int32)
    ctx_index, wt_index = lax.axis_index("ctx"), lax.axis_index("wt")
    m = jnp.arange(8, dtype=jnp.int32)
    d = jnp.arange(4, dtype=jnp.int32)
    places = ((ctx_index ^ m) * wt)[:, None] + ((wt_index - d) % wt)[None, :]
    return [packed_gather(x)], [32], places.reshape(-1).astype(jnp.int32)


def outer_sum(pairs, extra, widths):
    if lax.axis_size("ctx") != 8 or lax.axis_size("wt") != 4:
        parts = [dot_tn(a, b) for a, b in pairs] + [sum(dot_tn(a, b) for a, b in extra)]
        result = lax.psum_scatter(
            jnp.concatenate(parts, 1).astype(bf16), ALL, scatter_dimension=0, tiled=True
        ).astype(f32)
        edges = [sum(widths[: n + 1]) for n in range(len(widths) - 1)]
        return jnp.split(result, edges, 1)
    return full_sum(outer(pairs, extra), widths)


def after(x, *others):
    return lax.optimization_barrier((x,) + others)[0]


def rope_tables(positions, width):
    middle = HEAD_SIZE // 2
    frequency = jnp.power(
        jnp.float32(rope_base), -2.0 * jnp.arange(middle, dtype=f32) / HEAD_SIZE
    )
    angles = positions.astype(f32)[:, None] * frequency[None, :]
    times = width // middle
    return jnp.tile(jnp.cos(angles), (1, times)), jnp.tile(jnp.sin(angles), (1, times))


def turn(values, cosine, sine, direction):
    middle = HEAD_SIZE // 2
    first = lax.broadcasted_iota(jnp.int32, values.shape, 1) % HEAD_SIZE < middle
    turned = jnp.where(first, -jnp.roll(values, -middle, 1), jnp.roll(values, middle, 1))
    width = values.shape[1]
    return values * cosine[:, :width] + direction * turned * sine[:, :width]


def norm_forward(values, gain):
    inverse = lax.rsqrt(jnp.mean(values * values, -1, keepdims=True) + norm_eps)
    return (values * inverse * gain, inverse)


def norm_backward(values, inverse, gain, grad_out):
    scaled = gain * grad_out
    gain_grad = (grad_out * values * inverse).astype(bf16)
    projection = jnp.mean(scaled * values, -1, keepdims=True)
    return (inverse * scaled - values * inverse * inverse * inverse * projection, gain_grad)


def per_device(
    layer_input,
    attention_gain,
    query_weight,
    key_matrix,
    value_matrix,
    output_weight,
    mixture_gain,
    router_weight,
    gate_weight,
    up_weight,
    down_weight,
    expert_routes,
    prompt_deal,
    output_grad,
):
    tok = layer_input.shape[1]
    prompt_local = tok - CONT_DEV * CLEN
    block_rows = prompt_local // 2
    context_size = lax.axis_size("ctx")
    shard_count = lax.axis_size("wt")
    expert_count = gate_weight.shape[0]
    capacity = 8 * ((tok * TOP * 7 // (4 * EXPERTS) + 7) // 8)
    ctx_index = lax.axis_index("ctx")
    wt_index = lax.axis_index("wt")
    inputs = layer_input[0].astype(f32)
    routes = expert_routes[0]
    deal_row = prompt_deal[0]
    out_low = output_grad[0]
    out_grad = out_low.astype(f32)

    own_rows = query_weight.shape[0]
    packed = jnp.concatenate(
        [
            query_weight,
            key_matrix,
            value_matrix,
            output_weight.T,
            router_weight,
            attention_gain[:, None],
            mixture_gain[:, None],
            jnp.zeros((own_rows, 94), bf16),
        ],
        1,
    )
    pieces, counts, block_places = gather_all(packed)

    gate_full = lax.all_gather(gate_weight, "ctx", axis=0, tiled=False)
    up_full = lax.all_gather(up_weight, "ctx", axis=0, tiled=False)
    down_full = lax.all_gather(down_weight, "ctx", axis=0, tiled=False)

    mask = jnp.any(
        routes[:, :, None] == jnp.arange(EXPERTS, dtype=jnp.int32)[None, None, :], 1
    )
    order = jnp.arange(tok, dtype=jnp.int32)
    before = (order[None, :] < order[:, None]).astype(bf16)
    rank = jnp.where(mask, dot(before, mask.astype(bf16)), -1.0)
    ranks = lax.all_to_all(
        rank.T.reshape(shard_count, expert_count, 1, tok), "wt", 0, 0, tiled=True
    )
    last = shard_count - 1
    grads_in = {0: out_low, last: shift(after(out_low, pieces[0], ranks), -1)}
    grads_in[1] = shift(after(out_low, pieces[0], ranks), 1)

    pieces, ranks = beside(pieces, ranks)
    local_rows = jnp.arange(tok, dtype=jnp.int32)
    mine = lax.dynamic_slice_in_dim(deal_row, 2 * ctx_index, 2, 0)
    prompt_place = (
        jnp.where(local_rows < block_rows, mine[0], mine[1]) * block_rows
        + local_rows % block_rows
    )
    positions = jnp.where(
        local_rows < prompt_local, prompt_place, PROMPT + (local_rows - prompt_local) % CLEN
    )
    cosine, sine = rope_tables(positions, 128)
    normed_one, turned_query, kv_low, qkv_full, output_t, rest, gain_rows = project(
        layer_input[0], cosine, sine, pieces, counts, block_places
    )
    router_full = rest[:, :EXPERTS]
    first_gain, second_gain = gain_rows[0], gain_rows[1]
    inverse_one = lax.rsqrt(jnp.mean(inputs * inputs, -1, keepdims=True) + norm_eps)
    kv_own = kv_low[prompt_local:]
    kv_pieces, grads_in[last] = beside([gather_ctx(kv_low, prompt_local)], grads_in[last])

    places = deal_row
    if context_size == 8:
        pairs = deal_row.reshape(2, 2, 2, 2)
        for axis, bit in ((0, 4), (1, 2), (2, 1)):
            pairs = jnp.where(ctx_index & bit > 0, jnp.flip(pairs, axis), pairs)
        places = pairs.reshape(-1)
    low = (mine[0] > mine[1]).astype(jnp.int32)
    starts = jnp.stack(
        [
            low * block_rows,
            (1 - low) * block_rows,
            jnp.min(mine) * block_rows,
            jnp.max(mine) * block_rows,
        ]
    ).astype(jnp.int32)
    heads = []
    for half in range(2):
        result = attention_forward(
            turned_query, kv_pieces, kv_own, places, starts, block_rows, half
        )
        if half == 0:
            result, grads_in[1] = beside(result, grads_in[1])
        if half == 0:
            turned_query = after(turned_query, result[0])
        heads.append(result)
    for d in range(last - 1, 1, -1):
        grads_in[d] = shift(grads_in[d + 1], -1)
    attended = [out for out, _ in heads]
    lse = [row for _, row in heads]

    middle, normed_two, inverse_two, gates = to_gates(
        attended,
        layer_input[0],
        output_t,
        rest,
        gain_rows,
        jnp.pad(mask.astype(f32), ((0, 0), (0, 128 - EXPERTS))),
    )

    normed_two, grads_in[last - 1] = beside(normed_two, grads_in[last - 1])
    gates_out = gates.reshape(shard_count, expert_count, 1, tok)
    gates_in = []
    for d in range(shard_count):
        piece = lax.dynamic_index_in_dim(gates_out, (wt_index + d) % shard_count, 0, False)
        gates_in.append(shift(piece, d) if d else piece)
    got = {0: normed_two}
    partial, mixed, gate_grads, rows = {}, {}, {}, []
    carried = None

    def add(a, b):
        return b if a is None else (a.astype(f32) + b.astype(f32)).astype(bf16)

    for d in [0] + list(range(last, 0, -1)):
        source = (wt_index - d) % shard_count
        rank_in = lax.dynamic_index_in_dim(ranks, source, 0, False)
        result = expert_pass(
            got[d], grads_in[d], rank_in, gates_in[d], gate_full, up_full, down_full, capacity
        )
        coming = d - 1 if d else last
        if coming:
            result, got[coming] = beside(result, shift(got[(coming + 1) % shard_count], -1))
        if d == 0:
            result, gates_in = beside(result, gates_in)
        if 0 < d <= last - 2:
            carried = shift(after(add(carried, partial[d + 2]), got[d]), -1)
            result, carried = beside(result, carried)
        mixed[d], partial[d], d_gate, *kept = result
        rows.append(kept)
        gate_grads[d] = shift(d_gate, shard_count - d) if d else d_gate
        if coming:
            got[coming] = after(got[coming], partial[d])
    carried = shift(add(carried, partial[2]), -1)
    (gate_grad, up_grad), carried, gate_grads = beside(
        up_weight_grads([(after(r[0], partial[1]), r[3], r[4]) for r in rows], context_size),
        carried,
        gate_grads,
    )
    stacked = jnp.stack([gate_grads[d] for d in range(shard_count)], 0)
    for bit in (1, 2, 4):
        if bit < shard_count:
            stacked = jnp.where(wt_index & bit > 0, jnp.roll(stacked, bit, 0), stacked)
    stacked = stacked.reshape(EXPERTS, tok)
    grad_logits = gates * (stacked - jnp.sum(gates * stacked, 0, keepdims=True))
    grad_logits = grad_logits.T.astype(bf16)
    carried = shift(add(carried, partial[1]), -1)
    down_grad, home = beside(
        down_weight_grads([(after(r[2], gate_grad, grad_logits), r[1]) for r in rows], context_size), carried
    )

    grad_normed_two = partial[0].astype(f32) + home.astype(f32)
    grad_normed_two = grad_normed_two + dot_nt(grad_logits, router_full)
    grad_mid_norm, second_gain_grad = norm_backward(
        middle, inverse_two, second_gain, grad_normed_two
    )
    grad_middle = out_grad + grad_mid_norm
    grad_branch = (resid_scale * grad_middle).astype(bf16)
    grad_attended = dot(grad_branch, output_t).astype(bf16)
    gate_share, up_share, down_share = (
        lax.psum_scatter(grad, "ctx", scatter_dimension=0, tiled=False).astype(f32)
        for grad in (gate_grad, up_grad, down_grad)
    )
    carried = None
    query = after(turned_query, grad_attended)
    d_query, d_kv, ours = [], [], []
    for half in range(2):
        result = attention_backward(
            query,
            grad_attended,
            lse[half],
            attended[half],
            cosine,
            sine,
            kv_pieces,
            kv_own,
            places,
            starts,
            block_rows,
            half,
        )
        carried = shift(after(add(carried, mixed[last - half]), home), -1)
        result, carried = beside(result, carried)
        query = after(query, result[0])
        d_query.append(result[0])
        d_kv.append(result[1])
        ours.append(result[2:])
    carried = shift(add(carried, mixed[last - 2]), -1)
    owned, carried = beside(plane_sum(d_kv), carried)
    for d in range(last - 3, 0, -1):
        carried = shift(add(carried, mixed[d]), -1)
    mixture = mixed[0].astype(f32) + carried.astype(f32)
    layer_output = (middle + resid_scale * mixture).astype(bf16)
    d_query = jnp.concatenate(d_query, 1)
    d_key, d_value = (
        jnp.concatenate(
            [
                jnp.concatenate([owned[half][:, 256 * n : 256 * n + 256], ours[half][n]], 0)
                for half in range(2)
            ],
            1,
        )
        for n in range(2)
    )
    grad_key_low = turn(d_key, jnp.tile(cosine, (1, 4)), jnp.tile(sine, (1, 4)), -1.0).astype(
        bf16
    )
    grad_kv = jnp.concatenate([grad_key_low, d_value.astype(bf16)], 1)
    grad_normed_one = dot_nt(d_query, qkv_full[:, :1024]) + dot_nt(grad_kv, qkv_full[:, 1024:])
    grad_input_norm, first_gain_grad = norm_backward(
        inputs, inverse_one, first_gain, grad_normed_one
    )
    input_grad = (grad_middle + grad_input_norm).astype(bf16)

    column = lax.broadcasted_iota(jnp.int32, (tok, 128), 1)
    query_share, output_share, key_share, value_share, small = outer_sum(
        [(normed_one, d_query), (grad_branch, attended[0]), (grad_branch, attended[1]), (normed_one, grad_kv)],
        [
            (normed_two, jnp.pad(grad_logits, ((0, 0), (0, 128 - EXPERTS)))),
            (second_gain_grad, (column == EXPERTS).astype(bf16)),
            (first_gain_grad, (column == EXPERTS + 1).astype(bf16)),
        ],
        (1024, 1024, KV_WIDTH, KV_WIDTH, 128),
    )
    return (
        layer_output[None],
        input_grad[None],
        small[:, EXPERTS + 1],
        query_share,
        key_share,
        value_share,
        output_share.T,
        small[:, EXPERTS],
        small[:, :EXPERTS],
        gate_share,
        up_share,
        down_share,
    )


def solution(mesh):
    return jax.shard_map(
        per_device,
        mesh=mesh,
        in_specs=(
            P("wt", "ctx", None),
            P(("ctx", "wt")),
            P(("ctx", "wt"), None),
            P(("ctx", "wt"), None),
            P(("ctx", "wt"), None),
            P(None, ("ctx", "wt")),
            P(("ctx", "wt")),
            P(("ctx", "wt"), None),
            P("wt", "ctx", None),
            P("wt", "ctx", None),
            P("wt", None, "ctx"),
            P("wt", "ctx", None),
            P("wt", None),
            P("wt", "ctx", None),
        ),
        out_specs=(
            P("wt", "ctx", None),
            P("wt", "ctx", None),
            P(("ctx", "wt")),
            P(("ctx", "wt"), None),
            P(("ctx", "wt"), None),
            P(("ctx", "wt"), None),
            P(None, ("ctx", "wt")),
            P(("ctx", "wt")),
            P(("ctx", "wt"), None),
            P("wt", "ctx", None),
            P("wt", "ctx", None),
            P("wt", None, "ctx"),
        ),
        check_vma=False,
    )
```

```python
import functools

import jax
import jax.numpy as jnp
from jax import lax
from jax.experimental import pallas as pl
from jax.experimental.pallas import tpu as pltpu
from jax.sharding import PartitionSpec as P

MODEL_WIDTH = 1024
HQ = 16
KEY_VALUE_HEADS = 8
HEAD_SIZE = 64
EXPERTS = 32
TOP = 8
PROMPT = 2048
CLEN = 256
CONT_DEV = 2
FF = 512
QTILE = 128
PARTS = 4
KV_WIDTH = KEY_VALUE_HEADS * HEAD_SIZE
ALL = ("ctx", "wt")

att_scale = 0.015625
resid_scale = 0.22
norm_eps = 1e-06
rope_base = 10000.0
masked_score = -1e30

bf16 = jnp.bfloat16
f32 = jnp.float32
VMEM_LIMIT = 60 * 1024 * 1024
SMALL = pl.CostEstimate(flops=1_000_000_000, bytes_accessed=1_000_000, transcendentals=0)

NT = (((1,), (1,)), ((), ()))
TN = (((0,), (0,)), ((), ()))


def dot(a, b):
    return jnp.dot(a, b, preferred_element_type=f32)


def dot_nt(a, b):
    return lax.dot_general(a, b, NT, preferred_element_type=f32)


def dot_tn(a, b):
    return lax.dot_general(a, b, TN, preferred_element_type=f32)


def turn_tile(values, cosine, sine, direction):
    middle = HEAD_SIZE // 2
    first = lax.broadcasted_iota(jnp.int32, values.shape, 1) % HEAD_SIZE < middle
    turned = jnp.where(first, -pltpu.roll(values, 128 - middle, 1), pltpu.roll(values, middle, 1))
    return values * cosine + direction * turned * sine


def project_kernel(places, x_ref, cos_ref, sin_ref, *refs, counts):
    pieces = refs[: len(counts)]
    normed_ref, q_ref, kv_ref, qkv_ref, out_ref, rest_ref, gains_ref = refs[len(counts) :]
    rows = MODEL_WIDTH // sum(counts)
    at = 0
    for piece, count in zip(pieces, counts):
        for i in range(count):
            source = slice(i * rows, (i + 1) * rows)
            target = pl.ds(pl.multiple_of(places[at] * rows, rows), rows)
            qkv_ref[target, :] = piece[source, :2048]
            out_ref[target, :] = piece[source, 2048:3072]
            rest_ref[target, :] = piece[source, 3072:]
            at += 1
    gains = rest_ref[...].astype(f32).T[EXPERTS : EXPERTS + 8]
    gains_ref[...] = gains
    x = x_ref[...].astype(f32)
    inverse = lax.rsqrt(jnp.mean(x * x, -1, keepdims=True) + norm_eps)
    normed_ref[...] = (x * inverse * gains[:1]).astype(bf16)
    for c in range(8):
        raw = dot(normed_ref[...], qkv_ref[:, 256 * c : 256 * (c + 1)])
        for h in range(2):
            part = raw[:, 128 * h : 128 * (h + 1)]
            if c < 6:
                part = turn_tile(part, cos_ref[...], sin_ref[...], 1.0)
            column = 256 * c + 128 * h
            if column < 1024:
                q_ref[:, column : column + 128] = part.astype(bf16)
            else:
                column -= 1024
                at = column % KV_WIDTH // 256 * 512 + column // KV_WIDTH * 256 + column % 256
                kv_ref[:, at : at + 128] = part.astype(bf16)


def project(x, cosine, sine, pieces, counts, places):
    tok = x.shape[0]
    shape = jax.ShapeDtypeStruct
    whole = pl.BlockSpec(memory_space=pltpu.VMEM)
    return pl.pallas_call(
        functools.partial(project_kernel, counts=counts),
        in_specs=[pl.BlockSpec(memory_space=pltpu.SMEM)] + [whole] * (3 + len(pieces)),
        out_specs=[whole] * 7,
        out_shape=[
            shape((tok, MODEL_WIDTH), bf16),
            shape((tok, HQ * HEAD_SIZE), bf16),
            shape((tok, 2 * KV_WIDTH), bf16),
            shape((MODEL_WIDTH, 2048), bf16),
            shape((MODEL_WIDTH, 1024), bf16),
            shape((MODEL_WIDTH, 128), bf16),
            shape((8, MODEL_WIDTH), f32),
        ],
        compiler_params=pltpu.CompilerParams(vmem_limit_bytes=VMEM_LIMIT),
        cost_estimate=SMALL,
        name="project",
    )(places, x, cosine, sine, *pieces)


def middle_kernel(
    a_ref, b_ref, x_ref, out_ref, rest_ref, gains_ref, mask_ref, middle_ref, normed_ref, inv_ref, gates_ref
):
    half = a_ref.shape[1]
    branch = dot_nt(a_ref[...], out_ref[:, :half]) + dot_nt(b_ref[...], out_ref[:, half:])
    middle = x_ref[...].astype(f32) + resid_scale * branch
    middle_ref[...] = middle
    inverse = lax.rsqrt(jnp.mean(middle * middle, -1, keepdims=True) + norm_eps)
    inv_ref[...] = inverse
    normed = (middle * inverse * gains_ref[1:2]).astype(bf16)
    normed_ref[...] = normed
    mask = mask_ref[...] > 0.0
    logits = jnp.where(mask, dot(normed, rest_ref[...]), masked_score)
    top = jnp.max(logits, -1, keepdims=True)
    raised = jnp.where(mask, jnp.exp(logits - top), 0.0)
    gates_ref[...] = (raised / jnp.sum(raised, -1, keepdims=True)).T[:EXPERTS]


def to_gates(halves, x, output_t, rest, gain_rows, mask):
    tok = x.shape[0]
    shape = jax.ShapeDtypeStruct
    whole = pl.BlockSpec(memory_space=pltpu.VMEM)
    return pl.pallas_call(
        middle_kernel,
        in_specs=[whole] * 7,
        out_specs=[whole] * 4,
        out_shape=[
            shape((tok, MODEL_WIDTH), f32),
            shape((tok, MODEL_WIDTH), bf16),
            shape((tok, 1), f32),
            shape((EXPERTS, tok), f32),
        ],
        compiler_params=pltpu.CompilerParams(vmem_limit_bytes=VMEM_LIMIT),
        cost_estimate=SMALL,
        name="to_gates",
    )(*halves, x, output_t, rest, gain_rows, mask)


def outer_kernel(mine, *refs, count):
    out_ref = refs[-1]
    pairs = [(refs[n], refs[n + 1]) for n in range(0, len(refs) - 1, 2)]
    at = 0
    for a_ref, b_ref in pairs[:count]:
        columns = b_ref.shape[1]
        out_ref[:, at : at + columns] = dot_tn(a_ref[...], b_ref[...]).astype(bf16)
        at += columns
    if pairs[count:]:
        out_ref[:, at:] = sum(dot_tn(a[...], b[...]) for a, b in pairs[count:]).astype(bf16)


def outer(pairs, extra=()):
    tok = pairs[0][0].shape[0]
    mine = lax.axis_index("ctx").astype(jnp.int32).reshape(1)
    specs = []
    everything = [*pairs, *extra]
    for _, b in everything:
        specs.append(pl.BlockSpec((tok, 128), lambda m, mine: (0, m ^ mine[0])))
        specs.append(pl.BlockSpec(b.shape, lambda m, mine: (0, 0)))
    columns = sum(b.shape[1] for _, b in [*pairs, *extra[:1]])
    return pl.pallas_call(
        functools.partial(outer_kernel, count=len(pairs)),
        grid_spec=pltpu.PrefetchScalarGridSpec(
            num_scalar_prefetch=1,
            grid=(8,),
            in_specs=specs,
            out_specs=pl.BlockSpec((128, columns), lambda m, mine: (m, 0)),
        ),
        out_shape=jax.ShapeDtypeStruct((MODEL_WIDTH, columns), bf16),
        compiler_params=pltpu.CompilerParams(vmem_limit_bytes=VMEM_LIMIT),
        cost_estimate=SMALL,
        name="outer",
    )(mine, *[x for pair in everything for x in pair])


def gather_keys(pieces, scratch, places, block_rows):
    at = 0
    for piece in pieces:
        for b in range(piece.shape[0] // block_rows):
            start = pl.multiple_of(places[at] * block_rows, block_rows)
            scratch[pl.ds(start, block_rows), :] = piece[b * block_rows : (b + 1) * block_rows, :]
            at += 1


def pair_rows(ref, start, rows, j):
    both = ref[pl.ds(start, rows), 2 * HEAD_SIZE * j : 2 * HEAD_SIZE * (j + 1)]
    return jnp.concatenate([both[:, :HEAD_SIZE], both[:, HEAD_SIZE:]], 0)


def attention_forward_kernel(places, starts, q_ref, *refs, block_rows, pieces):
    k_refs, v_refs = refs[:pieces], refs[pieces : 2 * pieces]
    kc_ref, vc_ref, o_ref, lse_ref, k_scr, v_scr = refs[2 * pieces :]
    prompt_local = 2 * block_rows
    gather_keys(k_refs, k_scr, places, block_rows)
    gather_keys(v_refs, v_scr, places, block_rows)

    def store(start, rows, j, out, m, total, at):
        out = (out / total).astype(bf16)
        lse = m + jnp.log(total)
        o_ref[pl.ds(start, rows), 2 * HEAD_SIZE * j : 2 * HEAD_SIZE * (j + 1)] = jnp.concatenate(
            [out[:rows], out[rows:]], 1
        )
        row = jnp.broadcast_to(lse, (2 * rows, 128)).T[:1]
        lse_ref[0, 2 * j : 2 * j + 2, pl.ds(at, rows)] = jnp.concatenate(
            [row[:, :rows], row[:, rows:]], 0
        )

    def tile(i, _):
        start = pl.multiple_of(prompt_local + i * QTILE, 64)
        per = CLEN // QTILE
        seg = pl.multiple_of((i // per) * CLEN, CLEN)
        for j in range(2):
            lanes = slice(HEAD_SIZE * j, HEAD_SIZE * (j + 1))
            q = pair_rows(q_ref, start, QTILE, j) * bf16(att_scale)
            s1 = dot_nt(q, k_scr[:, lanes])
            s2 = dot_nt(q, kc_ref[pl.ds(seg, CLEN), lanes])
            place = lax.broadcasted_iota(jnp.int32, s2.shape, 0) % QTILE + (i % per) * QTILE
            s2 = jnp.where(lax.broadcasted_iota(jnp.int32, s2.shape, 1) <= place, s2, masked_score)
            m = jnp.maximum(jnp.max(s1, 1, keepdims=True), jnp.max(s2, 1, keepdims=True))
            e1 = jnp.exp(s1 - m)
            e2 = jnp.exp(s2 - m)
            total = jnp.sum(e1, 1, keepdims=True) + jnp.sum(e2, 1, keepdims=True)
            out = dot(e1.astype(bf16), v_scr[:, lanes])
            out = out + dot(e2.astype(bf16), vc_ref[pl.ds(seg, CLEN), lanes])
            store(start, QTILE, j, out, m, total, pl.multiple_of(i * QTILE, QTILE))
        return 0

    lax.fori_loop(0, CONT_DEV * CLEN // QTILE, tile, 0)

    for half, keys in enumerate((PROMPT // 2, PROMPT)):
        start = pl.multiple_of(starts[half], block_rows)
        for j in range(2):
            lanes = slice(HEAD_SIZE * j, HEAD_SIZE * (j + 1))
            q = pair_rows(q_ref, start, block_rows, j) * bf16(att_scale)
            s = dot_nt(q, k_scr[:keys, lanes])
            place = lax.broadcasted_iota(jnp.int32, s.shape, 0) % block_rows + starts[2 + half]
            s = jnp.where(lax.broadcasted_iota(jnp.int32, s.shape, 1) <= place, s, masked_score)
            m = jnp.max(s, 1, keepdims=True)
            e = jnp.exp(s - m)
            total = jnp.sum(e, 1, keepdims=True)
            out = dot(e.astype(bf16), v_scr[:keys, lanes])
            store(start, block_rows, j, out, m, total, CONT_DEV * CLEN + half * block_rows)


def finish_keys_kernel(*refs):
    cos_ref, sin_ref, out_ref = refs[6:]
    for half in range(2):
        owned, key, value = refs[half], refs[2 + 2 * half], refs[3 + 2 * half]
        for c in range(2):
            lanes = slice(128 * c, 128 * (c + 1))
            at = 256 * half + 128 * c
            d_key = jnp.concatenate([owned[:, lanes], key[:, lanes]], 0)
            d_key = turn_tile(d_key, cos_ref[...], sin_ref[...], -1.0)
            d_value = jnp.concatenate([owned[:, 256 + 128 * c : 384 + 128 * c], value[:, lanes]], 0)
            out_ref[:, at : at + 128] = d_key.astype(bf16)
            out_ref[:, KV_WIDTH + at : KV_WIDTH + at + 128] = d_value.astype(bf16)


def finish_keys(owned, ours, cosine, sine):
    whole = pl.BlockSpec(memory_space=pltpu.VMEM)
    return pl.pallas_call(
        finish_keys_kernel,
        in_specs=[whole] * 8,
        out_specs=whole,
        out_shape=jax.ShapeDtypeStruct((cosine.shape[0], 2 * KV_WIDTH), bf16),
        compiler_params=pltpu.CompilerParams(vmem_limit_bytes=VMEM_LIMIT),
        cost_estimate=SMALL,
        name="finish_keys",
    )(*owned, *ours[0], *ours[1], cosine, sine)


def key_specs(pieces, own, half):
    spec = pl.BlockSpec
    key, value = (lambda g, *_: (0, 4 * half + g)), (lambda g, *_: (0, 4 * half + 2 + g))
    keys = [spec((p.shape[0], 128), key) for p in pieces]
    values = [spec((p.shape[0], 128), value) for p in pieces]
    return keys + values + [spec((own, 128), key), spec((own, 128), value)]


def attention_forward(q, pieces, kv_own, places, starts, block_rows, half):
    tok = q.shape[0]
    spec = pl.BlockSpec
    return pl.pallas_call(
        functools.partial(
            attention_forward_kernel, block_rows=block_rows, pieces=len(pieces)
        ),
        grid_spec=pltpu.PrefetchScalarGridSpec(
            num_scalar_prefetch=2,
            grid=(2,),
            in_specs=[spec((tok, 256), lambda g, *_: (0, 2 * half + g))]
            + key_specs(pieces, kv_own.shape[0], half),
            out_specs=[
                spec((tok, 256), lambda g, *_: (0, g)),
                spec((1, 4, tok), lambda g, *_: (g, 0, 0)),
            ],
            scratch_shapes=[
                pltpu.VMEM((PROMPT, 2 * HEAD_SIZE), bf16),
                pltpu.VMEM((PROMPT, 2 * HEAD_SIZE), bf16),
            ],
        ),
        out_shape=[
            jax.ShapeDtypeStruct((tok, HQ * HEAD_SIZE // 2), bf16),
            jax.ShapeDtypeStruct((2, 4, tok), f32),
        ],
        compiler_params=pltpu.CompilerParams(vmem_limit_bytes=VMEM_LIMIT),
        cost_estimate=SMALL,
        name="attention_forward",
    )(places, starts, q, *pieces, *pieces, kv_own, kv_own)


def attention_backward_kernel(
    places, starts, q_ref, do_ref, lse_ref, o_ref, cos_ref, sin_ref, *refs, block_rows, pieces
):
    k_refs, v_refs = refs[:pieces], refs[pieces : 2 * pieces]
    kc_ref, vc_ref, dq_ref, dkv_ref, dkc_ref, dvc_ref = refs[2 * pieces : 2 * pieces + 6]
    k_scr, v_scr, dk_acc, dv_acc, dq_acc = refs[2 * pieces + 6 :]
    prompt_local = 2 * block_rows
    gather_keys(k_refs, k_scr, places, block_rows)
    gather_keys(v_refs, v_scr, places, block_rows)
    dk_acc[...] = jnp.zeros_like(dk_acc)
    dv_acc[...] = jnp.zeros_like(dv_acc)
    dkc_ref[...] = jnp.zeros_like(dkc_ref)
    dvc_ref[...] = jnp.zeros_like(dvc_ref)

    def row_pair(ref, start, rows, j):
        both = ref[0, 2 * j : 2 * j + 2, pl.ds(start, rows)]
        return jnp.concatenate([both[:1], both[1:]], 1)

    def centre(start, rows, j, d_out):
        product = d_out.astype(f32) * pair_rows(o_ref, start, rows, j).astype(f32)
        ones = jnp.ones((8, HEAD_SIZE), f32)
        return lax.dot_general(
            ones, product, NT, precision=lax.Precision.HIGHEST, preferred_element_type=f32
        )[:1]

    def part(k, v, q, d_out, lse, delta, allowed):
        s = dot_nt(k, q)
        if allowed is not None:
            s = jnp.where(allowed(s.shape), s, masked_score)
        p = jnp.exp(s - lse)
        d_p = dot_nt(v, d_out)
        d_s = (p * (d_p - delta)).astype(bf16)
        return dot_tn(d_s, k), dot(d_s, q), dot(p.astype(bf16), d_out)

    def store(start, rows, j, d_q):
        d_q = d_q * att_scale
        dq_acc[pl.ds(start, rows), 2 * HEAD_SIZE * j : 2 * HEAD_SIZE * (j + 1)] = jnp.concatenate(
            [d_q[:rows], d_q[rows:]], 1
        )

    def tile(i, _):
        start = pl.multiple_of(prompt_local + i * QTILE, 64)
        per = CLEN // QTILE
        seg = pl.multiple_of((i // per) * CLEN, CLEN)
        own = pl.ds(seg, CLEN)
        lane_start = pl.multiple_of(i * QTILE, QTILE)

        def allowed(shape):
            place = lax.broadcasted_iota(jnp.int32, shape, 1) % QTILE + (i % per) * QTILE
            return lax.broadcasted_iota(jnp.int32, shape, 0) <= place

        for j in range(2):
            lanes = slice(HEAD_SIZE * j, HEAD_SIZE * (j + 1))
            q = pair_rows(q_ref, start, QTILE, j) * bf16(att_scale)
            d_out = pair_rows(do_ref, start, QTILE, j)
            lse = row_pair(lse_ref, lane_start, QTILE, j)
            delta = centre(start, QTILE, j, d_out)
            a, b, c = part(k_scr[:, lanes], v_scr[:, lanes], q, d_out, lse, delta, None)
            dk_acc[:, lanes] += b
            dv_acc[:, lanes] += c
            d_q = a
            a, b, c = part(
                kc_ref[own, lanes], vc_ref[own, lanes], q, d_out, lse, delta, allowed
            )
            dkc_ref[own, lanes] += b
            dvc_ref[own, lanes] += c
            store(start, QTILE, j, d_q + a)
        return 0

    lax.fori_loop(0, CONT_DEV * CLEN // QTILE, tile, 0)

    for half, keys in enumerate((PROMPT // 2, PROMPT)):
        start = pl.multiple_of(starts[half], block_rows)
        at = CONT_DEV * CLEN + half * block_rows

        def allowed(shape):
            place = lax.broadcasted_iota(jnp.int32, shape, 1) % block_rows + starts[2 + half]
            return lax.broadcasted_iota(jnp.int32, shape, 0) <= place

        for j in range(2):
            lanes = slice(HEAD_SIZE * j, HEAD_SIZE * (j + 1))
            q = pair_rows(q_ref, start, block_rows, j) * bf16(att_scale)
            d_out = pair_rows(do_ref, start, block_rows, j)
            lse = row_pair(lse_ref, at, block_rows, j)
            delta = centre(start, block_rows, j, d_out)
            a, b, c = part(
                k_scr[:keys, lanes], v_scr[:keys, lanes], q, d_out, lse, delta, allowed
            )
            dk_acc[:keys, lanes] += b
            dv_acc[:keys, lanes] += c
            store(start, block_rows, j, a)

    g = pl.program_id(0)
    key_lanes = pl.ds(pl.multiple_of(g * 128, 128), 128)
    value_lanes = pl.ds(pl.multiple_of(256 + g * 128, 128), 128)
    for b in range(PROMPT // block_rows):
        source = pl.ds(pl.multiple_of(places[b] * block_rows, block_rows), block_rows)
        rows = slice(b * block_rows, (b + 1) * block_rows)
        dkv_ref[rows, key_lanes] = dk_acc[source, :].astype(bf16)
        dkv_ref[rows, value_lanes] = dv_acc[source, :].astype(bf16)
    for c in range(2):
        lanes = slice(128 * c, 128 * (c + 1))
        dq_ref[:, lanes] = turn_tile(dq_acc[:, lanes], cos_ref[...], sin_ref[...], -1.0).astype(
            bf16
        )


def attention_backward(
    q, d_out, lse, attended, cosine, sine, pieces, kv_own, places, starts, block_rows, half
):
    tok = q.shape[0]
    own = kv_own.shape[0]
    spec = pl.BlockSpec
    wide = spec((tok, 256), lambda g, *_: (0, 2 * half + g))
    narrow = spec((tok, 256), lambda g, *_: (0, g))
    ours = spec((own, 128), lambda g, *_: (0, g))
    table = spec((tok, 128), lambda g, *_: (0, 0))
    return pl.pallas_call(
        functools.partial(
            attention_backward_kernel, block_rows=block_rows, pieces=len(pieces)
        ),
        grid_spec=pltpu.PrefetchScalarGridSpec(
            num_scalar_prefetch=2,
            grid=(2,),
            in_specs=[wide, wide, spec((1, 4, tok), lambda g, *_: (g, 0, 0)), narrow, table, table]
            + key_specs(pieces, own, half),
            out_specs=[
                spec((tok, 256), lambda g, *_: (0, g)),
                spec((PROMPT, KV_WIDTH), lambda g, *_: (0, 0)),
                ours,
                ours,
            ],
            scratch_shapes=[
                pltpu.VMEM((PROMPT, 2 * HEAD_SIZE), bf16),
                pltpu.VMEM((PROMPT, 2 * HEAD_SIZE), bf16),
                pltpu.VMEM((PROMPT, 2 * HEAD_SIZE), f32),
                pltpu.VMEM((PROMPT, 2 * HEAD_SIZE), f32),
                pltpu.VMEM((tok, 4 * HEAD_SIZE), f32),
            ],
        ),
        out_shape=[
            jax.ShapeDtypeStruct((tok, HQ * HEAD_SIZE // 2), bf16),
            jax.ShapeDtypeStruct((PROMPT, KV_WIDTH), bf16),
            jax.ShapeDtypeStruct((own, KV_WIDTH // 2), f32),
            jax.ShapeDtypeStruct((own, KV_WIDTH // 2), f32),
        ],
        compiler_params=pltpu.CompilerParams(vmem_limit_bytes=VMEM_LIMIT),
        cost_estimate=SMALL,
        name="attention_backward",
    )(places, starts, q, d_out, lse, attended, cosine, sine, *pieces, *pieces, kv_own, kv_own)


def expert_kernel(
    counts,
    a2_ref,
    df_ref,
    rank_ref,
    gate_ref,
    wg_ref,
    wu_ref,
    wd_ref,
    mix_ref,
    da_ref,
    dg_ref,
    x_ref,
    dy_ref,
    z_ref,
    dgate_ref,
    dup_ref,
    mix_acc,
    da_acc,
    *,
    sizes,
):
    e = pl.program_id(0)

    @pl.when(e == 0)
    def _():
        mix_acc[...] = jnp.zeros_like(mix_acc)
        da_acc[...] = jnp.zeros_like(da_acc)

    def body(size):
        rank = rank_ref[0]
        gates = gate_ref[0]
        tok = rank.shape[1]
        slot = lax.broadcasted_iota(jnp.int32, (size, tok), 0).astype(f32)
        hit = slot == rank
        chosen = hit.astype(f32).astype(bf16)
        gate = jnp.sum(jnp.where(hit, gates, 0.0), 1, keepdims=True)
        x = dot(chosen, a2_ref[...]).astype(bf16)
        d_mix = resid_scale * dot(chosen, df_ref[...])
        wg = wg_ref[:, 0].reshape(MODEL_WIDTH, FF)
        wu = wu_ref[:, 0].reshape(MODEL_WIDTH, FF)
        wd = jnp.concatenate([wd_ref[c, 0] for c in range(wd_ref.shape[0])], 1)
        g = dot(x, wg)
        u = dot(x, wu)
        sig = jax.nn.sigmoid(g)
        z = (g * sig * u).astype(bf16)
        y = dot(z, wd).astype(bf16).astype(f32)
        d_gate_value = jnp.sum(d_mix * y, 1, keepdims=True)
        dg_ref[0] = jnp.sum(jnp.where(hit, d_gate_value, 0.0), 0, keepdims=True)
        mix_acc[...] += dot_tn(chosen, (gate * y).astype(bf16))
        d_y = (gate * d_mix).astype(bf16)
        d_z = dot_nt(d_y, wd)
        d_g = (d_z * u * sig * (1.0 + g * (1.0 - sig))).astype(bf16)
        d_u = (d_z * g * sig).astype(bf16)
        d_r = (dot_nt(d_g, wg) + dot_nt(d_u, wu)).astype(bf16)
        da_acc[...] += dot_tn(chosen, d_r)
        for ref, value in (
            (x_ref, x),
            (dy_ref, d_y),
            (z_ref, z),
            (dgate_ref, d_g),
            (dup_ref, d_u),
        ):
            ref[0, :size] = value
            if size < ref.shape[1]:
                ref[0, size:] = jnp.zeros((ref.shape[1] - size, ref.shape[2]), bf16)

    least = -1
    for size in sizes:
        pl.when((counts[e] > least) & (counts[e] <= size))(functools.partial(body, size))
        least = size

    @pl.when(e == pl.num_programs(0) - 1)
    def _():
        mix_ref[...] = mix_acc[...].astype(bf16)
        da_ref[...] = da_acc[...].astype(bf16)


def expert_pass(a2, df, rank, gates, wg, wu, wd, capacity):
    tok = a2.shape[0]
    parts, experts = wg.shape[0], wg.shape[1]
    sizes = sorted({min(size, capacity) for size in (128, 192, 256, capacity)})
    counts = (jnp.max(rank, (1, 2)) + 1.0).astype(jnp.int32)
    spec = pl.BlockSpec
    whole = spec((tok, MODEL_WIDTH), lambda e, *_: (0, 0))
    row = spec((1, 1, tok), lambda e, *_: (e, 0, 0))
    up = spec((parts, 1, MODEL_WIDTH // parts, FF), lambda e, *_: (0, e, 0, 0))
    down = spec((parts, 1, FF, MODEL_WIDTH // parts), lambda e, *_: (0, e, 0, 0))
    rows_wide = spec((1, capacity, MODEL_WIDTH), lambda e, *_: (e, 0, 0))
    rows_thin = spec((1, capacity, FF), lambda e, *_: (e, 0, 0))
    shape = jax.ShapeDtypeStruct
    return pl.pallas_call(
        functools.partial(expert_kernel, sizes=sizes),
        grid_spec=pltpu.PrefetchScalarGridSpec(
            num_scalar_prefetch=1,
            grid=(experts,),
            in_specs=[whole, whole, row, row, up, up, down],
            out_specs=[whole, whole, row, rows_wide, rows_wide, rows_thin, rows_thin, rows_thin],
            scratch_shapes=[
                pltpu.VMEM((tok, MODEL_WIDTH), f32),
                pltpu.VMEM((tok, MODEL_WIDTH), f32),
            ],
        ),
        out_shape=[
            shape((tok, MODEL_WIDTH), bf16),
            shape((tok, MODEL_WIDTH), bf16),
            shape((experts, 1, tok), f32),
            shape((experts, capacity, MODEL_WIDTH), bf16),
            shape((experts, capacity, MODEL_WIDTH), bf16),
            shape((experts, capacity, FF), bf16),
            shape((experts, capacity, FF), bf16),
            shape((experts, capacity, FF), bf16),
        ],
        compiler_params=pltpu.CompilerParams(vmem_limit_bytes=VMEM_LIMIT),
        cost_estimate=SMALL,
        name="expert_pass",
    )(counts, a2, df, rank, gates, wg, wu, wd)


def up_grad_kernel(*refs, sources):
    rows = refs[: 3 * sources]
    gate_ref, up_ref = refs[3 * sources :]
    for n, out_ref in ((1, gate_ref), (2, up_ref)):
        total = None
        for s in range(sources):
            term = dot_tn(rows[3 * s][0], rows[3 * s + n][0])
            total = term if total is None else total + term
        out_ref[...] = total.astype(bf16).reshape(out_ref.shape)


def down_grad_kernel(*refs, sources, parts):
    rows, down_ref = refs[: 2 * sources], refs[-1]
    width = MODEL_WIDTH // parts
    total = None
    for s in range(sources):
        term = dot_tn(rows[2 * s][0], rows[2 * s + 1][0])
        total = term if total is None else total + term
    total = total.astype(bf16)
    for c in range(parts):
        down_ref[c, 0] = total[:, c * width : (c + 1) * width]


def row_specs(rows):
    return [pl.BlockSpec((1,) + a.shape[1:], lambda e: (e, 0, 0)) for r in rows for a in r]


def up_weight_grads(rows, parts):
    experts = rows[0][0].shape[0]
    shape = (parts, experts, MODEL_WIDTH // parts, FF)
    out = pl.BlockSpec((parts, 1) + shape[2:], lambda e: (0, e, 0, 0))
    return pl.pallas_call(
        functools.partial(up_grad_kernel, sources=len(rows)),
        grid=(experts,),
        in_specs=row_specs(rows),
        out_specs=[out, out],
        out_shape=[jax.ShapeDtypeStruct(shape, bf16)] * 2,
        compiler_params=pltpu.CompilerParams(vmem_limit_bytes=VMEM_LIMIT),
        cost_estimate=SMALL,
        name="up_weight_grads",
    )(*[a for r in rows for a in r])


def down_weight_grads(rows, parts):
    experts = rows[0][0].shape[0]
    shape = (parts, experts, FF, MODEL_WIDTH // parts)
    return pl.pallas_call(
        functools.partial(down_grad_kernel, sources=len(rows), parts=parts),
        grid=(experts,),
        in_specs=row_specs(rows),
        out_specs=pl.BlockSpec((parts, 1) + shape[2:], lambda e: (0, e, 0, 0)),
        out_shape=jax.ShapeDtypeStruct(shape, bf16),
        compiler_params=pltpu.CompilerParams(vmem_limit_bytes=VMEM_LIMIT),
        cost_estimate=SMALL,
        name="down_weight_grads",
    )(*[a for r in rows for a in r])


def swap(x, mask):
    return lax.ppermute(x, "ctx", [(i, i ^ mask) for i in range(lax.axis_size("ctx"))])


def gather_ctx(x, rows):
    if lax.axis_size("ctx") != 8:
        return lax.all_gather(x[:rows], "ctx", axis=0, tiled=True)
    return plane_gather(x, rows)


MESH = pl.DeviceIdType.MESH
ANY = pl.BlockSpec(memory_space=pl.ANY)


def partner(mask):
    me = lax.axis_index("ctx")
    return me + mask - 2 * mask * ((me // mask) % 2)


def ahead(distance):
    return (lax.axis_index("wt") + distance) % lax.axis_size("wt")


class Copies:
    def __init__(self, send, recv):
        self.send, self.recv, self.made = send, recv, {}

    def start(self, name, source, target, device):
        n = len(self.made)
        self.made[name] = copy = pltpu.make_async_remote_copy(
            src_ref=source,
            dst_ref=target,
            send_sem=self.send.at[n],
            recv_sem=self.recv.at[n],
            device_id=device,
            device_id_type=MESH,
        )
        copy.start()

    def arrived(self, name):
        self.made[name].wait_recv()

    def close(self):
        for copy in self.made.values():
            copy.wait_send()


def greet(devices):
    barrier = pltpu.get_barrier_semaphore()
    for device in devices:
        pl.semaphore_signal(barrier, inc=1, device_id=device, device_id_type=MESH)
    pl.semaphore_wait(barrier, len(devices))


def plane_steps(copies, block, half, key):
    side, near, far = ({"ctx": partner(m)} for m in (1, 2, 4))
    top, end = (lambda m: block(m, 0, half)), (lambda m: block(m, half, half))

    def first():
        copies.start((key, 2), block(0), block(2), near)
        copies.start((key, 4), block(0), block(4), far)
        copies.start((key, 1), block(0), block(1), side)

    def second():
        copies.arrived((key, 2))
        copies.start((key, 6), top(2), top(6), far)
        copies.start((key, 3), block(2), block(3), side)

    def third():
        copies.arrived((key, 4))
        copies.start((key, 7), end(4), end(6), near)
        copies.start((key, 5), block(4), block(5), side)

    def fourth():
        copies.arrived((key, 6))
        copies.arrived((key, 7))
        copies.start((key, 8), block(6), block(7), side)

    def last():
        for m in (1, 3, 5, 8):
            copies.arrived((key, m))

    return [first, second, third, fourth, last]


def plane_gather_kernel(x_ref, out_ref, send, recv, own_sem):
    rows = out_ref.shape[0] // 8
    greet([{"ctx": partner(m)} for m in (1, 2, 4)])
    own = pltpu.make_async_copy(x_ref.at[pl.ds(0, rows)], out_ref.at[pl.ds(0, rows)], own_sem)
    own.start()
    copies = Copies(send, recv)

    def block(m, start=0, count=rows):
        if m == 0:
            return x_ref.at[pl.ds(start, count)]
        return out_ref.at[pl.ds(m * rows + start, count)]

    for step in plane_steps(copies, block, rows // 2, 0):
        step()
    own.wait()
    copies.close()


def plane_gather(x, rows):
    return pl.pallas_call(
        plane_gather_kernel,
        in_specs=[ANY],
        out_specs=ANY,
        out_shape=jax.ShapeDtypeStruct((8 * rows, x.shape[1]), x.dtype),
        scratch_shapes=[
            pltpu.SemaphoreType.DMA((8,)),
            pltpu.SemaphoreType.DMA((8,)),
            pltpu.SemaphoreType.DMA,
        ],
        compiler_params=pltpu.CompilerParams(collective_id=1, has_side_effects=True),
        cost_estimate=SMALL,
        name="plane_gather",
    )(x)


def packed_gather_kernel(x_ref, out_ref, send, recv, own_sem):
    rows = x_ref.shape[0]
    greet(
        [{"ctx": partner(m)} for m in (1, 2, 4)] + [{"wt": ahead(d)} for d in (1, 2, 3)]
    )
    own = pltpu.make_async_copy(x_ref, out_ref.at[pl.ds(0, rows)], own_sem)
    own.start()
    copies = Copies(send, recv)

    def block_of(d):
        def block(m, start=0, count=rows):
            if m == 0 and d == 0:
                return x_ref.at[pl.ds(start, count)]
            return out_ref.at[pl.ds((4 * m + d) * rows + start, count)]

        return block

    for d in (1, 3, 2):
        copies.start(d, x_ref, block_of(d)(0), {"wt": ahead(d)})
    steps = {d: plane_steps(copies, block_of(d), rows // 2, ("plane", d)) for d in range(4)}
    steps[0][0]()
    for d, before in ((1, 0), (3, 1), (2, 3)):
        copies.arrived(d)
        steps[d][0]()
        steps[before][1]()
        steps[before][2]()
        if d != 1:
            steps[{3: 0, 2: 1}[d]][3]()
    steps[2][1]()
    steps[2][2]()
    steps[3][3]()
    steps[2][3]()
    for d in range(4):
        steps[d][4]()
    own.wait()
    copies.close()


def packed_gather(x):
    return pl.pallas_call(
        packed_gather_kernel,
        in_specs=[ANY],
        out_specs=ANY,
        out_shape=jax.ShapeDtypeStruct((32 * x.shape[0], x.shape[1]), x.dtype),
        scratch_shapes=[
            pltpu.SemaphoreType.DMA((35,)),
            pltpu.SemaphoreType.DMA((35,)),
            pltpu.SemaphoreType.DMA,
        ],
        compiler_params=pltpu.CompilerParams(collective_id=2, has_side_effects=True),
        cost_estimate=SMALL,
        name="packed_gather",
    )(x)


def sum_steps(copies, x_ref, key, sib, low, recv, out_ref, columns):
    rows = x_ref.shape[0] // 8
    half = rows // 2
    side, near, far = ({"ctx": partner(m)} for m in (1, 2, 4))

    def blocks(ref, m, start=0, count=rows):
        return ref.at[pl.ds(m * rows + start, count), columns]

    def added(m, start, count):
        ours = x_ref[m * rows + start : m * rows + start + count, columns].astype(f32)
        at = m // 2 * rows + start
        return ours + sib[at : at + count, columns].astype(f32)

    def put(place, start, value, device):
        at = place * rows + start
        low[at : at + half, columns] = value.astype(bf16)
        copies.start(
            (key, "low", place, start),
            blocks(low, place, start, half),
            blocks(recv, place, start, half),
            device,
        )

    def first():
        for m in (7, 3, 5, 1):
            copies.start((key, m), blocks(x_ref, m), blocks(sib, m // 2), side)

    def second():
        copies.arrived((key, 7))
        put(0, 0, added(6, 0, half), far)
        put(0, half, added(6, half, half), near)

    def third():
        copies.arrived((key, 3))
        put(1, half, added(2, half, half), near)
        copies.arrived((key, 5))
        put(2, 0, added(4, 0, half), far)

    def fourth():
        copies.arrived((key, "low", 0, 0))
        put(1, 0, added(2, 0, half) + recv[0:half, columns].astype(f32), near)
        copies.arrived((key, "low", 0, half))
        put(2, half, added(4, half, half) + recv[half:rows, columns].astype(f32), far)

    def last():
        copies.arrived((key, 1))
        for place in (1, 2):
            for start in (0, half):
                copies.arrived((key, "low", place, start))
        out_ref[:, columns] = (
            added(0, 0, rows)
            + recv[rows : 2 * rows, columns].astype(f32)
            + recv[2 * rows :, columns].astype(f32)
        )

    return [first, second, third, fourth, last]


def plane_sum_kernel(*refs, sets):
    x_refs, out_refs = refs[:sets], refs[sets : 2 * sets]
    sibs, lows, recvs = (refs[(2 + n) * sets : (3 + n) * sets] for n in range(3))
    send, recv_sem = refs[5 * sets :]
    greet([{"ctx": partner(m)} for m in (1, 2, 4)])
    copies = Copies(send, recv_sem)
    steps = [
        sum_steps(copies, x_refs[n], n, sibs[n], lows[n], recvs[n], out_refs[n], slice(None))
        for n in range(sets)
    ]
    for n in range(5):
        for one in steps:
            one[n]()
    copies.close()


def plane_sum(arrays):
    if lax.axis_size("ctx") != 8:
        return [
            lax.psum_scatter(x, "ctx", scatter_dimension=0, tiled=True).astype(f32)
            for x in arrays
        ]
    sets = len(arrays)
    rows, columns = arrays[0].shape[0] // 8, arrays[0].shape[1]
    vmem = pl.BlockSpec(memory_space=pltpu.VMEM)
    return pl.pallas_call(
        functools.partial(plane_sum_kernel, sets=sets),
        in_specs=[vmem] * sets,
        out_specs=[vmem] * sets,
        out_shape=[jax.ShapeDtypeStruct((rows, columns), f32)] * sets,
        scratch_shapes=[pltpu.VMEM((4 * rows, columns), bf16)] * sets
        + [pltpu.VMEM((3 * rows, columns), bf16)] * (2 * sets)
        + [pltpu.SemaphoreType.DMA((10 * sets,)), pltpu.SemaphoreType.DMA((10 * sets,))],
        compiler_params=pltpu.CompilerParams(
            collective_id=3, has_side_effects=True, vmem_limit_bytes=VMEM_LIMIT
        ),
        cost_estimate=SMALL,
        name="plane_sum",
    )(*arrays)


def full_sum_kernel(x_ref, *refs, widths):
    out_refs, refs = refs[: len(widths)], refs[len(widths) :]
    sib, low, recv, total, total_low, arrived, result_ref, send, recv_sem = refs
    rows = result_ref.shape[0]
    greet(
        [{"ctx": partner(m)} for m in (1, 2, 4)] + [{"wt": ahead(d)} for d in (1, 2, 3)]
    )
    copies = Copies(send, recv_sem)
    wide = x_ref.shape[1]
    edges = [128 * (n * (wide // 128) // PARTS) for n in range(PARTS + 1)]
    parts = [slice(a, b) for a, b in zip(edges, edges[1:])]
    steps = [
        sum_steps(copies, x_ref, n, sib, low, recv, total, columns)
        for n, columns in enumerate(parts)
    ]

    def leave(n):
        total_low[:, parts[n]] = total[:, parts[n]].astype(bf16)
        for d in (2, 1, 3):
            copies.start(
                ("wt", n, d),
                total_low.at[pl.ds(pl.multiple_of(ahead(d) * rows, rows), rows), parts[n]],
                arrived.at[pl.ds((d - 1) * rows, rows), parts[n]],
                {"wt": ahead(d)},
            )

    def finish(n):
        own = pl.ds(pl.multiple_of(ahead(0) * rows, rows), rows)
        result = total[own, parts[n]]
        for d in (1, 3, 2):
            copies.arrived(("wt", n, d))
            result = result + arrived[(d - 1) * rows : d * rows, parts[n]].astype(f32)
        result_ref[:, parts[n]] = result

    for one in steps:
        one[0]()
    for n in range(PARTS + 2):
        if n < PARTS:
            steps[n][1]()
            steps[n][2]()
        if 1 <= n <= PARTS:
            steps[n - 1][3]()
        if n >= 2:
            steps[n - 2][4]()
            leave(n - 2)
    for n in range(PARTS):
        finish(n)
    at = 0
    for out_ref, width in zip(out_refs, widths):
        out_ref[...] = result_ref[:, at : at + width]
        at += width
    copies.close()


def full_sum(x, widths):
    rows, columns = x.shape[0] // 32, x.shape[1]
    vmem = pl.BlockSpec(memory_space=pltpu.VMEM)
    return pl.pallas_call(
        functools.partial(full_sum_kernel, widths=widths),
        in_specs=[vmem],
        out_specs=[vmem] * len(widths),
        out_shape=[jax.ShapeDtypeStruct((rows, width), f32) for width in widths],
        scratch_shapes=[
            pltpu.VMEM((16 * rows, columns), bf16),
            pltpu.VMEM((12 * rows, columns), bf16),
            pltpu.VMEM((12 * rows, columns), bf16),
            pltpu.VMEM((4 * rows, columns), f32),
            pltpu.VMEM((4 * rows, columns), bf16),
            pltpu.VMEM((3 * rows, columns), bf16),
            pltpu.VMEM((rows, columns), f32),
            pltpu.SemaphoreType.DMA((13 * PARTS,)),
            pltpu.SemaphoreType.DMA((13 * PARTS,)),
        ],
        compiler_params=pltpu.CompilerParams(
            collective_id=4, has_side_effects=True, vmem_limit_bytes=VMEM_LIMIT
        ),
        cost_estimate=SMALL,
        name="full_sum",
    )(x)


def shift(x, distance):
    n = lax.axis_size("wt")
    return lax.ppermute(x, "wt", [(i, (i + distance) % n) for i in range(n)])


def beside(results, *arrivals):
    out = lax.optimization_barrier((results, arrivals))
    return (out[0],) + tuple(out[1])


def gather_all(x):
    ctx, wt = lax.axis_size("ctx"), lax.axis_size("wt")
    if ctx != 8 or wt != 4:
        return [lax.all_gather(x, ALL, axis=0, tiled=True)], [1], jnp.zeros((1,), jnp.int32)
    ctx_index, wt_index = lax.axis_index("ctx"), lax.axis_index("wt")
    m = jnp.arange(8, dtype=jnp.int32)
    d = jnp.arange(4, dtype=jnp.int32)
    places = ((ctx_index ^ m) * wt)[:, None] + ((wt_index - d) % wt)[None, :]
    return [packed_gather(x)], [32], places.reshape(-1).astype(jnp.int32)


def outer_sum(pairs, extra, widths):
    if lax.axis_size("ctx") != 8 or lax.axis_size("wt") != 4:
        parts = [dot_tn(a, b) for a, b in pairs] + [sum(dot_tn(a, b) for a, b in extra)]
        result = lax.psum_scatter(
            jnp.concatenate(parts, 1).astype(bf16), ALL, scatter_dimension=0, tiled=True
        ).astype(f32)
        edges = [sum(widths[: n + 1]) for n in range(len(widths) - 1)]
        return jnp.split(result, edges, 1)
    return full_sum(outer(pairs, extra), widths)


def after(x, *others):
    return lax.optimization_barrier((x,) + others)[0]


def rope_tables(positions, width):
    middle = HEAD_SIZE // 2
    frequency = jnp.power(
        jnp.float32(rope_base), -2.0 * jnp.arange(middle, dtype=f32) / HEAD_SIZE
    )
    angles = positions.astype(f32)[:, None] * frequency[None, :]
    times = width // middle
    return jnp.tile(jnp.cos(angles), (1, times)), jnp.tile(jnp.sin(angles), (1, times))


def turn(values, cosine, sine, direction):
    middle = HEAD_SIZE // 2
    first = lax.broadcasted_iota(jnp.int32, values.shape, 1) % HEAD_SIZE < middle
    turned = jnp.where(first, -jnp.roll(values, -middle, 1), jnp.roll(values, middle, 1))
    width = values.shape[1]
    return values * cosine[:, :width] + direction * turned * sine[:, :width]


def norm_forward(values, gain):
    inverse = lax.rsqrt(jnp.mean(values * values, -1, keepdims=True) + norm_eps)
    return (values * inverse * gain, inverse)


def norm_backward(values, inverse, gain, grad_out):
    scaled = gain * grad_out
    gain_grad = (grad_out * values * inverse).astype(bf16)
    projection = jnp.mean(scaled * values, -1, keepdims=True)
    return (inverse * scaled - values * inverse * inverse * inverse * projection, gain_grad)


def per_device(
    layer_input,
    attention_gain,
    query_weight,
    key_matrix,
    value_matrix,
    output_weight,
    mixture_gain,
    router_weight,
    gate_weight,
    up_weight,
    down_weight,
    expert_routes,
    prompt_deal,
    output_grad,
):
    tok = layer_input.shape[1]
    prompt_local = tok - CONT_DEV * CLEN
    block_rows = prompt_local // 2
    context_size = lax.axis_size("ctx")
    shard_count = lax.axis_size("wt")
    expert_count = gate_weight.shape[0]
    capacity = 8 * ((tok * TOP * 7 // (4 * EXPERTS) + 7) // 8)
    ctx_index = lax.axis_index("ctx")
    wt_index = lax.axis_index("wt")
    inputs = layer_input[0].astype(f32)
    routes = expert_routes[0]
    deal_row = prompt_deal[0]
    out_low = output_grad[0]
    out_grad = out_low.astype(f32)

    own_rows = query_weight.shape[0]
    packed = jnp.concatenate(
        [
            query_weight,
            key_matrix,
            value_matrix,
            output_weight.T,
            router_weight,
            attention_gain[:, None],
            mixture_gain[:, None],
            jnp.zeros((own_rows, 94), bf16),
        ],
        1,
    )
    pieces, counts, block_places = gather_all(packed)

    gate_full = lax.all_gather(gate_weight, "ctx", axis=0, tiled=False)
    up_full = lax.all_gather(up_weight, "ctx", axis=0, tiled=False)
    down_full = lax.all_gather(down_weight, "ctx", axis=0, tiled=False)

    mask = jnp.any(
        routes[:, :, None] == jnp.arange(EXPERTS, dtype=jnp.int32)[None, None, :], 1
    )
    order = jnp.arange(tok, dtype=jnp.int32)
    before = (order[None, :] < order[:, None]).astype(bf16)
    rank = jnp.where(mask, dot(before, mask.astype(bf16)), -1.0)
    ranks = lax.all_to_all(
        rank.T.reshape(shard_count, expert_count, 1, tok), "wt", 0, 0, tiled=True
    )
    last = shard_count - 1
    grads_in = {0: out_low, last: shift(after(out_low, pieces[0], ranks), -1)}
    grads_in[1] = shift(after(out_low, pieces[0], ranks), 1)

    pieces, ranks = beside(pieces, ranks)
    local_rows = jnp.arange(tok, dtype=jnp.int32)
    mine = lax.dynamic_slice_in_dim(deal_row, 2 * ctx_index, 2, 0)
    prompt_place = (
        jnp.where(local_rows < block_rows, mine[0], mine[1]) * block_rows
        + local_rows % block_rows
    )
    positions = jnp.where(
        local_rows < prompt_local, prompt_place, PROMPT + (local_rows - prompt_local) % CLEN
    )
    cosine, sine = rope_tables(positions, 128)
    normed_one, turned_query, kv_low, qkv_full, output_t, rest, gain_rows = project(
        layer_input[0], cosine, sine, pieces, counts, block_places
    )
    router_full = rest[:, :EXPERTS]
    first_gain, second_gain = gain_rows[0], gain_rows[1]
    inverse_one = lax.rsqrt(jnp.mean(inputs * inputs, -1, keepdims=True) + norm_eps)
    kv_own = kv_low[prompt_local:]
    kv_pieces, grads_in[last] = beside([gather_ctx(kv_low, prompt_local)], grads_in[last])

    places = deal_row
    if context_size == 8:
        pairs = deal_row.reshape(2, 2, 2, 2)
        for axis, bit in ((0, 4), (1, 2), (2, 1)):
            pairs = jnp.where(ctx_index & bit > 0, jnp.flip(pairs, axis), pairs)
        places = pairs.reshape(-1)
    low = (mine[0] > mine[1]).astype(jnp.int32)
    starts = jnp.stack(
        [
            low * block_rows,
            (1 - low) * block_rows,
            jnp.min(mine) * block_rows,
            jnp.max(mine) * block_rows,
        ]
    ).astype(jnp.int32)
    heads = []
    for half in range(2):
        result = attention_forward(
            turned_query, kv_pieces, kv_own, places, starts, block_rows, half
        )
        if half == 0:
            result, grads_in[1] = beside(result, grads_in[1])
        if half == 0:
            turned_query = after(turned_query, result[0])
        heads.append(result)
    for d in range(last - 1, 1, -1):
        grads_in[d] = shift(grads_in[d + 1], -1)
    attended = [out for out, _ in heads]
    lse = [row for _, row in heads]

    middle, normed_two, inverse_two, gates = to_gates(
        attended,
        layer_input[0],
        output_t,
        rest,
        gain_rows,
        jnp.pad(mask.astype(f32), ((0, 0), (0, 128 - EXPERTS))),
    )

    normed_two, grads_in[last - 1] = beside(normed_two, grads_in[last - 1])
    gates_out = gates.reshape(shard_count, expert_count, 1, tok)
    gates_in = []
    for d in range(shard_count):
        piece = lax.dynamic_index_in_dim(gates_out, (wt_index + d) % shard_count, 0, False)
        gates_in.append(shift(piece, d) if d else piece)
    got = {0: normed_two}
    partial, mixed, gate_grads, rows = {}, {}, {}, []
    carried = None

    def add(a, b):
        return b if a is None else (a.astype(f32) + b.astype(f32)).astype(bf16)

    for d in [0] + list(range(last, 0, -1)):
        source = (wt_index - d) % shard_count
        rank_in = lax.dynamic_index_in_dim(ranks, source, 0, False)
        result = expert_pass(
            got[d], grads_in[d], rank_in, gates_in[d], gate_full, up_full, down_full, capacity
        )
        coming = d - 1 if d else last
        if coming:
            result, got[coming] = beside(result, shift(got[(coming + 1) % shard_count], -1))
        if d == 0:
            result, gates_in = beside(result, gates_in)
        if 0 < d <= last - 2:
            carried = shift(after(add(carried, partial[d + 2]), got[d]), -1)
            result, carried = beside(result, carried)
        mixed[d], partial[d], d_gate, *kept = result
        rows.append(kept)
        gate_grads[d] = shift(d_gate, shard_count - d) if d else d_gate
        if coming:
            got[coming] = after(got[coming], partial[d])
    carried = shift(add(carried, partial[2]), -1)
    (gate_grad, up_grad), carried, gate_grads = beside(
        up_weight_grads([(after(r[0], partial[1]), r[3], r[4]) for r in rows], context_size),
        carried,
        gate_grads,
    )
    stacked = jnp.stack([gate_grads[d] for d in range(shard_count)], 0)
    for bit in (1, 2, 4):
        if bit < shard_count:
            stacked = jnp.where(wt_index & bit > 0, jnp.roll(stacked, bit, 0), stacked)
    stacked = stacked.reshape(EXPERTS, tok)
    grad_logits = gates * (stacked - jnp.sum(gates * stacked, 0, keepdims=True))
    grad_logits = grad_logits.T.astype(bf16)
    carried = shift(add(carried, partial[1]), -1)
    down_grad, home = beside(
        down_weight_grads([(after(r[2], gate_grad, grad_logits), r[1]) for r in rows], context_size), carried
    )

    grad_normed_two = partial[0].astype(f32) + home.astype(f32)
    grad_normed_two = grad_normed_two + dot_nt(grad_logits, router_full)
    grad_mid_norm, second_gain_grad = norm_backward(
        middle, inverse_two, second_gain, grad_normed_two
    )
    grad_middle = out_grad + grad_mid_norm
    grad_branch = (resid_scale * grad_middle).astype(bf16)
    grad_attended = dot(grad_branch, output_t).astype(bf16)
    gate_share, up_share, down_share = (
        lax.psum_scatter(grad, "ctx", scatter_dimension=0, tiled=False).astype(f32)
        for grad in (gate_grad, up_grad, down_grad)
    )
    carried = None
    query = after(turned_query, grad_attended)
    d_query, d_kv, ours = [], [], []
    for half in range(2):
        result = attention_backward(
            query,
            grad_attended,
            lse[half],
            attended[half],
            cosine,
            sine,
            kv_pieces,
            kv_own,
            places,
            starts,
            block_rows,
            half,
        )
        carried = shift(after(add(carried, mixed[last - half]), home), -1)
        result, carried = beside(result, carried)
        query = after(query, result[0])
        d_query.append(result[0])
        d_kv.append(result[1])
        ours.append(result[2:])
    carried = shift(add(carried, mixed[last - 2]), -1)
    owned, carried = beside(plane_sum(d_kv), carried)
    for d in range(last - 3, 0, -1):
        carried = shift(add(carried, mixed[d]), -1)
    mixture = mixed[0].astype(f32) + carried.astype(f32)
    layer_output = (middle + resid_scale * mixture).astype(bf16)
    d_query = jnp.concatenate(d_query, 1)
    grad_kv = finish_keys(owned, ours, cosine, sine)
    grad_normed_one = dot_nt(d_query, qkv_full[:, :1024]) + dot_nt(grad_kv, qkv_full[:, 1024:])
    grad_input_norm, first_gain_grad = norm_backward(
        inputs, inverse_one, first_gain, grad_normed_one
    )
    input_grad = (grad_middle + grad_input_norm).astype(bf16)

    column = lax.broadcasted_iota(jnp.int32, (tok, 128), 1)
    query_share, output_share, key_share, value_share, small = outer_sum(
        [(normed_one, d_query), (grad_branch, attended[0]), (grad_branch, attended[1]), (normed_one, grad_kv)],
        [
            (normed_two, jnp.pad(grad_logits, ((0, 0), (0, 128 - EXPERTS)))),
            (second_gain_grad, (column == EXPERTS).astype(bf16)),
            (first_gain_grad, (column == EXPERTS + 1).astype(bf16)),
        ],
        (1024, 1024, KV_WIDTH, KV_WIDTH, 128),
    )
    return (
        layer_output[None],
        input_grad[None],
        small[:, EXPERTS + 1],
        query_share,
        key_share,
        value_share,
        output_share.T,
        small[:, EXPERTS],
        small[:, :EXPERTS],
        gate_share,
        up_share,
        down_share,
    )


def solution(mesh):
    return jax.shard_map(
        per_device,
        mesh=mesh,
        in_specs=(
            P("wt", "ctx", None),
            P(("ctx", "wt")),
            P(("ctx", "wt"), None),
            P(("ctx", "wt"), None),
            P(("ctx", "wt"), None),
            P(None, ("ctx", "wt")),
            P(("ctx", "wt")),
            P(("ctx", "wt"), None),
            P("wt", "ctx", None),
            P("wt", "ctx", None),
            P("wt", None, "ctx"),
            P("wt", "ctx", None),
            P("wt", None),
            P("wt", "ctx", None),
        ),
        out_specs=(
            P("wt", "ctx", None),
            P("wt", "ctx", None),
            P(("ctx", "wt")),
            P(("ctx", "wt"), None),
            P(("ctx", "wt"), None),
            P(("ctx", "wt"), None),
            P(None, ("ctx", "wt")),
            P(("ctx", "wt")),
            P(("ctx", "wt"), None),
            P("wt", "ctx", None),
            P("wt", "ctx", None),
            P("wt", None, "ctx"),
        ),
        check_vma=False,
    )
```
